32 devices in a mesh: section: 2 (over x), ctx: 4 (over y, core), fsdp: 4 (over z).
Axes of the slice: x: 2, y: 2, z: 4, core: 2. Of those that a mesh axis runs over, the one named last changes fastest.
Arguments:
- ends: bfloat16 [2, 2, 4, 1024, 1152], P('section', None, 'fsdp', 'ctx'), may hold values from -6 to 6
- segment_ids: int32 [2, 4, 1024], P(None, 'fsdp', 'ctx'), may hold values from 0 to 7, never falling along the last dimension, each value on 1 to 512 neighbouring positions
- w_qkv: bfloat16 [2, 1152, 1920], P('section', 'fsdp'), may hold values from -0.1875 to 0.1875
- w_out: bfloat16 [2, 1152, 1152], P('section', 'fsdp'), may hold values from -1 to 1
- w_gate_up: bfloat16 [2, 1152, 6144], P('section', 'fsdp'), may hold values from -0.1875 to 0.1875
- w_down: bfloat16 [2, 3072, 1152], P('section', 'fsdp'), may hold values from -0.109375 to 0.109375
- gains: float32 [2, 2, 1152], P('section'), may hold values from 0.5 to 1.5
Outputs:
- ends_out: float32 [2, 2, 4, 1024, 1152], P('section', None, 'fsdp', 'ctx')
- g_qkv: float32 [2, 1152, 1920], P('section', ('ctx', 'fsdp'))
- g_out: float32 [2, 1152, 1152], P('section', ('ctx', 'fsdp'))
- g_gate_up: float32 [2, 1152, 6144], P('section', ('ctx', 'fsdp'))
- g_down: float32 [2, 3072, 1152], P('section', ('ctx', 'fsdp'))
- g_gains: float32 [2, 2, 1152], P('section', None, ('ctx', 'fsdp'))
The draws below stay inside these ranges and needn't reach their ends.
Inputs may be any that keep to these rules, and one draw needn't show every extreme that they name: `segment_ids`: within a sequence the ids never fall; every document spans 1 to 512 tokens, and one spans exactly 512.
All inputs are finite; a program needn't handle non-finite values.
Results may differ from the reference program's by a relative error of at most 0.02.
Values may be sent and summed in bfloat16 or wider, within the bound.
A program may use at most 320 MiB of HBM per device.

```python
import math
import jax
import jax.numpy as jnp
import numpy as np
from jax import lax

D = 1152
HEADS = 18
KV_HEADS = 6
HEAD = 64
FF = 3072
MICRO = 2
STREAMS = 4
SEQ = 1024
DOC_MOST = 512
DOCS = 8
KVW = 384
QKV = 1920


def shard_levels(stream_key, dims, cuts, least, top_value):
    gain, own = 1.0, jax.random.fold_in(stream_key, 6)
    for axis_at, blocks in cuts:
        draws = jnp.exp(jax.random.uniform(jax.random.fold_in(own, axis_at), (blocks,), jnp.float32, least / len(cuts), top_value / len(cuts)))
        gain = gain * jnp.repeat(draws, dims[axis_at] // blocks).reshape([-1 if axis == axis_at else 1 for axis in range(len(dims))])
    return gain


def length_profile(amount, total, most, skew):
    weights = [(1 << 20) // math.isqrt(grade ** skew) + 1 for grade in range(2, amount + 1)]
    rest, given = total - most - (amount - 1), [1] * (amount - 1)
    while rest > 0:
        movable = [i for i in range(amount - 1) if given[i] < most]
        pool, remaining = sum([weights[i] for i in movable]), rest
        for i in movable:
            extra = min(most - given[i], max(1, remaining * weights[i] // pool), rest)
            given[i] = given[i] + extra
            rest = rest - extra
    return np.array([most] + given)


def ragged(own_key, count, total, reach, skew):
    if count == 2:
        one = jax.random.randint(own_key, (), max(1, total - reach), min(reach, total - 1) + 1)
        return jnp.stack([one, total - one])
    tallies = jnp.asarray(length_profile(count, total, reach, skew), jnp.int32)
    pairs = (count - 1) // 2
    donor, taker = tallies[1:1 + 2 * pairs:2], tallies[2:2 + 2 * pairs:2]
    slack = jnp.minimum(donor - 1, reach - taker)
    moved = jax.random.randint(jax.random.fold_in(own_key, 1), (pairs,), 0, 1 << 20) % (slack + 1)
    tallies = tallies.at[1:1 + 2 * pairs:2].set(donor - moved).at[2:2 + 2 * pairs:2].set(taker + moved)
    return tallies[jax.random.permutation(jax.random.fold_in(own_key, 2), count)]


def normal_values(own_key, shape, deviation, limit, cuts=(), kind=jnp.bfloat16):
    entries = deviation * jax.random.normal(own_key, shape, jnp.float32)
    if cuts:
        entries = entries * shard_levels(own_key, shape, cuts, -0.22, 0.18)
    return jnp.clip(entries, -limit, limit).astype(kind)


def setup_inputs(seed: int = 0) -> dict:
    streams_of = jax.random.split(jax.random.key(seed), 8)
    ends = normal_values(streams_of[0], (2, MICRO, STREAMS, SEQ, D), 1.0, 6.0, ((0, 2), (2, 4), (3, 4)))
    segment_ids = jax.vmap(lambda own: jnp.searchsorted(jnp.cumsum(ragged(own, DOCS, SEQ, DOC_MOST, 2)), jnp.arange(SEQ), side="right"))(jax.random.split(streams_of[1], MICRO * STREAMS)).reshape((MICRO, STREAMS, SEQ)).astype(jnp.int32)
    w_qkv = normal_values(streams_of[2], (2, D, QKV), D ** -0.5, 0.1875, ((0, 2), (1, 4)))
    w_out = normal_values(streams_of[3], (2, D, D), (D // 32) ** -0.5, 1.0, ((0, 2), (1, 4)))
    w_gate_up = normal_values(streams_of[4], (2, D, 2 * FF), D ** -0.5, 0.1875, ((0, 2), (1, 4)))
    w_down = normal_values(streams_of[5], (2, FF, D), FF ** -0.5, 0.109375, ((0, 2), (1, 4)))
    gains = jnp.clip(1.0 + 0.1 * jax.random.normal(streams_of[6], (2, 2, D), jnp.float32), 0.5, 1.5)
    return {"ends": ends, "segment_ids": segment_ids, "w_qkv": w_qkv, "w_out": w_out, "w_gate_up": w_gate_up, "w_down": w_down, "gains": gains}


@jax.custom_vjp
def low(v):
    return lax.optimization_barrier(v.astype(jnp.bfloat16)).astype(jnp.float32)

@jax.custom_vjp
def low_back(v):
    return v

def low_keep(v):
    return (low(v), None)

def low_pass(kept, grad):
    return (grad,)

def back_keep(v):
    return (v, None)

def back_low(kept, grad):
    return (low(grad),)
low.defvjp(low_keep, low_pass)
low_back.defvjp(back_keep, back_low)
EPS = 1e-05
PRECISE = lax.Precision.HIGHEST

def rms_scale(inputs, gain_row):
    scale_row = lax.rsqrt(lax.optimization_barrier(jnp.mean(inputs * inputs, axis=-1, keepdims=True)) + EPS)
    return inputs * scale_row * gain_row

def rotate(values_in, cosine, sine_table):
    half_size = values_in.shape[-1] // 2
    front = values_in[..., :half_size]
    back_half = values_in[..., half_size:]
    return jnp.concatenate([front * cosine - back_half * sine_table, back_half * cosine + front * sine_table], axis=-1)

def attend(queries, key_heads, value_heads, segment):
    block_rows = math.gcd(SEQ, 512)
    block_count = SEQ // block_rows
    places = jnp.arange(SEQ, dtype=jnp.int32)
    score_scale = HEAD ** (-0.5)

    def one_block(block_index):
        first_row = (block_index * block_rows).astype(jnp.int32)
        query_block = lax.dynamic_slice_in_dim(queries, first_row, block_rows, 0)
        query_seg = lax.dynamic_slice_in_dim(segment, first_row, block_rows, 0)
        query_pos = first_row + jnp.arange(block_rows, dtype=jnp.int32)
        scores = low_back(jnp.einsum('qkgd,tkd->kgqt', query_block, key_heads, precision=PRECISE) * score_scale)
        allowed = (places[None, :] <= query_pos[:, None]) & (segment[None, :] == query_seg[:, None])
        masked = jnp.where(allowed, scores, -1e+30)
        row_top = lax.optimization_barrier(jnp.max(masked, axis=-1, keepdims=True))
        row_total = lax.optimization_barrier(jnp.sum(jnp.exp(masked - row_top), axis=-1, keepdims=True))
        log_total = row_top + jnp.log(row_total)
        probs = low(jnp.where(allowed, jnp.exp(masked - log_total), 0.0))
        return jnp.einsum('kgqt,tkd->qkgd', probs, value_heads, precision=PRECISE)
    blocks_out = lax.map(jax.checkpoint(one_block), jnp.arange(block_count, dtype=jnp.int32))
    return blocks_out.reshape(SEQ, D)

def layer_forward(inputs, w_qkv, w_out, w_gate_up, w_down, gain_pair, segment, cosine, sine_table):
    group_size = HEADS // KV_HEADS
    normed = low(rms_scale(inputs, gain_pair[0]))
    mixed = jnp.dot(normed, w_qkv, precision=PRECISE)
    queries = low(rotate(low_back(mixed[:, :D]).reshape(SEQ, HEADS, HEAD), cosine, sine_table))
    key_heads = low(rotate(low_back(mixed[:, D:D + KVW]).reshape(SEQ, KV_HEADS, HEAD), cosine, sine_table))
    value_heads = low(low_back(mixed[:, D + KVW:])).reshape(SEQ, KV_HEADS, HEAD)
    attended = attend(queries.reshape(SEQ, KV_HEADS, group_size, HEAD), key_heads, value_heads, segment)
    context = low(low_back(attended))
    hidden = inputs + low_back(jnp.dot(context, w_out, precision=PRECISE))
    second = low(rms_scale(hidden, gain_pair[1]))
    gate_up = jnp.dot(second, w_gate_up, precision=PRECISE)
    gate_pre = low_back(gate_up[:, :FF])
    up_pre = low_back(gate_up[:, FF:])
    inner_act = low(jax.nn.silu(gate_pre) * up_pre)
    return hidden + low_back(jnp.dot(inner_act, w_down, precision=PRECISE))

def network(first_input, weights, segment, cosine, sine_table):
    w_qkv, w_out, w_gate_up, w_down, gains = weights
    hidden_one = layer_forward(first_input, w_qkv[0], w_out[0], w_gate_up[0], w_down[0], gains[0], segment, cosine, sine_table)
    passed = low_back(low(hidden_one))
    return layer_forward(passed, w_qkv[1], w_out[1], w_gate_up[1], w_down[1], gains[1], segment, cosine, sine_table)

def reference(ends, segment_ids, w_qkv, w_out, w_gate_up, w_down, gains):
    params = (w_qkv.astype(jnp.float32), w_out.astype(jnp.float32), w_gate_up.astype(jnp.float32), w_down.astype(jnp.float32), gains.astype(jnp.float32))
    positions = jnp.arange(SEQ).astype(jnp.float32)
    frequency = 10000.0 ** (-(jnp.arange(HEAD // 2).astype(jnp.float32) * 2.0 / HEAD))
    angle_table = positions[:, None] * frequency[None, :]
    cosine = jnp.cos(angle_table)[:, None, :]
    sine_table = jnp.sin(angle_table)[:, None, :]
    inputs = ends[0].astype(jnp.float32).reshape(MICRO * STREAMS, SEQ, D)
    cotangents = ends[1].astype(jnp.float32).reshape(MICRO * STREAMS, SEQ, D)
    segments = segment_ids.reshape(MICRO * STREAMS, SEQ)

    def one_sequence(grad_sums, sequence):
        layer_input, cotangent, segment = sequence

        def forward(first_input, *weights):
            return network(first_input, weights, segment, cosine, sine_table)
        output, pullback = jax.vjp(forward, layer_input, *params)
        gradients = pullback(cotangent)
        return (tuple((running + addend for running, addend in zip(grad_sums, gradients[1:]))), (output, gradients[0]))
    start_sums = tuple((jnp.zeros_like(weight) for weight in params))
    grad_sums, (outputs, input_grads) = lax.scan(one_sequence, start_sums, (inputs, cotangents, segments))
    ends_out = jnp.stack([input_grads, outputs]).reshape(2, MICRO, STREAMS, SEQ, D)
    return (ends_out, grad_sums[0], grad_sums[1], grad_sums[2], grad_sums[3], grad_sums[4])
```

```python
import math

import jax
import jax.numpy as jnp
from jax import lax
from jax.experimental import pallas as pl
from jax.experimental.pallas import tpu as pltpu
from jax.sharding import PartitionSpec as P

MESH = pl.DeviceIdType.MESH

D = 1152
HEADS = 18
KV_HEADS = 6
HEAD = 64
FF = 3072
KVW = 384


EPS = 1e-05


def shifted(x, axis, by):
    size = lax.axis_size(axis)
    pairs = [(i, i + by) for i in range(size) if 0 <= i + by < size]
    return lax.ppermute(x, axis, pairs)


def rotate(values_in, cosine, sine_table):
    half_size = values_in.shape[-1] // 2
    front = values_in[..., :half_size]
    back_half = values_in[..., half_size:]
    return jnp.concatenate(
        [front * cosine - back_half * sine_table, back_half * cosine + front * sine_table], axis=-1
    )


def rotate_back(gradient, cosine, sine_table):
    half_size = gradient.shape[-1] // 2
    front = gradient[..., :half_size]
    back_half = gradient[..., half_size:]
    return jnp.concatenate(
        [front * cosine + back_half * sine_table, back_half * cosine - front * sine_table], axis=-1
    )


def norm_forward(inputs, gain_row):
    scale_row = lax.rsqrt(jnp.mean(inputs * inputs, axis=-1, keepdims=True) + EPS)
    unit_rows = inputs * scale_row
    return (unit_rows * gain_row, unit_rows, scale_row)


def norm_backward(gradient, unit_rows, scale_row, gain_row):
    unit_grad = gradient * gain_row
    gain_grad = jnp.sum(gradient * unit_rows, axis=0)
    input_grad = scale_row * (
        unit_grad - unit_rows * jnp.mean(unit_grad * unit_rows, axis=-1, keepdims=True)
    )
    return (input_grad, gain_grad)


def outer_product(left, right):
    return lax.dot_general(
        left, right, (((0,), (0,)), ((), ())), preferred_element_type=jnp.float32
    )


def times_transposed(left, right):
    return lax.dot_general(
        left, right, (((1,), (1,)), ((), ())), preferred_element_type=jnp.float32
    )


def block_needed(first_row, block_rows, seg_full, seg_rows, query_pos):
    last_seg = lax.dynamic_index_in_dim(seg_full, first_row + block_rows - 1, 0, keepdims=False)
    return (first_row <= query_pos[-1]) & (last_seg >= seg_rows[0])


def attend_forward(queries4, key_all, value_all, seg_rows, seg_full, query_pos):
    tok_rows = queries4.shape[0]
    group_size = HEADS // KV_HEADS
    score_scale = HEAD ** (-0.5)
    total_rows = key_all.shape[0]
    block_rows = math.gcd(total_rows, 512)
    block_count = total_rows // block_rows
    key_heads = key_all.reshape(total_rows, KV_HEADS, HEAD)
    value_heads = value_all.reshape(total_rows, KV_HEADS, HEAD)

    def block_scores(block_index):
        first_row = block_index * block_rows
        key_block = lax.dynamic_slice_in_dim(key_heads, first_row, block_rows, 0)
        value_block = lax.dynamic_slice_in_dim(value_heads, first_row, block_rows, 0)
        seg_block = lax.dynamic_slice_in_dim(seg_full, first_row, block_rows, 0)
        key_pos = first_row + jnp.arange(block_rows, dtype=jnp.int32)
        raw_scores = (
            jnp.einsum("qkgd,tkd->kgqt", queries4, key_block, preferred_element_type=jnp.float32)
            * score_scale
        )
        allowed = (key_pos[None, :] <= query_pos[:, None]) & (
            seg_block[None, :] == seg_rows[:, None]
        )
        return (jnp.where(allowed, raw_scores, -1e30), allowed, value_block)

    def first_pass(state_pair, block_index):

        def first_work(state_in):
            row_top, row_total = state_in
            masked, allowed, value_block = block_scores(block_index)
            new_top = jnp.maximum(row_top, jnp.max(masked, axis=-1))
            new_total = row_total * jnp.exp(row_top - new_top) + jnp.sum(
                jnp.exp(masked - new_top[..., None]), axis=-1
            )
            return (new_top, new_total)

        needed = block_needed(block_index * block_rows, block_rows, seg_full, seg_rows, query_pos)
        return (lax.cond(needed, first_work, lambda state_in: state_in, state_pair), None)

    start_state = (
        jnp.full((KV_HEADS, group_size, tok_rows), -1e30, jnp.float32),
        jnp.zeros((KV_HEADS, group_size, tok_rows), jnp.float32),
    )
    block_ids = jnp.arange(block_count, dtype=jnp.int32)
    (row_top, row_total), ignored = lax.scan(first_pass, start_state, block_ids)
    log_total = row_top + jnp.log(row_total)

    def second_pass(summed, block_index):

        def second_work(summed_in):
            masked, allowed, value_block = block_scores(block_index)
            prob_low = jnp.where(allowed, jnp.exp(masked - log_total[..., None]), 0.0).astype(
                jnp.bfloat16
            )
            added = jnp.einsum(
                "kgqt,tkd->qkgd", prob_low, value_block, preferred_element_type=jnp.float32
            )
            return summed_in + added

        needed = block_needed(block_index * block_rows, block_rows, seg_full, seg_rows, query_pos)
        return (lax.cond(needed, second_work, lambda summed_in: summed_in, summed), None)

    start_sum = jnp.zeros((tok_rows, KV_HEADS, group_size, HEAD), jnp.float32)
    attended, ignored = lax.scan(second_pass, start_sum, block_ids)
    return (attended.reshape(tok_rows, D), log_total)


def layer_forward(inputs, weights, gain_pair, seg_rows, seg_full, query_pos, cosine, sine_table):
    w_qkv, w_out, w_gate_up, w_down = weights
    tok_rows = inputs.shape[0]
    group_size = HEADS // KV_HEADS
    normed, unit_one, scale_one = norm_forward(inputs, gain_pair[0])
    normed_low = normed.astype(jnp.bfloat16)
    mixed_proj = jnp.dot(normed_low, w_qkv, preferred_element_type=jnp.float32)
    queries = rotate(mixed_proj[:, :D].reshape(tok_rows, HEADS, HEAD), cosine, sine_table).astype(
        jnp.bfloat16
    )
    key_rows = rotate(
        mixed_proj[:, D : D + KVW].reshape(tok_rows, KV_HEADS, HEAD), cosine, sine_table
    )
    key_rows = key_rows.astype(jnp.bfloat16).reshape(tok_rows, KVW)
    value_rows = mixed_proj[:, D + KVW :].astype(jnp.bfloat16)
    key_all, value_all = (
        lax.all_gather(key_rows, "ctx", axis=0, tiled=True),
        lax.all_gather(value_rows, "ctx", axis=0, tiled=True),
    )
    queries4 = queries.reshape(tok_rows, KV_HEADS, group_size, HEAD)
    attended, log_total = attend_forward(
        queries4, key_all, value_all, seg_rows, seg_full, query_pos
    )
    context = attended.astype(jnp.bfloat16)
    hidden = inputs + jnp.dot(context, w_out, preferred_element_type=jnp.float32)
    second, unit_two, scale_two = norm_forward(hidden, gain_pair[1])
    second_low = second.astype(jnp.bfloat16)
    gate_up = jnp.dot(second_low, w_gate_up, preferred_element_type=jnp.float32)
    gate_pre = gate_up[:, :FF]
    up_pre = gate_up[:, FF:]
    inner_act = (jax.nn.silu(gate_pre) * up_pre).astype(jnp.bfloat16)
    result = hidden + jnp.dot(inner_act, w_down, preferred_element_type=jnp.float32)
    saved_acts = (
        normed_low,
        queries4,
        key_all,
        value_all,
        attended,
        log_total,
        context,
        unit_one,
        scale_one,
        unit_two,
        scale_two,
        second_low,
        gate_pre,
        up_pre,
        inner_act,
    )
    return (result, saved_acts)


def layer_backward(
    grad_low, saved_acts, weights, gain_pair, seg_rows, seg_full, query_pos, cosine, sine_table
):
    w_qkv, w_out, w_gate_up, w_down = weights
    (
        normed_low,
        queries4,
        key_all,
        value_all,
        attended,
        log_total,
        context,
        unit_one,
        scale_one,
        unit_two,
        scale_two,
        second_low,
        gate_pre,
        up_pre,
        inner_act,
    ) = saved_acts
    tok_rows = grad_low.shape[0]
    group_size = HEADS // KV_HEADS
    score_scale = HEAD ** (-0.5)
    grad_out = grad_low.astype(jnp.float32)
    grad_inner = times_transposed(grad_low, w_down)
    sigmoid_gate = jax.nn.sigmoid(gate_pre)
    silu_gate = gate_pre * sigmoid_gate
    grad_gate = grad_inner * up_pre * sigmoid_gate * (1.0 + gate_pre * (1.0 - sigmoid_gate))
    grad_up = grad_inner * silu_gate
    grad_both = jnp.concatenate([grad_gate, grad_up], axis=1).astype(jnp.bfloat16)
    grad_second = times_transposed(grad_both, w_gate_up)
    grad_norm_two, gain_two = norm_backward(grad_second, unit_two, scale_two, gain_pair[1])
    grad_hidden = grad_out + grad_norm_two
    hidden_low = grad_hidden.astype(jnp.bfloat16)
    grad_context = times_transposed(hidden_low, w_out).astype(jnp.bfloat16)
    grad_context4 = grad_context.reshape(tok_rows, KV_HEADS, group_size, HEAD)
    attended4 = attended.reshape(tok_rows, KV_HEADS, group_size, HEAD)
    row_delta = jnp.einsum("qkgd,qkgd->kgq", grad_context4.astype(jnp.float32), attended4)
    total_rows = seg_full.shape[0]
    start_state = (
        jnp.zeros((tok_rows, KV_HEADS, group_size, HEAD), jnp.float32),
        jnp.zeros((total_rows, 2 * KVW), jnp.float32),
    )
    key_piece, value_piece = key_all, value_all
    piece_rows = key_piece.shape[0]
    block_rows = math.gcd(piece_rows, 512)
    block_count = piece_rows // block_rows

    def one_block(block_index, inner_state):
        offset = block_index * block_rows

        def one_work(state_in):
            grad_query, grad_kv = state_in
            key_block = lax.dynamic_slice_in_dim(key_piece, offset, block_rows, 0).reshape(
                block_rows, KV_HEADS, HEAD
            )
            value_block = lax.dynamic_slice_in_dim(value_piece, offset, block_rows, 0).reshape(
                block_rows, KV_HEADS, HEAD
            )
            seg_block = lax.dynamic_slice_in_dim(seg_full, offset, block_rows, 0)
            key_pos = offset + jnp.arange(block_rows, dtype=jnp.int32)
            raw_scores = (
                jnp.einsum(
                    "qkgd,tkd->kgqt", queries4, key_block, preferred_element_type=jnp.float32
                )
                * score_scale
            )
            allowed = (key_pos[None, :] <= query_pos[:, None]) & (
                seg_block[None, :] == seg_rows[:, None]
            )
            prob_full = jnp.where(allowed, jnp.exp(raw_scores - log_total[..., None]), 0.0)
            prob_low = prob_full.astype(jnp.bfloat16)
            grad_value = jnp.einsum(
                "kgqt,qkgd->tkd", prob_low, grad_context4, preferred_element_type=jnp.float32
            )
            grad_prob = jnp.einsum(
                "qkgd,tkd->kgqt", grad_context4, value_block, preferred_element_type=jnp.float32
            )
            grad_scores = (prob_full * (grad_prob - row_delta[..., None])).astype(jnp.bfloat16)
            grad_query = (
                grad_query
                + jnp.einsum(
                    "kgqt,tkd->qkgd", grad_scores, key_block, preferred_element_type=jnp.float32
                )
                * score_scale
            )
            grad_key = (
                jnp.einsum(
                    "kgqt,qkgd->tkd", grad_scores, queries4, preferred_element_type=jnp.float32
                )
                * score_scale
            )
            new_rows = jnp.concatenate(
                [grad_key.reshape(block_rows, KVW), grad_value.reshape(block_rows, KVW)], axis=1
            )
            old_rows = lax.dynamic_slice_in_dim(grad_kv, offset, block_rows, 0)
            grad_kv = lax.dynamic_update_slice_in_dim(grad_kv, old_rows + new_rows, offset, 0)
            return (grad_query, grad_kv)

        needed = block_needed(offset, block_rows, seg_full, seg_rows, query_pos)
        return lax.cond(needed, one_work, lambda state_in: state_in, inner_state)

    grad_query, grad_kv_all = lax.fori_loop(0, block_count, one_block, start_state)
    grad_kv_own = lax.psum_scatter(
        grad_kv_all.astype(jnp.bfloat16), "ctx", scatter_dimension=0, tiled=True
    ).astype(jnp.float32)
    grad_q_pre = rotate_back(grad_query.reshape(tok_rows, HEADS, HEAD), cosine, sine_table).reshape(
        tok_rows, D
    )
    grad_k_pre = rotate_back(
        grad_kv_own[:, :KVW].reshape(tok_rows, KV_HEADS, HEAD), cosine, sine_table
    ).reshape(tok_rows, KVW)
    grad_mixed = jnp.concatenate([grad_q_pre, grad_k_pre, grad_kv_own[:, KVW:]], axis=1).astype(
        jnp.bfloat16
    )
    grad_normed = times_transposed(grad_mixed, w_qkv)
    grad_norm_one, gain_one = norm_backward(grad_normed, unit_one, scale_one, gain_pair[0])
    grad_input = grad_hidden + grad_norm_one
    operand_pairs = (
        normed_low,
        context,
        second_low,
        inner_act,
        grad_mixed,
        hidden_low,
        grad_both,
        grad_low,
    )
    return (grad_input, operand_pairs, jnp.stack([gain_one, gain_two]))


def gather_kernel(qo, gu, dn, fqo, fgu, fdn, own_sem, back_sem, zs, zr, ys, yr, cs, cr, es, er):
    place = lax.axis_index("ctx")
    z = lax.axis_index("fsdp")
    last = lax.axis_size("fsdp") - 1
    y, k = place // 2, place % 2
    y_mate = {"ctx": (1 - y) * 2 + k}
    k_mate = {"ctx": y * 2 + 1 - k}
    width = qo.shape[0]
    deep = dn.shape[0]
    half = width // 2
    chunks = [(0, p) for p in range(3)] + [(1, p) for p in range(3)] + [(2, p) for p in range(2)]
    wholes = (fqo, fgu, fdn)
    owns = (qo, gu, dn)

    def view(refs, shard, yy, kk, chunk):
        m, p = chunk
        ref = refs[m]
        if m == 2:
            rows = deep // 8
            first = shard * deep + (yy * 2 + kk) * (deep // 4) + p * rows
            return ref.at[pl.ds(pl.multiple_of(first, 16), rows), :]
        rows = half // 3
        cols = ref.shape[1] // 2
        first = shard * width + yy * half + p * rows
        return ref.at[pl.ds(pl.multiple_of(first, 16), rows), pl.ds(pl.multiple_of(kk * cols, 128), cols)]

    barrier = pltpu.get_barrier_semaphore()
    for mate in (y_mate, k_mate):
        pl.semaphore_signal(barrier, inc=1, device_id=mate, device_id_type=MESH)

    @pl.when(z > 0)
    def _():
        pl.semaphore_signal(barrier, inc=1, device_id={"fsdp": z - 1}, device_id_type=MESH)

    @pl.when(z < last)
    def _():
        pl.semaphore_signal(barrier, inc=1, device_id={"fsdp": z + 1}, device_id_type=MESH)

    pl.semaphore_wait(barrier, 2 + jnp.where(z > 0, 1, 0) + jnp.where(z < last, 1, 0))

    def z_copy(shard, j, to, first, back):
        chunk = chunks[j]
        src = view(owns, 0, y, k, chunk) if first else view(wholes, shard, y, k, chunk)
        return pltpu.make_async_remote_copy(
            src_ref=src, dst_ref=view(wholes, shard, y, k, chunk),
            send_sem=back_sem.at[j] if back else zs.at[shard, j], recv_sem=zr.at[shard, j],
            device_id={"fsdp": to}, device_id_type=MESH)

    def mate_copy(shard, j, yy, mate, send, recv):
        chunk = chunks[j]
        ref = view(wholes, shard, yy, k, chunk)
        return pltpu.make_async_remote_copy(
            src_ref=ref, dst_ref=ref, send_sem=send.at[shard, j], recv_sem=recv.at[shard, j],
            device_id=mate, device_id_type=MESH)

    def arrive(shard, j, yy, kk, recv):
        ref = view(wholes, shard, yy, kk, chunks[j])
        pltpu.make_async_remote_copy(
            src_ref=ref, dst_ref=ref, send_sem=recv.at[shard, j], recv_sem=recv.at[shard, j],
            device_id=k_mate, device_id_type=MESH).wait_recv()

    for j in range(len(chunks)):
        @pl.when(z < last)
        def _():
            z_copy(z, j, z + 1, True, False).start()

        @pl.when(z > 0)
        def _():
            z_copy(z, j, z - 1, True, True).start()
    locals_ = []
    for m in range(3):
        rows = owns[m].shape[0]
        locals_.append(pltpu.make_async_remote_copy(
            src_ref=owns[m], dst_ref=wholes[m].at[pl.ds(pl.multiple_of(z * rows, 16), rows), :],
            send_sem=own_sem.at[0, m], recv_sem=own_sem.at[1, m], device_id=k_mate, device_id_type=MESH))
    for copy in locals_:
        copy.start()

    def sides(d):
        return ((z - d >= 0, z - d, z + 1, z < last), (z + d <= last, z + d, z - 1, z > 0))

    def relay(d, j):
        for valid, shard, onward, more in sides(d):
            @pl.when(valid)
            def _():
                arrive(shard, j, y, k, zr)
                if d < 3:
                    @pl.when(more)
                    def _():
                        z_copy(shard, j, onward, False, False).start()
                mate_copy(shard, j, y, y_mate, ys, yr).start()
                mate_copy(shard, j, y, k_mate, cs, cr).start()

    def across(d, j):
        for valid, shard, onward, more in sides(d):
            @pl.when(valid)
            def _():
                arrive(shard, j, 1 - y, k, yr)
                mate_copy(shard, j, 1 - y, k_mate, es, er).start()

    order = [(d, j) for d in (1, 2, 3) for j in range(len(chunks))]
    lag = 1
    for i, (d, j) in enumerate(order):
        relay(d, j)
        if i >= lag:
            across(*order[i - lag])
    for d, j in order[len(order) - lag:]:
        across(d, j)
    for d, j in order:
        for valid, shard, onward, more in sides(d):
            @pl.when(valid)
            def _():
                arrive(shard, j, y, 1 - k, cr)
                arrive(shard, j, 1 - y, 1 - k, er)
                mate_copy(shard, j, y, y_mate, ys, yr).wait_send()
                mate_copy(shard, j, y, k_mate, cs, cr).wait_send()
                mate_copy(shard, j, 1 - y, k_mate, es, er).wait_send()
                if d < 3:
                    @pl.when(more)
                    def _():
                        z_copy(shard, j, onward, False, False).wait_send()
    for j in range(len(chunks)):
        @pl.when(z < last)
        def _():
            z_copy(z, j, z + 1, True, False).wait_send()

        @pl.when(z > 0)
        def _():
            z_copy(z, j, z - 1, True, True).wait_send()
    for copy in locals_:
        copy.wait()


def gather_weights(qo, gu, dn):
    size = lax.axis_size("fsdp")
    any_spec = pl.BlockSpec(memory_space=pl.ANY)
    return pl.pallas_call(
        gather_kernel,
        out_shape=tuple(jax.ShapeDtypeStruct((size * w.shape[0], w.shape[1]), w.dtype) for w in (qo, gu, dn)),
        in_specs=[any_spec] * 3,
        out_specs=(any_spec,) * 3,
        scratch_shapes=[pltpu.SemaphoreType.DMA((2, 3)), pltpu.SemaphoreType.DMA((8,))]
        + [pltpu.SemaphoreType.DMA((4, 8))] * 8,
        compiler_params=pltpu.CompilerParams(collective_id=1, has_side_effects=True),
        name="weights_gather",
    )(qo, gu, dn)


DOWN_COLS = 128
WIDE_COLS = 384
NEAR, MID, FAR, SUMS = 2, 4, 8, 12


def reduce_kernel(
    inner_t, second_t, normed_t, context_t, g_low, both, mixed, hidden_low,
    o_down, o_gate_up, o_qkv, o_out,
    *scratch,
):
    kinds = (scratch[0:9], scratch[9:18])
    (near_send, near_recv, mid_send, mid_recv, right_send, right_recv, left_send, left_recv,
     near_free, mid_free, right_free, left_free) = scratch[18:]
    place = lax.axis_index("ctx")
    z = lax.axis_index("fsdp")
    last = lax.axis_size("fsdp") - 1
    y, k = place // 2, place % 2
    y_mate = {"ctx": (1 - y) * 2 + k}
    k_mate = {"ctx": y * 2 + 1 - k}
    right, left = {"fsdp": z + 1}, {"fsdp": z - 1}
    f32, low = jnp.float32, jnp.bfloat16

    n_down = g_low.shape[1] // DOWN_COLS
    n_both = both.shape[1] // WIDE_COLS
    n_mixed = mixed.shape[1] // WIDE_COLS
    n_out = hidden_low.shape[1] // WIDE_COLS
    end_both = n_down + n_both
    end_mixed = end_both + n_mixed
    total = end_mixed + n_out
    hop = 2
    first_z = 3
    final_lag = first_z + hop * 3

    barrier = pltpu.get_barrier_semaphore()
    for mate in (y_mate, k_mate):
        pl.semaphore_signal(barrier, inc=1, device_id=mate, device_id_type=MESH)

    @pl.when(z > 0)
    def _():
        pl.semaphore_signal(barrier, inc=1, device_id=left, device_id_type=MESH)

    @pl.when(z < last)
    def _():
        pl.semaphore_signal(barrier, inc=1, device_id=right, device_id_type=MESH)

    pl.semaphore_wait(barrier, 2 + jnp.where(z > 0, 1, 0) + jnp.where(z < last, 1, 0))

    def typed(j, work):
        @pl.when((j >= 0) & (j < n_down))
        def _():
            work(0)

        @pl.when((j >= n_down) & (j < total))
        def _():
            work(1)

    def near_copy(kind, j):
        out_near, own_near, in_near = kinds[kind][0:3]
        slot = j % NEAR
        return pltpu.make_async_remote_copy(
            src_ref=out_near.at[slot], dst_ref=in_near.at[slot], send_sem=near_send.at[slot],
            recv_sem=near_recv.at[slot], device_id=k_mate, device_id_type=MESH)

    def mid_copy(kind, j):
        out_mid, in_mid = kinds[kind][3:5]
        slot = j % MID
        return pltpu.make_async_remote_copy(
            src_ref=out_mid.at[slot], dst_ref=in_mid.at[slot], send_sem=mid_send.at[slot],
            recv_sem=mid_recv.at[slot], device_id=y_mate, device_id_type=MESH)

    def line_rows(kind, step, rightward):
        rows = kinds[kind][5].shape[1]
        part = rows // 4
        if rightward:
            start = (part * (step + 1)) // 16 * 16
            return start, rows - start
        return 0, (part * step + 15) // 16 * 16

    def line_copy(kind, j, step, rightward):
        start, count = line_rows(kind, step, rightward)
        src, dst = (kinds[kind][6], kinds[kind][7]) if rightward else (kinds[kind][6], kinds[kind][8])
        lane = 0 if rightward else 1
        return pltpu.make_async_remote_copy(
            src_ref=src.at[lane, j % NEAR, pl.ds(start, count), :],
            dst_ref=dst.at[j % FAR, pl.ds(start, count), :],
            send_sem=(right_send if rightward else left_send).at[j % NEAR],
            recv_sem=(right_recv if rightward else left_recv).at[j % FAR],
            device_id=right if rightward else left, device_id_type=MESH)

    def multiply(kind, j, lhs, rhs, first, cols):
        out_near, own_near = kinds[kind][0:2]
        slot = j % NEAR
        rows = own_near.shape[2]
        columns = pl.ds(pl.multiple_of((j - first) * cols, 128), cols)
        block = rhs[:, columns]
        for yy in range(2):
            for mine in (False, True):
                kk = k if mine else 1 - k
                at = pl.ds(pl.multiple_of((yy * 2 + kk) * rows, 16), rows)
                part = jnp.dot(lhs[at, :], block, preferred_element_type=f32)
                (own_near if mine else out_near)[slot, yy] = part.astype(low)

    def stage_near(j):
        def work(kind):
            @pl.when(j >= NEAR)
            def _():
                near_copy(kind, j).wait_send()

        @pl.when((j >= NEAR) & (j < total))
        def _():
            typed(j - NEAR, lambda kind: near_copy(kind, j - NEAR).wait_send())

        @pl.when(j < n_down)
        def _():
            multiply(0, j, inner_t, g_low, 0, DOWN_COLS)

        @pl.when((j >= n_down) & (j < end_both))
        def _():
            multiply(1, j, second_t, both, n_down, WIDE_COLS)

        @pl.when((j >= end_both) & (j < end_mixed))
        def _():
            multiply(1, j, normed_t, mixed, end_both, WIDE_COLS)

        @pl.when((j >= end_mixed) & (j < total))
        def _():
            multiply(1, j, context_t, hidden_low, end_mixed, WIDE_COLS)

        @pl.when((j >= NEAR) & (j < total))
        def _():
            pl.semaphore_wait(near_free, 1)

        typed(j, lambda kind: near_copy(kind, j).start())

    def stage_mid(j):
        def work(kind):
            out_near, own_near, in_near, out_mid, in_mid, sums = kinds[kind][0:6]
            near_copy(kind, j).wait_recv()
            slot = j % NEAR
            out_mid[j % MID] = (own_near[slot, 1 - y].astype(f32) + in_near[slot, 1 - y].astype(f32)).astype(low)
            sums[j % SUMS] = own_near[slot, y].astype(f32) + in_near[slot, y].astype(f32)

        @pl.when((j >= MID) & (j < total))
        def _():
            typed(j - MID, lambda kind: mid_copy(kind, j - MID).wait_send())

        typed(j, work)

        @pl.when((j >= 0) & (j + NEAR < total))
        def _():
            pl.semaphore_signal(near_free, inc=1, device_id=k_mate, device_id_type=MESH)

        @pl.when((j >= MID) & (j < total))
        def _():
            pl.semaphore_wait(mid_free, 1)

        typed(j, lambda kind: mid_copy(kind, j).start())

    def stage_sum(j):
        def work(kind):
            in_mid, sums = kinds[kind][4:6]
            mid_copy(kind, j).wait_recv()
            sums[j % SUMS] = sums[j % SUMS] + in_mid[j % MID].astype(f32)

        typed(j, work)

        @pl.when((j >= 0) & (j + MID < total))
        def _():
            pl.semaphore_signal(mid_free, inc=1, device_id=y_mate, device_id_type=MESH)

    def stage_line(i, rightward):
        free = right_free if rightward else left_free
        for at in range(4):
            step = at if rightward else 3 - at
            if step == 3:
                continue
            j = i - first_z - hop * step

            @pl.when((z == at) & (j >= 0) & (j < total))
            def _(at=at, step=step, j=j):
                @pl.when(j >= NEAR)
                def _():
                    typed(j - NEAR, lambda kind: line_copy(kind, j - NEAR, at, rightward).wait_send())

                def work(kind):
                    sums, out_line, in_right, in_left = kinds[kind][5:9]
                    start, count = line_rows(kind, at, rightward)
                    rows = pl.ds(start, count)
                    value = sums[j % SUMS, rows, :]
                    if step > 0:
                        came = line_rows(kind, at - 1 if rightward else at + 1, rightward)
                        arrive = line_copy(kind, j, at - 1 if rightward else at + 1, rightward)
                        arrive.wait_recv()
                        value = value + (in_right if rightward else in_left)[j % FAR, rows, :].astype(f32)
                    out_line[0 if rightward else 1, j % NEAR, rows, :] = value.astype(low)

                typed(j, work)

                @pl.when(j >= FAR)
                def _():
                    pl.semaphore_wait(free, 1)

                typed(j, lambda kind: line_copy(kind, j, at, rightward).start())

    def store(kind, j, value):
        if kind == 0:
            o_down[:, pl.ds(pl.multiple_of(j * DOWN_COLS, 128), DOWN_COLS)] = value
            return
        for out, first, end in ((o_gate_up, n_down, end_both), (o_qkv, end_both, end_mixed), (o_out, end_mixed, total)):
            @pl.when((j >= first) & (j < end))
            def _(out=out, first=first):
                out[:, pl.ds(pl.multiple_of((j - first) * WIDE_COLS, 128), WIDE_COLS)] = value

    def stage_final(j):
        for at in range(4):
            @pl.when((z == at) & (j >= 0) & (j < total))
            def _(at=at):
                def work(kind):
                    sums, out_line, in_right, in_left = kinds[kind][5:9]
                    part = sums.shape[1] // 4
                    if at == 3:
                        line_copy(kind, j, 2, True).wait_recv()
                    if at == 0:
                        line_copy(kind, j, 1, False).wait_recv()
                    low_at = at * part // 16 * 16
                    high_at = (at * part + part + 15) // 16 * 16
                    rows = pl.ds(low_at, high_at - low_at)
                    value = sums[j % SUMS, rows, :]
                    if at > 0:
                        value = value + in_right[j % FAR, rows, :].astype(f32)
                    if at < 3:
                        value = value + in_left[j % FAR, rows, :].astype(f32)
                    shift = at * part - low_at
                    store(kind, j, value[shift:shift + part])

                typed(j, work)
                if at > 0:
                    @pl.when(j + FAR < total)
                    def _():
                        pl.semaphore_signal(right_free, inc=1, device_id=left, device_id_type=MESH)
                if at < 3:
                    @pl.when(j + FAR < total)
                    def _():
                        pl.semaphore_signal(left_free, inc=1, device_id=right, device_id_type=MESH)

    def iteration(i, carry):
        stage_near(i)
        stage_mid(i - 1)
        stage_sum(i - 3)
        stage_line(i, True)
        stage_line(i, False)
        stage_final(i - final_lag)
        return carry

    lax.fori_loop(0, total + final_lag, iteration, 0)
    for j in range(total - NEAR, total):
        near_copy(1, j).wait_send()
        for at in range(3):
            @pl.when(z == at)
            def _(at=at):
                line_copy(1, j, at, True).wait_send()

            @pl.when(z == at + 1)
            def _(at=at):
                line_copy(1, j, at + 1, False).wait_send()
    for j in range(total - MID, total):
        mid_copy(1, j).wait_send()


def reduce_grads(inner_t, second_t, normed_t, context_t, g_low, both, mixed, hidden_low):
    ops = (inner_t, second_t, normed_t, context_t, g_low, both, mixed, hidden_low)
    low, f32 = jnp.bfloat16, jnp.float32
    scratch = []
    for rows, cols in ((inner_t.shape[0] // 4, DOWN_COLS), (second_t.shape[0] // 4, WIDE_COLS)):
        scratch += [
            pltpu.VMEM((NEAR, 2, rows, cols), low), pltpu.VMEM((NEAR, 2, rows, cols), low), pltpu.VMEM((NEAR, 2, rows, cols), low),
            pltpu.VMEM((MID, rows, cols), low), pltpu.VMEM((MID, rows, cols), low),
            pltpu.VMEM((SUMS, rows, cols), f32),
            pltpu.VMEM((2, NEAR, rows, cols), low),
            pltpu.VMEM((FAR, rows, cols), low), pltpu.VMEM((FAR, rows, cols), low)]
    sem = pltpu.SemaphoreType
    scratch += [sem.DMA((NEAR,)), sem.DMA((NEAR,)), sem.DMA((MID,)), sem.DMA((MID,)),
                sem.DMA((NEAR,)), sem.DMA((FAR,)), sem.DMA((NEAR,)), sem.DMA((FAR,)),
                sem.REGULAR, sem.REGULAR, sem.REGULAR, sem.REGULAR]
    outs = ((inner_t.shape[0] // 16, g_low.shape[1]), (second_t.shape[0] // 16, both.shape[1]),
            (normed_t.shape[0] // 16, mixed.shape[1]), (context_t.shape[0] // 16, hidden_low.shape[1]))
    vm = pl.BlockSpec(memory_space=pltpu.VMEM)
    return pl.pallas_call(
        reduce_kernel,
        out_shape=tuple(jax.ShapeDtypeStruct(s, f32) for s in outs),
        in_specs=[vm] * 8,
        out_specs=(vm,) * 4,
        scratch_shapes=scratch,
        compiler_params=pltpu.CompilerParams(collective_id=2, has_side_effects=True, vmem_limit_bytes=60 * 2**20),
        name="grads_reduce",
    )(*ops)


def small_mesh():
    return lax.axis_size("ctx") == 4 and lax.axis_size("fsdp") == 4


def whole_weights(w_qkv, w_out, w_gate_up, w_down):
    if small_mesh():
        joint, gate_up, down = gather_weights(
            jnp.concatenate([w_qkv, w_out], axis=1), w_gate_up, w_down
        )
        return (joint[:, : w_qkv.shape[1]], joint[:, w_qkv.shape[1] :], gate_up, down)
    return tuple(
        lax.all_gather(w, "fsdp", axis=0, tiled=True) for w in (w_qkv, w_out, w_gate_up, w_down)
    )


def owned_grads(lefts, rights):
    if small_mesh():
        normed, context, second, inner = (left.T for left in lefts)
        mixed, hidden_low, both, g_low = rights
        g_down, g_gate_up, g_qkv, g_out = reduce_grads(
            inner, second, normed, context, g_low, both, mixed, hidden_low
        )
        return (g_qkv, g_out, g_gate_up, g_down)
    return tuple(
        lax.psum_scatter(
            outer_product(left, right).astype(jnp.bfloat16),
            ("ctx", "fsdp"),
            scatter_dimension=0,
            tiled=True,
        ).astype(jnp.float32)
        for left, right in zip(lefts, rights)
    )


def local(ends, segment_ids, w_qkv, w_out, w_gate_up, w_down, gains):
    section_index = lax.axis_index("section")
    fsdp_index = lax.axis_index("fsdp")
    ctx_count = lax.axis_size("ctx")
    fsdp_count = lax.axis_size("fsdp")
    micro_count = ends.shape[1]
    tok_rows = ends.shape[3]
    local_ends = ends[0, :, 0]
    seg_local = segment_ids[:, 0]
    seg_whole = lax.all_gather(seg_local, "ctx", axis=1, tiled=True)
    query_pos = lax.axis_index("ctx") * tok_rows + jnp.arange(tok_rows, dtype=jnp.int32)
    frequency = 10000.0 ** (-(jnp.arange(HEAD // 2).astype(jnp.float32) * 2.0 / HEAD))
    angle_table = query_pos.astype(jnp.float32)[:, None] * frequency[None, :]
    cosine = jnp.cos(angle_table)[:, None, :]
    sine_table = jnp.sin(angle_table)[:, None, :]
    gain_pair = gains[0]
    weights = whole_weights(w_qkv[0], w_out[0], w_gate_up[0], w_down[0])
    arrived = jnp.zeros((tok_rows, D), jnp.bfloat16)
    store_bufs = None
    outputs = jnp.zeros((micro_count + 1, tok_rows, D), jnp.float32)
    for tick_num in range(micro_count + 1):
        batch_index = tick_num - section_index
        is_valid = (batch_index >= 0) & (batch_index < micro_count)
        clipped = jnp.clip(batch_index, 0, micro_count - 1)
        slot_index = jnp.where(is_valid, batch_index, micro_count)
        own_rows = lax.dynamic_index_in_dim(local_ends, clipped, 0, keepdims=False)
        layer_in = jnp.where(section_index == 0, own_rows, arrived)
        seg_rows = lax.dynamic_index_in_dim(seg_local, clipped, 0, keepdims=False)
        seg_full = lax.dynamic_index_in_dim(seg_whole, clipped, 0, keepdims=False)
        result, saved_acts = layer_forward(
            layer_in.astype(jnp.float32),
            weights,
            gain_pair,
            seg_rows,
            seg_full,
            query_pos,
            cosine,
            sine_table,
        )
        if tick_num == 0:
            store_bufs = jax.tree.map(
                lambda update: jnp.zeros((micro_count + 1,) + update.shape, update.dtype),
                saved_acts,
            )
        store_bufs = jax.tree.map(
            lambda buffer, update: lax.dynamic_update_index_in_dim(buffer, update, slot_index, 0),
            store_bufs,
            saved_acts,
        )
        outputs = lax.dynamic_update_index_in_dim(outputs, result, slot_index, 0)
        arrived = shifted(result.astype(jnp.bfloat16), "section", 1)
    operand_bufs = None
    gain_sums = jnp.zeros((2, D), jnp.float32)
    arrived_grad = jnp.zeros((tok_rows, D), jnp.bfloat16)
    input_grads = jnp.zeros((micro_count + 1, tok_rows, D), jnp.float32)
    for tick_num in range(micro_count + 1):
        batch_index = tick_num - (1 - section_index)
        is_valid = (batch_index >= 0) & (batch_index < micro_count)
        clipped = jnp.clip(batch_index, 0, micro_count - 1)
        slot_index = jnp.where(is_valid, batch_index, micro_count)
        own_rows = lax.dynamic_index_in_dim(local_ends, clipped, 0, keepdims=False)
        incoming = jnp.where(section_index == 1, own_rows, arrived_grad)
        incoming = jnp.where(is_valid, incoming, jnp.zeros_like(incoming))
        seg_rows = lax.dynamic_index_in_dim(seg_local, clipped, 0, keepdims=False)
        seg_full = lax.dynamic_index_in_dim(seg_whole, clipped, 0, keepdims=False)
        saved_acts = jax.tree.map(
            lambda buffer: lax.dynamic_index_in_dim(buffer, clipped, 0, keepdims=False), store_bufs
        )
        grad_input, operand_pairs, gain_terms = layer_backward(
            incoming,
            saved_acts,
            weights,
            gain_pair,
            seg_rows,
            seg_full,
            query_pos,
            cosine,
            sine_table,
        )
        if tick_num == 0:
            operand_bufs = jax.tree.map(
                lambda update: jnp.zeros((micro_count + 1,) + update.shape, update.dtype),
                operand_pairs,
            )
        operand_bufs = jax.tree.map(
            lambda buffer, update: lax.dynamic_update_index_in_dim(buffer, update, slot_index, 0),
            operand_bufs,
            operand_pairs,
        )
        gain_sums = gain_sums + gain_terms
        input_grads = lax.dynamic_update_index_in_dim(input_grads, grad_input, slot_index, 0)
        arrived_grad = shifted(grad_input.astype(jnp.bfloat16), "section", -1)
    operands = [buffer[:micro_count].reshape(-1, buffer.shape[-1]) for buffer in operand_bufs]
    g_qkv, g_out, g_gate_up, g_down = owned_grads(operands[:4], operands[4:])
    g_gains = lax.psum_scatter(gain_sums, ("ctx", "fsdp"), scatter_dimension=1, tiled=True)
    final_rows = jnp.where(section_index == 0, input_grads[:micro_count], outputs[:micro_count])
    ends_out = final_rows[None, :, None]
    return (ends_out, g_qkv[None], g_out[None], g_gate_up[None], g_down[None], g_gains[None])


def solution(mesh):
    in_specs = (
        P("section", None, "fsdp", "ctx", None),
        P(None, "fsdp", "ctx"),
        P("section", "fsdp", None),
        P("section", "fsdp", None),
        P("section", "fsdp", None),
        P("section", "fsdp", None),
        P("section", None, None),
    )
    out_specs = (
        P("section", None, "fsdp", "ctx", None),
        P("section", ("ctx", "fsdp"), None),
        P("section", ("ctx", "fsdp"), None),
        P("section", ("ctx", "fsdp"), None),
        P("section", ("ctx", "fsdp"), None),
        P("section", None, ("ctx", "fsdp")),
    )
    return jax.shard_map(local, mesh=mesh, in_specs=in_specs, out_specs=out_specs, check_vma=False)
```

```python
import math

import jax
import jax.numpy as jnp
from jax import lax
from jax.experimental import pallas as pl
from jax.experimental.pallas import tpu as pltpu
from jax.sharding import PartitionSpec as P

MESH = pl.DeviceIdType.MESH

D = 1152
HEADS = 18
KV_HEADS = 6
HEAD = 64
FF = 3072
KVW = 384


EPS = 1e-05


def shifted(x, axis, by):
    size = lax.axis_size(axis)
    pairs = [(i, i + by) for i in range(size) if 0 <= i + by < size]
    return lax.ppermute(x, axis, pairs)


def rotate(values_in, cosine, sine_table):
    half_size = values_in.shape[-1] // 2
    front = values_in[..., :half_size]
    back_half = values_in[..., half_size:]
    return jnp.concatenate(
        [front * cosine - back_half * sine_table, back_half * cosine + front * sine_table], axis=-1
    )


def rotate_back(gradient, cosine, sine_table):
    half_size = gradient.shape[-1] // 2
    front = gradient[..., :half_size]
    back_half = gradient[..., half_size:]
    return jnp.concatenate(
        [front * cosine + back_half * sine_table, back_half * cosine - front * sine_table], axis=-1
    )


def norm_forward(inputs, gain_row):
    scale_row = lax.rsqrt(jnp.mean(inputs * inputs, axis=-1, keepdims=True) + EPS)
    unit_rows = inputs * scale_row
    return (unit_rows * gain_row, unit_rows, scale_row)


def norm_backward(gradient, unit_rows, scale_row, gain_row):
    unit_grad = gradient * gain_row
    gain_grad = jnp.sum(gradient * unit_rows, axis=0)
    input_grad = scale_row * (
        unit_grad - unit_rows * jnp.mean(unit_grad * unit_rows, axis=-1, keepdims=True)
    )
    return (input_grad, gain_grad)


def outer_product(left, right):
    return lax.dot_general(
        left, right, (((0,), (0,)), ((), ())), preferred_element_type=jnp.float32
    )


def times_transposed(left, right):
    return lax.dot_general(
        left, right, (((1,), (1,)), ((), ())), preferred_element_type=jnp.float32
    )


def block_needed(first_row, block_rows, seg_full, seg_rows, query_pos):
    last_seg = lax.dynamic_index_in_dim(seg_full, first_row + block_rows - 1, 0, keepdims=False)
    return (first_row <= query_pos[-1]) & (last_seg >= seg_rows[0])


def attend_forward(queries4, key_all, value_all, seg_rows, seg_full, query_pos):
    tok_rows = queries4.shape[0]
    group_size = HEADS // KV_HEADS
    score_scale = HEAD ** (-0.5)
    total_rows = key_all.shape[0]
    block_rows = math.gcd(total_rows, 512)
    block_count = total_rows // block_rows
    key_heads = key_all.reshape(total_rows, KV_HEADS, HEAD)
    value_heads = value_all.reshape(total_rows, KV_HEADS, HEAD)

    def block_scores(block_index):
        first_row = block_index * block_rows
        key_block = lax.dynamic_slice_in_dim(key_heads, first_row, block_rows, 0)
        value_block = lax.dynamic_slice_in_dim(value_heads, first_row, block_rows, 0)
        seg_block = lax.dynamic_slice_in_dim(seg_full, first_row, block_rows, 0)
        key_pos = first_row + jnp.arange(block_rows, dtype=jnp.int32)
        raw_scores = (
            jnp.einsum("qkgd,tkd->kgqt", queries4, key_block, preferred_element_type=jnp.float32)
            * score_scale
        )
        allowed = (key_pos[None, :] <= query_pos[:, None]) & (
            seg_block[None, :] == seg_rows[:, None]
        )
        return (jnp.where(allowed, raw_scores, -1e30), allowed, value_block)

    def first_pass(state_pair, block_index):

        def first_work(state_in):
            row_top, row_total = state_in
            masked, allowed, value_block = block_scores(block_index)
            new_top = jnp.maximum(row_top, jnp.max(masked, axis=-1))
            new_total = row_total * jnp.exp(row_top - new_top) + jnp.sum(
                jnp.exp(masked - new_top[..., None]), axis=-1
            )
            return (new_top, new_total)

        needed = block_needed(block_index * block_rows, block_rows, seg_full, seg_rows, query_pos)
        return (lax.cond(needed, first_work, lambda state_in: state_in, state_pair), None)

    start_state = (
        jnp.full((KV_HEADS, group_size, tok_rows), -1e30, jnp.float32),
        jnp.zeros((KV_HEADS, group_size, tok_rows), jnp.float32),
    )
    block_ids = jnp.arange(block_count, dtype=jnp.int32)
    (row_top, row_total), ignored = lax.scan(first_pass, start_state, block_ids)
    log_total = row_top + jnp.log(row_total)

    def second_pass(summed, block_index):

        def second_work(summed_in):
            masked, allowed, value_block = block_scores(block_index)
            prob_low = jnp.where(allowed, jnp.exp(masked - log_total[..., None]), 0.0).astype(
                jnp.bfloat16
            )
            added = jnp.einsum(
                "kgqt,tkd->qkgd", prob_low, value_block, preferred_element_type=jnp.float32
            )
            return summed_in + added

        needed = block_needed(block_index * block_rows, block_rows, seg_full, seg_rows, query_pos)
        return (lax.cond(needed, second_work, lambda summed_in: summed_in, summed), None)

    start_sum = jnp.zeros((tok_rows, KV_HEADS, group_size, HEAD), jnp.float32)
    attended, ignored = lax.scan(second_pass, start_sum, block_ids)
    return (attended.reshape(tok_rows, D), log_total)


def layer_forward(inputs, weights, gain_pair, seg_rows, seg_full, query_pos, cosine, sine_table):
    w_qkv, w_out, w_gate_up, w_down = weights
    tok_rows = inputs.shape[0]
    group_size = HEADS // KV_HEADS
    normed, unit_one, scale_one = norm_forward(inputs, gain_pair[0])
    normed_low = normed.astype(jnp.bfloat16)
    mixed_proj = jnp.dot(normed_low, w_qkv, preferred_element_type=jnp.float32)
    queries = rotate(mixed_proj[:, :D].reshape(tok_rows, HEADS, HEAD), cosine, sine_table).astype(
        jnp.bfloat16
    )
    key_rows = rotate(
        mixed_proj[:, D : D + KVW].reshape(tok_rows, KV_HEADS, HEAD), cosine, sine_table
    )
    key_rows = key_rows.astype(jnp.bfloat16).reshape(tok_rows, KVW)
    value_rows = mixed_proj[:, D + KVW :].astype(jnp.bfloat16)
    key_all, value_all = (
        lax.all_gather(key_rows, "ctx", axis=0, tiled=True),
        lax.all_gather(value_rows, "ctx", axis=0, tiled=True),
    )
    queries4 = queries.reshape(tok_rows, KV_HEADS, group_size, HEAD)
    attended, log_total = attend_forward(
        queries4, key_all, value_all, seg_rows, seg_full, query_pos
    )
    context = attended.astype(jnp.bfloat16)
    hidden = inputs + jnp.dot(context, w_out, preferred_element_type=jnp.float32)
    second, unit_two, scale_two = norm_forward(hidden, gain_pair[1])
    second_low = second.astype(jnp.bfloat16)
    gate_up = jnp.dot(second_low, w_gate_up, preferred_element_type=jnp.float32)
    gate_pre = gate_up[:, :FF]
    up_pre = gate_up[:, FF:]
    inner_act = (jax.nn.silu(gate_pre) * up_pre).astype(jnp.bfloat16)
    result = hidden + jnp.dot(inner_act, w_down, preferred_element_type=jnp.float32)
    saved_acts = (
        normed_low,
        queries4,
        key_all,
        value_all,
        attended,
        log_total,
        context,
        unit_one,
        scale_one,
        unit_two,
        scale_two,
        second_low,
        gate_pre,
        up_pre,
        inner_act,
    )
    return (result, saved_acts)


def layer_backward(
    grad_low, saved_acts, weights, gain_pair, seg_rows, seg_full, query_pos, cosine, sine_table
):
    w_qkv, w_out, w_gate_up, w_down = weights
    (
        normed_low,
        queries4,
        key_all,
        value_all,
        attended,
        log_total,
        context,
        unit_one,
        scale_one,
        unit_two,
        scale_two,
        second_low,
        gate_pre,
        up_pre,
        inner_act,
    ) = saved_acts
    tok_rows = grad_low.shape[0]
    group_size = HEADS // KV_HEADS
    score_scale = HEAD ** (-0.5)
    grad_out = grad_low.astype(jnp.float32)
    grad_inner = times_transposed(grad_low, w_down)
    sigmoid_gate = jax.nn.sigmoid(gate_pre)
    silu_gate = gate_pre * sigmoid_gate
    grad_gate = grad_inner * up_pre * sigmoid_gate * (1.0 + gate_pre * (1.0 - sigmoid_gate))
    grad_up = grad_inner * silu_gate
    grad_both = jnp.concatenate([grad_gate, grad_up], axis=1).astype(jnp.bfloat16)
    grad_second = times_transposed(grad_both, w_gate_up)
    grad_norm_two, gain_two = norm_backward(grad_second, unit_two, scale_two, gain_pair[1])
    grad_hidden = grad_out + grad_norm_two
    hidden_low = grad_hidden.astype(jnp.bfloat16)
    grad_context = times_transposed(hidden_low, w_out).astype(jnp.bfloat16)
    grad_context4 = grad_context.reshape(tok_rows, KV_HEADS, group_size, HEAD)
    attended4 = attended.reshape(tok_rows, KV_HEADS, group_size, HEAD)
    row_delta = jnp.einsum("qkgd,qkgd->kgq", grad_context4.astype(jnp.float32), attended4)
    total_rows = seg_full.shape[0]
    start_state = (
        jnp.zeros((tok_rows, KV_HEADS, group_size, HEAD), jnp.float32),
        jnp.zeros((total_rows, 2 * KVW), jnp.float32),
    )
    key_piece, value_piece = key_all, value_all
    piece_rows = key_piece.shape[0]
    block_rows = math.gcd(piece_rows, 512)
    block_count = piece_rows // block_rows

    def one_block(block_index, inner_state):
        offset = block_index * block_rows

        def one_work(state_in):
            grad_query, grad_kv = state_in
            key_block = lax.dynamic_slice_in_dim(key_piece, offset, block_rows, 0).reshape(
                block_rows, KV_HEADS, HEAD
            )
            value_block = lax.dynamic_slice_in_dim(value_piece, offset, block_rows, 0).reshape(
                block_rows, KV_HEADS, HEAD
            )
            seg_block = lax.dynamic_slice_in_dim(seg_full, offset, block_rows, 0)
            key_pos = offset + jnp.arange(block_rows, dtype=jnp.int32)
            raw_scores = (
                jnp.einsum(
                    "qkgd,tkd->kgqt", queries4, key_block, preferred_element_type=jnp.float32
                )
                * score_scale
            )
            allowed = (key_pos[None, :] <= query_pos[:, None]) & (
                seg_block[None, :] == seg_rows[:, None]
            )
            prob_full = jnp.where(allowed, jnp.exp(raw_scores - log_total[..., None]), 0.0)
            prob_low = prob_full.astype(jnp.bfloat16)
            grad_value = jnp.einsum(
                "kgqt,qkgd->tkd", prob_low, grad_context4, preferred_element_type=jnp.float32
            )
            grad_prob = jnp.einsum(
                "qkgd,tkd->kgqt", grad_context4, value_block, preferred_element_type=jnp.float32
            )
            grad_scores = (prob_full * (grad_prob - row_delta[..., None])).astype(jnp.bfloat16)
            grad_query = (
                grad_query
                + jnp.einsum(
                    "kgqt,tkd->qkgd", grad_scores, key_block, preferred_element_type=jnp.float32
                )
                * score_scale
            )
            grad_key = (
                jnp.einsum(
                    "kgqt,qkgd->tkd", grad_scores, queries4, preferred_element_type=jnp.float32
                )
                * score_scale
            )
            new_rows = jnp.concatenate(
                [grad_key.reshape(block_rows, KVW), grad_value.reshape(block_rows, KVW)], axis=1
            )
            old_rows = lax.dynamic_slice_in_dim(grad_kv, offset, block_rows, 0)
            grad_kv = lax.dynamic_update_slice_in_dim(grad_kv, old_rows + new_rows, offset, 0)
            return (grad_query, grad_kv)

        needed = block_needed(offset, block_rows, seg_full, seg_rows, query_pos)
        return lax.cond(needed, one_work, lambda state_in: state_in, inner_state)

    grad_query, grad_kv_all = lax.fori_loop(0, block_count, one_block, start_state)
    grad_kv_own = lax.psum_scatter(
        grad_kv_all.astype(jnp.bfloat16), "ctx", scatter_dimension=0, tiled=True
    ).astype(jnp.float32)
    grad_q_pre = rotate_back(grad_query.reshape(tok_rows, HEADS, HEAD), cosine, sine_table).reshape(
        tok_rows, D
    )
    grad_k_pre = rotate_back(
        grad_kv_own[:, :KVW].reshape(tok_rows, KV_HEADS, HEAD), cosine, sine_table
    ).reshape(tok_rows, KVW)
    grad_mixed = jnp.concatenate([grad_q_pre, grad_k_pre, grad_kv_own[:, KVW:]], axis=1).astype(
        jnp.bfloat16
    )
    grad_normed = times_transposed(grad_mixed, w_qkv)
    grad_norm_one, gain_one = norm_backward(grad_normed, unit_one, scale_one, gain_pair[0])
    grad_input = grad_hidden + grad_norm_one
    operand_pairs = (
        normed_low,
        context,
        second_low,
        inner_act,
        grad_mixed,
        hidden_low,
        grad_both,
        grad_low,
    )
    return (grad_input, operand_pairs, jnp.stack([gain_one, gain_two]))


def gather_kernel(qo, gu, dn, fqo, fgu, fdn, own_sem, back_sem, zs, zr, ys, yr, cs, cr, es, er):
    place = lax.axis_index("ctx")
    z = lax.axis_index("fsdp")
    last = lax.axis_size("fsdp") - 1
    y, k = place // 2, place % 2
    y_mate = {"ctx": (1 - y) * 2 + k}
    k_mate = {"ctx": y * 2 + 1 - k}
    width = qo.shape[0]
    deep = dn.shape[0]
    half = width // 2
    chunks = [(0, p) for p in range(3)] + [(1, p) for p in range(3)] + [(2, p) for p in range(2)]
    wholes = (fqo, fgu, fdn)
    owns = (qo, gu, dn)

    def view(refs, shard, yy, kk, chunk):
        m, p = chunk
        ref = refs[m]
        if m == 2:
            rows = deep // 8
            first = shard * deep + (yy * 2 + kk) * (deep // 4) + p * rows
            return ref.at[pl.ds(pl.multiple_of(first, 16), rows), :]
        rows = half // 3
        cols = ref.shape[1] // 2
        first = shard * width + yy * half + p * rows
        return ref.at[pl.ds(pl.multiple_of(first, 16), rows), pl.ds(pl.multiple_of(kk * cols, 128), cols)]

    barrier = pltpu.get_barrier_semaphore()
    for mate in (y_mate, k_mate):
        pl.semaphore_signal(barrier, inc=1, device_id=mate, device_id_type=MESH)

    @pl.when(z > 0)
    def _():
        pl.semaphore_signal(barrier, inc=1, device_id={"fsdp": z - 1}, device_id_type=MESH)

    @pl.when(z < last)
    def _():
        pl.semaphore_signal(barrier, inc=1, device_id={"fsdp": z + 1}, device_id_type=MESH)

    pl.semaphore_wait(barrier, 2 + jnp.where(z > 0, 1, 0) + jnp.where(z < last, 1, 0))

    def z_copy(shard, j, to, first, back):
        chunk = chunks[j]
        src = view(owns, 0, y, k, chunk) if first else view(wholes, shard, y, k, chunk)
        return pltpu.make_async_remote_copy(
            src_ref=src, dst_ref=view(wholes, shard, y, k, chunk),
            send_sem=back_sem.at[j] if back else zs.at[shard, j], recv_sem=zr.at[shard, j],
            device_id={"fsdp": to}, device_id_type=MESH)

    def mate_copy(shard, j, yy, mate, send, recv):
        chunk = chunks[j]
        ref = view(wholes, shard, yy, k, chunk)
        return pltpu.make_async_remote_copy(
            src_ref=ref, dst_ref=ref, send_sem=send.at[shard, j], recv_sem=recv.at[shard, j],
            device_id=mate, device_id_type=MESH)

    def arrive(shard, j, yy, kk, recv):
        ref = view(wholes, shard, yy, kk, chunks[j])
        pltpu.make_async_remote_copy(
            src_ref=ref, dst_ref=ref, send_sem=recv.at[shard, j], recv_sem=recv.at[shard, j],
            device_id=k_mate, device_id_type=MESH).wait_recv()

    for j in range(len(chunks)):
        @pl.when(z < last)
        def _():
            z_copy(z, j, z + 1, True, False).start()

        @pl.when(z > 0)
        def _():
            z_copy(z, j, z - 1, True, True).start()
    locals_ = []
    for m in range(3):
        rows = owns[m].shape[0]
        locals_.append(pltpu.make_async_remote_copy(
            src_ref=owns[m], dst_ref=wholes[m].at[pl.ds(pl.multiple_of(z * rows, 16), rows), :],
            send_sem=own_sem.at[0, m], recv_sem=own_sem.at[1, m], device_id=k_mate, device_id_type=MESH))
    for copy in locals_:
        copy.start()

    def sides(d):
        return ((z - d >= 0, z - d, z + 1, z < last), (z + d <= last, z + d, z - 1, z > 0))

    def relay(d, j):
        for valid, shard, onward, more in sides(d):
            @pl.when(valid)
            def _():
                arrive(shard, j, y, k, zr)
                if d < 3:
                    @pl.when(more)
                    def _():
                        z_copy(shard, j, onward, False, False).start()
                mate_copy(shard, j, y, y_mate, ys, yr).start()
                mate_copy(shard, j, y, k_mate, cs, cr).start()

    def across(d, j):
        for valid, shard, onward, more in sides(d):
            @pl.when(valid)
            def _():
                arrive(shard, j, 1 - y, k, yr)
                mate_copy(shard, j, 1 - y, k_mate, es, er).start()

    order = [(d, j) for d in (1, 2, 3) for j in range(len(chunks))]
    lag = 1
    for i, (d, j) in enumerate(order):
        relay(d, j)
        if i >= lag:
            across(*order[i - lag])
    for d, j in order[len(order) - lag:]:
        across(d, j)
    for d, j in order:
        for valid, shard, onward, more in sides(d):
            @pl.when(valid)
            def _():
                arrive(shard, j, y, 1 - k, cr)
                arrive(shard, j, 1 - y, 1 - k, er)
                mate_copy(shard, j, y, y_mate, ys, yr).wait_send()
                mate_copy(shard, j, y, k_mate, cs, cr).wait_send()
                mate_copy(shard, j, 1 - y, k_mate, es, er).wait_send()
                if d < 3:
                    @pl.when(more)
                    def _():
                        z_copy(shard, j, onward, False, False).wait_send()
    for j in range(len(chunks)):
        @pl.when(z < last)
        def _():
            z_copy(z, j, z + 1, True, False).wait_send()

        @pl.when(z > 0)
        def _():
            z_copy(z, j, z - 1, True, True).wait_send()
    for copy in locals_:
        copy.wait()


def gather_weights(qo, gu, dn):
    size = lax.axis_size("fsdp")
    any_spec = pl.BlockSpec(memory_space=pl.ANY)
    return pl.pallas_call(
        gather_kernel,
        out_shape=tuple(jax.ShapeDtypeStruct((size * w.shape[0], w.shape[1]), w.dtype) for w in (qo, gu, dn)),
        in_specs=[any_spec] * 3,
        out_specs=(any_spec,) * 3,
        scratch_shapes=[pltpu.SemaphoreType.DMA((2, 3)), pltpu.SemaphoreType.DMA((8,))]
        + [pltpu.SemaphoreType.DMA((4, 8))] * 8,
        compiler_params=pltpu.CompilerParams(collective_id=1, has_side_effects=True),
        name="weights_gather",
    )(qo, gu, dn)


DOWN_COLS = 128
WIDE_COLS = 384
NEAR, MID, FAR, SUMS = 2, 4, 8, 12


def reduce_kernel(
    inner_h, grad_h, second_h, both_h, normed_h, mixed_h, context_h, hidden_h, gain_tiles,
    o_down, o_gate_up, o_qkv, o_out, o_gain,
    *scratch,
):
    kinds = (scratch[0:9], scratch[9:18])
    (near_send, near_recv, mid_send, mid_recv, right_send, right_recv, left_send, left_recv,
     near_free, mid_free, right_free, left_free) = scratch[18:30]
    operands, load_sem, gain_in, gain_send, gain_recv = scratch[30:38], *scratch[38:42]
    inner_t, g_low, second_t, both, normed_t, mixed, context_t, hidden_low = operands
    loads = [
        pltpu.make_async_copy(src, dst, load_sem.at[i])
        for i, (src, dst) in enumerate(
            zip((inner_h, grad_h, second_h, both_h, normed_h, mixed_h, context_h, hidden_h), operands)
        )
    ]
    for load in loads:
        load.start()
    place = lax.axis_index("ctx")
    z = lax.axis_index("fsdp")
    last = lax.axis_size("fsdp") - 1
    y, k = place // 2, place % 2
    y_mate = {"ctx": (1 - y) * 2 + k}
    k_mate = {"ctx": y * 2 + 1 - k}
    right, left = {"fsdp": z + 1}, {"fsdp": z - 1}
    f32, low = jnp.float32, jnp.bfloat16

    n_down = g_low.shape[0] // DOWN_COLS
    n_both = both.shape[0] // WIDE_COLS
    n_mixed = mixed.shape[0] // WIDE_COLS
    n_out = hidden_low.shape[0] // WIDE_COLS
    end_both = n_down + n_both
    end_mixed = end_both + n_mixed
    total = end_mixed + n_out
    hop = 2
    first_z = 3
    final_lag = first_z + hop * 3

    barrier = pltpu.get_barrier_semaphore()
    me = place * 4 + z
    others = [((place + i // 4) % 4, (z + i % 4) % 4) for i in range(1, 16)]
    for to_place, to_z in others:
        pl.semaphore_signal(barrier, inc=1, device_id={"ctx": to_place, "fsdp": to_z}, device_id_type=MESH)
    pl.semaphore_wait(barrier, 15)

    def gain_copy(i):
        to_place, to_z = others[i - 1]
        return pltpu.make_async_remote_copy(
            src_ref=gain_tiles.at[to_place * 4 + to_z], dst_ref=gain_in.at[i],
            send_sem=gain_send.at[i], recv_sem=gain_recv.at[i],
            device_id={"ctx": to_place, "fsdp": to_z}, device_id_type=MESH)

    for i in range(1, 16):
        gain_copy(i).start()

    def typed(j, work):
        @pl.when((j >= 0) & (j < n_down))
        def _():
            work(0)

        @pl.when((j >= n_down) & (j < total))
        def _():
            work(1)

    def near_copy(kind, j):
        out_near, own_near, in_near = kinds[kind][0:3]
        slot = j % NEAR
        return pltpu.make_async_remote_copy(
            src_ref=out_near.at[slot], dst_ref=in_near.at[slot], send_sem=near_send.at[slot],
            recv_sem=near_recv.at[slot], device_id=k_mate, device_id_type=MESH)

    def mid_copy(kind, j):
        out_mid, in_mid = kinds[kind][3:5]
        slot = j % MID
        return pltpu.make_async_remote_copy(
            src_ref=out_mid.at[slot], dst_ref=in_mid.at[slot], send_sem=mid_send.at[slot],
            recv_sem=mid_recv.at[slot], device_id=y_mate, device_id_type=MESH)

    def line_rows(kind, step, rightward):
        rows = kinds[kind][5].shape[1]
        part = rows // 4
        if rightward:
            start = (part * (step + 1)) // 16 * 16
            return start, rows - start
        return 0, (part * step + 15) // 16 * 16

    def line_copy(kind, j, step, rightward):
        start, count = line_rows(kind, step, rightward)
        src, dst = (kinds[kind][6], kinds[kind][7]) if rightward else (kinds[kind][6], kinds[kind][8])
        lane = 0 if rightward else 1
        return pltpu.make_async_remote_copy(
            src_ref=src.at[lane, j % NEAR, pl.ds(start, count), :],
            dst_ref=dst.at[j % FAR, pl.ds(start, count), :],
            send_sem=(right_send if rightward else left_send).at[j % NEAR],
            recv_sem=(right_recv if rightward else left_recv).at[j % FAR],
            device_id=right if rightward else left, device_id_type=MESH)

    def multiply(kind, j, lhs, rhs, first, cols):
        out_near, own_near = kinds[kind][0:2]
        slot = j % NEAR
        rows = own_near.shape[2]
        columns = pl.ds(pl.multiple_of((j - first) * cols, 128), cols)
        block = rhs[columns, :]
        for yy in range(2):
            for mine in (False, True):
                kk = k if mine else 1 - k
                at = pl.ds(pl.multiple_of((yy * 2 + kk) * rows, 16), rows)
                part = lax.dot_general(lhs[at, :], block, (((1,), (1,)), ((), ())), preferred_element_type=f32)
                (own_near if mine else out_near)[slot, yy] = part.astype(low)

    def stage_near(j):
        for i, first in enumerate((0, n_down, end_both, end_mixed)):
            @pl.when(j == first)
            def _(i=i):
                loads[2 * i].wait()
                loads[2 * i + 1].wait()

        @pl.when((j >= NEAR) & (j < total))
        def _():
            typed(j - NEAR, lambda kind: near_copy(kind, j - NEAR).wait_send())

        @pl.when(j < n_down)
        def _():
            multiply(0, j, inner_t, g_low, 0, DOWN_COLS)

        @pl.when((j >= n_down) & (j < end_both))
        def _():
            multiply(1, j, second_t, both, n_down, WIDE_COLS)

        @pl.when((j >= end_both) & (j < end_mixed))
        def _():
            multiply(1, j, normed_t, mixed, end_both, WIDE_COLS)

        @pl.when((j >= end_mixed) & (j < total))
        def _():
            multiply(1, j, context_t, hidden_low, end_mixed, WIDE_COLS)

        @pl.when((j >= NEAR) & (j < total))
        def _():
            pl.semaphore_wait(near_free, 1)

        typed(j, lambda kind: near_copy(kind, j).start())

    def stage_mid(j):
        def work(kind):
            out_near, own_near, in_near, out_mid, in_mid, sums = kinds[kind][0:6]
            near_copy(kind, j).wait_recv()
            slot = j % NEAR
            out_mid[j % MID] = (own_near[slot, 1 - y].astype(f32) + in_near[slot, 1 - y].astype(f32)).astype(low)
            sums[j % SUMS] = own_near[slot, y].astype(f32) + in_near[slot, y].astype(f32)

        @pl.when((j >= MID) & (j < total))
        def _():
            typed(j - MID, lambda kind: mid_copy(kind, j - MID).wait_send())

        typed(j, work)

        @pl.when((j >= 0) & (j + NEAR < total))
        def _():
            pl.semaphore_signal(near_free, inc=1, device_id=k_mate, device_id_type=MESH)

        @pl.when((j >= MID) & (j < total))
        def _():
            pl.semaphore_wait(mid_free, 1)

        typed(j, lambda kind: mid_copy(kind, j).start())

    def stage_sum(j):
        def work(kind):
            in_mid, sums = kinds[kind][4:6]
            mid_copy(kind, j).wait_recv()
            sums[j % SUMS] = sums[j % SUMS] + in_mid[j % MID].astype(f32)

        typed(j, work)

        @pl.when((j >= 0) & (j + MID < total))
        def _():
            pl.semaphore_signal(mid_free, inc=1, device_id=y_mate, device_id_type=MESH)

    def stage_line(i, rightward):
        free = right_free if rightward else left_free
        for at in range(4):
            step = at if rightward else 3 - at
            if step == 3:
                continue
            j = i - first_z - hop * step

            @pl.when((z == at) & (j >= 0) & (j < total))
            def _(at=at, step=step, j=j):
                @pl.when(j >= NEAR)
                def _():
                    typed(j - NEAR, lambda kind: line_copy(kind, j - NEAR, at, rightward).wait_send())

                def work(kind):
                    sums, out_line, in_right, in_left = kinds[kind][5:9]
                    start, count = line_rows(kind, at, rightward)
                    rows = pl.ds(start, count)
                    value = sums[j % SUMS, rows, :]
                    if step > 0:
                        came = line_rows(kind, at - 1 if rightward else at + 1, rightward)
                        arrive = line_copy(kind, j, at - 1 if rightward else at + 1, rightward)
                        arrive.wait_recv()
                        value = value + (in_right if rightward else in_left)[j % FAR, rows, :].astype(f32)
                    out_line[0 if rightward else 1, j % NEAR, rows, :] = value.astype(low)

                typed(j, work)

                @pl.when(j >= FAR)
                def _():
                    pl.semaphore_wait(free, 1)

                typed(j, lambda kind: line_copy(kind, j, at, rightward).start())

    def store(kind, j, value):
        if kind == 0:
            o_down[:, pl.ds(pl.multiple_of(j * DOWN_COLS, 128), DOWN_COLS)] = value
            return
        for out, first, end in ((o_gate_up, n_down, end_both), (o_qkv, end_both, end_mixed), (o_out, end_mixed, total)):
            @pl.when((j >= first) & (j < end))
            def _(out=out, first=first):
                out[:, pl.ds(pl.multiple_of((j - first) * WIDE_COLS, 128), WIDE_COLS)] = value

    def stage_final(j):
        for at in range(4):
            @pl.when((z == at) & (j >= 0) & (j < total))
            def _(at=at):
                def work(kind):
                    sums, out_line, in_right, in_left = kinds[kind][5:9]
                    part = sums.shape[1] // 4
                    if at == 3:
                        line_copy(kind, j, 2, True).wait_recv()
                    if at == 0:
                        line_copy(kind, j, 1, False).wait_recv()
                    low_at = at * part // 16 * 16
                    high_at = (at * part + part + 15) // 16 * 16
                    rows = pl.ds(low_at, high_at - low_at)
                    value = sums[j % SUMS, rows, :]
                    if at > 0:
                        value = value + in_right[j % FAR, rows, :].astype(f32)
                    if at < 3:
                        value = value + in_left[j % FAR, rows, :].astype(f32)
                    shift = at * part - low_at
                    store(kind, j, value[shift:shift + part])

                typed(j, work)
                if at > 0:
                    @pl.when(j + FAR < total)
                    def _():
                        pl.semaphore_signal(right_free, inc=1, device_id=left, device_id_type=MESH)
                if at < 3:
                    @pl.when(j + FAR < total)
                    def _():
                        pl.semaphore_signal(left_free, inc=1, device_id=right, device_id_type=MESH)

    def iteration(i, carry):
        stage_near(i)
        stage_mid(i - 1)
        stage_sum(i - 3)
        stage_line(i, True)
        stage_line(i, False)
        stage_final(i - final_lag)
        return carry

    lax.fori_loop(0, total + final_lag, iteration, 0)
    gain = gain_tiles[me]
    for i in range(1, 16):
        gain_copy(i).wait()
        gain = gain + gain_in[i]
    o_gain[...] = gain
    for j in range(total - NEAR, total):
        near_copy(1, j).wait_send()
        for at in range(3):
            @pl.when(z == at)
            def _(at=at):
                line_copy(1, j, at, True).wait_send()

            @pl.when(z == at + 1)
            def _(at=at):
                line_copy(1, j, at + 1, False).wait_send()
    for j in range(total - MID, total):
        mid_copy(1, j).wait_send()


def reduce_grads(lefts, rights, gain_tiles):
    normed, context, second, inner = lefts
    both, mixed, hidden, grad = rights
    ops = (inner, grad, second, both, normed, mixed, context, hidden)
    low, f32 = jnp.bfloat16, jnp.float32
    scratch = []
    for rows, cols in ((inner.shape[0] // 4, DOWN_COLS), (second.shape[0] // 4, WIDE_COLS)):
        scratch += [
            pltpu.VMEM((NEAR, 2, rows, cols), low), pltpu.VMEM((NEAR, 2, rows, cols), low), pltpu.VMEM((NEAR, 2, rows, cols), low),
            pltpu.VMEM((MID, rows, cols), low), pltpu.VMEM((MID, rows, cols), low),
            pltpu.VMEM((SUMS, rows, cols), f32),
            pltpu.VMEM((2, NEAR, rows, cols), low),
            pltpu.VMEM((FAR, rows, cols), low), pltpu.VMEM((FAR, rows, cols), low)]
    sem = pltpu.SemaphoreType
    scratch += [sem.DMA((NEAR,)), sem.DMA((NEAR,)), sem.DMA((MID,)), sem.DMA((MID,)),
                sem.DMA((NEAR,)), sem.DMA((FAR,)), sem.DMA((NEAR,)), sem.DMA((FAR,)),
                sem.REGULAR, sem.REGULAR, sem.REGULAR, sem.REGULAR]
    scratch += [pltpu.VMEM(op.shape, low) for op in ops]
    scratch += [sem.DMA((8,)), pltpu.VMEM((16, 8, 128), f32), sem.DMA((16,)), sem.DMA((16,))]
    outs = [(a.shape[0] // 16, b.shape[0]) for a, b in zip(ops[0::2], ops[1::2])] + [(8, 128)]
    vm, hbm = pl.BlockSpec(memory_space=pltpu.VMEM), pl.BlockSpec(memory_space=pl.ANY)
    return pl.pallas_call(
        reduce_kernel,
        out_shape=tuple(jax.ShapeDtypeStruct(s, f32) for s in outs),
        in_specs=[hbm] * 8 + [vm],
        out_specs=(vm,) * 5,
        scratch_shapes=scratch,
        compiler_params=pltpu.CompilerParams(collective_id=2, has_side_effects=True, vmem_limit_bytes=62 * 2**20),
        name="grads_reduce",
    )(*ops, gain_tiles)


F32, LOW = jnp.float32, jnp.bfloat16
GROUP = HEADS // KV_HEADS
HALF = HEAD // 2
SCALE = HEAD ** (-0.5)
NONE = -1e30
TILE = 384
WIDE = 512


def dot(left, right, left_dim, right_dim):
    return lax.dot_general(
        left, right, (((left_dim,), (right_dim,)), ((), ())), preferred_element_type=F32
    )


def at(start, size, step=128):
    return pl.ds(pl.multiple_of(start, step), size)


def column_scale(v):
    return lax.rsqrt(jnp.mean(v * v, axis=0, keepdims=True) + EPS)


def greet(peers):
    barrier = pltpu.get_barrier_semaphore()
    for peer in peers:
        pl.semaphore_signal(barrier, inc=1, device_id=peer, device_id_type=MESH)
    pl.semaphore_wait(barrier, len(peers))


def remote(src, dst, send, recv, peer):
    return pltpu.make_async_remote_copy(
        src_ref=src, dst_ref=dst, send_sem=send, recv_sem=recv, device_id=peer, device_id_type=MESH
    )


def fill_bias(bias, seg_row, seg_col, m, place, toks):
    own = seg_row[m]
    rows = lax.broadcasted_iota(jnp.int32, (toks, toks), 0)
    cols = lax.broadcasted_iota(jnp.int32, (toks, toks), 1)
    for d in range(3):
        first = jnp.maximum(place - d, 0) * toks
        keys = seg_col[m, pl.ds(pl.multiple_of(first, 128), toks), :]
        allowed = keys == own
        if d == 0:
            allowed = allowed & (rows <= cols)
        bias[d] = jnp.where(allowed, 0.0, NONE)


def forward_kernel(
    ends, gains, cosine, sine, seg_row, seg_col, w_joint, w_gate_up, w_down,
    o_normed, o_context, o_second, o_inner, o_x, o_q, o_kv, o_att, o_lse, o_hidden, o_gu, o_result,
    v_joint, v_gate_up, v_down, x_in, x_now, s_normed, s_context, s_second, s_inner, s_x,
    s_q, s_kv, s_att, s_top, s_lse, s_hidden, s_gu, s_result, bias,
    w_sem, save_sem, kv_send, kv_recv, x_send, x_recv,
):
    section = lax.axis_index("section")
    place = lax.axis_index("ctx")
    micros, toks = ends.shape[0], ends.shape[1]
    qkv = D + 2 * KVW
    loads = [
        pltpu.make_async_copy(src, dst, w_sem.at[i])
        for i, (src, dst) in enumerate(
            ((w_joint, v_joint), (w_gate_up, v_gate_up), (w_down, v_down))
        )
    ]
    for load in loads:
        load.start()
    greet([{"ctx": (place + i) % 4} for i in (1, 2, 3)] + [{"section": 1 - section}])

    def saves(m):
        lanes = at(m * toks, toks)
        pairs = (
            (s_normed, o_normed.at[:, lanes]),
            (s_context, o_context.at[:, lanes]),
            (s_second, o_second.at[:, lanes]),
            (s_inner, o_inner.at[:, lanes]),
            (s_x, o_x.at[m]),
            (s_q, o_q.at[m]),
            (s_kv.at[m], o_kv.at[m]),
            (s_att, o_att.at[m]),
            (s_lse, o_lse.at[m]),
            (s_hidden, o_hidden.at[m]),
            (s_gu, o_gu.at[m]),
        )
        return [pltpu.make_async_copy(a, b, save_sem.at[i]) for i, (a, b) in enumerate(pairs)]

    def result_save(m):
        return pltpu.make_async_copy(s_result, o_result.at[m], save_sem.at[11])

    def x_copy(m):
        return remote(x_in.at[m], x_in.at[m], x_send.at[m], x_recv.at[m], {"section": 1})

    def kv_copy(m, source, slot, lane, to):
        return remote(
            s_kv.at[m, source], s_kv.at[m, slot], kv_send.at[m, lane], kv_recv.at[m, slot],
            {"ctx": to},
        )

    def kv_sends(m):
        return (
            (0, kv_copy(m, 0, 1, 0, 1)),
            (0, kv_copy(m, 0, 2, 1, 2)),
            (1, kv_copy(m, 0, 2, 0, 3)),
            (2, kv_copy(m, 0, 1, 0, 3)),
        )

    def attend(kv_at, m, blocks, fresh):
        rows = at(kv_at * HEAD, HEAD, 64)
        query = s_q[rows, :]
        parts = []
        for d in blocks:
            part = dot(s_kv[m, d, rows, :], query, 0, 0)
            mask = bias[d]
            parts.append(part + jnp.concatenate([mask] * GROUP, axis=1))
        scores = parts[0] if len(parts) == 1 else jnp.concatenate(parts, axis=0)
        top = jnp.max(scores, axis=0, keepdims=True)
        one = pl.ds(kv_at, 1)
        if not fresh:
            old_top, old_total = s_top[one, :], s_lse[one, :]
            top = jnp.maximum(top, old_top)
        probs = jnp.exp(scores - top)
        total = jnp.sum(probs, axis=0, keepdims=True)
        probs = probs.astype(LOW)
        value_rows = at(KVW + kv_at * HEAD, HEAD, 64)
        summed = None
        for i, d in enumerate(blocks):
            term = dot(s_kv[m, d, value_rows, :], probs[i * toks : (i + 1) * toks], 1, 0)
            summed = term if summed is None else summed + term
        if not fresh:
            keep = jnp.exp(old_top - top)
            total = total + old_total * keep
        s_top[one, :] = top
        s_lse[one, :] = total
        for g in range(GROUP):
            lanes = slice(g * toks, (g + 1) * toks)
            out_rows = at((kv_at * GROUP + g) * HEAD, HEAD, 64)
            value = summed[:, lanes]
            if not fresh:
                value = value + s_att[out_rows, :] * keep[:, lanes]
            s_att[out_rows, :] = value

    def micro(m, carry):
        @pl.when(m > 0)
        def _():
            for save in saves(m - 1):
                save.wait()

            @pl.when(section == 1)
            def _():
                result_save(m - 1).wait()

        @pl.when(section == 0)
        def _():
            x_now[...] = ends[m].astype(F32).T

        @pl.when(section == 1)
        def _():
            x_copy(m).wait_recv()
            x_now[...] = x_in[m].astype(F32)

        fill_bias(bias, seg_row, seg_col, m, place, toks)
        x = x_now[...]
        s_x[...] = x.astype(LOW)
        s_normed[...] = (x * column_scale(x) * gains[:, 0:1]).astype(LOW)

        @pl.when(m == 0)
        def _():
            loads[0].wait()

        cos, sin = cosine[...], sine[...]

        def rotated(block, head):
            front = block[head * HEAD : head * HEAD + HALF]
            back = block[head * HEAD + HALF : (head + 1) * HEAD]
            return jnp.concatenate([front * cos - back * sin, back * cos + front * sin], axis=0)

        keys = dot(v_joint[:, D : D + KVW], s_normed[...], 0, 0)
        for head in range(KV_HEADS):
            s_kv[m, 0, head * HEAD : (head + 1) * HEAD, :] = rotated(keys, head).astype(LOW)
        s_kv[m, 0, KVW : 2 * KVW, :] = dot(
            v_joint[:, D + KVW : qkv], s_normed[...], 0, 0
        ).astype(LOW)
        for who, copy in kv_sends(m):
            @pl.when(place == who)
            def _(copy=copy):
                copy.start()

        def query_tile(i, carry):
            block = dot(v_joint[:, at(i * TILE, TILE)], s_normed[...], 0, 0) * SCALE
            for head in range(TILE // HEAD):
                rows = at((i * (TILE // HEAD // GROUP) + head // GROUP) * HEAD, HEAD, 64)
                g = head % GROUP
                s_q[rows, g * toks : (g + 1) * toks] = rotated(block, head).astype(LOW)
            return carry

        lax.fori_loop(0, D // TILE, query_tile, 0)

        def each(blocks, fresh):
            def step(kv_at, carry):
                attend(kv_at, m, blocks, fresh)
                return carry

            lax.fori_loop(0, KV_HEADS, step, 0)

        each((0,), True)

        @pl.when(place == 1)
        def _():
            kv_copy(m, 0, 1, 0, 1).wait_recv()
            each((1,), False)

        @pl.when(place == 2)
        def _():
            kv_copy(m, 0, 2, 0, 2).wait_recv()
            each((2,), False)
            kv_copy(m, 0, 1, 0, 2).wait_recv()
            each((1,), False)

        @pl.when(place == 3)
        def _():
            kv_copy(m, 0, 2, 0, 3).wait_recv()
            kv_copy(m, 2, 1, 0, 2).start()
            kv_copy(m, 0, 1, 0, 3).wait_recv()
            each((1, 2), False)

        def finish(kv_at, carry):
            one = pl.ds(kv_at, 1)
            total = s_lse[one, :]
            for g in range(GROUP):
                rows = at((kv_at * GROUP + g) * HEAD, HEAD, 64)
                value = s_att[rows, :] / total[:, g * toks : (g + 1) * toks]
                s_att[rows, :] = value
                s_context[rows, :] = value.astype(LOW)
            s_lse[one, :] = s_top[one, :] + jnp.log(total)
            return carry

        lax.fori_loop(0, KV_HEADS, finish, 0)

        def out_tile(i, carry):
            rows = at(i * TILE, TILE)
            s_hidden[rows, :] = x_now[rows, :] + dot(
                v_joint[:, at(qkv + i * TILE, TILE)], s_context[...], 0, 0
            )
            return carry

        lax.fori_loop(0, D // TILE, out_tile, 0)
        hidden = s_hidden[...]
        s_second[...] = (hidden * column_scale(hidden) * gains[:, 1:2]).astype(LOW)

        @pl.when(m == 0)
        def _():
            loads[1].wait()

        def gate_tile(i, carry):
            rows, up_rows = at(i * WIDE, WIDE), at(FF + i * WIDE, WIDE)
            gate = dot(v_gate_up[:, rows], s_second[...], 0, 0)
            up = dot(v_gate_up[:, up_rows], s_second[...], 0, 0)
            s_gu[rows, :] = gate
            s_gu[up_rows, :] = up
            s_inner[rows, :] = (gate * jax.nn.sigmoid(gate) * up).astype(LOW)
            return carry

        lax.fori_loop(0, FF // WIDE, gate_tile, 0)

        @pl.when(m == 0)
        def _():
            loads[2].wait()

        def down_tile(i, carry):
            rows = at(i * TILE, TILE)
            value = s_hidden[rows, :] + dot(v_down[:, rows], s_inner[...], 0, 0)
            x_now[rows, :] = value
            x_in[m, rows, :] = value.astype(LOW)
            return carry

        lax.fori_loop(0, D // TILE, down_tile, 0)

        @pl.when(section == 0)
        def _():
            x_copy(m).start()

        for save in saves(m):
            save.start()

        @pl.when(section == 1)
        def _():
            s_result[...] = x_now[...].T
            result_save(m).start()

        return carry

    lax.fori_loop(0, micros, micro, 0)
    for save in saves(micros - 1):
        save.wait()

    @pl.when(section == 1)
    def _():
        result_save(micros - 1).wait()

    for m in range(2):
        @pl.when(section == 0)
        def _(m=m):
            x_copy(m).wait_send()

        for who, copy in kv_sends(m):
            @pl.when(place == who)
            def _(copy=copy):
                copy.wait_send()

        @pl.when(place == 3)
        def _(m=m):
            kv_copy(m, 2, 1, 0, 2).wait_send()


def backward_kernel(
    ends, gains, cosine, sine, seg_row, seg_col, w_joint, w_gate_up, w_down,
    i_x, i_q, i_kv, i_att, i_lse, i_hidden, i_gu,
    o_both, o_mixed, o_hidden, o_grad, o_gains, o_result,
    v_joint, v_gate_up, v_down, g_in, g_now, s_x, s_q, s_kv, s_att, s_lse, s_hid, s_gu,
    s_both, s_mixed, s_hidden, s_grad, s_sum, s_context, s_delta, s_dq, s_dkv, kv_out, kv_in,
    s_gains, s_result, bias,
    w_sem, load_sem, save_sem, kv_send, kv_recv, x_send, x_recv,
):
    section = lax.axis_index("section")
    place = lax.axis_index("ctx")
    micros, toks = ends.shape[0], ends.shape[1]
    qkv = D + 2 * KVW
    w_loads = [
        pltpu.make_async_copy(src, dst, w_sem.at[i])
        for i, (src, dst) in enumerate(
            ((w_joint, v_joint), (w_gate_up, v_gate_up), (w_down, v_down))
        )
    ]

    def loads(m):
        pairs = (
            (i_gu, s_gu), (i_hidden, s_hid), (i_att, s_att), (i_q, s_q), (i_kv, s_kv),
            (i_lse, s_lse), (i_x, s_x),
        )
        return [pltpu.make_async_copy(a.at[m], b, load_sem.at[i]) for i, (a, b) in enumerate(pairs)]

    w_loads[2].start()
    for load in loads(0):
        load.start()
    w_loads[1].start()
    w_loads[0].start()
    greet([{"ctx": (place + i) % 4} for i in (1, 2, 3)] + [{"section": 1 - section}])
    s_gains[...] = jnp.zeros_like(s_gains)

    def saves(m):
        lanes = at(m * toks, toks)
        pairs = (
            (s_both, o_both.at[:, lanes]), (s_mixed, o_mixed.at[:, lanes]),
            (s_hidden, o_hidden.at[:, lanes]), (s_grad, o_grad.at[:, lanes]),
        )
        return [pltpu.make_async_copy(a, b, save_sem.at[i]) for i, (a, b) in enumerate(pairs)]

    def result_save(m):
        return pltpu.make_async_copy(s_result, o_result.at[m], save_sem.at[4])

    def g_copy(m):
        return remote(g_in.at[m], g_in.at[m], x_send.at[m], x_recv.at[m], {"section": 0})

    def kv_copy(m, source, slot, lane, to):
        return remote(
            kv_out.at[m, source], kv_in.at[m, slot], kv_send.at[m, lane], kv_recv.at[m, slot],
            {"ctx": to},
        )

    def kv_sends(m):
        return (
            (1, kv_copy(m, 0, 0, 0, 0)),
            (2, kv_copy(m, 0, 0, 0, 3)),
            (2, kv_copy(m, 1, 1, 1, 0)),
            (3, kv_copy(m, 0, 0, 0, 2)),
            (3, kv_copy(m, 1, 0, 1, 1)),
        )

    def block_grads(d, m, fresh):
        def step(kv_at, carry):
            rows = at(kv_at * HEAD, HEAD, 64)
            value_rows = at(KVW + kv_at * HEAD, HEAD, 64)
            one = pl.ds(kv_at, 1)
            query, grad = s_q[rows, :], s_context[rows, :]
            key, value = s_kv[d, rows, :], s_kv[d, value_rows, :]
            mask = bias[d]
            scores = dot(key, query, 0, 0) + jnp.concatenate([mask] * GROUP, axis=1)
            probs = jnp.exp(scores - s_lse[one, :])
            grad_probs = dot(value, grad, 0, 0)
            grad_scores = (probs * (grad_probs - s_delta[one, :])).astype(LOW)
            s_dkv[rows, :] = dot(query, grad_scores, 1, 1)
            s_dkv[value_rows, :] = dot(grad, probs.astype(LOW), 1, 1)
            grad_query = dot(key, grad_scores, 1, 0)
            if fresh:
                s_dq[rows, :] = grad_query
            else:
                s_dq[rows, :] = s_dq[rows, :] + grad_query
            return carry

        lax.fori_loop(0, KV_HEADS, step, 0)

    def norm_back(grad, source, gain, row):
        scale = column_scale(source)
        unit = source * scale
        product = grad * unit
        fold = product[:, :128]
        for i in range(1, toks // 128):
            fold = fold + product[:, i * 128 : (i + 1) * 128]
        s_gains[row] = s_gains[row] + fold
        inner = grad * gain
        return scale * (inner - unit * jnp.mean(inner * unit, axis=0, keepdims=True))

    def micro(m, carry):
        @pl.when(m > 0)
        def _():
            for save in saves(m - 1):
                save.wait()

            @pl.when(section == 0)
            def _():
                result_save(m - 1).wait()

        fill_bias(bias, seg_row, seg_col, m, place, toks)

        @pl.when(section == 1)
        def _():
            s_grad[...] = ends[m].astype(F32).T.astype(LOW)

        @pl.when(section == 0)
        def _():
            g_copy(m).wait_recv()
            s_grad[...] = g_in[m]

        @pl.when(m == 0)
        def _():
            w_loads[2].wait()

        now = loads(m)
        now[0].wait()

        def inner_tile(i, carry):
            rows, up_rows = at(i * TILE, TILE), at(FF + i * TILE, TILE)
            grad_inner = dot(v_down[rows, :], s_grad[...], 1, 0)
            gate, up = s_gu[rows, :], s_gu[up_rows, :]
            sig = jax.nn.sigmoid(gate)
            s_both[rows, :] = (grad_inner * up * sig * (1.0 + gate * (1.0 - sig))).astype(LOW)
            s_both[up_rows, :] = (grad_inner * (gate * sig)).astype(LOW)
            return carry

        lax.fori_loop(0, FF // TILE, inner_tile, 0)

        @pl.when(m == 0)
        def _():
            w_loads[1].wait()

        @pl.when(m + 1 < micros)
        def _():
            loads(m + 1)[0].start()

        def second_tile(i, carry):
            rows = at(i * TILE, TILE)
            s_sum[rows, :] = dot(v_gate_up[rows, :], s_both[...], 1, 0)
            return carry

        lax.fori_loop(0, D // TILE, second_tile, 0)
        now[1].wait()
        g_now[...] = s_grad[...].astype(F32) + norm_back(s_sum[...], s_hid[...], gains[:, 1:2], 1)
        s_hidden[...] = g_now[...].astype(LOW)

        @pl.when(m == 0)
        def _():
            w_loads[0].wait()

        for i in (2, 3, 4, 5):
            now[i].wait()

        def context_tile(i, carry):
            block = dot(v_joint[at(i * TILE, TILE), qkv:], s_hidden[...], 1, 0).astype(LOW)
            for head in range(TILE // HEAD):
                kv_at = i * (TILE // HEAD // GROUP) + head // GROUP
                g = head % GROUP
                part = block[head * HEAD : (head + 1) * HEAD]
                s_context[at(kv_at * HEAD, HEAD, 64), g * toks : (g + 1) * toks] = part
                seen = s_att[at(i * TILE + head * HEAD, HEAD, 64), :]
                s_delta[pl.ds(kv_at, 1), g * toks : (g + 1) * toks] = jnp.sum(
                    part.astype(F32) * seen, axis=0, keepdims=True
                )
            return carry

        lax.fori_loop(0, D // TILE, context_tile, 0)
        sends = kv_sends(m)

        @pl.when(place == 0)
        def _():
            block_grads(0, m, True)

        @pl.when(place == 1)
        def _():
            block_grads(1, m, True)
            kv_out[m, 0] = s_dkv[...].astype(LOW)
            sends[0][1].start()
            block_grads(0, m, False)

        @pl.when(place == 2)
        def _():
            block_grads(1, m, True)
            kv_out[m, 0] = s_dkv[...].astype(LOW)
            sends[1][1].start()
            block_grads(2, m, False)
            kv_out[m, 1] = s_dkv[...].astype(LOW)
            sends[2][1].start()
            block_grads(0, m, False)

        @pl.when(place == 3)
        def _():
            block_grads(2, m, True)
            kv_copy(m, 0, 0, 0, 3).wait_recv()
            kv_out[m, 1] = (s_dkv[...] + kv_in[m, 0].astype(F32)).astype(LOW)
            sends[4][1].start()
            block_grads(1, m, False)
            kv_out[m, 0] = s_dkv[...].astype(LOW)
            sends[3][1].start()
            block_grads(0, m, False)

        cos, sin = cosine[...], sine[...]

        def rotated_back(front, back):
            return jnp.concatenate([front * cos + back * sin, back * cos - front * sin], axis=0)

        def query_back(kv_at, carry):
            for g in range(GROUP):
                lanes = slice(g * toks, (g + 1) * toks)
                front = s_dq[at(kv_at * HEAD, HALF, 32), lanes] * SCALE
                back = s_dq[at(kv_at * HEAD + HALF, HALF, 32), lanes] * SCALE
                rows = at((kv_at * GROUP + g) * HEAD, HEAD, 64)
                s_mixed[rows, :] = rotated_back(front, back).astype(LOW)
            return carry

        lax.fori_loop(0, KV_HEADS, query_back, 0)

        def normed_tile(i, carry):
            rows = at(i * TILE, TILE)
            s_sum[rows, :] = dot(v_joint[rows, :D], s_mixed[:D, :], 1, 0)
            return carry

        lax.fori_loop(0, D // TILE, normed_tile, 0)

        @pl.when(place == 0)
        def _():
            kv_copy(m, 0, 0, 0, 0).wait_recv()
            kv_copy(m, 0, 1, 0, 0).wait_recv()
            s_dkv[...] = s_dkv[...] + kv_in[m, 0].astype(F32) + kv_in[m, 1].astype(F32)

        @pl.when((place == 1) | (place == 2))
        def _():
            kv_copy(m, 0, 0, 0, 0).wait_recv()
            s_dkv[...] = s_dkv[...] + kv_in[m, 0].astype(F32)

        for head in range(KV_HEADS):
            front = s_dkv[head * HEAD : head * HEAD + HALF, :]
            back = s_dkv[head * HEAD + HALF : (head + 1) * HEAD, :]
            s_mixed[D + head * HEAD : D + (head + 1) * HEAD, :] = rotated_back(front, back).astype(LOW)
        s_mixed[D + KVW : qkv, :] = s_dkv[KVW : 2 * KVW, :].astype(LOW)

        def rest_tile(i, carry):
            rows = at(i * TILE, TILE)
            s_sum[rows, :] = s_sum[rows, :] + dot(v_joint[rows, D:qkv], s_mixed[D:qkv, :], 1, 0)
            return carry

        lax.fori_loop(0, D // TILE, rest_tile, 0)
        now[6].wait()
        g_now[...] = g_now[...] + norm_back(s_sum[...], s_x[...].astype(F32), gains[:, 0:1], 0)

        @pl.when(section == 1)
        def _():
            g_in[m] = g_now[...].astype(LOW)
            g_copy(m).start()

        @pl.when(m + 1 < micros)
        def _():
            for load in loads(m + 1)[1:]:
                load.start()

        for save in saves(m):
            save.start()

        @pl.when(section == 0)
        def _():
            s_result[...] = g_now[...].T
            result_save(m).start()

        return carry

    lax.fori_loop(0, micros, micro, 0)
    gains_save = pltpu.make_async_copy(s_gains, o_gains, save_sem.at[5])
    gains_save.start()
    for save in saves(micros - 1):
        save.wait()

    @pl.when(section == 0)
    def _():
        result_save(micros - 1).wait()

    gains_save.wait()
    for m in range(2):
        @pl.when(section == 1)
        def _(m=m):
            g_copy(m).wait_send()

        for who, copy in kv_sends(m):
            @pl.when(place == who)
            def _(copy=copy):
                copy.wait_send()


def run_forward(ends, gains, cosine, sine, seg_row, seg_col, joint, gate_up, down):
    micros, toks = ends.shape[0], ends.shape[1]
    width = GROUP * toks
    vm, hbm = pl.BlockSpec(memory_space=pltpu.VMEM), pl.BlockSpec(memory_space=pl.ANY)
    sem = pltpu.SemaphoreType.DMA
    outs = [
        ((D, micros * toks), LOW), ((D, micros * toks), LOW), ((D, micros * toks), LOW),
        ((FF, micros * toks), LOW), ((micros, D, toks), LOW), ((micros, KVW, width), LOW),
        ((micros, 3, 2 * KVW, toks), LOW), ((micros, D, toks), F32), ((micros, 8, width), F32),
        ((micros, D, toks), F32), ((micros, 2 * FF, toks), F32), ((micros, toks, D), F32),
    ]
    scratch = [
        (joint.shape, LOW), (gate_up.shape, LOW), (down.shape, LOW),
        ((micros, D, toks), LOW), ((D, toks), F32),
        ((D, toks), LOW), ((D, toks), LOW), ((D, toks), LOW), ((FF, toks), LOW), ((D, toks), LOW),
        ((KVW, width), LOW), ((micros, 3, 2 * KVW, toks), LOW), ((D, toks), F32), ((8, width), F32),
        ((8, width), F32), ((D, toks), F32), ((2 * FF, toks), F32), ((toks, D), F32), ((3, toks, toks), F32),
    ]
    return pl.pallas_call(
        forward_kernel,
        out_shape=tuple(jax.ShapeDtypeStruct(s, t) for s, t in outs),
        in_specs=[vm] * 6 + [hbm] * 3,
        out_specs=(hbm,) * len(outs),
        scratch_shapes=[pltpu.VMEM(s, t) for s, t in scratch]
        + [sem((3,)), sem((12,)), sem((micros, 2)), sem((micros, 3)), sem((micros,)), sem((micros,))],
        compiler_params=pltpu.CompilerParams(
            collective_id=3, has_side_effects=True, vmem_limit_bytes=62 * 2**20
        ),
        name="layer_forward",
    )(ends, gains, cosine, sine, seg_row, seg_col, joint, gate_up, down)


def run_backward(ends, gains, cosine, sine, seg_row, seg_col, joint, gate_up, down, saved):
    micros, toks = ends.shape[0], ends.shape[1]
    width = GROUP * toks
    vm, hbm = pl.BlockSpec(memory_space=pltpu.VMEM), pl.BlockSpec(memory_space=pl.ANY)
    sem = pltpu.SemaphoreType.DMA
    qkv = D + 2 * KVW
    outs = [
        ((2 * FF, micros * toks), LOW), ((qkv, micros * toks), LOW), ((D, micros * toks), LOW),
        ((D, micros * toks), LOW), ((2, D, 128), F32), ((micros, toks, D), F32),
    ]
    scratch = [
        (joint.shape, LOW), (gate_up.shape, LOW), (down.shape, LOW),
        ((micros, D, toks), LOW), ((D, toks), F32),
        ((D, toks), LOW), ((KVW, width), LOW), ((3, 2 * KVW, toks), LOW), ((D, toks), F32), ((8, width), F32),
        ((D, toks), F32), ((2 * FF, toks), F32),
        ((2 * FF, toks), LOW), ((qkv, toks), LOW), ((D, toks), LOW), ((D, toks), LOW), ((D, toks), F32),
        ((KVW, width), LOW), ((8, width), F32), ((KVW, width), F32), ((2 * KVW, toks), F32),
        ((micros, 2, 2 * KVW, toks), LOW), ((micros, 2, 2 * KVW, toks), LOW),
        ((2, D, 128), F32), ((toks, D), F32), ((3, toks, toks), F32),
    ]
    return pl.pallas_call(
        backward_kernel,
        out_shape=tuple(jax.ShapeDtypeStruct(s, t) for s, t in outs),
        in_specs=[vm] * 6 + [hbm] * 10,
        out_specs=(hbm,) * len(outs),
        scratch_shapes=[pltpu.VMEM(s, t) for s, t in scratch]
        + [sem((3,)), sem((7,)), sem((6,)), sem((micros, 2)), sem((micros, 2)), sem((micros,)), sem((micros,))],
        compiler_params=pltpu.CompilerParams(
            collective_id=4, has_side_effects=True, vmem_limit_bytes=62 * 2**20
        ),
        name="layer_backward",
    )(ends, gains, cosine, sine, seg_row, seg_col, joint, gate_up, down, *saved)


def small_mesh():
    return lax.axis_size("ctx") == 4 and lax.axis_size("fsdp") == 4


def whole_weights(w_qkv, w_out, w_gate_up, w_down):
    return tuple(
        lax.all_gather(w, "fsdp", axis=0, tiled=True) for w in (w_qkv, w_out, w_gate_up, w_down)
    )


def owned_grads(lefts, rights):
    return tuple(
        lax.psum_scatter(
            outer_product(left, right).astype(jnp.bfloat16),
            ("ctx", "fsdp"),
            scatter_dimension=0,
            tiled=True,
        ).astype(jnp.float32)
        for left, right in zip(lefts, rights)
    )


def local_small(ends, segment_ids, w_qkv, w_out, w_gate_up, w_down, gains):
    section_index = lax.axis_index("section")
    tok_rows = ends.shape[3]
    local_ends = ends[0, :, 0]
    seg_local = segment_ids[:, 0]
    seg_whole = lax.all_gather(seg_local, "ctx", axis=1, tiled=True)
    query_pos = lax.axis_index("ctx") * tok_rows + jnp.arange(tok_rows, dtype=jnp.int32)
    frequency = 10000.0 ** (-(jnp.arange(HEAD // 2).astype(jnp.float32) * 2.0 / HEAD))
    angle_table = frequency[:, None] * query_pos.astype(jnp.float32)[None, :]
    shared = (
        local_ends,
        gains[0].T,
        jnp.cos(angle_table),
        jnp.sin(angle_table),
        seg_local[:, None, :],
        seg_whole[:, :, None],
    ) + tuple(gather_weights(jnp.concatenate([w_qkv[0], w_out[0]], axis=1), w_gate_up[0], w_down[0]))
    normed, context, second, inner, *saved, result = run_forward(*shared)
    x, q, kv, att, lse, hidden, gate_up = saved
    both, mixed, hidden_low, grad, gain_parts, input_grads = run_backward(
        *shared, (x, q, kv, att, lse, hidden, gate_up)
    )
    gain_rows = jnp.sum(gain_parts, axis=-1).reshape(2, 16, D // 16)
    gain_tiles = jnp.pad(jnp.swapaxes(gain_rows, 0, 1), ((0, 0), (0, 6), (0, 128 - D // 16)))
    g_down, g_gate_up, g_qkv, g_out, gain = reduce_grads(
        (normed, context, second, inner), (both, mixed, hidden_low, grad), gain_tiles
    )
    ends_out = jnp.where(section_index == 0, input_grads, result)[None, :, None]
    return (
        ends_out, g_qkv[None], g_out[None], g_gate_up[None], g_down[None],
        gain[None, :2, : D // 16],
    )


def local(ends, segment_ids, w_qkv, w_out, w_gate_up, w_down, gains):
    if small_mesh():
        return local_small(ends, segment_ids, w_qkv, w_out, w_gate_up, w_down, gains)
    section_index = lax.axis_index("section")
    micro_count = ends.shape[1]
    tok_rows = ends.shape[3]
    local_ends = ends[0, :, 0]
    seg_local = segment_ids[:, 0]
    seg_whole = lax.all_gather(seg_local, "ctx", axis=1, tiled=True)
    query_pos = lax.axis_index("ctx") * tok_rows + jnp.arange(tok_rows, dtype=jnp.int32)
    frequency = 10000.0 ** (-(jnp.arange(HEAD // 2).astype(jnp.float32) * 2.0 / HEAD))
    angle_table = query_pos.astype(jnp.float32)[:, None] * frequency[None, :]
    cosine = jnp.cos(angle_table)[:, None, :]
    sine_table = jnp.sin(angle_table)[:, None, :]
    gain_pair = gains[0]
    weights = whole_weights(w_qkv[0], w_out[0], w_gate_up[0], w_down[0])
    arrived = jnp.zeros((tok_rows, D), jnp.bfloat16)
    store_bufs = None
    outputs = jnp.zeros((micro_count + 1, tok_rows, D), jnp.float32)
    for tick_num in range(micro_count + 1):
        batch_index = tick_num - section_index
        is_valid = (batch_index >= 0) & (batch_index < micro_count)
        clipped = jnp.clip(batch_index, 0, micro_count - 1)
        slot_index = jnp.where(is_valid, batch_index, micro_count)
        own_rows = lax.dynamic_index_in_dim(local_ends, clipped, 0, keepdims=False)
        layer_in = jnp.where(section_index == 0, own_rows, arrived)
        seg_rows = lax.dynamic_index_in_dim(seg_local, clipped, 0, keepdims=False)
        seg_full = lax.dynamic_index_in_dim(seg_whole, clipped, 0, keepdims=False)
        result, saved_acts = layer_forward(
            layer_in.astype(jnp.float32),
            weights,
            gain_pair,
            seg_rows,
            seg_full,
            query_pos,
            cosine,
            sine_table,
        )
        if tick_num == 0:
            store_bufs = jax.tree.map(
                lambda update: jnp.zeros((micro_count + 1,) + update.shape, update.dtype),
                saved_acts,
            )
        store_bufs = jax.tree.map(
            lambda buffer, update: lax.dynamic_update_index_in_dim(buffer, update, slot_index, 0),
            store_bufs,
            saved_acts,
        )
        outputs = lax.dynamic_update_index_in_dim(outputs, result, slot_index, 0)
        arrived = shifted(result.astype(jnp.bfloat16), "section", 1)
    operand_bufs = None
    gain_sums = jnp.zeros((2, D), jnp.float32)
    arrived_grad = jnp.zeros((tok_rows, D), jnp.bfloat16)
    input_grads = jnp.zeros((micro_count + 1, tok_rows, D), jnp.float32)
    for tick_num in range(micro_count + 1):
        batch_index = tick_num - (1 - section_index)
        is_valid = (batch_index >= 0) & (batch_index < micro_count)
        clipped = jnp.clip(batch_index, 0, micro_count - 1)
        slot_index = jnp.where(is_valid, batch_index, micro_count)
        own_rows = lax.dynamic_index_in_dim(local_ends, clipped, 0, keepdims=False)
        incoming = jnp.where(section_index == 1, own_rows, arrived_grad)
        incoming = jnp.where(is_valid, incoming, jnp.zeros_like(incoming))
        seg_rows = lax.dynamic_index_in_dim(seg_local, clipped, 0, keepdims=False)
        seg_full = lax.dynamic_index_in_dim(seg_whole, clipped, 0, keepdims=False)
        saved_acts = jax.tree.map(
            lambda buffer: lax.dynamic_index_in_dim(buffer, clipped, 0, keepdims=False), store_bufs
        )
        grad_input, operand_pairs, gain_terms = layer_backward(
            incoming,
            saved_acts,
            weights,
            gain_pair,
            seg_rows,
            seg_full,
            query_pos,
            cosine,
            sine_table,
        )
        if tick_num == 0:
            operand_bufs = jax.tree.map(
                lambda update: jnp.zeros((micro_count + 1,) + update.shape, update.dtype),
                operand_pairs,
            )
        operand_bufs = jax.tree.map(
            lambda buffer, update: lax.dynamic_update_index_in_dim(buffer, update, slot_index, 0),
            operand_bufs,
            operand_pairs,
        )
        gain_sums = gain_sums + gain_terms
        input_grads = lax.dynamic_update_index_in_dim(input_grads, grad_input, slot_index, 0)
        arrived_grad = shifted(grad_input.astype(jnp.bfloat16), "section", -1)
    operands = [buffer[:micro_count].reshape(-1, buffer.shape[-1]) for buffer in operand_bufs]
    g_qkv, g_out, g_gate_up, g_down = owned_grads(operands[:4], operands[4:])
    g_gains = lax.psum_scatter(gain_sums, ("ctx", "fsdp"), scatter_dimension=1, tiled=True)
    final_rows = jnp.where(section_index == 0, input_grads[:micro_count], outputs[:micro_count])
    ends_out = final_rows[None, :, None]
    return (ends_out, g_qkv[None], g_out[None], g_gate_up[None], g_down[None], g_gains[None])


def solution(mesh):
    in_specs = (
        P("section", None, "fsdp", "ctx", None),
        P(None, "fsdp", "ctx"),
        P("section", "fsdp", None),
        P("section", "fsdp", None),
        P("section", "fsdp", None),
        P("section", "fsdp", None),
        P("section", None, None),
    )
    out_specs = (
        P("section", None, "fsdp", "ctx", None),
        P("section", ("ctx", "fsdp"), None),
        P("section", ("ctx", "fsdp"), None),
        P("section", ("ctx", "fsdp"), None),
        P("section", ("ctx", "fsdp"), None),
        P("section", None, ("ctx", "fsdp")),
    )
    return jax.shard_map(local, mesh=mesh, in_specs=in_specs, out_specs=out_specs, check_vma=False)
```

```python
import math

import jax
import jax.numpy as jnp
from jax import lax
from jax.experimental import pallas as pl
from jax.experimental.pallas import tpu as pltpu
from jax.sharding import PartitionSpec as P

MESH = pl.DeviceIdType.MESH

D = 1152
HEADS = 18
KV_HEADS = 6
HEAD = 64
FF = 3072
KVW = 384


EPS = 1e-05


def shifted(x, axis, by):
    size = lax.axis_size(axis)
    pairs = [(i, i + by) for i in range(size) if 0 <= i + by < size]
    return lax.ppermute(x, axis, pairs)


def rotate(values_in, cosine, sine_table):
    half_size = values_in.shape[-1] // 2
    front = values_in[..., :half_size]
    back_half = values_in[..., half_size:]
    return jnp.concatenate(
        [front * cosine - back_half * sine_table, back_half * cosine + front * sine_table], axis=-1
    )


def rotate_back(gradient, cosine, sine_table):
    half_size = gradient.shape[-1] // 2
    front = gradient[..., :half_size]
    back_half = gradient[..., half_size:]
    return jnp.concatenate(
        [front * cosine + back_half * sine_table, back_half * cosine - front * sine_table], axis=-1
    )


def norm_forward(inputs, gain_row):
    scale_row = lax.rsqrt(jnp.mean(inputs * inputs, axis=-1, keepdims=True) + EPS)
    unit_rows = inputs * scale_row
    return (unit_rows * gain_row, unit_rows, scale_row)


def norm_backward(gradient, unit_rows, scale_row, gain_row):
    unit_grad = gradient * gain_row
    gain_grad = jnp.sum(gradient * unit_rows, axis=0)
    input_grad = scale_row * (
        unit_grad - unit_rows * jnp.mean(unit_grad * unit_rows, axis=-1, keepdims=True)
    )
    return (input_grad, gain_grad)


def outer_product(left, right):
    return lax.dot_general(
        left, right, (((0,), (0,)), ((), ())), preferred_element_type=jnp.float32
    )


def times_transposed(left, right):
    return lax.dot_general(
        left, right, (((1,), (1,)), ((), ())), preferred_element_type=jnp.float32
    )


def block_needed(first_row, block_rows, seg_full, seg_rows, query_pos):
    last_seg = lax.dynamic_index_in_dim(seg_full, first_row + block_rows - 1, 0, keepdims=False)
    return (first_row <= query_pos[-1]) & (last_seg >= seg_rows[0])


def attend_forward(queries4, key_all, value_all, seg_rows, seg_full, query_pos):
    tok_rows = queries4.shape[0]
    group_size = HEADS // KV_HEADS
    score_scale = HEAD ** (-0.5)
    total_rows = key_all.shape[0]
    block_rows = math.gcd(total_rows, 512)
    block_count = total_rows // block_rows
    key_heads = key_all.reshape(total_rows, KV_HEADS, HEAD)
    value_heads = value_all.reshape(total_rows, KV_HEADS, HEAD)

    def block_scores(block_index):
        first_row = block_index * block_rows
        key_block = lax.dynamic_slice_in_dim(key_heads, first_row, block_rows, 0)
        value_block = lax.dynamic_slice_in_dim(value_heads, first_row, block_rows, 0)
        seg_block = lax.dynamic_slice_in_dim(seg_full, first_row, block_rows, 0)
        key_pos = first_row + jnp.arange(block_rows, dtype=jnp.int32)
        raw_scores = (
            jnp.einsum("qkgd,tkd->kgqt", queries4, key_block, preferred_element_type=jnp.float32)
            * score_scale
        )
        allowed = (key_pos[None, :] <= query_pos[:, None]) & (
            seg_block[None, :] == seg_rows[:, None]
        )
        return (jnp.where(allowed, raw_scores, -1e30), allowed, value_block)

    def first_pass(state_pair, block_index):

        def first_work(state_in):
            row_top, row_total = state_in
            masked, allowed, value_block = block_scores(block_index)
            new_top = jnp.maximum(row_top, jnp.max(masked, axis=-1))
            new_total = row_total * jnp.exp(row_top - new_top) + jnp.sum(
                jnp.exp(masked - new_top[..., None]), axis=-1
            )
            return (new_top, new_total)

        needed = block_needed(block_index * block_rows, block_rows, seg_full, seg_rows, query_pos)
        return (lax.cond(needed, first_work, lambda state_in: state_in, state_pair), None)

    start_state = (
        jnp.full((KV_HEADS, group_size, tok_rows), -1e30, jnp.float32),
        jnp.zeros((KV_HEADS, group_size, tok_rows), jnp.float32),
    )
    block_ids = jnp.arange(block_count, dtype=jnp.int32)
    (row_top, row_total), ignored = lax.scan(first_pass, start_state, block_ids)
    log_total = row_top + jnp.log(row_total)

    def second_pass(summed, block_index):

        def second_work(summed_in):
            masked, allowed, value_block = block_scores(block_index)
            prob_low = jnp.where(allowed, jnp.exp(masked - log_total[..., None]), 0.0).astype(
                jnp.bfloat16
            )
            added = jnp.einsum(
                "kgqt,tkd->qkgd", prob_low, value_block, preferred_element_type=jnp.float32
            )
            return summed_in + added

        needed = block_needed(block_index * block_rows, block_rows, seg_full, seg_rows, query_pos)
        return (lax.cond(needed, second_work, lambda summed_in: summed_in, summed), None)

    start_sum = jnp.zeros((tok_rows, KV_HEADS, group_size, HEAD), jnp.float32)
    attended, ignored = lax.scan(second_pass, start_sum, block_ids)
    return (attended.reshape(tok_rows, D), log_total)


def layer_forward(inputs, weights, gain_pair, seg_rows, seg_full, query_pos, cosine, sine_table):
    w_qkv, w_out, w_gate_up, w_down = weights
    tok_rows = inputs.shape[0]
    group_size = HEADS // KV_HEADS
    normed, unit_one, scale_one = norm_forward(inputs, gain_pair[0])
    normed_low = normed.astype(jnp.bfloat16)
    mixed_proj = jnp.dot(normed_low, w_qkv, preferred_element_type=jnp.float32)
    queries = rotate(mixed_proj[:, :D].reshape(tok_rows, HEADS, HEAD), cosine, sine_table).astype(
        jnp.bfloat16
    )
    key_rows = rotate(
        mixed_proj[:, D : D + KVW].reshape(tok_rows, KV_HEADS, HEAD), cosine, sine_table
    )
    key_rows = key_rows.astype(jnp.bfloat16).reshape(tok_rows, KVW)
    value_rows = mixed_proj[:, D + KVW :].astype(jnp.bfloat16)
    key_all, value_all = (
        lax.all_gather(key_rows, "ctx", axis=0, tiled=True),
        lax.all_gather(value_rows, "ctx", axis=0, tiled=True),
    )
    queries4 = queries.reshape(tok_rows, KV_HEADS, group_size, HEAD)
    attended, log_total = attend_forward(
        queries4, key_all, value_all, seg_rows, seg_full, query_pos
    )
    context = attended.astype(jnp.bfloat16)
    hidden = inputs + jnp.dot(context, w_out, preferred_element_type=jnp.float32)
    second, unit_two, scale_two = norm_forward(hidden, gain_pair[1])
    second_low = second.astype(jnp.bfloat16)
    gate_up = jnp.dot(second_low, w_gate_up, preferred_element_type=jnp.float32)
    gate_pre = gate_up[:, :FF]
    up_pre = gate_up[:, FF:]
    inner_act = (jax.nn.silu(gate_pre) * up_pre).astype(jnp.bfloat16)
    result = hidden + jnp.dot(inner_act, w_down, preferred_element_type=jnp.float32)
    saved_acts = (
        normed_low,
        queries4,
        key_all,
        value_all,
        attended,
        log_total,
        context,
        unit_one,
        scale_one,
        unit_two,
        scale_two,
        second_low,
        gate_pre,
        up_pre,
        inner_act,
    )
    return (result, saved_acts)


def layer_backward(
    grad_low, saved_acts, weights, gain_pair, seg_rows, seg_full, query_pos, cosine, sine_table
):
    w_qkv, w_out, w_gate_up, w_down = weights
    (
        normed_low,
        queries4,
        key_all,
        value_all,
        attended,
        log_total,
        context,
        unit_one,
        scale_one,
        unit_two,
        scale_two,
        second_low,
        gate_pre,
        up_pre,
        inner_act,
    ) = saved_acts
    tok_rows = grad_low.shape[0]
    group_size = HEADS // KV_HEADS
    score_scale = HEAD ** (-0.5)
    grad_out = grad_low.astype(jnp.float32)
    grad_inner = times_transposed(grad_low, w_down)
    sigmoid_gate = jax.nn.sigmoid(gate_pre)
    silu_gate = gate_pre * sigmoid_gate
    grad_gate = grad_inner * up_pre * sigmoid_gate * (1.0 + gate_pre * (1.0 - sigmoid_gate))
    grad_up = grad_inner * silu_gate
    grad_both = jnp.concatenate([grad_gate, grad_up], axis=1).astype(jnp.bfloat16)
    grad_second = times_transposed(grad_both, w_gate_up)
    grad_norm_two, gain_two = norm_backward(grad_second, unit_two, scale_two, gain_pair[1])
    grad_hidden = grad_out + grad_norm_two
    hidden_low = grad_hidden.astype(jnp.bfloat16)
    grad_context = times_transposed(hidden_low, w_out).astype(jnp.bfloat16)
    grad_context4 = grad_context.reshape(tok_rows, KV_HEADS, group_size, HEAD)
    attended4 = attended.reshape(tok_rows, KV_HEADS, group_size, HEAD)
    row_delta = jnp.einsum("qkgd,qkgd->kgq", grad_context4.astype(jnp.float32), attended4)
    total_rows = seg_full.shape[0]
    start_state = (
        jnp.zeros((tok_rows, KV_HEADS, group_size, HEAD), jnp.float32),
        jnp.zeros((total_rows, 2 * KVW), jnp.float32),
    )
    key_piece, value_piece = key_all, value_all
    piece_rows = key_piece.shape[0]
    block_rows = math.gcd(piece_rows, 512)
    block_count = piece_rows // block_rows

    def one_block(block_index, inner_state):
        offset = block_index * block_rows

        def one_work(state_in):
            grad_query, grad_kv = state_in
            key_block = lax.dynamic_slice_in_dim(key_piece, offset, block_rows, 0).reshape(
                block_rows, KV_HEADS, HEAD
            )
            value_block = lax.dynamic_slice_in_dim(value_piece, offset, block_rows, 0).reshape(
                block_rows, KV_HEADS, HEAD
            )
            seg_block = lax.dynamic_slice_in_dim(seg_full, offset, block_rows, 0)
            key_pos = offset + jnp.arange(block_rows, dtype=jnp.int32)
            raw_scores = (
                jnp.einsum(
                    "qkgd,tkd->kgqt", queries4, key_block, preferred_element_type=jnp.float32
                )
                * score_scale
            )
            allowed = (key_pos[None, :] <= query_pos[:, None]) & (
                seg_block[None, :] == seg_rows[:, None]
            )
            prob_full = jnp.where(allowed, jnp.exp(raw_scores - log_total[..., None]), 0.0)
            prob_low = prob_full.astype(jnp.bfloat16)
            grad_value = jnp.einsum(
                "kgqt,qkgd->tkd", prob_low, grad_context4, preferred_element_type=jnp.float32
            )
            grad_prob = jnp.einsum(
                "qkgd,tkd->kgqt", grad_context4, value_block, preferred_element_type=jnp.float32
            )
            grad_scores = (prob_full * (grad_prob - row_delta[..., None])).astype(jnp.bfloat16)
            grad_query = (
                grad_query
                + jnp.einsum(
                    "kgqt,tkd->qkgd", grad_scores, key_block, preferred_element_type=jnp.float32
                )
                * score_scale
            )
            grad_key = (
                jnp.einsum(
                    "kgqt,qkgd->tkd", grad_scores, queries4, preferred_element_type=jnp.float32
                )
                * score_scale
            )
            new_rows = jnp.concatenate(
                [grad_key.reshape(block_rows, KVW), grad_value.reshape(block_rows, KVW)], axis=1
            )
            old_rows = lax.dynamic_slice_in_dim(grad_kv, offset, block_rows, 0)
            grad_kv = lax.dynamic_update_slice_in_dim(grad_kv, old_rows + new_rows, offset, 0)
            return (grad_query, grad_kv)

        needed = block_needed(offset, block_rows, seg_full, seg_rows, query_pos)
        return lax.cond(needed, one_work, lambda state_in: state_in, inner_state)

    grad_query, grad_kv_all = lax.fori_loop(0, block_count, one_block, start_state)
    grad_kv_own = lax.psum_scatter(
        grad_kv_all.astype(jnp.bfloat16), "ctx", scatter_dimension=0, tiled=True
    ).astype(jnp.float32)
    grad_q_pre = rotate_back(grad_query.reshape(tok_rows, HEADS, HEAD), cosine, sine_table).reshape(
        tok_rows, D
    )
    grad_k_pre = rotate_back(
        grad_kv_own[:, :KVW].reshape(tok_rows, KV_HEADS, HEAD), cosine, sine_table
    ).reshape(tok_rows, KVW)
    grad_mixed = jnp.concatenate([grad_q_pre, grad_k_pre, grad_kv_own[:, KVW:]], axis=1).astype(
        jnp.bfloat16
    )
    grad_normed = times_transposed(grad_mixed, w_qkv)
    grad_norm_one, gain_one = norm_backward(grad_normed, unit_one, scale_one, gain_pair[0])
    grad_input = grad_hidden + grad_norm_one
    operand_pairs = (
        normed_low,
        context,
        second_low,
        inner_act,
        grad_mixed,
        hidden_low,
        grad_both,
        grad_low,
    )
    return (grad_input, operand_pairs, jnp.stack([gain_one, gain_two]))


DOWN_COLS = 128
WIDE_COLS = 384
NEAR, MID, FAR, SUMS = 2, 4, 8, 12


def reduce_kernel(
    inner_h, grad_h, second_h, both_h, normed_h, mixed_h, context_h, hidden_h, gain_tiles,
    o_down, o_gate_up, o_qkv, o_out, o_gain,
    *scratch,
):
    kinds = (scratch[0:9], scratch[9:18])
    (near_send, near_recv, mid_send, mid_recv, right_send, right_recv, left_send, left_recv,
     near_free, mid_free, right_free, left_free) = scratch[18:30]
    operands, load_sem, gain_in, gain_send, gain_recv = scratch[30:38], *scratch[38:42]
    inner_t, g_low, second_t, both, normed_t, mixed, context_t, hidden_low = operands
    loads = [
        pltpu.make_async_copy(src, dst, load_sem.at[i])
        for i, (src, dst) in enumerate(
            zip((inner_h, grad_h, second_h, both_h, normed_h, mixed_h, context_h, hidden_h), operands)
        )
    ]
    for load in loads:
        load.start()
    place = lax.axis_index("ctx")
    z = lax.axis_index("fsdp")
    last = lax.axis_size("fsdp") - 1
    y, k = place // 2, place % 2
    y_mate = {"ctx": (1 - y) * 2 + k}
    k_mate = {"ctx": y * 2 + 1 - k}
    right, left = {"fsdp": z + 1}, {"fsdp": z - 1}
    f32, low = jnp.float32, jnp.bfloat16

    n_down = g_low.shape[0] // DOWN_COLS
    n_both = both.shape[0] // WIDE_COLS
    n_mixed = mixed.shape[0] // WIDE_COLS
    n_out = hidden_low.shape[0] // WIDE_COLS
    end_both = n_down + n_both
    end_mixed = end_both + n_mixed
    total = end_mixed + n_out
    hop = 2
    first_z = 3
    final_lag = first_z + hop * 3

    barrier = pltpu.get_barrier_semaphore()
    me = place * 4 + z
    others = [((place + i // 4) % 4, (z + i % 4) % 4) for i in range(1, 16)]
    for to_place, to_z in others:
        pl.semaphore_signal(barrier, inc=1, device_id={"ctx": to_place, "fsdp": to_z}, device_id_type=MESH)
    pl.semaphore_wait(barrier, 15)

    def gain_copy(i):
        to_place, to_z = others[i - 1]
        return pltpu.make_async_remote_copy(
            src_ref=gain_tiles.at[to_place * 4 + to_z], dst_ref=gain_in.at[i],
            send_sem=gain_send.at[i], recv_sem=gain_recv.at[i],
            device_id={"ctx": to_place, "fsdp": to_z}, device_id_type=MESH)

    for i in range(1, 16):
        gain_copy(i).start()

    def typed(j, work):
        @pl.when((j >= 0) & (j < n_down))
        def _():
            work(0)

        @pl.when((j >= n_down) & (j < total))
        def _():
            work(1)

    def near_copy(kind, j):
        out_near, own_near, in_near = kinds[kind][0:3]
        slot = j % NEAR
        return pltpu.make_async_remote_copy(
            src_ref=out_near.at[slot], dst_ref=in_near.at[slot], send_sem=near_send.at[slot],
            recv_sem=near_recv.at[slot], device_id=k_mate, device_id_type=MESH)

    def mid_copy(kind, j):
        out_mid, in_mid = kinds[kind][3:5]
        slot = j % MID
        return pltpu.make_async_remote_copy(
            src_ref=out_mid.at[slot], dst_ref=in_mid.at[slot], send_sem=mid_send.at[slot],
            recv_sem=mid_recv.at[slot], device_id=y_mate, device_id_type=MESH)

    def line_rows(kind, step, rightward):
        rows = kinds[kind][5].shape[1]
        part = rows // 4
        if rightward:
            start = (part * (step + 1)) // 16 * 16
            return start, rows - start
        return 0, (part * step + 15) // 16 * 16

    def line_copy(kind, j, step, rightward):
        start, count = line_rows(kind, step, rightward)
        src, dst = (kinds[kind][6], kinds[kind][7]) if rightward else (kinds[kind][6], kinds[kind][8])
        lane = 0 if rightward else 1
        return pltpu.make_async_remote_copy(
            src_ref=src.at[lane, j % NEAR, pl.ds(start, count), :],
            dst_ref=dst.at[j % FAR, pl.ds(start, count), :],
            send_sem=(right_send if rightward else left_send).at[j % NEAR],
            recv_sem=(right_recv if rightward else left_recv).at[j % FAR],
            device_id=right if rightward else left, device_id_type=MESH)

    def multiply(kind, j, lhs, rhs, first, cols):
        out_near, own_near = kinds[kind][0:2]
        slot = j % NEAR
        rows = own_near.shape[2]
        columns = pl.ds(pl.multiple_of((j - first) * cols, 128), cols)
        block = rhs[columns, :]
        for yy in range(2):
            for mine in (False, True):
                kk = k if mine else 1 - k
                at = pl.ds(pl.multiple_of((yy * 2 + kk) * rows, 16), rows)
                part = lax.dot_general(lhs[at, :], block, (((1,), (1,)), ((), ())), preferred_element_type=f32)
                (own_near if mine else out_near)[slot, yy] = part.astype(low)

    def stage_near(j):
        for i, first in enumerate((0, n_down, end_both, end_mixed)):
            @pl.when(j == first)
            def _(i=i):
                loads[2 * i].wait()
                loads[2 * i + 1].wait()

        @pl.when((j >= NEAR) & (j < total))
        def _():
            typed(j - NEAR, lambda kind: near_copy(kind, j - NEAR).wait_send())

        @pl.when(j < n_down)
        def _():
            multiply(0, j, inner_t, g_low, 0, DOWN_COLS)

        @pl.when((j >= n_down) & (j < end_both))
        def _():
            multiply(1, j, second_t, both, n_down, WIDE_COLS)

        @pl.when((j >= end_both) & (j < end_mixed))
        def _():
            multiply(1, j, normed_t, mixed, end_both, WIDE_COLS)

        @pl.when((j >= end_mixed) & (j < total))
        def _():
            multiply(1, j, context_t, hidden_low, end_mixed, WIDE_COLS)

        @pl.when((j >= NEAR) & (j < total))
        def _():
            pl.semaphore_wait(near_free, 1)

        typed(j, lambda kind: near_copy(kind, j).start())

    def stage_mid(j):
        def work(kind):
            out_near, own_near, in_near, out_mid, in_mid, sums = kinds[kind][0:6]
            near_copy(kind, j).wait_recv()
            slot = j % NEAR
            out_mid[j % MID] = (own_near[slot, 1 - y].astype(f32) + in_near[slot, 1 - y].astype(f32)).astype(low)
            sums[j % SUMS] = own_near[slot, y].astype(f32) + in_near[slot, y].astype(f32)

        @pl.when((j >= MID) & (j < total))
        def _():
            typed(j - MID, lambda kind: mid_copy(kind, j - MID).wait_send())

        typed(j, work)

        @pl.when((j >= 0) & (j + NEAR < total))
        def _():
            pl.semaphore_signal(near_free, inc=1, device_id=k_mate, device_id_type=MESH)

        @pl.when((j >= MID) & (j < total))
        def _():
            pl.semaphore_wait(mid_free, 1)

        typed(j, lambda kind: mid_copy(kind, j).start())

    def stage_sum(j):
        def work(kind):
            in_mid, sums = kinds[kind][4:6]
            mid_copy(kind, j).wait_recv()
            sums[j % SUMS] = sums[j % SUMS] + in_mid[j % MID].astype(f32)

        typed(j, work)

        @pl.when((j >= 0) & (j + MID < total))
        def _():
            pl.semaphore_signal(mid_free, inc=1, device_id=y_mate, device_id_type=MESH)

    def stage_line(i, rightward):
        free = right_free if rightward else left_free
        for at in range(4):
            step = at if rightward else 3 - at
            if step == 3:
                continue
            j = i - first_z - hop * step

            @pl.when((z == at) & (j >= 0) & (j < total))
            def _(at=at, step=step, j=j):
                @pl.when(j >= NEAR)
                def _():
                    typed(j - NEAR, lambda kind: line_copy(kind, j - NEAR, at, rightward).wait_send())

                def work(kind):
                    sums, out_line, in_right, in_left = kinds[kind][5:9]
                    start, count = line_rows(kind, at, rightward)
                    rows = pl.ds(start, count)
                    value = sums[j % SUMS, rows, :]
                    if step > 0:
                        came = line_rows(kind, at - 1 if rightward else at + 1, rightward)
                        arrive = line_copy(kind, j, at - 1 if rightward else at + 1, rightward)
                        arrive.wait_recv()
                        value = value + (in_right if rightward else in_left)[j % FAR, rows, :].astype(f32)
                    out_line[0 if rightward else 1, j % NEAR, rows, :] = value.astype(low)

                typed(j, work)

                @pl.when(j >= FAR)
                def _():
                    pl.semaphore_wait(free, 1)

                typed(j, lambda kind: line_copy(kind, j, at, rightward).start())

    def store(kind, j, value):
        if kind == 0:
            o_down[:, pl.ds(pl.multiple_of(j * DOWN_COLS, 128), DOWN_COLS)] = value
            return
        for out, first, end in ((o_gate_up, n_down, end_both), (o_qkv, end_both, end_mixed), (o_out, end_mixed, total)):
            @pl.when((j >= first) & (j < end))
            def _(out=out, first=first):
                out[:, pl.ds(pl.multiple_of((j - first) * WIDE_COLS, 128), WIDE_COLS)] = value

    def stage_final(j):
        for at in range(4):
            @pl.when((z == at) & (j >= 0) & (j < total))
            def _(at=at):
                def work(kind):
                    sums, out_line, in_right, in_left = kinds[kind][5:9]
                    part = sums.shape[1] // 4
                    if at == 3:
                        line_copy(kind, j, 2, True).wait_recv()
                    if at == 0:
                        line_copy(kind, j, 1, False).wait_recv()
                    low_at = at * part // 16 * 16
                    high_at = (at * part + part + 15) // 16 * 16
                    rows = pl.ds(low_at, high_at - low_at)
                    value = sums[j % SUMS, rows, :]
                    if at > 0:
                        value = value + in_right[j % FAR, rows, :].astype(f32)
                    if at < 3:
                        value = value + in_left[j % FAR, rows, :].astype(f32)
                    shift = at * part - low_at
                    store(kind, j, value[shift:shift + part])

                typed(j, work)
                if at > 0:
                    @pl.when(j + FAR < total)
                    def _():
                        pl.semaphore_signal(right_free, inc=1, device_id=left, device_id_type=MESH)
                if at < 3:
                    @pl.when(j + FAR < total)
                    def _():
                        pl.semaphore_signal(left_free, inc=1, device_id=right, device_id_type=MESH)

    def iteration(i, carry):
        stage_near(i)
        stage_mid(i - 1)
        stage_sum(i - 3)
        stage_line(i, True)
        stage_line(i, False)
        stage_final(i - final_lag)
        return carry

    lax.fori_loop(0, total + final_lag, iteration, 0)
    gain = gain_tiles[me]
    for i in range(1, 16):
        gain_copy(i).wait()
        gain = gain + gain_in[i]
    o_gain[...] = gain
    for j in range(total - NEAR, total):
        near_copy(1, j).wait_send()
        for at in range(3):
            @pl.when(z == at)
            def _(at=at):
                line_copy(1, j, at, True).wait_send()

            @pl.when(z == at + 1)
            def _(at=at):
                line_copy(1, j, at + 1, False).wait_send()
    for j in range(total - MID, total):
        mid_copy(1, j).wait_send()


def reduce_grads(lefts, rights, gain_tiles):
    normed, context, second, inner = lefts
    both, mixed, hidden, grad = rights
    ops = (inner, grad, second, both, normed, mixed, context, hidden)
    low, f32 = jnp.bfloat16, jnp.float32
    scratch = []
    for rows, cols in ((inner.shape[0] // 4, DOWN_COLS), (second.shape[0] // 4, WIDE_COLS)):
        scratch += [
            pltpu.VMEM((NEAR, 2, rows, cols), low), pltpu.VMEM((NEAR, 2, rows, cols), low), pltpu.VMEM((NEAR, 2, rows, cols), low),
            pltpu.VMEM((MID, rows, cols), low), pltpu.VMEM((MID, rows, cols), low),
            pltpu.VMEM((SUMS, rows, cols), f32),
            pltpu.VMEM((2, NEAR, rows, cols), low),
            pltpu.VMEM((FAR, rows, cols), low), pltpu.VMEM((FAR, rows, cols), low)]
    sem = pltpu.SemaphoreType
    scratch += [sem.DMA((NEAR,)), sem.DMA((NEAR,)), sem.DMA((MID,)), sem.DMA((MID,)),
                sem.DMA((NEAR,)), sem.DMA((FAR,)), sem.DMA((NEAR,)), sem.DMA((FAR,)),
                sem.REGULAR, sem.REGULAR, sem.REGULAR, sem.REGULAR]
    scratch += [pltpu.VMEM(op.shape, low) for op in ops]
    scratch += [sem.DMA((8,)), pltpu.VMEM((16, 8, 128), f32), sem.DMA((16,)), sem.DMA((16,))]
    outs = [(a.shape[0] // 16, b.shape[0]) for a, b in zip(ops[0::2], ops[1::2])] + [(8, 128)]
    vm, hbm = pl.BlockSpec(memory_space=pltpu.VMEM), pl.BlockSpec(memory_space=pl.ANY)
    return pl.pallas_call(
        reduce_kernel,
        out_shape=tuple(jax.ShapeDtypeStruct(s, f32) for s in outs),
        in_specs=[hbm] * 8 + [vm],
        out_specs=(vm,) * 5,
        scratch_shapes=scratch,
        compiler_params=pltpu.CompilerParams(collective_id=2, has_side_effects=True, vmem_limit_bytes=62 * 2**20),
        name="grads_reduce",
    )(*ops, gain_tiles)


F32, LOW = jnp.float32, jnp.bfloat16
GROUP = HEADS // KV_HEADS
HALF = HEAD // 2
SCALE = HEAD ** (-0.5)
NONE = -1e30
TILE = 384
WIDE = 512


def dot(left, right, left_dim, right_dim):
    return lax.dot_general(
        left, right, (((left_dim,), (right_dim,)), ((), ())), preferred_element_type=F32
    )


def at(start, size, step=128):
    return pl.ds(pl.multiple_of(start, step), size)


def column_scale(v):
    return lax.rsqrt(jnp.mean(v * v, axis=0, keepdims=True) + EPS)


def greet(peers):
    barrier = pltpu.get_barrier_semaphore()
    for peer in peers:
        pl.semaphore_signal(barrier, inc=1, device_id=peer, device_id_type=MESH)
    pl.semaphore_wait(barrier, len(peers))


def remote(src, dst, send, recv, peer):
    return pltpu.make_async_remote_copy(
        src_ref=src, dst_ref=dst, send_sem=send, recv_sem=recv, device_id=peer, device_id_type=MESH
    )


def fill_bias(bias, segments, m, place, toks):
    own = segments[place, pl.ds(m, 1), :]
    rows = lax.broadcasted_iota(jnp.int32, (toks, toks), 0)
    cols = lax.broadcasted_iota(jnp.int32, (toks, toks), 1)
    for d in range(3):
        seen = segments[jnp.maximum(place - d, 0), pl.ds(m, 1), :]
        keys = jnp.broadcast_to(seen, (8, toks)).T[:, 0:1]
        allowed = keys == own
        if d == 0:
            allowed = allowed & (rows <= cols)
        bias[d] = jnp.where(allowed, 0.0, NONE)


def gain_columns(gains, columns):
    for row in range(2):
        columns[:, row : row + 1] = jnp.broadcast_to(gains[row : row + 1, :], (8, D)).T[:, 0:1]


JOINT_CHUNKS, WIDE_CHUNKS, DOWN_CHUNKS = 3, 3, 4
CHUNKS = JOINT_CHUNKS + WIDE_CHUNKS + DOWN_CHUNKS
SLAB = 1024


def forward_kernel(
    ends, gains, cosine, sine, seg_own, w_qkv, w_out, w_gate_up, w_down,
    f_joint, f_gate_up, f_down, o_seg,
    o_normed, o_context, o_second, o_inner, o_x, o_q, o_kv, o_att, o_lse, o_hidden, o_gu, o_result,
    t_joint, t_gate_up, t_down, stage, stage_down, x_in, x_now, s_normed, s_context, s_second,
    s_inner, s_x, s_q, s_kv, s_att, s_top, s_lse, s_hidden, s_gu, s_result, bias, segments, columns,
    stage_sem, seg_sem, save_sem, kv_send, kv_recv, x_send, x_recv,
    own_sem, back_sem, zs, zr, ys, yr, cs, cr, es, er,
):
    section = lax.axis_index("section")
    place = lax.axis_index("ctx")
    z = lax.axis_index("fsdp")
    last = lax.axis_size("fsdp") - 1
    y, k = place // 2, place % 2
    y_mate = {"ctx": (1 - y) * 2 + k}
    k_mate = {"ctx": y * 2 + 1 - k}
    micros, toks = ends.shape[0], ends.shape[1]
    qkv = D + 2 * KVW
    width, deep = w_gate_up.shape[0], w_down.shape[0]
    half, joint_half, wide_half = width // 2, f_joint.shape[1] // 2, f_gate_up.shape[1] // 2

    barrier = pltpu.get_barrier_semaphore()
    for peer in [{"ctx": (place + i) % 4} for i in (1, 2, 3)] + [{"section": 1 - section}]:
        pl.semaphore_signal(barrier, inc=1, device_id=peer, device_id_type=MESH)

    @pl.when(z > 0)
    def _():
        pl.semaphore_signal(barrier, inc=1, device_id={"fsdp": z - 1}, device_id_type=MESH)

    @pl.when(z < last)
    def _():
        pl.semaphore_signal(barrier, inc=1, device_id={"fsdp": z + 1}, device_id_type=MESH)

    pl.semaphore_wait(barrier, 4 + jnp.where(z > 0, 1, 0) + jnp.where(z < last, 1, 0))

    def view(shard, yy, kk, j, own=False):
        if j < JOINT_CHUNKS:
            rows = half // JOINT_CHUNKS
            return f_joint.at[
                at(shard * width + yy * half + j * rows, rows, 16), at(kk * joint_half, joint_half)
            ]
        j = j - JOINT_CHUNKS
        if j < WIDE_CHUNKS:
            cols = wide_half // WIDE_CHUNKS
            ref, first = (w_gate_up, 0) if own else (f_gate_up, shard * width)
            return ref.at[at(first + yy * half, half, 16), at(kk * wide_half + j * cols, cols)]
        j = j - WIDE_CHUNKS
        rows = deep // 4 // DOWN_CHUNKS
        ref, first = (w_down, 0) if own else (f_down, shard * deep)
        return ref.at[at(first + (yy * 2 + kk) * (deep // 4) + j * rows, rows, 16), :]

    def z_copy(shard, j, to, own, back):
        ref = view(shard, y, k, j)
        src = view(shard, y, k, j, True) if own and j >= JOINT_CHUNKS else ref
        return remote(
            src, ref, back_sem.at[j] if back else zs.at[shard, j], zr.at[shard, j], {"fsdp": to}
        )

    def own_start(j, to, back):
        if j >= JOINT_CHUNKS:
            z_copy(z, j, to, True, back).start()
            return
        rows = half // JOINT_CHUNKS
        here = at(y * half + j * rows, rows, 16)
        there = at(z * width + y * half + j * rows, rows, 16)
        send, recv = back_sem.at[j] if back else zs.at[z, j], zr.at[z, j]

        @pl.when(k == 0)
        def _():
            remote(
                w_qkv.at[here, 0:joint_half], f_joint.at[there, 0:joint_half], send, recv, {"fsdp": to}
            ).start()

        @pl.when(k == 1)
        def _():
            remote(
                w_qkv.at[here, joint_half:qkv], f_joint.at[there, joint_half:qkv], send, recv, {"fsdp": to}
            ).start()
            remote(w_out.at[here, :], f_joint.at[there, qkv:], send, recv, {"fsdp": to}).start()

    def own_sends(j):
        @pl.when(z < last)
        def _():
            own_start(j, z + 1, False)

        @pl.when(z > 0)
        def _():
            own_start(j, z - 1, True)

    def mate_copy(shard, j, yy, mate, send, recv):
        ref = view(shard, yy, k, j)
        return remote(ref, ref, send.at[shard, j], recv.at[shard, j], mate)

    def arrive(shard, j, yy, kk, recv):
        ref = view(shard, yy, kk, j)
        remote(ref, ref, recv.at[shard, j], recv.at[shard, j], k_mate).wait_recv()

    rows_z, rows_deep = at(z * width, width, 16), at(z * deep, deep, 16)
    own_pairs = (
        (w_qkv, f_joint.at[rows_z, 0:qkv]), (w_out, f_joint.at[rows_z, qkv:]),
        (w_gate_up, f_gate_up.at[rows_z, :]), (w_down, f_down.at[rows_deep, :]),
    )
    own_copies = [
        remote(a, b, own_sem.at[0, i], own_sem.at[1, i], k_mate) for i, (a, b) in enumerate(own_pairs)
    ]

    def sides(d):
        return ((z - d >= 0, z - d, z + 1, z < last), (z + d <= last, z + d, z - 1, z > 0))

    def relay(d, j):
        for valid, shard, onward, more in sides(d):
            @pl.when(valid)
            def _(shard=shard, onward=onward, more=more):
                arrive(shard, j, y, k, zr)
                if d < 3:
                    @pl.when(more)
                    def _():
                        z_copy(shard, j, onward, False, False).start()
                mate_copy(shard, j, y, y_mate, ys, yr).start()
                mate_copy(shard, j, y, k_mate, cs, cr).start()

    def across(d, j):
        for valid, shard, onward, more in sides(d):
            @pl.when(valid)
            def _(shard=shard):
                arrive(shard, j, 1 - y, k, yr)
                mate_copy(shard, j, 1 - y, k_mate, es, er).start()

    def complete(d, j):
        for valid, shard, onward, more in sides(d):
            @pl.when(valid)
            def _(shard=shard):
                arrive(shard, j, y, 1 - k, cr)
                arrive(shard, j, 1 - y, 1 - k, er)

    first_down = JOINT_CHUNKS + WIDE_CHUNKS
    order = [(d, j) for d in (1, 2, 3) for j in range(JOINT_CHUNKS)]
    order += [(d, j) for d in (1, 2, 3) for j in range(JOINT_CHUNKS, CHUNKS)]
    refill = {2: (3,), 3: (4,), 4: (5,), 5: (6, 7), 6: (8, 9)}
    done = {"relay": 0, "across": 0}

    def pump(upto, lag=3):
        while done["relay"] < min(upto, len(order)):
            relay(*order[done["relay"]])
            for extra in refill.get(done["relay"], ()):
                own_sends(extra)
            done["relay"] += 1
            while done["across"] < done["relay"] - lag:
                across(*order[done["across"]])
                done["across"] += 1

    def flush(upto):
        while done["across"] < upto:
            across(*order[done["across"]])
            done["across"] += 1

    def turn_slabs(ref, out, slabs, first, end):
        rows = slice(first, end)
        copies = [
            pltpu.make_async_copy(
                ref.at[rows, q * SLAB : (q + 1) * SLAB], stage.at[i, rows, :], stage_sem.at[i]
            )
            for i, q in enumerate(slabs)
        ]
        for copy in copies:
            copy.start()
        for i, q in enumerate(slabs):
            copies[i].wait()

            def step(c, carry, i=i, q=q):
                cols = at(c * 256, 256)
                out[at(q * SLAB + c * 256, 256), rows] = stage[i, rows, cols].T
                return carry

            lax.fori_loop(0, SLAB // 256, step, 0)

    third = D // 3

    def turn_near(ref, out, slabs):
        for when, first, end in (
            (z == 0, 0, 2 * third), (z == last, third, D), ((z > 0) & (z < last), 0, D),
        ):
            @pl.when(when)
            def _(first=first, end=end):
                turn_slabs(ref, out, slabs, first, end)

    def turn_rest(ref, out, slabs):
        for when, first, end in ((z == 0, 2 * third, D), (z == last, 0, third)):
            @pl.when(when)
            def _(first=first, end=end):
                turn_slabs(ref, out, slabs, first, end)

    def turn_down(shard):
        copy = pltpu.make_async_copy(f_down.at[at(shard * deep, deep), :], stage_down, stage_sem.at[2])
        copy.start()
        copy.wait()

        def step(i, carry):
            t_down[at(i * TILE, TILE), at(shard * deep, deep)] = stage_down[:, at(i * TILE, TILE)].T
            return carry

        lax.fori_loop(0, D // TILE, step, 0)

    def saves(m):
        lanes = at(m * toks, toks)
        pairs = (
            (s_normed, o_normed.at[:, lanes]), (s_context, o_context.at[:, lanes]),
            (s_second, o_second.at[:, lanes]), (s_inner, o_inner.at[:, lanes]),
            (s_x, o_x.at[m]), (s_q, o_q.at[m]), (s_kv.at[m], o_kv.at[m]), (s_att, o_att.at[m]),
            (s_lse, o_lse.at[m]), (s_hidden, o_hidden.at[m]), (s_gu, o_gu.at[m]),
        )
        return [pltpu.make_async_copy(a, b, save_sem.at[i]) for i, (a, b) in enumerate(pairs)]

    def result_save(m):
        return pltpu.make_async_copy(s_result, o_result.at[m], save_sem.at[11])

    def x_copy(m, i):
        part = x_in.at[m, at(i * TILE, TILE), :]
        return remote(part, part, x_send.at[m, i], x_recv.at[m, i], {"section": 1})

    def kv_copy(m, source, slot, lane, to):
        return remote(
            s_kv.at[m, source], s_kv.at[m, slot], kv_send.at[m, lane], kv_recv.at[m, slot],
            {"ctx": to},
        )

    def kv_sends(m):
        return (
            (0, kv_copy(m, 0, 2, 1, 2)),
            (0, kv_copy(m, 0, 1, 0, 1)),
            (1, kv_copy(m, 0, 2, 0, 3)),
            (2, kv_copy(m, 0, 1, 0, 3)),
        )

    def attend(kv_at, m, blocks, fresh):
        rows = at(kv_at * HEAD, HEAD, 64)
        query = s_q[rows, :]
        parts = []
        for d in blocks:
            part = dot(s_kv[m, d, rows, :], query, 0, 0)
            mask = bias[d]
            parts.append(part + jnp.concatenate([mask] * GROUP, axis=1))
        scores = parts[0] if len(parts) == 1 else jnp.concatenate(parts, axis=0)
        top = jnp.max(scores, axis=0, keepdims=True)
        one = pl.ds(kv_at, 1)
        if not fresh:
            old_top, old_total = s_top[one, :], s_lse[one, :]
            top = jnp.maximum(top, old_top)
        probs = jnp.exp(scores - top)
        total = jnp.sum(probs, axis=0, keepdims=True)
        probs = probs.astype(LOW)
        value_rows = at(KVW + kv_at * HEAD, HEAD, 64)
        summed = None
        for i, d in enumerate(blocks):
            term = dot(s_kv[m, d, value_rows, :], probs[i * toks : (i + 1) * toks], 1, 0)
            summed = term if summed is None else summed + term
        if not fresh:
            keep = jnp.exp(old_top - top)
            total = total + old_total * keep
        s_top[one, :] = top
        s_lse[one, :] = total
        for g in range(GROUP):
            lanes = slice(g * toks, (g + 1) * toks)
            out_rows = at((kv_at * GROUP + g) * HEAD, HEAD, 64)
            value = summed[:, lanes]
            if not fresh:
                value = value + s_att[out_rows, :] * keep[:, lanes]
            s_att[out_rows, :] = value

    def each(m, blocks, fresh):
        def step(kv_at, carry):
            attend(kv_at, m, blocks, fresh)
            return carry

        lax.fori_loop(0, KV_HEADS, step, 0)

    def take_own(m):
        x_now[...] = ends[m].astype(F32).T

    def take_sent(m):
        for i in range(D // TILE):
            x_copy(m, i).wait_recv()
        x_now[...] = x_in[m].astype(F32)

    def first_norm(m):
        x = x_now[...]
        s_x[...] = x.astype(LOW)
        s_normed[...] = (x * column_scale(x) * columns[:, 0:1]).astype(LOW)
        fill_bias(bias, segments, m, place, toks)

    def rotated(block, head):
        cos, sin = cosine[...], sine[...]
        front = block[head * HEAD : head * HEAD + HALF]
        back = block[head * HEAD + HALF : (head + 1) * HEAD]
        return jnp.concatenate([front * cos - back * sin, back * cos + front * sin], axis=0)

    def keys_values(m):
        keys = dot(t_joint[D : D + KVW, :], s_normed[...], 1, 0)
        for head in range(KV_HEADS):
            s_kv[m, 0, head * HEAD : (head + 1) * HEAD, :] = rotated(keys, head).astype(LOW)
        s_kv[m, 0, KVW : 2 * KVW, :] = dot(t_joint[D + KVW : qkv, :], s_normed[...], 1, 0).astype(LOW)
        for who, copy in kv_sends(m):
            @pl.when(place == who)
            def _(copy=copy):
                copy.start()

    def queries(m):
        def query_tile(i, carry):
            block = dot(t_joint[at(i * TILE, TILE), :], s_normed[...], 1, 0) * SCALE
            for head in range(TILE // HEAD):
                rows = at((i * (TILE // HEAD // GROUP) + head // GROUP) * HEAD, HEAD, 64)
                g = head % GROUP
                s_q[rows, g * toks : (g + 1) * toks] = rotated(block, head).astype(LOW)
            return carry

        lax.fori_loop(0, D // TILE, query_tile, 0)

    def near_block(m):
        each(m, (0,), True)

    def far_blocks(m):
        @pl.when(place == 1)
        def _():
            kv_copy(m, 0, 1, 0, 1).wait_recv()
            each(m, (1,), False)

        @pl.when(place == 2)
        def _():
            kv_copy(m, 0, 2, 0, 2).wait_recv()
            each(m, (2,), False)
            kv_copy(m, 0, 1, 0, 2).wait_recv()
            each(m, (1,), False)

        @pl.when(place == 3)
        def _():
            kv_copy(m, 0, 1, 0, 3).wait_recv()
            each(m, (1,), False)
            kv_copy(m, 0, 2, 0, 3).wait_recv()
            kv_copy(m, 2, 1, 0, 2).start()
            each(m, (2,), False)

    def contexts(m):
        def finish(kv_at, carry):
            one = pl.ds(kv_at, 1)
            total = s_lse[one, :]
            inverse = 1.0 / total
            for g in range(GROUP):
                rows = at((kv_at * GROUP + g) * HEAD, HEAD, 64)
                value = s_att[rows, :] * inverse[:, g * toks : (g + 1) * toks]
                s_att[rows, :] = value
                s_context[rows, :] = value.astype(LOW)
            s_lse[one, :] = s_top[one, :] + jnp.log(total)
            return carry

        lax.fori_loop(0, KV_HEADS, finish, 0)

    def seconds(m):
        def out_tile(i, carry):
            rows = at(i * TILE, TILE)
            s_hidden[rows, :] = x_now[rows, :] + dot(
                t_joint[at(qkv + i * TILE, TILE), :], s_context[...], 1, 0
            )
            return carry

        lax.fori_loop(0, D // TILE, out_tile, 0)
        hidden = s_hidden[...]
        s_second[...] = (hidden * column_scale(hidden) * columns[:, 1:2]).astype(LOW)

    def gates(first, end):
        def gate_tile(i, carry):
            rows, up_rows = at(i * WIDE, WIDE), at(FF + i * WIDE, WIDE)
            gate = dot(t_gate_up[rows, :], s_second[...], 1, 0)
            up = dot(t_gate_up[up_rows, :], s_second[...], 1, 0)
            s_gu[rows, :] = gate
            s_gu[up_rows, :] = up
            s_inner[rows, :] = (gate * jax.nn.sigmoid(gate) * up).astype(LOW)
            return carry

        lax.fori_loop(first, end, gate_tile, 0)

    def early(work):
        @pl.when(section == 0)
        def _():
            work()

    for j in range(JOINT_CHUNKS):
        own_sends(j)
    for copy in own_copies:
        copy.start()
    segments[place] = seg_own[...]

    def seg_copy(i):
        return remote(
            seg_own, segments.at[place], seg_sem.at[0, i], seg_sem.at[1, i], {"ctx": (place + i) % 4}
        )

    for i in (1, 2, 3):
        seg_copy(i).start()
    gain_columns(gains, columns)
    early(lambda: take_own(0))
    for i in (1, 2, 3):
        seg_copy(i).wait()
    early(lambda: first_norm(0))

    joint_items = 3 * JOINT_CHUNKS
    lap = CHUNKS - JOINT_CHUNKS
    pump(joint_items + 3)
    for j in range(JOINT_CHUNKS):
        for d in (1, 2, 3):
            complete(d, j)
    own_copies[0].wait_recv()
    own_copies[1].wait_recv()

    def turn_all(ref, out, slabs):
        turn_slabs(ref, out, slabs, 0, D)

    turn_all(f_joint, t_joint, (0, 1))
    pump(joint_items + 4)
    turn_all(f_joint, t_joint, (2,))
    pump(joint_items + 5)
    early(lambda: keys_values(0))
    pump(joint_items + 6)
    early(lambda: queries(0))
    pump(joint_items + lap)
    early(lambda: near_block(0))
    pump(joint_items + lap + 5)
    early(lambda: far_blocks(0))
    pump(joint_items + lap + 6)
    early(lambda: contexts(0))
    early(lambda: seconds(0))
    pump(joint_items + 2 * lap)
    own_copies[2].wait_recv()
    for d in (1, 2):
        for j in range(JOINT_CHUNKS, first_down):
            complete(d, j)
    for p in range(WIDE_CHUNKS):
        turn_near(f_gate_up, t_gate_up, (p, WIDE_CHUNKS + p))
        pump(joint_items + 2 * lap + p + 1)

    def turn_downs(d):
        for j in range(first_down, CHUNKS):
            complete(d, j)
        for valid, shard, onward, more in sides(d):
            @pl.when(valid)
            def _(shard=shard):
                turn_down(shard)

    own_copies[3].wait_recv()
    turn_down(z)
    pump(joint_items + 3 * lap - 3)
    turn_downs(1)
    pump(joint_items + 3 * lap - 2)
    turn_downs(2)
    pump(joint_items + 3 * lap - 1)
    per_slab = SLAB // WIDE
    for p in range(WIDE_CHUNKS):
        complete(3, JOINT_CHUNKS + p)
        turn_rest(f_gate_up, t_gate_up, (p, WIDE_CHUNKS + p))
        early(lambda p=p: gates(p * per_slab, (p + 1) * per_slab))
        if p == 0:
            pump(joint_items + 3 * lap)
        flush(joint_items + 3 * lap - 2 + p)
    turn_downs(3)

    def micro(m, carry):
        @pl.when(m > 0)
        def _():
            for save in saves(m - 1):
                save.wait()

            @pl.when(section == 1)
            def _():
                result_save(m - 1).wait()

        @pl.when((section == 1) | (m > 0))
        def _():
            @pl.when(section == 0)
            def _():
                take_own(m)

            @pl.when(section == 1)
            def _():
                take_sent(m)

            first_norm(m)
            keys_values(m)
            queries(m)
            near_block(m)
            far_blocks(m)
            contexts(m)
            seconds(m)
            gates(0, FF // WIDE)

        for i in range(D // TILE):
            rows = slice(i * TILE, (i + 1) * TILE)
            value = s_hidden[rows, :] + dot(t_down[rows, :], s_inner[...], 1, 0)
            x_now[rows, :] = value

            @pl.when(section == 0)
            def _(i=i, rows=rows, value=value):
                x_in[m, rows, :] = value.astype(LOW)
                x_copy(m, i).start()

        for save in saves(m):
            save.start()

        @pl.when(section == 1)
        def _():
            s_result[...] = x_now[...].T
            result_save(m).start()

        return carry

    lax.fori_loop(0, micros, micro, 0)
    seg_save = pltpu.make_async_copy(segments, o_seg, seg_sem.at[0, 0])
    seg_save.start()
    for save in saves(micros - 1):
        save.wait()
    seg_save.wait()

    @pl.when(section == 1)
    def _():
        result_save(micros - 1).wait()

    for m in range(2):
        @pl.when(section == 0)
        def _(m=m):
            for i in range(D // TILE):
                x_copy(m, i).wait_send()

        for who, copy in kv_sends(m):
            @pl.when(place == who)
            def _(copy=copy):
                copy.wait_send()

        @pl.when(place == 3)
        def _(m=m):
            kv_copy(m, 2, 1, 0, 2).wait_send()

    for d, j in order:
        for valid, shard, onward, more in sides(d):
            @pl.when(valid)
            def _(shard=shard, onward=onward, more=more):
                mate_copy(shard, j, y, y_mate, ys, yr).wait_send()
                mate_copy(shard, j, y, k_mate, cs, cr).wait_send()
                mate_copy(shard, j, 1 - y, k_mate, es, er).wait_send()
                if d < 3:
                    @pl.when(more)
                    def _():
                        z_copy(shard, j, onward, False, False).wait_send()
    for j in range(CHUNKS):
        @pl.when(z < last)
        def _(j=j):
            z_copy(z, j, z + 1, True, False).wait_send()

        @pl.when(z > 0)
        def _(j=j):
            z_copy(z, j, z - 1, True, True).wait_send()
    for copy in own_copies:
        copy.wait_send()


def backward_kernel(
    ends, gains, cosine, sine, segments, w_joint, w_gate_up, w_down,
    i_x, i_q, i_kv, i_att, i_lse, i_hidden, i_gu, i_result,
    o_both, o_mixed, o_hidden, o_grad, o_gains, o_result,
    v_joint, v_gate_up, v_down, g_in, g_now, s_x, s_q, s_kv, s_att, s_lse, s_hid, s_gu,
    s_both, s_mixed, s_hidden, s_grad, s_sum, s_context, s_delta, s_dq, s_dkv, kv_out, kv_in,
    s_gains, s_result, bias, columns,
    w_sem, load_sem, save_sem, kv_send, kv_recv, x_send, x_recv,
):
    section = lax.axis_index("section")
    place = lax.axis_index("ctx")
    micros, toks = ends.shape[0], ends.shape[1]
    qkv = D + 2 * KVW
    w_loads = [
        pltpu.make_async_copy(src, dst, w_sem.at[i])
        for i, (src, dst) in enumerate(
            ((w_joint, v_joint), (w_gate_up, v_gate_up), (w_down, v_down))
        )
    ]

    def loads(m):
        pairs = (
            (i_gu, s_gu), (i_hidden, s_hid), (i_att, s_att), (i_q, s_q), (i_kv, s_kv),
            (i_lse, s_lse), (i_x, s_x),
        )
        return [pltpu.make_async_copy(a.at[m], b, load_sem.at[i]) for i, (a, b) in enumerate(pairs)]

    w_loads[2].start()
    for load in loads(0):
        load.start()
    w_loads[1].start()
    w_loads[0].start()
    greet([{"ctx": (place + i) % 4} for i in (1, 2, 3)] + [{"section": 1 - section}])
    s_gains[...] = jnp.zeros_like(s_gains)
    gain_columns(gains, columns)

    def saves(m):
        lanes = at(m * toks, toks)
        pairs = (
            (s_both, o_both.at[:, lanes]), (s_mixed, o_mixed.at[:, lanes]),
            (s_hidden, o_hidden.at[:, lanes]), (s_grad, o_grad.at[:, lanes]),
        )
        return [pltpu.make_async_copy(a, b, save_sem.at[i]) for i, (a, b) in enumerate(pairs)]

    def result_save(m):
        return pltpu.make_async_copy(s_result, o_result.at[m], save_sem.at[4])

    def g_copy(m):
        return remote(g_in.at[m], g_in.at[m], x_send.at[m], x_recv.at[m], {"section": 0})

    def kv_copy(m, source, slot, lane, to):
        return remote(
            kv_out.at[m, source], kv_in.at[m, slot], kv_send.at[m, lane], kv_recv.at[m, slot],
            {"ctx": to},
        )

    def kv_sends(m):
        return (
            (1, kv_copy(m, 0, 0, 0, 0)),
            (2, kv_copy(m, 0, 0, 0, 3)),
            (2, kv_copy(m, 1, 1, 1, 0)),
            (3, kv_copy(m, 0, 0, 0, 2)),
            (3, kv_copy(m, 1, 0, 1, 1)),
        )

    def block_grads(d, m, fresh):
        def step(kv_at, carry):
            rows = at(kv_at * HEAD, HEAD, 64)
            value_rows = at(KVW + kv_at * HEAD, HEAD, 64)
            one = pl.ds(kv_at, 1)
            query, grad = s_q[rows, :], s_context[rows, :]
            key, value = s_kv[d, rows, :], s_kv[d, value_rows, :]
            mask = bias[d]
            scores = dot(key, query, 0, 0) + jnp.concatenate([mask] * GROUP, axis=1)
            probs = jnp.exp(scores - s_lse[one, :])
            grad_probs = dot(value, grad, 0, 0)
            grad_scores = (probs * (grad_probs - s_delta[one, :])).astype(LOW)
            s_dkv[rows, :] = dot(query, grad_scores, 1, 1)
            s_dkv[value_rows, :] = dot(grad, probs.astype(LOW), 1, 1)
            grad_query = dot(key, grad_scores, 1, 0)
            if fresh:
                s_dq[rows, :] = grad_query
            else:
                s_dq[rows, :] = s_dq[rows, :] + grad_query
            return carry

        lax.fori_loop(0, KV_HEADS, step, 0)

    def norm_back(grad, source, gain, row):
        scale = column_scale(source)
        unit = source * scale
        product = grad * unit
        fold = product[:, :128]
        for i in range(1, toks // 128):
            fold = fold + product[:, i * 128 : (i + 1) * 128]
        s_gains[row] = s_gains[row] + fold
        inner = grad * gain
        return scale * (inner - unit * jnp.mean(inner * unit, axis=0, keepdims=True))

    def micro(m, carry):
        @pl.when(m > 0)
        def _():
            for save in saves(m - 1):
                save.wait()

            @pl.when(section == 0)
            def _():
                result_save(m - 1).wait()

        fill_bias(bias, segments, m, place, toks)

        @pl.when(section == 1)
        def _():
            s_grad[...] = ends[m].astype(F32).T.astype(LOW)

        @pl.when(section == 0)
        def _():
            g_copy(m).wait_recv()
            s_grad[...] = g_in[m]

        @pl.when(m == 0)
        def _():
            w_loads[2].wait()

        now = loads(m)
        now[0].wait()

        def inner_tile(i, carry):
            rows, up_rows = at(i * TILE, TILE), at(FF + i * TILE, TILE)
            grad_inner = dot(v_down[rows, :], s_grad[...], 1, 0)
            gate, up = s_gu[rows, :], s_gu[up_rows, :]
            sig = jax.nn.sigmoid(gate)
            s_both[rows, :] = (grad_inner * up * sig * (1.0 + gate * (1.0 - sig))).astype(LOW)
            s_both[up_rows, :] = (grad_inner * (gate * sig)).astype(LOW)
            return carry

        lax.fori_loop(0, FF // TILE, inner_tile, 0)

        @pl.when(m == 0)
        def _():
            w_loads[1].wait()

        @pl.when(m + 1 < micros)
        def _():
            loads(m + 1)[0].start()

        def second_tile(i, carry):
            rows = at(i * TILE, TILE)
            s_sum[rows, :] = dot(v_gate_up[rows, :], s_both[...], 1, 0)
            return carry

        lax.fori_loop(0, D // TILE, second_tile, 0)
        now[1].wait()
        g_now[...] = s_grad[...].astype(F32) + norm_back(s_sum[...], s_hid[...], columns[:, 1:2], 1)
        s_hidden[...] = g_now[...].astype(LOW)

        @pl.when(m == 0)
        def _():
            w_loads[0].wait()

        for i in (2, 3, 4, 5):
            now[i].wait()

        def context_tile(i, carry):
            block = dot(v_joint[at(i * TILE, TILE), qkv:], s_hidden[...], 1, 0).astype(LOW)
            for head in range(TILE // HEAD):
                kv_at = i * (TILE // HEAD // GROUP) + head // GROUP
                g = head % GROUP
                part = block[head * HEAD : (head + 1) * HEAD]
                s_context[at(kv_at * HEAD, HEAD, 64), g * toks : (g + 1) * toks] = part
                seen = s_att[at(i * TILE + head * HEAD, HEAD, 64), :]
                s_delta[pl.ds(kv_at, 1), g * toks : (g + 1) * toks] = jnp.sum(
                    part.astype(F32) * seen, axis=0, keepdims=True
                )
            return carry

        lax.fori_loop(0, D // TILE, context_tile, 0)
        sends = kv_sends(m)

        @pl.when(place == 0)
        def _():
            block_grads(0, m, True)

        @pl.when(place == 1)
        def _():
            block_grads(1, m, True)
            kv_out[m, 0] = s_dkv[...].astype(LOW)
            sends[0][1].start()
            block_grads(0, m, False)

        @pl.when(place == 2)
        def _():
            block_grads(1, m, True)
            kv_out[m, 0] = s_dkv[...].astype(LOW)
            sends[1][1].start()
            block_grads(2, m, False)
            kv_out[m, 1] = s_dkv[...].astype(LOW)
            sends[2][1].start()
            block_grads(0, m, False)

        @pl.when(place == 3)
        def _():
            block_grads(2, m, True)
            kv_copy(m, 0, 0, 0, 3).wait_recv()
            kv_out[m, 1] = (s_dkv[...] + kv_in[m, 0].astype(F32)).astype(LOW)
            sends[4][1].start()
            block_grads(1, m, False)
            kv_out[m, 0] = s_dkv[...].astype(LOW)
            sends[3][1].start()
            block_grads(0, m, False)

        cos, sin = cosine[...], sine[...]

        def rotated_back(front, back):
            return jnp.concatenate([front * cos + back * sin, back * cos - front * sin], axis=0)

        def query_back(kv_at, carry):
            for g in range(GROUP):
                lanes = slice(g * toks, (g + 1) * toks)
                front = s_dq[at(kv_at * HEAD, HALF, 32), lanes] * SCALE
                back = s_dq[at(kv_at * HEAD + HALF, HALF, 32), lanes] * SCALE
                rows = at((kv_at * GROUP + g) * HEAD, HEAD, 64)
                s_mixed[rows, :] = rotated_back(front, back).astype(LOW)
            return carry

        lax.fori_loop(0, KV_HEADS, query_back, 0)

        def normed_tile(i, carry):
            rows = at(i * TILE, TILE)
            s_sum[rows, :] = dot(v_joint[rows, :D], s_mixed[:D, :], 1, 0)
            return carry

        lax.fori_loop(0, D // TILE, normed_tile, 0)

        @pl.when(place == 0)
        def _():
            kv_copy(m, 0, 0, 0, 0).wait_recv()
            kv_copy(m, 0, 1, 0, 0).wait_recv()
            s_dkv[...] = s_dkv[...] + kv_in[m, 0].astype(F32) + kv_in[m, 1].astype(F32)

        @pl.when((place == 1) | (place == 2))
        def _():
            kv_copy(m, 0, 0, 0, 0).wait_recv()
            s_dkv[...] = s_dkv[...] + kv_in[m, 0].astype(F32)

        for head in range(KV_HEADS):
            front = s_dkv[head * HEAD : head * HEAD + HALF, :]
            back = s_dkv[head * HEAD + HALF : (head + 1) * HEAD, :]
            s_mixed[D + head * HEAD : D + (head + 1) * HEAD, :] = rotated_back(front, back).astype(LOW)
        s_mixed[D + KVW : qkv, :] = s_dkv[KVW : 2 * KVW, :].astype(LOW)

        def rest_tile(i, carry):
            rows = at(i * TILE, TILE)
            s_sum[rows, :] = s_sum[rows, :] + dot(v_joint[rows, D:qkv], s_mixed[D:qkv, :], 1, 0)
            return carry

        lax.fori_loop(0, D // TILE, rest_tile, 0)
        now[6].wait()
        g_now[...] = g_now[...] + norm_back(s_sum[...], s_x[...].astype(F32), columns[:, 0:1], 0)

        @pl.when(section == 1)
        def _():
            g_in[m] = g_now[...].astype(LOW)
            g_copy(m).start()

        @pl.when(m + 1 < micros)
        def _():
            for load in loads(m + 1)[1:]:
                load.start()

        for save in saves(m):
            save.start()

        @pl.when(section == 0)
        def _():
            s_result[...] = g_now[...].T
            result_save(m).start()

        return carry

    lax.fori_loop(0, micros, micro, 0)
    gains_save = pltpu.make_async_copy(s_gains, o_gains, save_sem.at[5])
    gains_save.start()
    for save in saves(micros - 1):
        save.wait()

    @pl.when(section == 0)
    def _():
        result_save(micros - 1).wait()

    gains_save.wait()
    for m in range(2):
        @pl.when(section == 1)
        def _(m=m):
            g_copy(m).wait_send()

        for who, copy in kv_sends(m):
            @pl.when(place == who)
            def _(copy=copy):
                copy.wait_send()


def run_forward(ends, gains, cosine, sine, seg_own, w_qkv, w_out, w_gate_up, w_down):
    micros, toks = ends.shape[0], ends.shape[1]
    width = GROUP * toks
    vm, hbm = pl.BlockSpec(memory_space=pltpu.VMEM), pl.BlockSpec(memory_space=pl.ANY)
    sem = pltpu.SemaphoreType.DMA
    joint = w_qkv.shape[1] + w_out.shape[1]
    outs = [
        ((D, joint), LOW), ((D, 2 * FF), LOW), ((FF, D), LOW), ((4, micros, toks), jnp.int32),
        ((D, micros * toks), LOW), ((D, micros * toks), LOW), ((D, micros * toks), LOW),
        ((FF, micros * toks), LOW), ((micros, D, toks), LOW), ((micros, KVW, width), LOW),
        ((micros, 3, 2 * KVW, toks), LOW), ((micros, D, toks), F32), ((micros, 8, width), F32),
        ((micros, D, toks), F32), ((micros, 2 * FF, toks), F32), ((micros, toks, D), F32),
    ]
    scratch = [
        ((joint, D), LOW), ((2 * FF, D), LOW), ((D, FF), LOW), ((2, D, SLAB), LOW), (w_down.shape, LOW),
        ((micros, D, toks), LOW), ((D, toks), F32),
        ((D, toks), LOW), ((D, toks), LOW), ((D, toks), LOW), ((FF, toks), LOW), ((D, toks), LOW),
        ((KVW, width), LOW), ((micros, 3, 2 * KVW, toks), LOW), ((D, toks), F32), ((8, width), F32),
        ((8, width), F32), ((D, toks), F32), ((2 * FF, toks), F32), ((toks, D), F32), ((3, toks, toks), F32),
        ((4, micros, toks), jnp.int32), ((D, 2), F32),
    ]
    return pl.pallas_call(
        forward_kernel,
        out_shape=tuple(jax.ShapeDtypeStruct(s, t) for s, t in outs),
        in_specs=[vm] * 5 + [hbm] * 4,
        out_specs=(hbm,) * len(outs),
        scratch_shapes=[pltpu.VMEM(s, t) for s, t in scratch]
        + [sem((3,)), sem((2, 4)), sem((12,)), sem((micros, 2)), sem((micros, 3)), sem((micros, 3)), sem((micros, 3))]
        + [sem((2, 4)), sem((CHUNKS,))] + [sem((4, CHUNKS))] * 8,
        compiler_params=pltpu.CompilerParams(
            collective_id=3, has_side_effects=True, vmem_limit_bytes=62 * 2**20
        ),
        name="layer_forward",
    )(ends, gains, cosine, sine, seg_own, w_qkv, w_out, w_gate_up, w_down)


def run_backward(ends, gains, cosine, sine, segments, joint, gate_up, down, saved):
    micros, toks = ends.shape[0], ends.shape[1]
    width = GROUP * toks
    vm, hbm = pl.BlockSpec(memory_space=pltpu.VMEM), pl.BlockSpec(memory_space=pl.ANY)
    sem = pltpu.SemaphoreType.DMA
    qkv = D + 2 * KVW
    outs = [
        ((2 * FF, micros * toks), LOW), ((qkv, micros * toks), LOW), ((D, micros * toks), LOW),
        ((D, micros * toks), LOW), ((2, D, 128), F32), ((micros, toks, D), F32),
    ]
    scratch = [
        (joint.shape, LOW), (gate_up.shape, LOW), (down.shape, LOW),
        ((micros, D, toks), LOW), ((D, toks), F32),
        ((D, toks), LOW), ((KVW, width), LOW), ((3, 2 * KVW, toks), LOW), ((D, toks), F32), ((8, width), F32),
        ((D, toks), F32), ((2 * FF, toks), F32),
        ((2 * FF, toks), LOW), ((qkv, toks), LOW), ((D, toks), LOW), ((D, toks), LOW), ((D, toks), F32),
        ((KVW, width), LOW), ((8, width), F32), ((KVW, width), F32), ((2 * KVW, toks), F32),
        ((micros, 2, 2 * KVW, toks), LOW), ((micros, 2, 2 * KVW, toks), LOW),
        ((2, D, 128), F32), ((toks, D), F32), ((3, toks, toks), F32), ((D, 2), F32),
    ]
    return pl.pallas_call(
        backward_kernel,
        out_shape=tuple(jax.ShapeDtypeStruct(s, t) for s, t in outs),
        in_specs=[vm] * 5 + [hbm] * 11,
        out_specs=(hbm,) * len(outs),
        scratch_shapes=[pltpu.VMEM(s, t) for s, t in scratch]
        + [sem((3,)), sem((7,)), sem((6,)), sem((micros, 2)), sem((micros, 2)), sem((micros,)), sem((micros,))],
        compiler_params=pltpu.CompilerParams(
            collective_id=4, has_side_effects=True, vmem_limit_bytes=62 * 2**20
        ),
        input_output_aliases={15: 5},
        name="layer_backward",
    )(ends, gains, cosine, sine, segments, joint, gate_up, down, *saved)


def small_mesh():
    return lax.axis_size("ctx") == 4 and lax.axis_size("fsdp") == 4


def whole_weights(w_qkv, w_out, w_gate_up, w_down):
    return tuple(
        lax.all_gather(w, "fsdp", axis=0, tiled=True) for w in (w_qkv, w_out, w_gate_up, w_down)
    )


def owned_grads(lefts, rights):
    return tuple(
        lax.psum_scatter(
            outer_product(left, right).astype(jnp.bfloat16),
            ("ctx", "fsdp"),
            scatter_dimension=0,
            tiled=True,
        ).astype(jnp.float32)
        for left, right in zip(lefts, rights)
    )


def local_small(ends, segment_ids, w_qkv, w_out, w_gate_up, w_down, gains):
    tok_rows = ends.shape[3]
    local_ends = ends[0, :, 0]
    seg_local = segment_ids[:, 0]
    query_pos = lax.axis_index("ctx") * tok_rows + jnp.arange(tok_rows, dtype=jnp.int32)
    frequency = 10000.0 ** (-(jnp.arange(HEAD // 2).astype(jnp.float32) * 2.0 / HEAD))
    angle_table = frequency[:, None] * query_pos.astype(jnp.float32)[None, :]
    shared = (local_ends, gains[0], jnp.cos(angle_table), jnp.sin(angle_table))
    joint, gate_up, down, segments, normed, context, second, inner, *saved, result = run_forward(
        *shared, seg_local, w_qkv[0], w_out[0], w_gate_up[0], w_down[0]
    )
    both, mixed, hidden_low, grad, gain_parts, ends_rows = run_backward(
        *shared, segments, joint, gate_up, down, (*saved, result)
    )
    gain_rows = jnp.sum(gain_parts, axis=-1).reshape(2, 16, D // 16)
    gain_tiles = jnp.pad(jnp.swapaxes(gain_rows, 0, 1), ((0, 0), (0, 6), (0, 128 - D // 16)))
    g_down, g_gate_up, g_qkv, g_out, gain = reduce_grads(
        (normed, context, second, inner), (both, mixed, hidden_low, grad), gain_tiles
    )
    return (
        ends_rows[None, :, None], g_qkv[None], g_out[None], g_gate_up[None], g_down[None],
        gain[None, :2, : D // 16],
    )


def local(ends, segment_ids, w_qkv, w_out, w_gate_up, w_down, gains):
    if small_mesh():
        return local_small(ends, segment_ids, w_qkv, w_out, w_gate_up, w_down, gains)
    section_index = lax.axis_index("section")
    micro_count = ends.shape[1]
    tok_rows = ends.shape[3]
    local_ends = ends[0, :, 0]
    seg_local = segment_ids[:, 0]
    seg_whole = lax.all_gather(seg_local, "ctx", axis=1, tiled=True)
    query_pos = lax.axis_index("ctx") * tok_rows + jnp.arange(tok_rows, dtype=jnp.int32)
    frequency = 10000.0 ** (-(jnp.arange(HEAD // 2).astype(jnp.float32) * 2.0 / HEAD))
    angle_table = query_pos.astype(jnp.float32)[:, None] * frequency[None, :]
    cosine = jnp.cos(angle_table)[:, None, :]
    sine_table = jnp.sin(angle_table)[:, None, :]
    gain_pair = gains[0]
    weights = whole_weights(w_qkv[0], w_out[0], w_gate_up[0], w_down[0])
    arrived = jnp.zeros((tok_rows, D), jnp.bfloat16)
    store_bufs = None
    outputs = jnp.zeros((micro_count + 1, tok_rows, D), jnp.float32)
    for tick_num in range(micro_count + 1):
        batch_index = tick_num - section_index
        is_valid = (batch_index >= 0) & (batch_index < micro_count)
        clipped = jnp.clip(batch_index, 0, micro_count - 1)
        slot_index = jnp.where(is_valid, batch_index, micro_count)
        own_rows = lax.dynamic_index_in_dim(local_ends, clipped, 0, keepdims=False)
        layer_in = jnp.where(section_index == 0, own_rows, arrived)
        seg_rows = lax.dynamic_index_in_dim(seg_local, clipped, 0, keepdims=False)
        seg_full = lax.dynamic_index_in_dim(seg_whole, clipped, 0, keepdims=False)
        result, saved_acts = layer_forward(
            layer_in.astype(jnp.float32),
            weights,
            gain_pair,
            seg_rows,
            seg_full,
            query_pos,
            cosine,
            sine_table,
        )
        if tick_num == 0:
            store_bufs = jax.tree.map(
                lambda update: jnp.zeros((micro_count + 1,) + update.shape, update.dtype),
                saved_acts,
            )
        store_bufs = jax.tree.map(
            lambda buffer, update: lax.dynamic_update_index_in_dim(buffer, update, slot_index, 0),
            store_bufs,
            saved_acts,
        )
        outputs = lax.dynamic_update_index_in_dim(outputs, result, slot_index, 0)
        arrived = shifted(result.astype(jnp.bfloat16), "section", 1)
    operand_bufs = None
    gain_sums = jnp.zeros((2, D), jnp.float32)
    arrived_grad = jnp.zeros((tok_rows, D), jnp.bfloat16)
    input_grads = jnp.zeros((micro_count + 1, tok_rows, D), jnp.float32)
    for tick_num in range(micro_count + 1):
        batch_index = tick_num - (1 - section_index)
        is_valid = (batch_index >= 0) & (batch_index < micro_count)
        clipped = jnp.clip(batch_index, 0, micro_count - 1)
        slot_index = jnp.where(is_valid, batch_index, micro_count)
        own_rows = lax.dynamic_index_in_dim(local_ends, clipped, 0, keepdims=False)
        incoming = jnp.where(section_index == 1, own_rows, arrived_grad)
        incoming = jnp.where(is_valid, incoming, jnp.zeros_like(incoming))
        seg_rows = lax.dynamic_index_in_dim(seg_local, clipped, 0, keepdims=False)
        seg_full = lax.dynamic_index_in_dim(seg_whole, clipped, 0, keepdims=False)
        saved_acts = jax.tree.map(
            lambda buffer: lax.dynamic_index_in_dim(buffer, clipped, 0, keepdims=False), store_bufs
        )
        grad_input, operand_pairs, gain_terms = layer_backward(
            incoming,
            saved_acts,
            weights,
            gain_pair,
            seg_rows,
            seg_full,
            query_pos,
            cosine,
            sine_table,
        )
        if tick_num == 0:
            operand_bufs = jax.tree.map(
                lambda update: jnp.zeros((micro_count + 1,) + update.shape, update.dtype),
                operand_pairs,
            )
        operand_bufs = jax.tree.map(
            lambda buffer, update: lax.dynamic_update_index_in_dim(buffer, update, slot_index, 0),
            operand_bufs,
            operand_pairs,
        )
        gain_sums = gain_sums + gain_terms
        input_grads = lax.dynamic_update_index_in_dim(input_grads, grad_input, slot_index, 0)
        arrived_grad = shifted(grad_input.astype(jnp.bfloat16), "section", -1)
    operands = [buffer[:micro_count].reshape(-1, buffer.shape[-1]) for buffer in operand_bufs]
    g_qkv, g_out, g_gate_up, g_down = owned_grads(operands[:4], operands[4:])
    g_gains = lax.psum_scatter(gain_sums, ("ctx", "fsdp"), scatter_dimension=1, tiled=True)
    final_rows = jnp.where(section_index == 0, input_grads[:micro_count], outputs[:micro_count])
    ends_out = final_rows[None, :, None]
    return (ends_out, g_qkv[None], g_out[None], g_gate_up[None], g_down[None], g_gains[None])


def solution(mesh):
    in_specs = (
        P("section", None, "fsdp", "ctx", None),
        P(None, "fsdp", "ctx"),
        P("section", "fsdp", None),
        P("section", "fsdp", None),
        P("section", "fsdp", None),
        P("section", "fsdp", None),
        P("section", None, None),
    )
    out_specs = (
        P("section", None, "fsdp", "ctx", None),
        P("section", ("ctx", "fsdp"), None),
        P("section", ("ctx", "fsdp"), None),
        P("section", ("ctx", "fsdp"), None),
        P("section", ("ctx", "fsdp"), None),
        P("section", None, ("ctx", "fsdp")),
    )
    return jax.shard_map(local, mesh=mesh, in_specs=in_specs, out_specs=out_specs, check_vma=False)
```

```python
import math

import jax
import jax.numpy as jnp
from jax import lax
from jax.experimental import pallas as pl
from jax.experimental.pallas import tpu as pltpu
from jax.sharding import PartitionSpec as P

MESH = pl.DeviceIdType.MESH

D = 1152
HEADS = 18
KV_HEADS = 6
HEAD = 64
FF = 3072
KVW = 384


EPS = 1e-05


def shifted(x, axis, by):
    size = lax.axis_size(axis)
    pairs = [(i, i + by) for i in range(size) if 0 <= i + by < size]
    return lax.ppermute(x, axis, pairs)


def rotate(values_in, cosine, sine_table):
    half_size = values_in.shape[-1] // 2
    front = values_in[..., :half_size]
    back_half = values_in[..., half_size:]
    return jnp.concatenate(
        [front * cosine - back_half * sine_table, back_half * cosine + front * sine_table], axis=-1
    )


def rotate_back(gradient, cosine, sine_table):
    half_size = gradient.shape[-1] // 2
    front = gradient[..., :half_size]
    back_half = gradient[..., half_size:]
    return jnp.concatenate(
        [front * cosine + back_half * sine_table, back_half * cosine - front * sine_table], axis=-1
    )


def norm_forward(inputs, gain_row):
    scale_row = lax.rsqrt(jnp.mean(inputs * inputs, axis=-1, keepdims=True) + EPS)
    unit_rows = inputs * scale_row
    return (unit_rows * gain_row, unit_rows, scale_row)


def norm_backward(gradient, unit_rows, scale_row, gain_row):
    unit_grad = gradient * gain_row
    gain_grad = jnp.sum(gradient * unit_rows, axis=0)
    input_grad = scale_row * (
        unit_grad - unit_rows * jnp.mean(unit_grad * unit_rows, axis=-1, keepdims=True)
    )
    return (input_grad, gain_grad)


def outer_product(left, right):
    return lax.dot_general(
        left, right, (((0,), (0,)), ((), ())), preferred_element_type=jnp.float32
    )


def times_transposed(left, right):
    return lax.dot_general(
        left, right, (((1,), (1,)), ((), ())), preferred_element_type=jnp.float32
    )


def block_needed(first_row, block_rows, seg_full, seg_rows, query_pos):
    last_seg = lax.dynamic_index_in_dim(seg_full, first_row + block_rows - 1, 0, keepdims=False)
    return (first_row <= query_pos[-1]) & (last_seg >= seg_rows[0])


def attend_forward(queries4, key_all, value_all, seg_rows, seg_full, query_pos):
    tok_rows = queries4.shape[0]
    group_size = HEADS // KV_HEADS
    score_scale = HEAD ** (-0.5)
    total_rows = key_all.shape[0]
    block_rows = math.gcd(total_rows, 512)
    block_count = total_rows // block_rows
    key_heads = key_all.reshape(total_rows, KV_HEADS, HEAD)
    value_heads = value_all.reshape(total_rows, KV_HEADS, HEAD)

    def block_scores(block_index):
        first_row = block_index * block_rows
        key_block = lax.dynamic_slice_in_dim(key_heads, first_row, block_rows, 0)
        value_block = lax.dynamic_slice_in_dim(value_heads, first_row, block_rows, 0)
        seg_block = lax.dynamic_slice_in_dim(seg_full, first_row, block_rows, 0)
        key_pos = first_row + jnp.arange(block_rows, dtype=jnp.int32)
        raw_scores = (
            jnp.einsum("qkgd,tkd->kgqt", queries4, key_block, preferred_element_type=jnp.float32)
            * score_scale
        )
        allowed = (key_pos[None, :] <= query_pos[:, None]) & (
            seg_block[None, :] == seg_rows[:, None]
        )
        return (jnp.where(allowed, raw_scores, -1e30), allowed, value_block)

    def first_pass(state_pair, block_index):

        def first_work(state_in):
            row_top, row_total = state_in
            masked, allowed, value_block = block_scores(block_index)
            new_top = jnp.maximum(row_top, jnp.max(masked, axis=-1))
            new_total = row_total * jnp.exp(row_top - new_top) + jnp.sum(
                jnp.exp(masked - new_top[..., None]), axis=-1
            )
            return (new_top, new_total)

        needed = block_needed(block_index * block_rows, block_rows, seg_full, seg_rows, query_pos)
        return (lax.cond(needed, first_work, lambda state_in: state_in, state_pair), None)

    start_state = (
        jnp.full((KV_HEADS, group_size, tok_rows), -1e30, jnp.float32),
        jnp.zeros((KV_HEADS, group_size, tok_rows), jnp.float32),
    )
    block_ids = jnp.arange(block_count, dtype=jnp.int32)
    (row_top, row_total), ignored = lax.scan(first_pass, start_state, block_ids)
    log_total = row_top + jnp.log(row_total)

    def second_pass(summed, block_index):

        def second_work(summed_in):
            masked, allowed, value_block = block_scores(block_index)
            prob_low = jnp.where(allowed, jnp.exp(masked - log_total[..., None]), 0.0).astype(
                jnp.bfloat16
            )
            added = jnp.einsum(
                "kgqt,tkd->qkgd", prob_low, value_block, preferred_element_type=jnp.float32
            )
            return summed_in + added

        needed = block_needed(block_index * block_rows, block_rows, seg_full, seg_rows, query_pos)
        return (lax.cond(needed, second_work, lambda summed_in: summed_in, summed), None)

    start_sum = jnp.zeros((tok_rows, KV_HEADS, group_size, HEAD), jnp.float32)
    attended, ignored = lax.scan(second_pass, start_sum, block_ids)
    return (attended.reshape(tok_rows, D), log_total)


def layer_forward(inputs, weights, gain_pair, seg_rows, seg_full, query_pos, cosine, sine_table):
    w_qkv, w_out, w_gate_up, w_down = weights
    tok_rows = inputs.shape[0]
    group_size = HEADS // KV_HEADS
    normed, unit_one, scale_one = norm_forward(inputs, gain_pair[0])
    normed_low = normed.astype(jnp.bfloat16)
    mixed_proj = jnp.dot(normed_low, w_qkv, preferred_element_type=jnp.float32)
    queries = rotate(mixed_proj[:, :D].reshape(tok_rows, HEADS, HEAD), cosine, sine_table).astype(
        jnp.bfloat16
    )
    key_rows = rotate(
        mixed_proj[:, D : D + KVW].reshape(tok_rows, KV_HEADS, HEAD), cosine, sine_table
    )
    key_rows = key_rows.astype(jnp.bfloat16).reshape(tok_rows, KVW)
    value_rows = mixed_proj[:, D + KVW :].astype(jnp.bfloat16)
    key_all, value_all = (
        lax.all_gather(key_rows, "ctx", axis=0, tiled=True),
        lax.all_gather(value_rows, "ctx", axis=0, tiled=True),
    )
    queries4 = queries.reshape(tok_rows, KV_HEADS, group_size, HEAD)
    attended, log_total = attend_forward(
        queries4, key_all, value_all, seg_rows, seg_full, query_pos
    )
    context = attended.astype(jnp.bfloat16)
    hidden = inputs + jnp.dot(context, w_out, preferred_element_type=jnp.float32)
    second, unit_two, scale_two = norm_forward(hidden, gain_pair[1])
    second_low = second.astype(jnp.bfloat16)
    gate_up = jnp.dot(second_low, w_gate_up, preferred_element_type=jnp.float32)
    gate_pre = gate_up[:, :FF]
    up_pre = gate_up[:, FF:]
    inner_act = (jax.nn.silu(gate_pre) * up_pre).astype(jnp.bfloat16)
    result = hidden + jnp.dot(inner_act, w_down, preferred_element_type=jnp.float32)
    saved_acts = (
        normed_low,
        queries4,
        key_all,
        value_all,
        attended,
        log_total,
        context,
        unit_one,
        scale_one,
        unit_two,
        scale_two,
        second_low,
        gate_pre,
        up_pre,
        inner_act,
    )
    return (result, saved_acts)


def layer_backward(
    grad_low, saved_acts, weights, gain_pair, seg_rows, seg_full, query_pos, cosine, sine_table
):
    w_qkv, w_out, w_gate_up, w_down = weights
    (
        normed_low,
        queries4,
        key_all,
        value_all,
        attended,
        log_total,
        context,
        unit_one,
        scale_one,
        unit_two,
        scale_two,
        second_low,
        gate_pre,
        up_pre,
        inner_act,
    ) = saved_acts
    tok_rows = grad_low.shape[0]
    group_size = HEADS // KV_HEADS
    score_scale = HEAD ** (-0.5)
    grad_out = grad_low.astype(jnp.float32)
    grad_inner = times_transposed(grad_low, w_down)
    sigmoid_gate = jax.nn.sigmoid(gate_pre)
    silu_gate = gate_pre * sigmoid_gate
    grad_gate = grad_inner * up_pre * sigmoid_gate * (1.0 + gate_pre * (1.0 - sigmoid_gate))
    grad_up = grad_inner * silu_gate
    grad_both = jnp.concatenate([grad_gate, grad_up], axis=1).astype(jnp.bfloat16)
    grad_second = times_transposed(grad_both, w_gate_up)
    grad_norm_two, gain_two = norm_backward(grad_second, unit_two, scale_two, gain_pair[1])
    grad_hidden = grad_out + grad_norm_two
    hidden_low = grad_hidden.astype(jnp.bfloat16)
    grad_context = times_transposed(hidden_low, w_out).astype(jnp.bfloat16)
    grad_context4 = grad_context.reshape(tok_rows, KV_HEADS, group_size, HEAD)
    attended4 = attended.reshape(tok_rows, KV_HEADS, group_size, HEAD)
    row_delta = jnp.einsum("qkgd,qkgd->kgq", grad_context4.astype(jnp.float32), attended4)
    total_rows = seg_full.shape[0]
    start_state = (
        jnp.zeros((tok_rows, KV_HEADS, group_size, HEAD), jnp.float32),
        jnp.zeros((total_rows, 2 * KVW), jnp.float32),
    )
    key_piece, value_piece = key_all, value_all
    piece_rows = key_piece.shape[0]
    block_rows = math.gcd(piece_rows, 512)
    block_count = piece_rows // block_rows

    def one_block(block_index, inner_state):
        offset = block_index * block_rows

        def one_work(state_in):
            grad_query, grad_kv = state_in
            key_block = lax.dynamic_slice_in_dim(key_piece, offset, block_rows, 0).reshape(
                block_rows, KV_HEADS, HEAD
            )
            value_block = lax.dynamic_slice_in_dim(value_piece, offset, block_rows, 0).reshape(
                block_rows, KV_HEADS, HEAD
            )
            seg_block = lax.dynamic_slice_in_dim(seg_full, offset, block_rows, 0)
            key_pos = offset + jnp.arange(block_rows, dtype=jnp.int32)
            raw_scores = (
                jnp.einsum(
                    "qkgd,tkd->kgqt", queries4, key_block, preferred_element_type=jnp.float32
                )
                * score_scale
            )
            allowed = (key_pos[None, :] <= query_pos[:, None]) & (
                seg_block[None, :] == seg_rows[:, None]
            )
            prob_full = jnp.where(allowed, jnp.exp(raw_scores - log_total[..., None]), 0.0)
            prob_low = prob_full.astype(jnp.bfloat16)
            grad_value = jnp.einsum(
                "kgqt,qkgd->tkd", prob_low, grad_context4, preferred_element_type=jnp.float32
            )
            grad_prob = jnp.einsum(
                "qkgd,tkd->kgqt", grad_context4, value_block, preferred_element_type=jnp.float32
            )
            grad_scores = (prob_full * (grad_prob - row_delta[..., None])).astype(jnp.bfloat16)
            grad_query = (
                grad_query
                + jnp.einsum(
                    "kgqt,tkd->qkgd", grad_scores, key_block, preferred_element_type=jnp.float32
                )
                * score_scale
            )
            grad_key = (
                jnp.einsum(
                    "kgqt,qkgd->tkd", grad_scores, queries4, preferred_element_type=jnp.float32
                )
                * score_scale
            )
            new_rows = jnp.concatenate(
                [grad_key.reshape(block_rows, KVW), grad_value.reshape(block_rows, KVW)], axis=1
            )
            old_rows = lax.dynamic_slice_in_dim(grad_kv, offset, block_rows, 0)
            grad_kv = lax.dynamic_update_slice_in_dim(grad_kv, old_rows + new_rows, offset, 0)
            return (grad_query, grad_kv)

        needed = block_needed(offset, block_rows, seg_full, seg_rows, query_pos)
        return lax.cond(needed, one_work, lambda state_in: state_in, inner_state)

    grad_query, grad_kv_all = lax.fori_loop(0, block_count, one_block, start_state)
    grad_kv_own = lax.psum_scatter(
        grad_kv_all.astype(jnp.bfloat16), "ctx", scatter_dimension=0, tiled=True
    ).astype(jnp.float32)
    grad_q_pre = rotate_back(grad_query.reshape(tok_rows, HEADS, HEAD), cosine, sine_table).reshape(
        tok_rows, D
    )
    grad_k_pre = rotate_back(
        grad_kv_own[:, :KVW].reshape(tok_rows, KV_HEADS, HEAD), cosine, sine_table
    ).reshape(tok_rows, KVW)
    grad_mixed = jnp.concatenate([grad_q_pre, grad_k_pre, grad_kv_own[:, KVW:]], axis=1).astype(
        jnp.bfloat16
    )
    grad_normed = times_transposed(grad_mixed, w_qkv)
    grad_norm_one, gain_one = norm_backward(grad_normed, unit_one, scale_one, gain_pair[0])
    grad_input = grad_hidden + grad_norm_one
    operand_pairs = (
        normed_low,
        context,
        second_low,
        inner_act,
        grad_mixed,
        hidden_low,
        grad_both,
        grad_low,
    )
    return (grad_input, operand_pairs, jnp.stack([gain_one, gain_two]))


DOWN_COLS = 128
WIDE_COLS = 384
NEAR, MID, FAR, SUMS = 2, 4, 8, 12
OWNERS = 16
EMBEDDED, DEFERRED = 6, 6
AHEAD = 4


F32, LOW = jnp.float32, jnp.bfloat16
GROUP = HEADS // KV_HEADS
HALF = HEAD // 2
SCALE = HEAD ** (-0.5)
NONE = -1e30
TILE = 384
WIDE = 512


def dot(left, right, left_dim, right_dim):
    return lax.dot_general(
        left, right, (((left_dim,), (right_dim,)), ((), ())), preferred_element_type=F32
    )


def at(start, size, step=128):
    return pl.ds(pl.multiple_of(start, step), size)


def column_scale(v):
    return lax.rsqrt(jnp.mean(v * v, axis=0, keepdims=True) + EPS)


def greet(peers):
    barrier = pltpu.get_barrier_semaphore()
    for peer in peers:
        pl.semaphore_signal(barrier, inc=1, device_id=peer, device_id_type=MESH)
    pl.semaphore_wait(barrier, len(peers))


def remote(src, dst, send, recv, peer):
    return pltpu.make_async_remote_copy(
        src_ref=src, dst_ref=dst, send_sem=send, recv_sem=recv, device_id=peer, device_id_type=MESH
    )


def fill_bias(bias, segments, m, place, toks):
    own = segments[place, pl.ds(m, 1), :]
    rows = lax.broadcasted_iota(jnp.int32, (toks, toks), 0)
    cols = lax.broadcasted_iota(jnp.int32, (toks, toks), 1)
    for d in range(3):
        seen = segments[jnp.maximum(place - d, 0), pl.ds(m, 1), :]
        keys = jnp.broadcast_to(seen, (8, toks)).T[:, 0:1]
        allowed = keys == own
        if d == 0:
            allowed = allowed & (rows <= cols)
        bias[d] = jnp.where(allowed, 0.0, NONE)


def gain_columns(gains, columns):
    for row in range(2):
        columns[:, row : row + 1] = jnp.broadcast_to(gains[row : row + 1, :], (8, D)).T[:, 0:1]


JOINT_CHUNKS, WIDE_CHUNKS, DOWN_CHUNKS = 3, 3, 4
CHUNKS = JOINT_CHUNKS + WIDE_CHUNKS + DOWN_CHUNKS
SLAB = 1024


def forward_kernel(
    ends, gains, cosine, sine, seg_own, w_qkv, w_out, w_gate_up, w_down,
    f_joint, f_gate_up, f_down, o_seg,
    o_normed, o_context, o_second, o_inner, o_x, o_q, o_kv, o_att, o_lse, o_hidden, o_gu, o_result,
    t_joint, t_gate_up, t_down, stage, stage_down, x_in, x_now, s_normed, s_context, s_second,
    s_inner, s_x, s_q, s_kv, s_att, s_top, s_lse, s_hidden, s_gu, s_result, bias, segments, columns,
    stage_sem, seg_sem, save_sem, kv_send, kv_recv, x_send, x_recv,
    own_sem, back_sem, zs, zr, ys, yr, cs, cr, es, er,
):
    section = lax.axis_index("section")
    place = lax.axis_index("ctx")
    z = lax.axis_index("fsdp")
    last = lax.axis_size("fsdp") - 1
    y, k = place // 2, place % 2
    y_mate = {"ctx": (1 - y) * 2 + k}
    k_mate = {"ctx": y * 2 + 1 - k}
    micros, toks = ends.shape[0], ends.shape[1]
    qkv = D + 2 * KVW
    width, deep = w_gate_up.shape[0], w_down.shape[0]
    half, joint_half, wide_half = width // 2, f_joint.shape[1] // 2, f_gate_up.shape[1] // 2

    barrier = pltpu.get_barrier_semaphore()
    for peer in [{"ctx": (place + i) % 4} for i in (1, 2, 3)] + [{"section": 1 - section}]:
        pl.semaphore_signal(barrier, inc=1, device_id=peer, device_id_type=MESH)

    @pl.when(z > 0)
    def _():
        pl.semaphore_signal(barrier, inc=1, device_id={"fsdp": z - 1}, device_id_type=MESH)

    @pl.when(z < last)
    def _():
        pl.semaphore_signal(barrier, inc=1, device_id={"fsdp": z + 1}, device_id_type=MESH)

    pl.semaphore_wait(barrier, 4 + jnp.where(z > 0, 1, 0) + jnp.where(z < last, 1, 0))

    def view(shard, yy, kk, j, own=False):
        if j < JOINT_CHUNKS:
            rows = half // JOINT_CHUNKS
            return f_joint.at[
                at(shard * width + yy * half + j * rows, rows, 16), at(kk * joint_half, joint_half)
            ]
        j = j - JOINT_CHUNKS
        if j < WIDE_CHUNKS:
            cols = wide_half // WIDE_CHUNKS
            ref, first = (w_gate_up, 0) if own else (f_gate_up, shard * width)
            return ref.at[at(first + yy * half, half, 16), at(kk * wide_half + j * cols, cols)]
        j = j - WIDE_CHUNKS
        rows = deep // 4 // DOWN_CHUNKS
        ref, first = (w_down, 0) if own else (f_down, shard * deep)
        return ref.at[at(first + (yy * 2 + kk) * (deep // 4) + j * rows, rows, 16), :]

    def z_copy(shard, j, to, own, back):
        ref = view(shard, y, k, j)
        src = view(shard, y, k, j, True) if own and j >= JOINT_CHUNKS else ref
        return remote(
            src, ref, back_sem.at[j] if back else zs.at[shard, j], zr.at[shard, j], {"fsdp": to}
        )

    def own_start(j, to, back):
        if j >= JOINT_CHUNKS:
            z_copy(z, j, to, True, back).start()
            return
        rows = half // JOINT_CHUNKS
        here = at(y * half + j * rows, rows, 16)
        there = at(z * width + y * half + j * rows, rows, 16)
        send, recv = back_sem.at[j] if back else zs.at[z, j], zr.at[z, j]

        @pl.when(k == 0)
        def _():
            remote(
                w_qkv.at[here, 0:joint_half], f_joint.at[there, 0:joint_half], send, recv, {"fsdp": to}
            ).start()

        @pl.when(k == 1)
        def _():
            remote(
                w_qkv.at[here, joint_half:qkv], f_joint.at[there, joint_half:qkv], send, recv, {"fsdp": to}
            ).start()
            remote(w_out.at[here, :], f_joint.at[there, qkv:], send, recv, {"fsdp": to}).start()

    def own_sends(j):
        @pl.when(z < last)
        def _():
            own_start(j, z + 1, False)

        @pl.when(z > 0)
        def _():
            own_start(j, z - 1, True)

    def mate_copy(shard, j, yy, mate, send, recv):
        ref = view(shard, yy, k, j)
        return remote(ref, ref, send.at[shard, j], recv.at[shard, j], mate)

    def arrive(shard, j, yy, kk, recv):
        ref = view(shard, yy, kk, j)
        remote(ref, ref, recv.at[shard, j], recv.at[shard, j], k_mate).wait_recv()

    rows_z, rows_deep = at(z * width, width, 16), at(z * deep, deep, 16)
    own_pairs = (
        (w_qkv, f_joint.at[rows_z, 0:qkv]), (w_out, f_joint.at[rows_z, qkv:]),
        (w_gate_up, f_gate_up.at[rows_z, :]), (w_down, f_down.at[rows_deep, :]),
    )
    own_copies = [
        remote(a, b, own_sem.at[0, i], own_sem.at[1, i], k_mate) for i, (a, b) in enumerate(own_pairs)
    ]

    def sides(d):
        return ((z - d >= 0, z - d, z + 1, z < last), (z + d <= last, z + d, z - 1, z > 0))

    def relay(d, j):
        for valid, shard, onward, more in sides(d):
            @pl.when(valid)
            def _(shard=shard, onward=onward, more=more):
                arrive(shard, j, y, k, zr)
                if d < 3:
                    @pl.when(more)
                    def _():
                        z_copy(shard, j, onward, False, False).start()
                mate_copy(shard, j, y, y_mate, ys, yr).start()
                mate_copy(shard, j, y, k_mate, cs, cr).start()

    def across(d, j):
        for valid, shard, onward, more in sides(d):
            @pl.when(valid)
            def _(shard=shard):
                arrive(shard, j, 1 - y, k, yr)
                mate_copy(shard, j, 1 - y, k_mate, es, er).start()

    def complete(d, j):
        for valid, shard, onward, more in sides(d):
            @pl.when(valid)
            def _(shard=shard):
                arrive(shard, j, y, 1 - k, cr)
                arrive(shard, j, 1 - y, 1 - k, er)

    first_down = JOINT_CHUNKS + WIDE_CHUNKS
    order = [(d, j) for d in (1, 2, 3) for j in range(JOINT_CHUNKS)]
    order += [(d, j) for d in (1, 2, 3) for j in range(JOINT_CHUNKS, CHUNKS)]
    refill = {2: (3,), 3: (4,), 4: (5,), 5: (6, 7), 6: (8, 9)}
    done = {"relay": 0, "across": 0}

    def pump(upto, lag=3):
        while done["relay"] < min(upto, len(order)):
            relay(*order[done["relay"]])
            for extra in refill.get(done["relay"], ()):
                own_sends(extra)
            done["relay"] += 1
            while done["across"] < done["relay"] - lag:
                across(*order[done["across"]])
                done["across"] += 1

    def flush(upto):
        while done["across"] < upto:
            across(*order[done["across"]])
            done["across"] += 1

    def turn_slabs(ref, out, slabs, first, end):
        rows = slice(first, end)
        copies = [
            pltpu.make_async_copy(
                ref.at[rows, q * SLAB : (q + 1) * SLAB], stage.at[i, rows, :], stage_sem.at[i]
            )
            for i, q in enumerate(slabs)
        ]
        for copy in copies:
            copy.start()
        for i, q in enumerate(slabs):
            copies[i].wait()

            def step(c, carry, i=i, q=q):
                cols = at(c * 256, 256)
                out[at(q * SLAB + c * 256, 256), rows] = stage[i, rows, cols].T
                return carry

            lax.fori_loop(0, SLAB // 256, step, 0)

    third = D // 3

    def turn_near(ref, out, slabs):
        for when, first, end in (
            (z == 0, 0, 2 * third), (z == last, third, D), ((z > 0) & (z < last), 0, D),
        ):
            @pl.when(when)
            def _(first=first, end=end):
                turn_slabs(ref, out, slabs, first, end)

    def turn_rest(ref, out, slabs):
        for when, first, end in ((z == 0, 2 * third, D), (z == last, 0, third)):
            @pl.when(when)
            def _(first=first, end=end):
                turn_slabs(ref, out, slabs, first, end)

    def turn_down(shard):
        copy = pltpu.make_async_copy(f_down.at[at(shard * deep, deep), :], stage_down, stage_sem.at[2])
        copy.start()
        copy.wait()

        def step(i, carry):
            t_down[at(i * TILE, TILE), at(shard * deep, deep)] = stage_down[:, at(i * TILE, TILE)].T
            return carry

        lax.fori_loop(0, D // TILE, step, 0)

    def saves(m):
        lanes = at(m * toks, toks)
        pairs = (
            (s_normed, o_normed.at[:, lanes]), (s_context, o_context.at[:, lanes]),
            (s_second, o_second.at[:, lanes]), (s_inner, o_inner.at[:, lanes]),
            (s_x, o_x.at[m]), (s_q, o_q.at[m]), (s_kv.at[m], o_kv.at[m]), (s_att, o_att.at[m]),
            (s_lse, o_lse.at[m]), (s_hidden, o_hidden.at[m]), (s_gu, o_gu.at[m]),
        )
        return [pltpu.make_async_copy(a, b, save_sem.at[i]) for i, (a, b) in enumerate(pairs)]

    def result_save(m):
        return pltpu.make_async_copy(s_result, o_result.at[m], save_sem.at[11])

    def x_copy(m, i):
        part = x_in.at[m, at(i * TILE, TILE), :]
        return remote(part, part, x_send.at[m, i], x_recv.at[m, i], {"section": 1})

    def kv_copy(m, source, slot, lane, to):
        return remote(
            s_kv.at[m, source], s_kv.at[m, slot], kv_send.at[m, lane], kv_recv.at[m, slot],
            {"ctx": to},
        )

    def kv_sends(m):
        return (
            (0, kv_copy(m, 0, 2, 1, 2)),
            (0, kv_copy(m, 0, 1, 0, 1)),
            (1, kv_copy(m, 0, 2, 0, 3)),
            (2, kv_copy(m, 0, 1, 0, 3)),
        )

    def attend(kv_at, m, blocks, fresh):
        rows = at(kv_at * HEAD, HEAD, 64)
        query = s_q[rows, :]
        parts = []
        for d in blocks:
            part = dot(s_kv[m, d, rows, :], query, 0, 0)
            mask = bias[d]
            parts.append(part + jnp.concatenate([mask] * GROUP, axis=1))
        scores = parts[0] if len(parts) == 1 else jnp.concatenate(parts, axis=0)
        top = jnp.max(scores, axis=0, keepdims=True)
        one = pl.ds(kv_at, 1)
        if not fresh:
            old_top, old_total = s_top[one, :], s_lse[one, :]
            top = jnp.maximum(top, old_top)
        probs = jnp.exp(scores - top)
        total = jnp.sum(probs, axis=0, keepdims=True)
        probs = probs.astype(LOW)
        value_rows = at(KVW + kv_at * HEAD, HEAD, 64)
        summed = None
        for i, d in enumerate(blocks):
            term = dot(s_kv[m, d, value_rows, :], probs[i * toks : (i + 1) * toks], 1, 0)
            summed = term if summed is None else summed + term
        if not fresh:
            keep = jnp.exp(old_top - top)
            total = total + old_total * keep
        s_top[one, :] = top
        s_lse[one, :] = total
        for g in range(GROUP):
            lanes = slice(g * toks, (g + 1) * toks)
            out_rows = at((kv_at * GROUP + g) * HEAD, HEAD, 64)
            value = summed[:, lanes]
            if not fresh:
                value = value + s_att[out_rows, :] * keep[:, lanes]
            s_att[out_rows, :] = value

    def each(m, blocks, fresh):
        def step(kv_at, carry):
            attend(kv_at, m, blocks, fresh)
            return carry

        lax.fori_loop(0, KV_HEADS, step, 0)

    def take_own(m):
        x_now[...] = ends[m].astype(F32).T

    def take_sent(m):
        for i in range(D // TILE):
            x_copy(m, i).wait_recv()
        x_now[...] = x_in[m].astype(F32)

    def first_norm(m):
        x = x_now[...]
        s_x[...] = x.astype(LOW)
        s_normed[...] = (x * column_scale(x) * columns[:, 0:1]).astype(LOW)
        fill_bias(bias, segments, m, place, toks)

    def rotated(block, head):
        cos, sin = cosine[...], sine[...]
        front = block[head * HEAD : head * HEAD + HALF]
        back = block[head * HEAD + HALF : (head + 1) * HEAD]
        return jnp.concatenate([front * cos - back * sin, back * cos + front * sin], axis=0)

    def keys_values(m):
        keys = dot(t_joint[D : D + KVW, :], s_normed[...], 1, 0)
        for head in range(KV_HEADS):
            s_kv[m, 0, head * HEAD : (head + 1) * HEAD, :] = rotated(keys, head).astype(LOW)
        s_kv[m, 0, KVW : 2 * KVW, :] = dot(t_joint[D + KVW : qkv, :], s_normed[...], 1, 0).astype(LOW)
        for who, copy in kv_sends(m):
            @pl.when(place == who)
            def _(copy=copy):
                copy.start()

    def queries(m):
        def query_tile(i, carry):
            block = dot(t_joint[at(i * TILE, TILE), :], s_normed[...], 1, 0) * SCALE
            for head in range(TILE // HEAD):
                rows = at((i * (TILE // HEAD // GROUP) + head // GROUP) * HEAD, HEAD, 64)
                g = head % GROUP
                s_q[rows, g * toks : (g + 1) * toks] = rotated(block, head).astype(LOW)
            return carry

        lax.fori_loop(0, D // TILE, query_tile, 0)

    def near_block(m):
        each(m, (0,), True)

    def far_blocks(m):
        @pl.when(place == 1)
        def _():
            kv_copy(m, 0, 1, 0, 1).wait_recv()
            each(m, (1,), False)

        @pl.when(place == 2)
        def _():
            kv_copy(m, 0, 2, 0, 2).wait_recv()
            each(m, (2,), False)
            kv_copy(m, 0, 1, 0, 2).wait_recv()
            each(m, (1,), False)

        @pl.when(place == 3)
        def _():
            kv_copy(m, 0, 1, 0, 3).wait_recv()
            each(m, (1,), False)
            kv_copy(m, 0, 2, 0, 3).wait_recv()
            kv_copy(m, 2, 1, 0, 2).start()
            each(m, (2,), False)

    def contexts(m):
        def finish(kv_at, carry):
            one = pl.ds(kv_at, 1)
            total = s_lse[one, :]
            inverse = 1.0 / total
            for g in range(GROUP):
                rows = at((kv_at * GROUP + g) * HEAD, HEAD, 64)
                value = s_att[rows, :] * inverse[:, g * toks : (g + 1) * toks]
                s_att[rows, :] = value
                s_context[rows, :] = value.astype(LOW)
            s_lse[one, :] = s_top[one, :] + jnp.log(total)
            return carry

        lax.fori_loop(0, KV_HEADS, finish, 0)

    def seconds(m):
        def out_tile(i, carry):
            rows = at(i * TILE, TILE)
            s_hidden[rows, :] = x_now[rows, :] + dot(
                t_joint[at(qkv + i * TILE, TILE), :], s_context[...], 1, 0
            )
            return carry

        lax.fori_loop(0, D // TILE, out_tile, 0)
        hidden = s_hidden[...]
        s_second[...] = (hidden * column_scale(hidden) * columns[:, 1:2]).astype(LOW)

    def gates(first, end):
        def gate_tile(i, carry):
            rows, up_rows = at(i * WIDE, WIDE), at(FF + i * WIDE, WIDE)
            gate = dot(t_gate_up[rows, :], s_second[...], 1, 0)
            up = dot(t_gate_up[up_rows, :], s_second[...], 1, 0)
            s_gu[rows, :] = gate.astype(LOW)
            s_gu[up_rows, :] = up.astype(LOW)
            s_inner[rows, :] = (gate * jax.nn.sigmoid(gate) * up).astype(LOW)
            return carry

        lax.fori_loop(first, end, gate_tile, 0)

    def early(work):
        @pl.when(section == 0)
        def _():
            work()

    for j in range(JOINT_CHUNKS):
        own_sends(j)
    for copy in own_copies:
        copy.start()
    segments[place] = seg_own[...]

    def seg_copy(i):
        return remote(
            seg_own, segments.at[place], seg_sem.at[0, i], seg_sem.at[1, i], {"ctx": (place + i) % 4}
        )

    for i in (1, 2, 3):
        seg_copy(i).start()
    gain_columns(gains, columns)
    early(lambda: take_own(0))
    for i in (1, 2, 3):
        seg_copy(i).wait()
    early(lambda: first_norm(0))

    joint_items = 3 * JOINT_CHUNKS
    lap = CHUNKS - JOINT_CHUNKS
    pump(joint_items + 3)
    for j in range(JOINT_CHUNKS):
        for d in (1, 2, 3):
            complete(d, j)
    own_copies[0].wait_recv()
    own_copies[1].wait_recv()

    def turn_all(ref, out, slabs):
        turn_slabs(ref, out, slabs, 0, D)

    turn_all(f_joint, t_joint, (0, 1))
    pump(joint_items + 4)
    turn_all(f_joint, t_joint, (2,))
    pump(joint_items + 5)
    early(lambda: keys_values(0))
    pump(joint_items + 6)
    early(lambda: queries(0))
    pump(joint_items + lap)
    early(lambda: near_block(0))
    pump(joint_items + lap + 5)
    early(lambda: far_blocks(0))
    pump(joint_items + lap + 6)
    early(lambda: contexts(0))
    early(lambda: seconds(0))
    pump(joint_items + 2 * lap)
    own_copies[2].wait_recv()
    for d in (1, 2):
        for j in range(JOINT_CHUNKS, first_down):
            complete(d, j)
    for p in range(WIDE_CHUNKS):
        turn_near(f_gate_up, t_gate_up, (p, WIDE_CHUNKS + p))
        pump(joint_items + 2 * lap + p + 1)

    def turn_downs(d):
        for j in range(first_down, CHUNKS):
            complete(d, j)
        for valid, shard, onward, more in sides(d):
            @pl.when(valid)
            def _(shard=shard):
                turn_down(shard)

    own_copies[3].wait_recv()
    turn_down(z)
    pump(joint_items + 3 * lap - 3)
    turn_downs(1)
    pump(joint_items + 3 * lap - 2)
    turn_downs(2)
    pump(joint_items + 3 * lap - 1)
    per_slab = SLAB // WIDE
    for p in range(WIDE_CHUNKS):
        complete(3, JOINT_CHUNKS + p)
        turn_rest(f_gate_up, t_gate_up, (p, WIDE_CHUNKS + p))
        early(lambda p=p: gates(p * per_slab, (p + 1) * per_slab))
        if p == 0:
            pump(joint_items + 3 * lap)
        flush(joint_items + 3 * lap - 2 + p)
    turn_downs(3)

    def micro(m, carry):
        @pl.when(m > 0)
        def _():
            for save in saves(m - 1):
                save.wait()

            @pl.when(section == 1)
            def _():
                result_save(m - 1).wait()

        @pl.when((section == 1) | (m > 0))
        def _():
            @pl.when(section == 0)
            def _():
                take_own(m)

            @pl.when(section == 1)
            def _():
                take_sent(m)

            first_norm(m)
            keys_values(m)
            queries(m)
            near_block(m)
            far_blocks(m)
            contexts(m)
            seconds(m)
            gates(0, FF // WIDE)

        for i in range(D // TILE):
            rows = slice(i * TILE, (i + 1) * TILE)
            value = s_hidden[rows, :] + dot(t_down[rows, :], s_inner[...], 1, 0)
            x_now[rows, :] = value

            @pl.when(section == 0)
            def _(i=i, rows=rows, value=value):
                x_in[m, rows, :] = value.astype(LOW)
                x_copy(m, i).start()

        for save in saves(m):
            save.start()

        @pl.when(section == 1)
        def _():
            s_result[...] = x_now[...].T
            result_save(m).start()

        return carry

    lax.fori_loop(0, micros, micro, 0)
    seg_save = pltpu.make_async_copy(segments, o_seg, seg_sem.at[0, 0])
    seg_save.start()
    for save in saves(micros - 1):
        save.wait()
    seg_save.wait()

    @pl.when(section == 1)
    def _():
        result_save(micros - 1).wait()

    for m in range(2):
        @pl.when(section == 0)
        def _(m=m):
            for i in range(D // TILE):
                x_copy(m, i).wait_send()

        for who, copy in kv_sends(m):
            @pl.when(place == who)
            def _(copy=copy):
                copy.wait_send()

        @pl.when(place == 3)
        def _(m=m):
            kv_copy(m, 2, 1, 0, 2).wait_send()

    for d, j in order:
        for valid, shard, onward, more in sides(d):
            @pl.when(valid)
            def _(shard=shard, onward=onward, more=more):
                mate_copy(shard, j, y, y_mate, ys, yr).wait_send()
                mate_copy(shard, j, y, k_mate, cs, cr).wait_send()
                mate_copy(shard, j, 1 - y, k_mate, es, er).wait_send()
                if d < 3:
                    @pl.when(more)
                    def _():
                        z_copy(shard, j, onward, False, False).wait_send()
    for j in range(CHUNKS):
        @pl.when(z < last)
        def _(j=j):
            z_copy(z, j, z + 1, True, False).wait_send()

        @pl.when(z > 0)
        def _(j=j):
            z_copy(z, j, z - 1, True, True).wait_send()
    for copy in own_copies:
        copy.wait_send()


def backward_kernel(
    ends, gains, cosine, sine, segments, w_joint, w_gate_up, w_down,
    i_x, i_q, i_kv, i_att, i_lse, i_hidden, i_gu, i_result, i_normed, i_context, i_second, i_inner,
    o_result, o_down, o_gate_up, o_qkv, o_out, o_gain,
    v_joint, v_gate_up, v_down, g_in, g_now, s_x, s_q, s_kv, s_att, s_lse, s_hid, s_gu,
    s_both, s_mixed, s_hidden, s_grad, s_sum, s_context, s_delta, s_dq, s_dkv, kv_out, kv_in,
    s_gains, bias, columns, wide_out, down_out, gain_out, gain_in,
    w_sem, load_sem, gu_sem, save_sem, kv_send, kv_recv, x_send, x_recv,
    left_sem, near_send, near_recv, mid_send, mid_recv, right_send, right_recv, left_send, left_recv,
    out_sem, gain_send, gain_recv, near_free, mid_free, right_free, left_free,
):
    section = lax.axis_index("section")
    place = lax.axis_index("ctx")
    micros, toks = ends.shape[0], ends.shape[1]
    qkv = D + 2 * KVW
    w_loads = [
        pltpu.make_async_copy(src, dst, w_sem.at[i])
        for i, (src, dst) in enumerate(
            ((w_joint, v_joint), (w_gate_up, v_gate_up), (w_down, v_down))
        )
    ]

    def loads(m):
        pairs = (
            (i_hidden, s_hid), (i_att, s_att), (i_q, s_q), (i_kv, s_kv),
            (i_lse, s_lse), (i_x, s_x),
        )
        return [pltpu.make_async_copy(a.at[m], b, load_sem.at[i]) for i, (a, b) in enumerate(pairs)]

    tiles = FF // TILE

    def gu_loads(m, i):
        slot = i % AHEAD
        return [
            pltpu.make_async_copy(
                i_gu.at[m, at(part * FF + i * TILE, TILE), :], s_gu.at[slot, part], gu_sem.at[slot, part]
            )
            for part in range(2)
        ]

    w_loads[2].start()
    for i in range(AHEAD):
        for load in gu_loads(0, i):
            load.start()
    for load in loads(0):
        load.start()
    w_loads[1].start()
    w_loads[0].start()
    z = lax.axis_index("fsdp")
    last = lax.axis_size("fsdp") - 1
    others = [((place + i // 4) % 4, (z + i % 4) % 4) for i in range(1, OWNERS)]
    greet([{"ctx": a, "fsdp": b} for a, b in others] + [{"section": 1 - section}])
    s_gains[...] = jnp.zeros_like(s_gains)
    gain_columns(gains, columns)

    def result_saves(m):
        return [
            pltpu.make_async_copy(
                s_dq.at[0:toks, at(i % 2 * TILE, TILE)], o_result.at[m, :, i * TILE : (i + 1) * TILE], save_sem.at[i]
            )
            for i in range(D // TILE)
        ]

    def g_copy(m):
        return remote(g_in.at[m], g_in.at[m], x_send.at[m], x_recv.at[m], {"section": 0})

    def kv_copy(m, source, slot, lane, to):
        return remote(
            kv_out.at[source], kv_in.at[m, slot], kv_send.at[m, lane], kv_recv.at[m, slot],
            {"ctx": to},
        )

    def kv_sends(m):
        return (
            (1, kv_copy(m, 0, 0, 0, 0)),
            (2, kv_copy(m, 0, 0, 0, 3)),
            (2, kv_copy(m, 1, 1, 1, 0)),
            (3, kv_copy(m, 0, 0, 0, 2)),
            (3, kv_copy(m, 1, 0, 1, 1)),
        )

    def block_grads(d, m, fresh):
        def step(kv_at, carry):
            rows = at(kv_at * HEAD, HEAD, 64)
            value_rows = at(KVW + kv_at * HEAD, HEAD, 64)
            one = pl.ds(kv_at, 1)
            query, grad = s_q[rows, :], s_context[rows, :]
            key, value = s_kv[d, rows, :], s_kv[d, value_rows, :]
            mask = bias[d]
            scores = dot(key, query, 0, 0) + jnp.concatenate([mask] * GROUP, axis=1)
            probs = jnp.exp(scores - s_lse[one, :])
            grad_probs = dot(value, grad, 0, 0)
            grad_scores = (probs * (grad_probs - s_delta[one, :])).astype(LOW)
            s_dkv[rows, :] = dot(query, grad_scores, 1, 1)
            s_dkv[value_rows, :] = dot(grad, probs.astype(LOW), 1, 1)
            grad_query = dot(key, grad_scores, 1, 0)
            if fresh:
                s_dq[rows, :] = grad_query
            else:
                s_dq[rows, :] = s_dq[rows, :] + grad_query
            return carry

        lax.fori_loop(0, KV_HEADS, step, 0)

    y, k = place // 2, place % 2
    y_mate = {"ctx": (1 - y) * 2 + k}
    k_mate = {"ctx": y * 2 + 1 - k}
    right, left = {"fsdp": z + 1}, {"fsdp": z - 1}
    n_down, n_both = D // DOWN_COLS, 2 * FF // WIDE_COLS
    n_mixed, n_out = qkv // WIDE_COLS, D // WIDE_COLS
    end_both = n_down + n_both
    end_mixed = end_both + n_mixed
    total = end_mixed + n_out
    hop, first_z = 2, 4
    final_lag = first_z + hop * 3
    block = D // 4
    parts = (FF // OWNERS // 3, D // OWNERS)
    used = (4 * parts[0], block)
    spare = 13 * WIDE_COLS
    both_toks = micros * toks
    inner_t = v_down.at[:, 0:both_toks]
    normed_t = v_down.at[0:D, both_toks : 2 * both_toks]
    context_t = v_gate_up.at[:, spare : spare + both_toks]
    second_t = v_gate_up.at[:, spare + both_toks : spare + 2 * both_toks]
    left_loads = [
        pltpu.make_async_copy(a, b, left_sem.at[i])
        for i, (a, b) in enumerate(
            ((i_inner, inner_t), (i_normed, normed_t), (i_context, context_t), (i_second, second_t))
        )
    ]

    def cell(column, slot, first=0, count=block):
        rows = at(slot % 4 * block + first, count, 16)
        return v_gate_up.at[rows, at((column + slot // 4) * WIDE_COLS, WIDE_COLS)]

    def out_near(slot, yy):
        return cell(0, slot * 2 + yy)

    def own_near(slot, yy):
        return cell(1, slot * 2 + yy)

    def in_near(slot, yy):
        return cell(2, slot * 2 + yy)

    def gain_copy(i):
        to_place, to_z = others[i - 1]
        return remote(
            gain_out.at[to_place * 4 + to_z], gain_in.at[i], gain_send.at[i], gain_recv.at[i],
            {"ctx": to_place, "fsdp": to_z},
        )

    def near_copy(j):
        slot = j % NEAR
        return remote(
            cell(0, slot * 2, 0, 2 * block), cell(2, slot * 2, 0, 2 * block),
            near_send.at[slot], near_recv.at[slot], k_mate,
        )

    def mid_copy(kind, j):
        slot = j % MID
        return remote(
            cell(3, slot, 0, used[kind]), cell(4, slot, 0, used[kind]),
            mid_send.at[slot], mid_recv.at[slot], y_mate,
        )

    def line_rows(kind, here, rightward):
        part = parts[kind]
        if rightward:
            start = (part * (here + 1)) // 16 * 16
            return start, used[kind] - start
        return 0, (part * here + 15) // 16 * 16

    def line_copy(kind, j, here, rightward):
        start, count = line_rows(kind, here, rightward)
        lane, slot = (0 if rightward else 1), j % NEAR
        return remote(
            cell(8, lane * NEAR + slot, start, count), cell(9 if rightward else 11, j % FAR, start, count),
            (right_send if rightward else left_send).at[slot],
            (right_recv if rightward else left_recv).at[j % FAR],
            right if rightward else left,
        )

    def out_copy(kind, j, first):
        slot = j % NEAR
        if kind == 0:
            return pltpu.make_async_copy(
                down_out.at[slot], o_down.at[:, at(j * DOWN_COLS, DOWN_COLS)], out_sem.at[slot]
            )
        out = {n_down: o_gate_up, end_both: o_qkv, end_mixed: o_out}[first]
        return pltpu.make_async_copy(
            wide_out.at[slot], out.at[:, at((j - first) * WIDE_COLS, WIDE_COLS)], out_sem.at[slot]
        )

    def out_wait(kind, slot):
        src, dst = (wide_out, o_out.at[:, 0:WIDE_COLS]) if kind else (down_out, o_down.at[:, 0:DOWN_COLS])
        pltpu.make_async_copy(src.at[slot], dst, out_sem.at[slot]).wait()

    def open_buffers():
        pl.semaphore_signal(near_free, inc=NEAR, device_id=k_mate, device_id_type=MESH)
        pl.semaphore_signal(mid_free, inc=MID, device_id=y_mate, device_id_type=MESH)

        @pl.when(z > 0)
        def _():
            pl.semaphore_signal(right_free, inc=FAR, device_id=left, device_id_type=MESH)

        @pl.when(z < last)
        def _():
            pl.semaphore_signal(left_free, inc=FAR, device_id=right, device_id_type=MESH)

    def when(condition):
        if isinstance(condition, bool):
            return (lambda work: work()) if condition else (lambda work: None)
        return pl.when(condition)

    def inside(j, first, end):
        if isinstance(j, int):
            return first <= j < end
        return (j >= first) & (j < end)

    def typed(j, work):
        @when(inside(j, 0, n_down))
        def _():
            work(0)

        @when(inside(j, n_down, total))
        def _():
            work(1)

    def multiply_down(j):
        rhs = s_grad[at(j * DOWN_COLS, DOWN_COLS), :]
        rows, piece = FF // 4, parts[0]
        for yy in range(2):
            for mine in (False, True):
                kk = k if mine else 1 - k
                lhs = v_down[at((yy * 2 + kk) * rows, rows), 0:both_toks]
                value = dot(lhs, rhs, 1, 1).astype(LOW)
                out = (own_near if mine else out_near)(j % NEAR, yy)
                for zz in range(4):
                    for t in range(3):
                        start = (zz * 3 + t) * piece
                        out[zz * piece : (zz + 1) * piece, t * 128 : (t + 1) * 128] = value[start : start + piece]

    def multiply_wide(j, lhs, rhs, first):
        right_rows = rhs[at((j - first) * WIDE_COLS, WIDE_COLS), :]
        for yy in range(2):
            for mine in (False, True):
                kk = k if mine else 1 - k
                value = dot(lhs[at((yy * 2 + kk) * block, block, 16), :], right_rows, 1, 1)
                (own_near if mine else out_near)(j % NEAR, yy)[...] = value.astype(LOW)

    def stage_near(j):
        for first, load in ((0, 0), (n_down, 3), (end_both, 1), (end_mixed, 2)):
            @when(inside(j, first, first + 1))
            def _(load=load):
                left_loads[load].wait()

        @when(inside(j, NEAR, total))
        def _():
            near_copy(j - NEAR).wait_send()

        @when(inside(j, 0, n_down))
        def _():
            multiply_down(j)

        @when(inside(j, n_down, end_both))
        def _():
            multiply_wide(j, second_t, s_both, n_down)

        @when(inside(j, end_both, end_mixed))
        def _():
            multiply_wide(j, normed_t, s_mixed, end_both)

        @when(inside(j, end_mixed, total))
        def _():
            multiply_wide(j, context_t, s_hidden, end_mixed)

        @when(inside(j, 0, total))
        def _():
            pl.semaphore_wait(near_free, 1)
            near_copy(j).start()

    def stage_mid(j):
        @when(inside(j, MID, total))
        def _():
            typed(j - MID, lambda kind: mid_copy(kind, j - MID).wait_send())

        @when(inside(j, 0, total))
        def _():
            near_copy(j).wait_recv()
            slot = j % NEAR
            for yy in range(2):
                value = (own_near(slot, yy)[...].astype(F32) + in_near(slot, yy)[...].astype(F32)).astype(LOW)

                @pl.when(y == yy)
                def _(value=value):
                    cell(5, j % SUMS)[...] = value

                @pl.when(y != yy)
                def _(value=value):
                    cell(3, j % MID)[...] = value

            pl.semaphore_wait(mid_free, 1)

        @when(inside(j, 0, total - NEAR))
        def _():
            pl.semaphore_signal(near_free, inc=1, device_id=k_mate, device_id_type=MESH)

        typed(j, lambda kind: mid_copy(kind, j).start())

    def stage_sum(j):
        typed(j, lambda kind: mid_copy(kind, j).wait_recv())

        @when(inside(j, 0, total))
        def _():
            sums = cell(5, j % SUMS)
            sums[...] = (sums[...].astype(F32) + cell(4, j % MID)[...].astype(F32)).astype(LOW)

        @when(inside(j, 0, total - MID))
        def _():
            pl.semaphore_signal(mid_free, inc=1, device_id=y_mate, device_id_type=MESH)

    def stage_line(i, rightward):
        free = right_free if rightward else left_free
        for here in range(4):
            step = here if rightward else 3 - here
            j = i - first_z - hop * step
            if step == 3 or (isinstance(j, int) and not 0 <= j < total):
                continue

            def device(here=here, step=step, j=j):
                @when(inside(j, NEAR, total))
                def _():
                    typed(j - NEAR, lambda kind: line_copy(kind, j - NEAR, here, rightward).wait_send())

                def work(kind):
                    start, count = line_rows(kind, here, rightward)
                    value = cell(5, j % SUMS, start, count)[...].astype(F32)
                    if step > 0:
                        line_copy(kind, j, here - 1 if rightward else here + 1, rightward).wait_recv()
                        came = cell(9 if rightward else 11, j % FAR, start, count)
                        value = value + came[...].astype(F32)
                    cell(8, (0 if rightward else NEAR) + j % NEAR, start, count)[...] = value.astype(LOW)

                typed(j, work)
                pl.semaphore_wait(free, 1)
                typed(j, lambda kind: line_copy(kind, j, here, rightward).start())

            @pl.when(z == here)
            def _(device=device, j=j):
                when(inside(j, 0, total))(device)

    def store(kind, j, value):
        if kind == 0:
            @when(inside(j, NEAR, total))
            def _():
                out_wait(0, j % NEAR)

            piece = parts[0]
            for t in range(3):
                down_out[j % NEAR, t * piece : (t + 1) * piece, :] = value[:, t * 128 : (t + 1) * 128]
            out_copy(0, j, 0).start()
            return
        typed(j - NEAR, lambda old: out_wait(old, j % NEAR))
        wide_out[j % NEAR] = value
        for first, end in ((n_down, end_both), (end_both, end_mixed), (end_mixed, total)):
            @when(inside(j, first, end))
            def _(first=first):
                out_copy(1, j, first).start()

    def stage_final(j):
        if isinstance(j, int) and not 0 <= j < total:
            return

        def device(here):
            def work(kind):
                part = parts[kind]
                if here == 3:
                    line_copy(kind, j, 2, True).wait_recv()
                if here == 0:
                    line_copy(kind, j, 1, False).wait_recv()
                low_at = here * part // 16 * 16
                count = (here * part + part + 15) // 16 * 16 - low_at
                value = cell(5, j % SUMS, low_at, count)[...].astype(F32)
                if here > 0:
                    value = value + cell(9, j % FAR, low_at, count)[...].astype(F32)
                if here < 3:
                    value = value + cell(11, j % FAR, low_at, count)[...].astype(F32)
                shift = here * part - low_at
                store(kind, j, value[shift : shift + part])

            typed(j, work)

            @when(inside(j, 0, total - FAR))
            def _():
                if here > 0:
                    pl.semaphore_signal(right_free, inc=1, device_id=left, device_id_type=MESH)
                if here < 3:
                    pl.semaphore_signal(left_free, inc=1, device_id=right, device_id_type=MESH)

        for here in range(4):
            @pl.when(z == here)
            def _(here=here):
                when(inside(j, 0, total))(lambda: device(here))

    def reduce_step(i):
        stage_near(i)
        stage_mid(i - 1)
        stage_sum(i - 4)
        stage_line(i, True)
        stage_line(i, False)
        stage_final(i - final_lag)

    def reduce_steps(final, first, end):
        @pl.when(final & (section == 0))
        def _():
            for i in range(first, end):
                reduce_step(i)

    def norm_back(grad, source, gain, row):
        scale = column_scale(source)
        unit = source * scale
        folded = jnp.sum(grad * unit, axis=1, keepdims=True)
        s_gains[:, row : row + 1] = s_gains[:, row : row + 1] + folded
        inner = grad * gain
        return scale * (inner - unit * jnp.mean(inner * unit, axis=0, keepdims=True))

    def rotated_back(front, back):
        cos, sin = cosine[...], sine[...]
        return jnp.concatenate([front * cos + back * sin, back * cos - front * sin], axis=0)

    def finish_micro(m):
        own = at(m * toks, toks)

        @pl.when(place == 0)
        def _():
            kv_copy(m, 0, 0, 0, 0).wait_recv()
            kv_copy(m, 0, 1, 0, 0).wait_recv()
            s_dkv[...] = s_dkv[...] + kv_in[m, 0].astype(F32) + kv_in[m, 1].astype(F32)

        @pl.when((place == 1) | (place == 2))
        def _():
            kv_copy(m, 0, 0, 0, 0).wait_recv()
            s_dkv[...] = s_dkv[...] + kv_in[m, 0].astype(F32)

        for head in range(KV_HEADS):
            front = s_dkv[head * HEAD : head * HEAD + HALF, :]
            back = s_dkv[head * HEAD + HALF : (head + 1) * HEAD, :]
            s_mixed[D + head * HEAD : D + (head + 1) * HEAD, own] = rotated_back(front, back).astype(LOW)
        s_mixed[D + KVW : qkv, own] = s_dkv[KVW : 2 * KVW, :].astype(LOW)

        def rest_tile(i, carry):
            rows = at(i * TILE, TILE)
            s_sum[rows, :] = s_sum[rows, :] + dot(v_joint[rows, D:qkv], s_mixed[D:qkv, own], 1, 0)
            return carry

        lax.fori_loop(0, D // TILE, rest_tile, 0)
        loads(m)[5].wait()
        g_now[...] = g_now[...] + norm_back(s_sum[...], s_x[...].astype(F32), columns[:, 0:1], 0)

        @pl.when(section == 1)
        def _():
            g_in[m] = g_now[...].astype(LOW)
            g_copy(m).start()

        @pl.when(m + 1 < micros)
        def _():
            for load in loads(m + 1):
                load.start()

        @pl.when(section == 0)
        def _():
            copies = result_saves(m)
            for i, save in enumerate(copies):
                if i > 1:
                    copies[i - 2].wait()
                s_dq[0:toks, i % 2 * TILE : (i % 2 + 1) * TILE] = g_now[i * TILE : (i + 1) * TILE, :].T
                save.start()

    def micro(m, carry):
        @pl.when(m > 0)
        def _():
            @pl.when(section == 0)
            def _():
                for save in result_saves(m - 1)[-2:]:
                    save.wait()

        @pl.when(m > 0)
        def _():
            for who, copy in kv_sends(m - 1):
                @pl.when(place == who)
                def _(copy=copy):
                    copy.wait_send()

        fill_bias(bias, segments, m, place, toks)
        own = at(m * toks, toks)
        final = m == micros - 1

        @pl.when(section == 1)
        def _():
            s_grad[:, own] = ends[m].astype(F32).T.astype(LOW)

        @pl.when(section == 0)
        def _():
            g_copy(m).wait_recv()
            s_grad[:, own] = g_in[m]

        @pl.when(m == 0)
        def _():
            w_loads[2].wait()

        now = loads(m)

        def inner_tile(i, carry):
            rows, up_rows = at(i * TILE, TILE), at(FF + i * TILE, TILE)
            for load in gu_loads(m, i):
                load.wait()

            grad_inner = dot(v_down[rows, :], s_grad[:, own], 1, 0)
            gate, up = s_gu[i % AHEAD, 0].astype(F32), s_gu[i % AHEAD, 1].astype(F32)
            sig = jax.nn.sigmoid(gate)
            s_both[rows, own] = (grad_inner * up * sig * (1.0 + gate * (1.0 - sig))).astype(LOW)
            s_both[up_rows, own] = (grad_inner * (gate * sig)).astype(LOW)

            @pl.when(i + AHEAD < tiles)
            def _():
                for load in gu_loads(m, i + AHEAD):
                    load.start()

            return carry

        lax.fori_loop(0, tiles, inner_tile, 0)

        @pl.when(final)
        def _():
            left_loads[0].start()
            left_loads[1].start()

        @pl.when(m == 0)
        def _():
            w_loads[1].wait()

        @pl.when(m + 1 < micros)
        def _():
            for i in range(AHEAD):
                for load in gu_loads(m + 1, i):
                    load.start()

        def second_tile(i, carry):
            rows = at(i * TILE, TILE)
            s_sum[rows, :] = dot(v_gate_up[rows, :], s_both[:, own], 1, 0)
            return carry

        lax.fori_loop(0, D // TILE, second_tile, 0)

        @pl.when(final)
        def _():
            left_loads[2].start()
            left_loads[3].start()
            open_buffers()

        now[0].wait()
        g_now[...] = s_grad[:, own].astype(F32) + norm_back(s_sum[...], s_hid[...], columns[:, 1:2], 1)
        s_hidden[:, own] = g_now[...].astype(LOW)

        @pl.when(m == 0)
        def _():
            w_loads[0].wait()

        for i in (1, 2, 3, 4):
            now[i].wait()
        reduce_steps(final, 0, 1)

        def context_tile(i, carry):
            block = dot(v_joint[at(i * TILE, TILE), qkv:], s_hidden[:, own], 1, 0).astype(LOW)
            for head in range(TILE // HEAD):
                kv_at = i * (TILE // HEAD // GROUP) + head // GROUP
                g = head % GROUP
                part = block[head * HEAD : (head + 1) * HEAD]
                s_context[at(kv_at * HEAD, HEAD, 64), g * toks : (g + 1) * toks] = part
                seen = s_att[at(i * TILE + head * HEAD, HEAD, 64), :]
                s_delta[pl.ds(kv_at, 1), g * toks : (g + 1) * toks] = jnp.sum(
                    part.astype(F32) * seen, axis=0, keepdims=True
                )
            return carry

        lax.fori_loop(0, D // TILE, context_tile, 0)
        sends = kv_sends(m)

        reduce_steps(final, 1, 2)

        @pl.when(place == 2)
        def _():
            block_grads(1, m, True)
            kv_out[0] = s_dkv[...].astype(LOW)
            sends[1][1].start()

        @pl.when(place == 3)
        def _():
            block_grads(2, m, True)
            kv_copy(m, 0, 0, 0, 3).wait_recv()
            kv_out[1] = (s_dkv[...] + kv_in[m, 0].astype(F32)).astype(LOW)
            sends[4][1].start()

        reduce_steps(final, 2, 3)

        @pl.when(place == 1)
        def _():
            block_grads(1, m, True)
            kv_out[0] = s_dkv[...].astype(LOW)
            sends[0][1].start()

        @pl.when(place == 2)
        def _():
            block_grads(2, m, False)
            kv_out[1] = s_dkv[...].astype(LOW)
            sends[2][1].start()

        @pl.when(place == 3)
        def _():
            block_grads(1, m, False)
            kv_out[0] = s_dkv[...].astype(LOW)
            sends[3][1].start()

        reduce_steps(final, 3, 4)

        @pl.when(place == 0)
        def _():
            block_grads(0, m, True)

        @pl.when(place > 0)
        def _():
            block_grads(0, m, False)

        reduce_steps(final, 4, 5)
        def query_back(kv_at, carry):
            for g in range(GROUP):
                lanes = slice(g * toks, (g + 1) * toks)
                front = s_dq[at(kv_at * HEAD, HALF, 32), lanes] * SCALE
                back = s_dq[at(kv_at * HEAD + HALF, HALF, 32), lanes] * SCALE
                rows = at((kv_at * GROUP + g) * HEAD, HEAD, 64)
                s_mixed[rows, own] = rotated_back(front, back).astype(LOW)
            return carry

        lax.fori_loop(0, KV_HEADS, query_back, 0)

        def normed_tile(i, carry):
            rows = at(i * TILE, TILE)
            s_sum[rows, :] = dot(v_joint[rows, :D], s_mixed[:D, own], 1, 0)
            return carry

        lax.fori_loop(0, D // TILE, normed_tile, 0)
        reduce_steps(final, 5, EMBEDDED)

        @pl.when((section == 1) | (m + 1 < micros))
        def _():
            finish_micro(m)

        return carry

    lax.fori_loop(0, micros, micro, 0)
    def reduce_loop(i, carry):
        reduce_step(i)
        return carry

    @pl.when(section == 0)
    def _():
        lax.fori_loop(EMBEDDED, DEFERRED, reduce_loop, 0)
        finish_micro(micros - 1)

    rows = jnp.concatenate([s_gains[...], jnp.zeros((D, 126), F32)], axis=1).T[0:8]
    for owner in range(OWNERS):
        shift = (D - owner * (D // OWNERS)) % D
        gain_out[owner] = (pltpu.roll(rows, shift, 1) if shift else rows)[:, :128]
    for i in range(1, OWNERS):
        gain_copy(i).start()

    lax.fori_loop(jnp.where(section == 0, DEFERRED, 0), total + final_lag, reduce_loop, 0)
    gain = gain_out[place * 4 + z]
    for i in range(1, OWNERS):
        gain_copy(i).wait()
        gain = gain + gain_in[i]
    o_gain[...] = gain

    @pl.when(section == 0)
    def _():
        for save in result_saves(micros - 1)[-2:]:
            save.wait()

    for m in range(2):
        @pl.when(section == 1)
        def _(m=m):
            g_copy(m).wait_send()

    for who, copy in kv_sends(micros - 1):
        @pl.when(place == who)
        def _(copy=copy):
            copy.wait_send()

    for j in range(total - NEAR, total):
        near_copy(j).wait_send()
        for at_z in range(3):
            @pl.when(z == at_z)
            def _(at_z=at_z, j=j):
                line_copy(1, j, at_z, True).wait_send()

            @pl.when(z == at_z + 1)
            def _(at_z=at_z, j=j):
                line_copy(1, j, at_z + 1, False).wait_send()
    for j in range(total - MID, total):
        mid_copy(1, j).wait_send()
    for j in range(total - NEAR, total):
        out_wait(1, j % NEAR)


def run_forward(ends, gains, cosine, sine, seg_own, w_qkv, w_out, w_gate_up, w_down):
    micros, toks = ends.shape[0], ends.shape[1]
    width = GROUP * toks
    vm, hbm = pl.BlockSpec(memory_space=pltpu.VMEM), pl.BlockSpec(memory_space=pl.ANY)
    sem = pltpu.SemaphoreType.DMA
    joint = w_qkv.shape[1] + w_out.shape[1]
    outs = [
        ((D, joint), LOW), ((D, 2 * FF), LOW), ((FF, D), LOW), ((4, micros, toks), jnp.int32),
        ((D, micros * toks), LOW), ((D, micros * toks), LOW), ((D, micros * toks), LOW),
        ((FF, micros * toks), LOW), ((micros, D, toks), LOW), ((micros, KVW, width), LOW),
        ((micros, 3, 2 * KVW, toks), LOW), ((micros, D, toks), F32), ((micros, 8, width), F32),
        ((micros, D, toks), F32), ((micros, 2 * FF, toks), LOW), ((micros, toks, D), F32),
    ]
    scratch = [
        ((joint, D), LOW), ((2 * FF, D), LOW), ((D, FF), LOW), ((2, D, SLAB), LOW), (w_down.shape, LOW),
        ((micros, D, toks), LOW), ((D, toks), F32),
        ((D, toks), LOW), ((D, toks), LOW), ((D, toks), LOW), ((FF, toks), LOW), ((D, toks), LOW),
        ((KVW, width), LOW), ((micros, 3, 2 * KVW, toks), LOW), ((D, toks), F32), ((8, width), F32),
        ((8, width), F32), ((D, toks), F32), ((2 * FF, toks), LOW), ((toks, D), F32), ((3, toks, toks), F32),
        ((4, micros, toks), jnp.int32), ((D, 2), F32),
    ]
    return pl.pallas_call(
        forward_kernel,
        out_shape=tuple(jax.ShapeDtypeStruct(s, t) for s, t in outs),
        in_specs=[vm] * 5 + [hbm] * 4,
        out_specs=(hbm,) * len(outs),
        scratch_shapes=[pltpu.VMEM(s, t) for s, t in scratch]
        + [sem((3,)), sem((2, 4)), sem((12,)), sem((micros, 2)), sem((micros, 3)), sem((micros, 3)), sem((micros, 3))]
        + [sem((2, 4)), sem((CHUNKS,))] + [sem((4, CHUNKS))] * 8,
        compiler_params=pltpu.CompilerParams(
            collective_id=3, has_side_effects=True, vmem_limit_bytes=62 * 2**20
        ),
        name="layer_forward",
    )(ends, gains, cosine, sine, seg_own, w_qkv, w_out, w_gate_up, w_down)


def run_backward(ends, gains, cosine, sine, segments, joint, gate_up, down, saved):
    micros, toks = ends.shape[0], ends.shape[1]
    width = GROUP * toks
    vm, hbm = pl.BlockSpec(memory_space=pltpu.VMEM), pl.BlockSpec(memory_space=pl.ANY)
    sem, plain = pltpu.SemaphoreType.DMA, pltpu.SemaphoreType.REGULAR
    qkv = D + 2 * KVW
    outs = [
        (micros, toks, D), (FF // OWNERS, D), (D // OWNERS, 2 * FF), (D // OWNERS, qkv), (D // OWNERS, D),
        (8, 128),
    ]
    scratch = [
        (joint.shape, LOW), (gate_up.shape, LOW), (down.shape, LOW),
        ((micros, D, toks), LOW), ((D, toks), F32),
        ((D, toks), LOW), ((KVW, width), LOW), ((3, 2 * KVW, toks), LOW), ((D, toks), F32), ((8, width), F32),
        ((D, toks), F32), ((AHEAD, 2, TILE, toks), LOW),
        ((2 * FF, micros * toks), LOW), ((qkv, micros * toks), LOW), ((D, micros * toks), LOW),
        ((D, micros * toks), LOW), ((D, toks), F32),
        ((KVW, width), LOW), ((8, width), F32), ((KVW, width), F32), ((2 * KVW, toks), F32),
        ((2, 2 * KVW, toks), LOW), ((micros, 2, 2 * KVW, toks), LOW),
        ((D, 2), F32), ((3, toks, toks), F32), ((D, 2), F32),
        ((NEAR, D // OWNERS, WIDE_COLS), F32), ((NEAR, FF // OWNERS, DOWN_COLS), F32),
        ((OWNERS, 8, 128), F32), ((OWNERS, 8, 128), F32),
    ]
    return pl.pallas_call(
        backward_kernel,
        out_shape=tuple(jax.ShapeDtypeStruct(s, F32) for s in outs),
        in_specs=[vm] * 5 + [hbm] * 15,
        out_specs=(hbm,) * 5 + (vm,),
        scratch_shapes=[pltpu.VMEM(s, t) for s, t in scratch]
        + [sem((3,)), sem((6,)), sem((AHEAD, 2)), sem((3,)), sem((micros, 2)), sem((micros, 2)), sem((micros,)), sem((micros,))]
        + [sem((4,)), sem((NEAR,)), sem((NEAR,)), sem((MID,)), sem((MID,)), sem((NEAR,)), sem((FAR,)), sem((NEAR,)), sem((FAR,))]
        + [sem((NEAR,)), sem((OWNERS,)), sem((OWNERS,)), plain, plain, plain, plain],
        compiler_params=pltpu.CompilerParams(
            collective_id=4, has_side_effects=True, vmem_limit_bytes=63 * 2**20
        ),
        input_output_aliases={15: 0},
        name="layer_backward",
    )(ends, gains, cosine, sine, segments, joint, gate_up, down, *saved)


def small_mesh():
    return lax.axis_size("ctx") == 4 and lax.axis_size("fsdp") == 4


def whole_weights(w_qkv, w_out, w_gate_up, w_down):
    return tuple(
        lax.all_gather(w, "fsdp", axis=0, tiled=True) for w in (w_qkv, w_out, w_gate_up, w_down)
    )


def owned_grads(lefts, rights):
    return tuple(
        lax.psum_scatter(
            outer_product(left, right).astype(jnp.bfloat16),
            ("ctx", "fsdp"),
            scatter_dimension=0,
            tiled=True,
        ).astype(jnp.float32)
        for left, right in zip(lefts, rights)
    )


def local_small(ends, segment_ids, w_qkv, w_out, w_gate_up, w_down, gains):
    tok_rows = ends.shape[3]
    local_ends = ends[0, :, 0]
    seg_local = segment_ids[:, 0]
    query_pos = lax.axis_index("ctx") * tok_rows + jnp.arange(tok_rows, dtype=jnp.int32)
    frequency = 10000.0 ** (-(jnp.arange(HEAD // 2).astype(jnp.float32) * 2.0 / HEAD))
    angle_table = frequency[:, None] * query_pos.astype(jnp.float32)[None, :]
    shared = (local_ends, gains[0], jnp.cos(angle_table), jnp.sin(angle_table))
    joint, gate_up, down, segments, normed, context, second, inner, *saved, result = run_forward(
        *shared, seg_local, w_qkv[0], w_out[0], w_gate_up[0], w_down[0]
    )
    ends_rows, g_down, g_gate_up, g_qkv, g_out, gain = run_backward(
        *shared, segments, joint, gate_up, down, (*saved, result, normed, context, second, inner)
    )
    return (
        ends_rows[None, :, None], g_qkv[None], g_out[None], g_gate_up[None], g_down[None],
        gain[None, :2, : D // 16],
    )


def local(ends, segment_ids, w_qkv, w_out, w_gate_up, w_down, gains):
    if small_mesh():
        return local_small(ends, segment_ids, w_qkv, w_out, w_gate_up, w_down, gains)
    section_index = lax.axis_index("section")
    micro_count = ends.shape[1]
    tok_rows = ends.shape[3]
    local_ends = ends[0, :, 0]
    seg_local = segment_ids[:, 0]
    seg_whole = lax.all_gather(seg_local, "ctx", axis=1, tiled=True)
    query_pos = lax.axis_index("ctx") * tok_rows + jnp.arange(tok_rows, dtype=jnp.int32)
    frequency = 10000.0 ** (-(jnp.arange(HEAD // 2).astype(jnp.float32) * 2.0 / HEAD))
    angle_table = query_pos.astype(jnp.float32)[:, None] * frequency[None, :]
    cosine = jnp.cos(angle_table)[:, None, :]
    sine_table = jnp.sin(angle_table)[:, None, :]
    gain_pair = gains[0]
    weights = whole_weights(w_qkv[0], w_out[0], w_gate_up[0], w_down[0])
    arrived = jnp.zeros((tok_rows, D), jnp.bfloat16)
    store_bufs = None
    outputs = jnp.zeros((micro_count + 1, tok_rows, D), jnp.float32)
    for tick_num in range(micro_count + 1):
        batch_index = tick_num - section_index
        is_valid = (batch_index >= 0) & (batch_index < micro_count)
        clipped = jnp.clip(batch_index, 0, micro_count - 1)
        slot_index = jnp.where(is_valid, batch_index, micro_count)
        own_rows = lax.dynamic_index_in_dim(local_ends, clipped, 0, keepdims=False)
        layer_in = jnp.where(section_index == 0, own_rows, arrived)
        seg_rows = lax.dynamic_index_in_dim(seg_local, clipped, 0, keepdims=False)
        seg_full = lax.dynamic_index_in_dim(seg_whole, clipped, 0, keepdims=False)
        result, saved_acts = layer_forward(
            layer_in.astype(jnp.float32),
            weights,
            gain_pair,
            seg_rows,
            seg_full,
            query_pos,
            cosine,
            sine_table,
        )
        if tick_num == 0:
            store_bufs = jax.tree.map(
                lambda update: jnp.zeros((micro_count + 1,) + update.shape, update.dtype),
                saved_acts,
            )
        store_bufs = jax.tree.map(
            lambda buffer, update: lax.dynamic_update_index_in_dim(buffer, update, slot_index, 0),
            store_bufs,
            saved_acts,
        )
        outputs = lax.dynamic_update_index_in_dim(outputs, result, slot_index, 0)
        arrived = shifted(result.astype(jnp.bfloat16), "section", 1)
    operand_bufs = None
    gain_sums = jnp.zeros((2, D), jnp.float32)
    arrived_grad = jnp.zeros((tok_rows, D), jnp.bfloat16)
    input_grads = jnp.zeros((micro_count + 1, tok_rows, D), jnp.float32)
    for tick_num in range(micro_count + 1):
        batch_index = tick_num - (1 - section_index)
        is_valid = (batch_index >= 0) & (batch_index < micro_count)
        clipped = jnp.clip(batch_index, 0, micro_count - 1)
        slot_index = jnp.where(is_valid, batch_index, micro_count)
        own_rows = lax.dynamic_index_in_dim(local_ends, clipped, 0, keepdims=False)
        incoming = jnp.where(section_index == 1, own_rows, arrived_grad)
        incoming = jnp.where(is_valid, incoming, jnp.zeros_like(incoming))
        seg_rows = lax.dynamic_index_in_dim(seg_local, clipped, 0, keepdims=False)
        seg_full = lax.dynamic_index_in_dim(seg_whole, clipped, 0, keepdims=False)
        saved_acts = jax.tree.map(
            lambda buffer: lax.dynamic_index_in_dim(buffer, clipped, 0, keepdims=False), store_bufs
        )
        grad_input, operand_pairs, gain_terms = layer_backward(
            incoming,
            saved_acts,
            weights,
            gain_pair,
            seg_rows,
            seg_full,
            query_pos,
            cosine,
            sine_table,
        )
        if tick_num == 0:
            operand_bufs = jax.tree.map(
                lambda update: jnp.zeros((micro_count + 1,) + update.shape, update.dtype),
                operand_pairs,
            )
        operand_bufs = jax.tree.map(
            lambda buffer, update: lax.dynamic_update_index_in_dim(buffer, update, slot_index, 0),
            operand_bufs,
            operand_pairs,
        )
        gain_sums = gain_sums + gain_terms
        input_grads = lax.dynamic_update_index_in_dim(input_grads, grad_input, slot_index, 0)
        arrived_grad = shifted(grad_input.astype(jnp.bfloat16), "section", -1)
    operands = [buffer[:micro_count].reshape(-1, buffer.shape[-1]) for buffer in operand_bufs]
    g_qkv, g_out, g_gate_up, g_down = owned_grads(operands[:4], operands[4:])
    g_gains = lax.psum_scatter(gain_sums, ("ctx", "fsdp"), scatter_dimension=1, tiled=True)
    final_rows = jnp.where(section_index == 0, input_grads[:micro_count], outputs[:micro_count])
    ends_out = final_rows[None, :, None]
    return (ends_out, g_qkv[None], g_out[None], g_gate_up[None], g_down[None], g_gains[None])


def solution(mesh):
    in_specs = (
        P("section", None, "fsdp", "ctx", None),
        P(None, "fsdp", "ctx"),
        P("section", "fsdp", None),
        P("section", "fsdp", None),
        P("section", "fsdp", None),
        P("section", "fsdp", None),
        P("section", None, None),
    )
    out_specs = (
        P("section", None, "fsdp", "ctx", None),
        P("section", ("ctx", "fsdp"), None),
        P("section", ("ctx", "fsdp"), None),
        P("section", ("ctx", "fsdp"), None),
        P("section", ("ctx", "fsdp"), None),
        P("section", None, ("ctx", "fsdp")),
    )
    return jax.shard_map(local, mesh=mesh, in_specs=in_specs, out_specs=out_specs, check_vma=False)
```

```python
import math

import jax
import jax.numpy as jnp
from jax import lax
from jax.experimental import pallas as pl
from jax.experimental.pallas import tpu as pltpu
from jax.sharding import PartitionSpec as P

MESH = pl.DeviceIdType.MESH

D = 1152
HEADS = 18
KV_HEADS = 6
HEAD = 64
FF = 3072
KVW = 384


EPS = 1e-05


def shifted(x, axis, by):
    size = lax.axis_size(axis)
    pairs = [(i, i + by) for i in range(size) if 0 <= i + by < size]
    return lax.ppermute(x, axis, pairs)


def rotate(values_in, cosine, sine_table):
    half_size = values_in.shape[-1] // 2
    front = values_in[..., :half_size]
    back_half = values_in[..., half_size:]
    return jnp.concatenate(
        [front * cosine - back_half * sine_table, back_half * cosine + front * sine_table], axis=-1
    )


def rotate_back(gradient, cosine, sine_table):
    half_size = gradient.shape[-1] // 2
    front = gradient[..., :half_size]
    back_half = gradient[..., half_size:]
    return jnp.concatenate(
        [front * cosine + back_half * sine_table, back_half * cosine - front * sine_table], axis=-1
    )


def norm_forward(inputs, gain_row):
    scale_row = lax.rsqrt(jnp.mean(inputs * inputs, axis=-1, keepdims=True) + EPS)
    unit_rows = inputs * scale_row
    return (unit_rows * gain_row, unit_rows, scale_row)


def norm_backward(gradient, unit_rows, scale_row, gain_row):
    unit_grad = gradient * gain_row
    gain_grad = jnp.sum(gradient * unit_rows, axis=0)
    input_grad = scale_row * (
        unit_grad - unit_rows * jnp.mean(unit_grad * unit_rows, axis=-1, keepdims=True)
    )
    return (input_grad, gain_grad)


def outer_product(left, right):
    return lax.dot_general(
        left, right, (((0,), (0,)), ((), ())), preferred_element_type=jnp.float32
    )


def times_transposed(left, right):
    return lax.dot_general(
        left, right, (((1,), (1,)), ((), ())), preferred_element_type=jnp.float32
    )


def block_needed(first_row, block_rows, seg_full, seg_rows, query_pos):
    last_seg = lax.dynamic_index_in_dim(seg_full, first_row + block_rows - 1, 0, keepdims=False)
    return (first_row <= query_pos[-1]) & (last_seg >= seg_rows[0])


def attend_forward(queries4, key_all, value_all, seg_rows, seg_full, query_pos):
    tok_rows = queries4.shape[0]
    group_size = HEADS // KV_HEADS
    score_scale = HEAD ** (-0.5)
    total_rows = key_all.shape[0]
    block_rows = math.gcd(total_rows, 512)
    block_count = total_rows // block_rows
    key_heads = key_all.reshape(total_rows, KV_HEADS, HEAD)
    value_heads = value_all.reshape(total_rows, KV_HEADS, HEAD)

    def block_scores(block_index):
        first_row = block_index * block_rows
        key_block = lax.dynamic_slice_in_dim(key_heads, first_row, block_rows, 0)
        value_block = lax.dynamic_slice_in_dim(value_heads, first_row, block_rows, 0)
        seg_block = lax.dynamic_slice_in_dim(seg_full, first_row, block_rows, 0)
        key_pos = first_row + jnp.arange(block_rows, dtype=jnp.int32)
        raw_scores = (
            jnp.einsum("qkgd,tkd->kgqt", queries4, key_block, preferred_element_type=jnp.float32)
            * score_scale
        )
        allowed = (key_pos[None, :] <= query_pos[:, None]) & (
            seg_block[None, :] == seg_rows[:, None]
        )
        return (jnp.where(allowed, raw_scores, -1e30), allowed, value_block)

    def first_pass(state_pair, block_index):

        def first_work(state_in):
            row_top, row_total = state_in
            masked, allowed, value_block = block_scores(block_index)
            new_top = jnp.maximum(row_top, jnp.max(masked, axis=-1))
            new_total = row_total * jnp.exp(row_top - new_top) + jnp.sum(
                jnp.exp(masked - new_top[..., None]), axis=-1
            )
            return (new_top, new_total)

        needed = block_needed(block_index * block_rows, block_rows, seg_full, seg_rows, query_pos)
        return (lax.cond(needed, first_work, lambda state_in: state_in, state_pair), None)

    start_state = (
        jnp.full((KV_HEADS, group_size, tok_rows), -1e30, jnp.float32),
        jnp.zeros((KV_HEADS, group_size, tok_rows), jnp.float32),
    )
    block_ids = jnp.arange(block_count, dtype=jnp.int32)
    (row_top, row_total), ignored = lax.scan(first_pass, start_state, block_ids)
    log_total = row_top + jnp.log(row_total)

    def second_pass(summed, block_index):

        def second_work(summed_in):
            masked, allowed, value_block = block_scores(block_index)
            prob_low = jnp.where(allowed, jnp.exp(masked - log_total[..., None]), 0.0).astype(
                jnp.bfloat16
            )
            added = jnp.einsum(
                "kgqt,tkd->qkgd", prob_low, value_block, preferred_element_type=jnp.float32
            )
            return summed_in + added

        needed = block_needed(block_index * block_rows, block_rows, seg_full, seg_rows, query_pos)
        return (lax.cond(needed, second_work, lambda summed_in: summed_in, summed), None)

    start_sum = jnp.zeros((tok_rows, KV_HEADS, group_size, HEAD), jnp.float32)
    attended, ignored = lax.scan(second_pass, start_sum, block_ids)
    return (attended.reshape(tok_rows, D), log_total)


def layer_forward(inputs, weights, gain_pair, seg_rows, seg_full, query_pos, cosine, sine_table):
    w_qkv, w_out, w_gate_up, w_down = weights
    tok_rows = inputs.shape[0]
    group_size = HEADS // KV_HEADS
    normed, unit_one, scale_one = norm_forward(inputs, gain_pair[0])
    normed_low = normed.astype(jnp.bfloat16)
    mixed_proj = jnp.dot(normed_low, w_qkv, preferred_element_type=jnp.float32)
    queries = rotate(mixed_proj[:, :D].reshape(tok_rows, HEADS, HEAD), cosine, sine_table).astype(
        jnp.bfloat16
    )
    key_rows = rotate(
        mixed_proj[:, D : D + KVW].reshape(tok_rows, KV_HEADS, HEAD), cosine, sine_table
    )
    key_rows = key_rows.astype(jnp.bfloat16).reshape(tok_rows, KVW)
    value_rows = mixed_proj[:, D + KVW :].astype(jnp.bfloat16)
    key_all, value_all = (
        lax.all_gather(key_rows, "ctx", axis=0, tiled=True),
        lax.all_gather(value_rows, "ctx", axis=0, tiled=True),
    )
    queries4 = queries.reshape(tok_rows, KV_HEADS, group_size, HEAD)
    attended, log_total = attend_forward(
        queries4, key_all, value_all, seg_rows, seg_full, query_pos
    )
    context = attended.astype(jnp.bfloat16)
    hidden = inputs + jnp.dot(context, w_out, preferred_element_type=jnp.float32)
    second, unit_two, scale_two = norm_forward(hidden, gain_pair[1])
    second_low = second.astype(jnp.bfloat16)
    gate_up = jnp.dot(second_low, w_gate_up, preferred_element_type=jnp.float32)
    gate_pre = gate_up[:, :FF]
    up_pre = gate_up[:, FF:]
    inner_act = (jax.nn.silu(gate_pre) * up_pre).astype(jnp.bfloat16)
    result = hidden + jnp.dot(inner_act, w_down, preferred_element_type=jnp.float32)
    saved_acts = (
        normed_low,
        queries4,
        key_all,
        value_all,
        attended,
        log_total,
        context,
        unit_one,
        scale_one,
        unit_two,
        scale_two,
        second_low,
        gate_pre,
        up_pre,
        inner_act,
    )
    return (result, saved_acts)


def layer_backward(
    grad_low, saved_acts, weights, gain_pair, seg_rows, seg_full, query_pos, cosine, sine_table
):
    w_qkv, w_out, w_gate_up, w_down = weights
    (
        normed_low,
        queries4,
        key_all,
        value_all,
        attended,
        log_total,
        context,
        unit_one,
        scale_one,
        unit_two,
        scale_two,
        second_low,
        gate_pre,
        up_pre,
        inner_act,
    ) = saved_acts
    tok_rows = grad_low.shape[0]
    group_size = HEADS // KV_HEADS
    score_scale = HEAD ** (-0.5)
    grad_out = grad_low.astype(jnp.float32)
    grad_inner = times_transposed(grad_low, w_down)
    sigmoid_gate = jax.nn.sigmoid(gate_pre)
    silu_gate = gate_pre * sigmoid_gate
    grad_gate = grad_inner * up_pre * sigmoid_gate * (1.0 + gate_pre * (1.0 - sigmoid_gate))
    grad_up = grad_inner * silu_gate
    grad_both = jnp.concatenate([grad_gate, grad_up], axis=1).astype(jnp.bfloat16)
    grad_second = times_transposed(grad_both, w_gate_up)
    grad_norm_two, gain_two = norm_backward(grad_second, unit_two, scale_two, gain_pair[1])
    grad_hidden = grad_out + grad_norm_two
    hidden_low = grad_hidden.astype(jnp.bfloat16)
    grad_context = times_transposed(hidden_low, w_out).astype(jnp.bfloat16)
    grad_context4 = grad_context.reshape(tok_rows, KV_HEADS, group_size, HEAD)
    attended4 = attended.reshape(tok_rows, KV_HEADS, group_size, HEAD)
    row_delta = jnp.einsum("qkgd,qkgd->kgq", grad_context4.astype(jnp.float32), attended4)
    total_rows = seg_full.shape[0]
    start_state = (
        jnp.zeros((tok_rows, KV_HEADS, group_size, HEAD), jnp.float32),
        jnp.zeros((total_rows, 2 * KVW), jnp.float32),
    )
    key_piece, value_piece = key_all, value_all
    piece_rows = key_piece.shape[0]
    block_rows = math.gcd(piece_rows, 512)
    block_count = piece_rows // block_rows

    def one_block(block_index, inner_state):
        offset = block_index * block_rows

        def one_work(state_in):
            grad_query, grad_kv = state_in
            key_block = lax.dynamic_slice_in_dim(key_piece, offset, block_rows, 0).reshape(
                block_rows, KV_HEADS, HEAD
            )
            value_block = lax.dynamic_slice_in_dim(value_piece, offset, block_rows, 0).reshape(
                block_rows, KV_HEADS, HEAD
            )
            seg_block = lax.dynamic_slice_in_dim(seg_full, offset, block_rows, 0)
            key_pos = offset + jnp.arange(block_rows, dtype=jnp.int32)
            raw_scores = (
                jnp.einsum(
                    "qkgd,tkd->kgqt", queries4, key_block, preferred_element_type=jnp.float32
                )
                * score_scale
            )
            allowed = (key_pos[None, :] <= query_pos[:, None]) & (
                seg_block[None, :] == seg_rows[:, None]
            )
            prob_full = jnp.where(allowed, jnp.exp(raw_scores - log_total[..., None]), 0.0)
            prob_low = prob_full.astype(jnp.bfloat16)
            grad_value = jnp.einsum(
                "kgqt,qkgd->tkd", prob_low, grad_context4, preferred_element_type=jnp.float32
            )
            grad_prob = jnp.einsum(
                "qkgd,tkd->kgqt", grad_context4, value_block, preferred_element_type=jnp.float32
            )
            grad_scores = (prob_full * (grad_prob - row_delta[..., None])).astype(jnp.bfloat16)
            grad_query = (
                grad_query
                + jnp.einsum(
                    "kgqt,tkd->qkgd", grad_scores, key_block, preferred_element_type=jnp.float32
                )
                * score_scale
            )
            grad_key = (
                jnp.einsum(
                    "kgqt,qkgd->tkd", grad_scores, queries4, preferred_element_type=jnp.float32
                )
                * score_scale
            )
            new_rows = jnp.concatenate(
                [grad_key.reshape(block_rows, KVW), grad_value.reshape(block_rows, KVW)], axis=1
            )
            old_rows = lax.dynamic_slice_in_dim(grad_kv, offset, block_rows, 0)
            grad_kv = lax.dynamic_update_slice_in_dim(grad_kv, old_rows + new_rows, offset, 0)
            return (grad_query, grad_kv)

        needed = block_needed(offset, block_rows, seg_full, seg_rows, query_pos)
        return lax.cond(needed, one_work, lambda state_in: state_in, inner_state)

    grad_query, grad_kv_all = lax.fori_loop(0, block_count, one_block, start_state)
    grad_kv_own = lax.psum_scatter(
        grad_kv_all.astype(jnp.bfloat16), "ctx", scatter_dimension=0, tiled=True
    ).astype(jnp.float32)
    grad_q_pre = rotate_back(grad_query.reshape(tok_rows, HEADS, HEAD), cosine, sine_table).reshape(
        tok_rows, D
    )
    grad_k_pre = rotate_back(
        grad_kv_own[:, :KVW].reshape(tok_rows, KV_HEADS, HEAD), cosine, sine_table
    ).reshape(tok_rows, KVW)
    grad_mixed = jnp.concatenate([grad_q_pre, grad_k_pre, grad_kv_own[:, KVW:]], axis=1).astype(
        jnp.bfloat16
    )
    grad_normed = times_transposed(grad_mixed, w_qkv)
    grad_norm_one, gain_one = norm_backward(grad_normed, unit_one, scale_one, gain_pair[0])
    grad_input = grad_hidden + grad_norm_one
    operand_pairs = (
        normed_low,
        context,
        second_low,
        inner_act,
        grad_mixed,
        hidden_low,
        grad_both,
        grad_low,
    )
    return (grad_input, operand_pairs, jnp.stack([gain_one, gain_two]))


DOWN_COLS = 128
WIDE_COLS = 384
NEAR, MID, FAR, SUMS = 2, 4, 8, 12
OWNERS = 16
EMBEDDED, DEFERRED = 6, 6
AHEAD = 4


F32, LOW = jnp.float32, jnp.bfloat16
GROUP = HEADS // KV_HEADS
HALF = HEAD // 2
SCALE = HEAD ** (-0.5)
NONE = -1e30
TILE = 384
WIDE = 512


def dot(left, right, left_dim, right_dim):
    return lax.dot_general(
        left, right, (((left_dim,), (right_dim,)), ((), ())), preferred_element_type=F32
    )


def at(start, size, step=128):
    return pl.ds(pl.multiple_of(start, step), size)


def column_scale(v):
    return lax.rsqrt(jnp.mean(v * v, axis=0, keepdims=True) + EPS)


def greet(peers):
    barrier = pltpu.get_barrier_semaphore()
    for peer in peers:
        pl.semaphore_signal(barrier, inc=1, device_id=peer, device_id_type=MESH)
    pl.semaphore_wait(barrier, len(peers))


def remote(src, dst, send, recv, peer):
    return pltpu.make_async_remote_copy(
        src_ref=src, dst_ref=dst, send_sem=send, recv_sem=recv, device_id=peer, device_id_type=MESH
    )


def fill_bias(bias, segments, m, place, toks):
    own = segments[place, pl.ds(m, 1), :]
    rows = lax.broadcasted_iota(jnp.int32, (toks, toks), 0)
    cols = lax.broadcasted_iota(jnp.int32, (toks, toks), 1)
    for d in range(3):
        seen = segments[jnp.maximum(place - d, 0), pl.ds(m, 1), :]
        keys = jnp.broadcast_to(seen, (8, toks)).T[:, 0:1]
        allowed = keys == own
        if d == 0:
            allowed = allowed & (rows <= cols)
        bias[d] = jnp.where(allowed, 0.0, NONE)


def gain_columns(gains, columns):
    for row in range(2):
        columns[:, row : row + 1] = jnp.broadcast_to(gains[row : row + 1, :], (8, D)).T[:, 0:1]


JOINT_CHUNKS, WIDE_CHUNKS, DOWN_CHUNKS = 3, 3, 4
CHUNKS = JOINT_CHUNKS + WIDE_CHUNKS + DOWN_CHUNKS
SLAB = 1024


def forward_kernel(
    ends, gains, cosine, sine, seg_own, w_qkv, w_out, w_gate_up, w_down,
    f_joint, f_gate_up, f_down, o_seg,
    o_normed, o_context, o_second, o_inner, o_x, o_q, o_kv, o_att, o_lse, o_hidden, o_gu, o_result,
    t_joint, t_gate_up, t_down, stage, stage_down, x_in, x_now, s_normed, s_context, s_second,
    s_inner, s_x, s_q, s_kv, s_att, s_top, s_lse, s_hidden, s_gu, s_result, bias, segments, columns,
    stage_sem, seg_sem, save_sem, kv_send, kv_recv, x_send, x_recv,
    own_sem, back_sem, zs, zr, ys, yr, cs, cr, es, er,
):
    section = lax.axis_index("section")
    place = lax.axis_index("ctx")
    z = lax.axis_index("fsdp")
    last = lax.axis_size("fsdp") - 1
    y, k = place // 2, place % 2
    y_mate = {"ctx": (1 - y) * 2 + k}
    k_mate = {"ctx": y * 2 + 1 - k}
    micros, toks = ends.shape[0], ends.shape[1]
    qkv = D + 2 * KVW
    width, deep = w_gate_up.shape[0], w_down.shape[0]
    half, joint_half, wide_half = width // 2, f_joint.shape[1] // 2, f_gate_up.shape[1] // 2

    barrier = pltpu.get_barrier_semaphore()
    for peer in [{"ctx": (place + i) % 4} for i in (1, 2, 3)] + [{"section": 1 - section}]:
        pl.semaphore_signal(barrier, inc=1, device_id=peer, device_id_type=MESH)

    @pl.when(z > 0)
    def _():
        pl.semaphore_signal(barrier, inc=1, device_id={"fsdp": z - 1}, device_id_type=MESH)

    @pl.when(z < last)
    def _():
        pl.semaphore_signal(barrier, inc=1, device_id={"fsdp": z + 1}, device_id_type=MESH)

    pl.semaphore_wait(barrier, 4 + jnp.where(z > 0, 1, 0) + jnp.where(z < last, 1, 0))

    def view(shard, yy, kk, j, own=False):
        if j < JOINT_CHUNKS:
            rows = half // JOINT_CHUNKS
            return f_joint.at[
                at(shard * width + yy * half + j * rows, rows, 16), at(kk * joint_half, joint_half)
            ]
        j = j - JOINT_CHUNKS
        if j < WIDE_CHUNKS:
            cols = wide_half // WIDE_CHUNKS
            ref, first = (w_gate_up, 0) if own else (f_gate_up, shard * width)
            return ref.at[at(first + yy * half, half, 16), at(kk * wide_half + j * cols, cols)]
        j = j - WIDE_CHUNKS
        rows = deep // 4 // DOWN_CHUNKS
        ref, first = (w_down, 0) if own else (f_down, shard * deep)
        return ref.at[at(first + (yy * 2 + kk) * (deep // 4) + j * rows, rows, 16), :]

    def z_copy(shard, j, to, own, back):
        ref = view(shard, y, k, j)
        src = view(shard, y, k, j, True) if own and j >= JOINT_CHUNKS else ref
        return remote(
            src, ref, back_sem.at[j] if back else zs.at[shard, j], zr.at[shard, j], {"fsdp": to}
        )

    def own_start(j, to, back):
        if j >= JOINT_CHUNKS:
            z_copy(z, j, to, True, back).start()
            return
        rows = half // JOINT_CHUNKS
        here = at(y * half + j * rows, rows, 16)
        there = at(z * width + y * half + j * rows, rows, 16)
        send, recv = back_sem.at[j] if back else zs.at[z, j], zr.at[z, j]

        @pl.when(k == 0)
        def _():
            remote(
                w_qkv.at[here, 0:joint_half], f_joint.at[there, 0:joint_half], send, recv, {"fsdp": to}
            ).start()

        @pl.when(k == 1)
        def _():
            remote(
                w_qkv.at[here, joint_half:qkv], f_joint.at[there, joint_half:qkv], send, recv, {"fsdp": to}
            ).start()
            remote(w_out.at[here, :], f_joint.at[there, qkv:], send, recv, {"fsdp": to}).start()

    def own_sends(j):
        @pl.when(z < last)
        def _():
            own_start(j, z + 1, False)

        @pl.when(z > 0)
        def _():
            own_start(j, z - 1, True)

    def mate_copy(shard, j, yy, mate, send, recv):
        ref = view(shard, yy, k, j)
        return remote(ref, ref, send.at[shard, j], recv.at[shard, j], mate)

    def arrive(shard, j, yy, kk, recv):
        ref = view(shard, yy, kk, j)
        remote(ref, ref, recv.at[shard, j], recv.at[shard, j], k_mate).wait_recv()

    rows_z, rows_deep = at(z * width, width, 16), at(z * deep, deep, 16)
    own_pairs = (
        (w_qkv, f_joint.at[rows_z, 0:qkv]), (w_out, f_joint.at[rows_z, qkv:]),
        (w_gate_up, f_gate_up.at[rows_z, :]), (w_down, f_down.at[rows_deep, :]),
    )
    own_copies = [
        remote(a, b, own_sem.at[0, i], own_sem.at[1, i], k_mate) for i, (a, b) in enumerate(own_pairs)
    ]

    def sides(d):
        return ((z - d >= 0, z - d, z + 1, z < last), (z + d <= last, z + d, z - 1, z > 0))

    def relay(d, j):
        for valid, shard, onward, more in sides(d):
            @pl.when(valid)
            def _(shard=shard, onward=onward, more=more):
                arrive(shard, j, y, k, zr)
                if d < 3:
                    @pl.when(more)
                    def _():
                        z_copy(shard, j, onward, False, False).start()
                mate_copy(shard, j, y, y_mate, ys, yr).start()
                mate_copy(shard, j, y, k_mate, cs, cr).start()

    def across(d, j):
        for valid, shard, onward, more in sides(d):
            @pl.when(valid)
            def _(shard=shard):
                arrive(shard, j, 1 - y, k, yr)
                mate_copy(shard, j, 1 - y, k_mate, es, er).start()

    def complete(d, j):
        for valid, shard, onward, more in sides(d):
            @pl.when(valid)
            def _(shard=shard):
                arrive(shard, j, y, 1 - k, cr)
                arrive(shard, j, 1 - y, 1 - k, er)

    first_down = JOINT_CHUNKS + WIDE_CHUNKS
    order = [(d, j) for d in (1, 2, 3) for j in range(JOINT_CHUNKS)]
    order += [(d, j) for d in (1, 2, 3) for j in range(JOINT_CHUNKS, CHUNKS)]
    refill = {3: (3,), 5: (4,), 6: (5,), 7: (6, 7), 8: (8, 9)}
    done = {"relay": 0, "across": 0}

    def pump(upto, lag=3):
        while done["relay"] < min(upto, len(order)):
            relay(*order[done["relay"]])
            for extra in refill.get(done["relay"], ()):
                own_sends(extra)
            done["relay"] += 1
            while done["across"] < done["relay"] - lag:
                across(*order[done["across"]])
                done["across"] += 1

    def flush(upto):
        while done["across"] < upto:
            across(*order[done["across"]])
            done["across"] += 1

    def turn_slabs(ref, out, slabs, first, end):
        rows = slice(first, end)
        copies = [
            pltpu.make_async_copy(
                ref.at[rows, q * SLAB : (q + 1) * SLAB], stage.at[i, rows, :], stage_sem.at[i]
            )
            for i, q in enumerate(slabs)
        ]
        for copy in copies:
            copy.start()
        for i, q in enumerate(slabs):
            copies[i].wait()

            def step(c, carry, i=i, q=q):
                cols = at(c * 256, 256)
                out[at(q * SLAB + c * 256, 256), rows] = stage[i, rows, cols].T
                return carry

            lax.fori_loop(0, SLAB // 256, step, 0)

    third = D // 3

    def turn_near(ref, out, slabs):
        for when, first, end in (
            (z == 0, 0, 2 * third), (z == last, third, D), ((z > 0) & (z < last), 0, D),
        ):
            @pl.when(when)
            def _(first=first, end=end):
                turn_slabs(ref, out, slabs, first, end)

    def turn_rest(ref, out, slabs):
        for when, first, end in ((z == 0, 2 * third, D), (z == last, 0, third)):
            @pl.when(when)
            def _(first=first, end=end):
                turn_slabs(ref, out, slabs, first, end)

    def turn_down(shard):
        copy = pltpu.make_async_copy(f_down.at[at(shard * deep, deep), :], stage_down, stage_sem.at[2])
        copy.start()
        copy.wait()

        def step(i, carry):
            t_down[at(i * TILE, TILE), at(shard * deep, deep)] = stage_down[:, at(i * TILE, TILE)].T
            return carry

        lax.fori_loop(0, D // TILE, step, 0)

    def saves(m):
        lanes = at(m * toks, toks)
        pairs = (
            (s_normed, o_normed.at[:, lanes]), (s_context, o_context.at[:, lanes]),
            (s_second, o_second.at[:, lanes]), (s_inner, o_inner.at[:, lanes]),
            (s_x, o_x.at[m]), (s_q, o_q.at[m]), (s_kv.at[m], o_kv.at[m]), (s_att, o_att.at[m]),
            (s_lse, o_lse.at[m]), (s_hidden, o_hidden.at[m]), (s_gu, o_gu.at[m]),
        )
        return [pltpu.make_async_copy(a, b, save_sem.at[i]) for i, (a, b) in enumerate(pairs)]

    def keep(m, *items):
        copies = saves(m)
        for i in items:
            copies[i].start()

    def result_save(m):
        return pltpu.make_async_copy(s_result, o_result.at[m], save_sem.at[11])

    def x_copy(m, i):
        part = x_in.at[m, at(i * TILE, TILE), :]
        return remote(part, part, x_send.at[m, i], x_recv.at[m, i], {"section": 1})

    def kv_copy(m, source, slot, lane, to):
        return remote(
            s_kv.at[m, source], s_kv.at[m, slot], kv_send.at[m, lane], kv_recv.at[m, slot],
            {"ctx": to},
        )

    def kv_sends(m):
        return (
            (0, kv_copy(m, 0, 2, 1, 2)),
            (0, kv_copy(m, 0, 1, 0, 1)),
            (1, kv_copy(m, 0, 2, 0, 3)),
            (2, kv_copy(m, 0, 1, 0, 3)),
        )

    def attend(kv_at, m, blocks, fresh):
        rows = at(kv_at * HEAD, HEAD, 64)
        query = s_q[rows, :]
        parts = []
        for d in blocks:
            part = dot(s_kv[m, d, rows, :], query, 0, 0)
            mask = bias[d]
            parts.append(part + jnp.concatenate([mask] * GROUP, axis=1))
        scores = parts[0] if len(parts) == 1 else jnp.concatenate(parts, axis=0)
        top = jnp.max(scores, axis=0, keepdims=True)
        one = pl.ds(kv_at, 1)
        if not fresh:
            old_top, old_total = s_top[one, :], s_lse[one, :]
            top = jnp.maximum(top, old_top)
        probs = jnp.exp(scores - top)
        total = jnp.sum(probs, axis=0, keepdims=True)
        probs = probs.astype(LOW)
        value_rows = at(KVW + kv_at * HEAD, HEAD, 64)
        summed = None
        for i, d in enumerate(blocks):
            term = dot(s_kv[m, d, value_rows, :], probs[i * toks : (i + 1) * toks], 1, 0)
            summed = term if summed is None else summed + term
        if not fresh:
            keep = jnp.exp(old_top - top)
            total = total + old_total * keep
        s_top[one, :] = top
        s_lse[one, :] = total
        for g in range(GROUP):
            lanes = slice(g * toks, (g + 1) * toks)
            out_rows = at((kv_at * GROUP + g) * HEAD, HEAD, 64)
            value = summed[:, lanes]
            if not fresh:
                value = value + s_att[out_rows, :] * keep[:, lanes]
            s_att[out_rows, :] = value

    def each(m, blocks, fresh):
        def step(kv_at, carry):
            attend(kv_at, m, blocks, fresh)
            return carry

        lax.fori_loop(0, KV_HEADS, step, 0)

    def take_own(m):
        x_now[...] = ends[m].astype(F32).T

    def take_sent(m):
        for i in range(D // TILE):
            x_copy(m, i).wait_recv()
        x_now[...] = x_in[m].astype(F32)

    def first_norm(m):
        x = x_now[...]
        s_x[...] = x.astype(LOW)
        s_normed[...] = (x * column_scale(x) * columns[:, 0:1]).astype(LOW)
        keep(m, 0, 4)
        fill_bias(bias, segments, m, place, toks)

    def rotated(block, head):
        cos, sin = cosine[...], sine[...]
        front = block[head * HEAD : head * HEAD + HALF]
        back = block[head * HEAD + HALF : (head + 1) * HEAD]
        return jnp.concatenate([front * cos - back * sin, back * cos + front * sin], axis=0)

    def keys_values(m):
        keys = dot(t_joint[D : D + KVW, :], s_normed[...], 1, 0)
        for head in range(KV_HEADS):
            s_kv[m, 0, head * HEAD : (head + 1) * HEAD, :] = rotated(keys, head).astype(LOW)
        s_kv[m, 0, KVW : 2 * KVW, :] = dot(t_joint[D + KVW : qkv, :], s_normed[...], 1, 0).astype(LOW)
        for who, copy in kv_sends(m):
            @pl.when(place == who)
            def _(copy=copy):
                copy.start()

    def queries(m):
        def query_tile(i, carry):
            block = dot(t_joint[at(i * TILE, TILE), :], s_normed[...], 1, 0) * SCALE
            for head in range(TILE // HEAD):
                rows = at((i * (TILE // HEAD // GROUP) + head // GROUP) * HEAD, HEAD, 64)
                g = head % GROUP
                s_q[rows, g * toks : (g + 1) * toks] = rotated(block, head).astype(LOW)
            return carry

        lax.fori_loop(0, D // TILE, query_tile, 0)
        keep(m, 5)

    def near_block(m):
        each(m, (0,), True)

    def far_blocks(m):
        @pl.when(place == 1)
        def _():
            kv_copy(m, 0, 1, 0, 1).wait_recv()
            each(m, (1,), False)

        @pl.when(place == 2)
        def _():
            kv_copy(m, 0, 2, 0, 2).wait_recv()
            each(m, (2,), False)
            kv_copy(m, 0, 1, 0, 2).wait_recv()
            each(m, (1,), False)

        @pl.when(place == 3)
        def _():
            kv_copy(m, 0, 1, 0, 3).wait_recv()
            each(m, (1,), False)
            kv_copy(m, 0, 2, 0, 3).wait_recv()
            kv_copy(m, 2, 1, 0, 2).start()
            each(m, (2,), False)

    def contexts(m):
        def finish(kv_at, carry):
            one = pl.ds(kv_at, 1)
            total = s_lse[one, :]
            inverse = 1.0 / total
            for g in range(GROUP):
                rows = at((kv_at * GROUP + g) * HEAD, HEAD, 64)
                value = s_att[rows, :] * inverse[:, g * toks : (g + 1) * toks]
                s_att[rows, :] = value
                s_context[rows, :] = value.astype(LOW)
            s_lse[one, :] = s_top[one, :] + jnp.log(total)
            return carry

        lax.fori_loop(0, KV_HEADS, finish, 0)
        keep(m, 1, 6, 7, 8)

    def seconds(m):
        def out_tile(i, carry):
            rows = at(i * TILE, TILE)
            s_hidden[rows, :] = x_now[rows, :] + dot(
                t_joint[at(qkv + i * TILE, TILE), :], s_context[...], 1, 0
            )
            return carry

        lax.fori_loop(0, D // TILE, out_tile, 0)
        hidden = s_hidden[...]
        s_second[...] = (hidden * column_scale(hidden) * columns[:, 1:2]).astype(LOW)
        keep(m, 2, 9)

    def gates(first, end):
        def gate_tile(i, carry):
            rows, up_rows = at(i * WIDE, WIDE), at(FF + i * WIDE, WIDE)
            gate = dot(t_gate_up[rows, :], s_second[...], 1, 0)
            up = dot(t_gate_up[up_rows, :], s_second[...], 1, 0)
            s_gu[rows, :] = gate.astype(LOW)
            s_gu[up_rows, :] = up.astype(LOW)
            s_inner[rows, :] = (gate * jax.nn.sigmoid(gate) * up).astype(LOW)
            return carry

        lax.fori_loop(first, end, gate_tile, 0)

    def early(work):
        @pl.when(section == 0)
        def _():
            work()

    for j in range(JOINT_CHUNKS):
        own_sends(j)
    for copy in own_copies:
        copy.start()
    segments[place] = seg_own[...]

    def seg_copy(i):
        return remote(
            seg_own, segments.at[place], seg_sem.at[0, i], seg_sem.at[1, i], {"ctx": (place + i) % 4}
        )

    for i in (1, 2, 3):
        seg_copy(i).start()
    gain_columns(gains, columns)
    early(lambda: take_own(0))
    for i in (1, 2, 3):
        seg_copy(i).wait()
    early(lambda: first_norm(0))

    joint_items = 3 * JOINT_CHUNKS
    lap = CHUNKS - JOINT_CHUNKS
    pump(joint_items + 3)
    for j in range(JOINT_CHUNKS):
        for d in (1, 2, 3):
            complete(d, j)
    own_copies[0].wait_recv()
    own_copies[1].wait_recv()

    def turn_all(ref, out, slabs):
        turn_slabs(ref, out, slabs, 0, D)

    turn_all(f_joint, t_joint, (0, 1))
    pump(joint_items + 4)
    turn_all(f_joint, t_joint, (2,))
    pump(joint_items + 5)
    early(lambda: keys_values(0))
    pump(joint_items + 6)
    early(lambda: queries(0))
    pump(joint_items + lap)
    early(lambda: near_block(0))
    pump(joint_items + lap + 3)
    early(lambda: far_blocks(0))
    pump(joint_items + lap + 5)
    early(lambda: contexts(0))
    early(lambda: seconds(0))
    pump(joint_items + 2 * lap)
    own_copies[2].wait_recv()
    for d in (1, 2):
        for j in range(JOINT_CHUNKS, first_down):
            complete(d, j)
    for p in range(WIDE_CHUNKS):
        turn_near(f_gate_up, t_gate_up, (p, WIDE_CHUNKS + p))
        pump(joint_items + 2 * lap + p + 1)

    def turn_downs(d):
        for j in range(first_down, CHUNKS):
            complete(d, j)
        for valid, shard, onward, more in sides(d):
            @pl.when(valid)
            def _(shard=shard):
                turn_down(shard)

    own_copies[3].wait_recv()
    turn_down(z)
    pump(joint_items + 3 * lap - 3)
    turn_downs(1)
    pump(joint_items + 3 * lap - 2)
    turn_downs(2)
    pump(joint_items + 3 * lap - 1)
    per_slab = SLAB // WIDE
    for p in range(WIDE_CHUNKS):
        complete(3, JOINT_CHUNKS + p)
        turn_rest(f_gate_up, t_gate_up, (p, WIDE_CHUNKS + p))
        early(lambda p=p: gates(p * per_slab, (p + 1) * per_slab))
        if p == 0:
            pump(joint_items + 3 * lap)
        flush(joint_items + 3 * lap - 2 + p)
    turn_downs(3)

    def micro(m, carry):
        @pl.when(m > 0)
        def _():
            for save in saves(m - 1):
                save.wait()

            @pl.when(section == 1)
            def _():
                result_save(m - 1).wait()

        @pl.when((section == 1) | (m > 0))
        def _():
            @pl.when(section == 0)
            def _():
                take_own(m)

            @pl.when(section == 1)
            def _():
                take_sent(m)

            first_norm(m)
            keys_values(m)
            queries(m)
            near_block(m)
            far_blocks(m)
            contexts(m)
            seconds(m)
            gates(0, FF // WIDE)

        keep(m, 3, 10)
        for i in range(D // TILE):
            rows = slice(i * TILE, (i + 1) * TILE)
            value = s_hidden[rows, :] + dot(t_down[rows, :], s_inner[...], 1, 0)
            x_now[rows, :] = value

            @pl.when(section == 0)
            def _(i=i, rows=rows, value=value):
                x_in[m, rows, :] = value.astype(LOW)
                x_copy(m, i).start()

        @pl.when(section == 1)
        def _():
            s_result[...] = x_now[...].T
            result_save(m).start()

        return carry

    lax.fori_loop(0, micros, micro, 0)
    seg_save = pltpu.make_async_copy(segments, o_seg, seg_sem.at[0, 0])
    seg_save.start()
    for save in saves(micros - 1):
        save.wait()
    seg_save.wait()

    @pl.when(section == 1)
    def _():
        result_save(micros - 1).wait()

    for m in range(2):
        @pl.when(section == 0)
        def _(m=m):
            for i in range(D // TILE):
                x_copy(m, i).wait_send()

        for who, copy in kv_sends(m):
            @pl.when(place == who)
            def _(copy=copy):
                copy.wait_send()

        @pl.when(place == 3)
        def _(m=m):
            kv_copy(m, 2, 1, 0, 2).wait_send()

    for d, j in order:
        for valid, shard, onward, more in sides(d):
            @pl.when(valid)
            def _(shard=shard, onward=onward, more=more):
                mate_copy(shard, j, y, y_mate, ys, yr).wait_send()
                mate_copy(shard, j, y, k_mate, cs, cr).wait_send()
                mate_copy(shard, j, 1 - y, k_mate, es, er).wait_send()
                if d < 3:
                    @pl.when(more)
                    def _():
                        z_copy(shard, j, onward, False, False).wait_send()
    for j in range(CHUNKS):
        @pl.when(z < last)
        def _(j=j):
            z_copy(z, j, z + 1, True, False).wait_send()

        @pl.when(z > 0)
        def _(j=j):
            z_copy(z, j, z - 1, True, True).wait_send()
    for copy in own_copies:
        copy.wait_send()


def backward_kernel(
    ends, gains, cosine, sine, segments, w_joint, w_gate_up, w_down,
    i_x, i_q, i_kv, i_att, i_lse, i_hidden, i_gu, i_result, i_normed, i_context, i_second, i_inner,
    o_result, o_down, o_gate_up, o_qkv, o_out, o_gain,
    v_joint, v_gate_up, v_down, g_in, g_now, s_x, s_q, s_kv, s_att, s_lse, s_hid, s_gu,
    s_both, s_mixed, s_hidden, s_grad, s_sum, s_context, s_delta, s_dq, s_dkv, kv_out, kv_in,
    s_gains, bias, columns, wide_out, down_out, gain_out, gain_in,
    w_sem, load_sem, gu_sem, save_sem, kv_send, kv_recv, x_send, x_recv,
    left_sem, near_send, near_recv, mid_send, mid_recv, right_send, right_recv, left_send, left_recv,
    out_sem, gain_send, gain_recv, near_free, mid_free, right_free, left_free,
):
    section = lax.axis_index("section")
    place = lax.axis_index("ctx")
    micros, toks = ends.shape[0], ends.shape[1]
    qkv = D + 2 * KVW
    w_loads = [
        pltpu.make_async_copy(src, dst, w_sem.at[i])
        for i, (src, dst) in enumerate(
            ((w_joint, v_joint), (w_gate_up, v_gate_up), (w_down, v_down))
        )
    ]

    def loads(m):
        pairs = (
            (i_hidden, s_hid), (i_att, s_att), (i_q, s_q), (i_kv, s_kv),
            (i_lse, s_lse), (i_x, s_x),
        )
        return [pltpu.make_async_copy(a.at[m], b, load_sem.at[i]) for i, (a, b) in enumerate(pairs)]

    tiles = FF // TILE

    def gu_loads(m, i):
        slot = i % AHEAD
        return [
            pltpu.make_async_copy(
                i_gu.at[m, at(part * FF + i * TILE, TILE), :], s_gu.at[slot, part], gu_sem.at[slot, part]
            )
            for part in range(2)
        ]

    w_loads[2].start()
    for i in range(AHEAD):
        for load in gu_loads(0, i):
            load.start()
    for load in loads(0):
        load.start()
    w_loads[1].start()
    w_loads[0].start()
    z = lax.axis_index("fsdp")
    last = lax.axis_size("fsdp") - 1
    others = [((place + i // 4) % 4, (z + i % 4) % 4) for i in range(1, OWNERS)]
    greet([{"ctx": a, "fsdp": b} for a, b in others] + [{"section": 1 - section}])
    s_gains[...] = jnp.zeros_like(s_gains)
    gain_columns(gains, columns)

    def result_saves(m):
        return [
            pltpu.make_async_copy(
                s_dq.at[0:toks, at(i % 2 * TILE, TILE)], o_result.at[m, :, i * TILE : (i + 1) * TILE], save_sem.at[i]
            )
            for i in range(D // TILE)
        ]

    def g_copy(m):
        return remote(g_in.at[m], g_in.at[m], x_send.at[m], x_recv.at[m], {"section": 0})

    def kv_copy(m, source, slot, lane, to):
        return remote(
            kv_out.at[source], kv_in.at[m, slot], kv_send.at[m, lane], kv_recv.at[m, slot],
            {"ctx": to},
        )

    def kv_sends(m):
        return (
            (1, kv_copy(m, 0, 0, 0, 0)),
            (2, kv_copy(m, 0, 0, 0, 3)),
            (2, kv_copy(m, 1, 1, 1, 0)),
            (3, kv_copy(m, 0, 0, 0, 2)),
            (3, kv_copy(m, 1, 0, 1, 1)),
        )

    def block_grads(d, m, fresh):
        def step(kv_at, carry):
            rows = at(kv_at * HEAD, HEAD, 64)
            value_rows = at(KVW + kv_at * HEAD, HEAD, 64)
            one = pl.ds(kv_at, 1)
            query, grad = s_q[rows, :], s_context[rows, :]
            key, value = s_kv[d, rows, :], s_kv[d, value_rows, :]
            mask = bias[d]
            scores = dot(key, query, 0, 0) + jnp.concatenate([mask] * GROUP, axis=1)
            probs = jnp.exp(scores - s_lse[one, :])
            grad_probs = dot(value, grad, 0, 0)
            grad_scores = (probs * (grad_probs - s_delta[one, :])).astype(LOW)
            s_dkv[rows, :] = dot(query, grad_scores, 1, 1)
            s_dkv[value_rows, :] = dot(grad, probs.astype(LOW), 1, 1)
            grad_query = dot(key, grad_scores, 1, 0)
            if fresh:
                s_dq[rows, :] = grad_query
            else:
                s_dq[rows, :] = s_dq[rows, :] + grad_query
            return carry

        lax.fori_loop(0, KV_HEADS, step, 0)

    y, k = place // 2, place % 2
    y_mate = {"ctx": (1 - y) * 2 + k}
    k_mate = {"ctx": y * 2 + 1 - k}
    right, left = {"fsdp": z + 1}, {"fsdp": z - 1}
    n_down, n_both = D // DOWN_COLS, 2 * FF // WIDE_COLS
    n_mixed, n_out = qkv // WIDE_COLS, D // WIDE_COLS
    end_both = n_down + n_both
    end_mixed = end_both + n_mixed
    total = end_mixed + n_out
    hop, first_z = 2, 4
    final_lag = first_z + hop * 3
    block = D // 4
    parts = (FF // OWNERS // 3, D // OWNERS)
    used = (4 * parts[0], block)
    spare = 13 * WIDE_COLS
    both_toks = micros * toks
    inner_t = v_down.at[:, 0:both_toks]
    normed_t = v_down.at[0:D, both_toks : 2 * both_toks]
    context_t = v_gate_up.at[:, spare : spare + both_toks]
    second_t = v_gate_up.at[:, spare + both_toks : spare + 2 * both_toks]
    left_loads = [
        pltpu.make_async_copy(a, b, left_sem.at[i])
        for i, (a, b) in enumerate(
            ((i_inner, inner_t), (i_normed, normed_t), (i_context, context_t), (i_second, second_t))
        )
    ]

    def cell(column, slot, first=0, count=block):
        rows = at(slot % 4 * block + first, count, 16)
        return v_gate_up.at[rows, at((column + slot // 4) * WIDE_COLS, WIDE_COLS)]

    def out_near(slot, yy):
        return cell(0, slot * 2 + yy)

    def own_near(slot, yy):
        return cell(1, slot * 2 + yy)

    def in_near(slot, yy):
        return cell(2, slot * 2 + yy)

    def gain_copy(i):
        to_place, to_z = others[i - 1]
        return remote(
            gain_out.at[to_place * 4 + to_z], gain_in.at[i], gain_send.at[i], gain_recv.at[i],
            {"ctx": to_place, "fsdp": to_z},
        )

    def near_copy(j):
        slot = j % NEAR
        return remote(
            cell(0, slot * 2, 0, 2 * block), cell(2, slot * 2, 0, 2 * block),
            near_send.at[slot], near_recv.at[slot], k_mate,
        )

    def mid_copy(kind, j):
        slot = j % MID
        return remote(
            cell(3, slot, 0, used[kind]), cell(4, slot, 0, used[kind]),
            mid_send.at[slot], mid_recv.at[slot], y_mate,
        )

    def line_rows(kind, here, rightward):
        part = parts[kind]
        if rightward:
            start = (part * (here + 1)) // 16 * 16
            return start, used[kind] - start
        return 0, (part * here + 15) // 16 * 16

    def line_copy(kind, j, here, rightward):
        start, count = line_rows(kind, here, rightward)
        lane, slot = (0 if rightward else 1), j % NEAR
        return remote(
            cell(8, lane * NEAR + slot, start, count), cell(9 if rightward else 11, j % FAR, start, count),
            (right_send if rightward else left_send).at[slot],
            (right_recv if rightward else left_recv).at[j % FAR],
            right if rightward else left,
        )

    def out_copy(kind, j, first):
        slot = j % NEAR
        if kind == 0:
            return pltpu.make_async_copy(
                down_out.at[slot], o_down.at[:, at(j * DOWN_COLS, DOWN_COLS)], out_sem.at[slot]
            )
        out = {n_down: o_gate_up, end_both: o_qkv, end_mixed: o_out}[first]
        return pltpu.make_async_copy(
            wide_out.at[slot], out.at[:, at((j - first) * WIDE_COLS, WIDE_COLS)], out_sem.at[slot]
        )

    def out_wait(kind, slot):
        src, dst = (wide_out, o_out.at[:, 0:WIDE_COLS]) if kind else (down_out, o_down.at[:, 0:DOWN_COLS])
        pltpu.make_async_copy(src.at[slot], dst, out_sem.at[slot]).wait()

    def open_buffers():
        pl.semaphore_signal(near_free, inc=NEAR, device_id=k_mate, device_id_type=MESH)
        pl.semaphore_signal(mid_free, inc=MID, device_id=y_mate, device_id_type=MESH)

        @pl.when(z > 0)
        def _():
            pl.semaphore_signal(right_free, inc=FAR, device_id=left, device_id_type=MESH)

        @pl.when(z < last)
        def _():
            pl.semaphore_signal(left_free, inc=FAR, device_id=right, device_id_type=MESH)

    def when(condition):
        if isinstance(condition, bool):
            return (lambda work: work()) if condition else (lambda work: None)
        return pl.when(condition)

    def inside(j, first, end):
        if isinstance(j, int):
            return first <= j < end
        return (j >= first) & (j < end)

    def typed(j, work):
        @when(inside(j, 0, n_down))
        def _():
            work(0)

        @when(inside(j, n_down, total))
        def _():
            work(1)

    def multiply_down(j):
        rhs = s_grad[at(j * DOWN_COLS, DOWN_COLS), :]
        rows, piece = FF // 4, parts[0]
        for yy in range(2):
            for mine in (False, True):
                kk = k if mine else 1 - k
                lhs = v_down[at((yy * 2 + kk) * rows, rows), 0:both_toks]
                value = dot(lhs, rhs, 1, 1).astype(LOW)
                out = (own_near if mine else out_near)(j % NEAR, yy)
                for zz in range(4):
                    for t in range(3):
                        start = (zz * 3 + t) * piece
                        out[zz * piece : (zz + 1) * piece, t * 128 : (t + 1) * 128] = value[start : start + piece]

    def multiply_wide(j, lhs, rhs, first):
        right_rows = rhs[at((j - first) * WIDE_COLS, WIDE_COLS), :]
        for yy in range(2):
            for mine in (False, True):
                kk = k if mine else 1 - k
                value = dot(lhs[at((yy * 2 + kk) * block, block, 16), :], right_rows, 1, 1)
                (own_near if mine else out_near)(j % NEAR, yy)[...] = value.astype(LOW)

    def stage_near(j):
        for first, load in ((0, 0), (n_down, 3), (end_both, 1), (end_mixed, 2)):
            @when(inside(j, first, first + 1))
            def _(load=load):
                left_loads[load].wait()

        @when(inside(j, NEAR, total))
        def _():
            near_copy(j - NEAR).wait_send()

        @when(inside(j, 0, n_down))
        def _():
            multiply_down(j)

        @when(inside(j, n_down, end_both))
        def _():
            multiply_wide(j, second_t, s_both, n_down)

        @when(inside(j, end_both, end_mixed))
        def _():
            multiply_wide(j, normed_t, s_mixed, end_both)

        @when(inside(j, end_mixed, total))
        def _():
            multiply_wide(j, context_t, s_hidden, end_mixed)

        @when(inside(j, 0, total))
        def _():
            pl.semaphore_wait(near_free, 1)
            near_copy(j).start()

    def stage_mid(j):
        @when(inside(j, MID, total))
        def _():
            typed(j - MID, lambda kind: mid_copy(kind, j - MID).wait_send())

        @when(inside(j, 0, total))
        def _():
            near_copy(j).wait_recv()
            slot = j % NEAR
            for yy in range(2):
                value = (own_near(slot, yy)[...].astype(F32) + in_near(slot, yy)[...].astype(F32)).astype(LOW)

                @pl.when(y == yy)
                def _(value=value):
                    cell(5, j % SUMS)[...] = value

                @pl.when(y != yy)
                def _(value=value):
                    cell(3, j % MID)[...] = value

            pl.semaphore_wait(mid_free, 1)

        @when(inside(j, 0, total - NEAR))
        def _():
            pl.semaphore_signal(near_free, inc=1, device_id=k_mate, device_id_type=MESH)

        typed(j, lambda kind: mid_copy(kind, j).start())

    def stage_sum(j):
        typed(j, lambda kind: mid_copy(kind, j).wait_recv())

        @when(inside(j, 0, total))
        def _():
            sums = cell(5, j % SUMS)
            sums[...] = (sums[...].astype(F32) + cell(4, j % MID)[...].astype(F32)).astype(LOW)

        @when(inside(j, 0, total - MID))
        def _():
            pl.semaphore_signal(mid_free, inc=1, device_id=y_mate, device_id_type=MESH)

    def stage_line(i, rightward):
        free = right_free if rightward else left_free
        for here in range(4):
            step = here if rightward else 3 - here
            j = i - first_z - hop * step
            if step == 3 or (isinstance(j, int) and not 0 <= j < total):
                continue

            def device(here=here, step=step, j=j):
                @when(inside(j, NEAR, total))
                def _():
                    typed(j - NEAR, lambda kind: line_copy(kind, j - NEAR, here, rightward).wait_send())

                def work(kind):
                    start, count = line_rows(kind, here, rightward)
                    value = cell(5, j % SUMS, start, count)[...].astype(F32)
                    if step > 0:
                        line_copy(kind, j, here - 1 if rightward else here + 1, rightward).wait_recv()
                        came = cell(9 if rightward else 11, j % FAR, start, count)
                        value = value + came[...].astype(F32)
                    cell(8, (0 if rightward else NEAR) + j % NEAR, start, count)[...] = value.astype(LOW)

                typed(j, work)
                pl.semaphore_wait(free, 1)
                typed(j, lambda kind: line_copy(kind, j, here, rightward).start())

            @pl.when(z == here)
            def _(device=device, j=j):
                when(inside(j, 0, total))(device)

    def store(kind, j, value):
        if kind == 0:
            @when(inside(j, NEAR, total))
            def _():
                out_wait(0, j % NEAR)

            piece = parts[0]
            for t in range(3):
                down_out[j % NEAR, t * piece : (t + 1) * piece, :] = value[:, t * 128 : (t + 1) * 128]
            out_copy(0, j, 0).start()
            return
        typed(j - NEAR, lambda old: out_wait(old, j % NEAR))
        wide_out[j % NEAR] = value
        for first, end in ((n_down, end_both), (end_both, end_mixed), (end_mixed, total)):
            @when(inside(j, first, end))
            def _(first=first):
                out_copy(1, j, first).start()

    def stage_final(j):
        if isinstance(j, int) and not 0 <= j < total:
            return

        def device(here):
            def work(kind):
                part = parts[kind]
                if here == 3:
                    line_copy(kind, j, 2, True).wait_recv()
                if here == 0:
                    line_copy(kind, j, 1, False).wait_recv()
                low_at = here * part // 16 * 16
                count = (here * part + part + 15) // 16 * 16 - low_at
                value = cell(5, j % SUMS, low_at, count)[...].astype(F32)
                if here > 0:
                    value = value + cell(9, j % FAR, low_at, count)[...].astype(F32)
                if here < 3:
                    value = value + cell(11, j % FAR, low_at, count)[...].astype(F32)
                shift = here * part - low_at
                store(kind, j, value[shift : shift + part])

            typed(j, work)

            @when(inside(j, 0, total - FAR))
            def _():
                if here > 0:
                    pl.semaphore_signal(right_free, inc=1, device_id=left, device_id_type=MESH)
                if here < 3:
                    pl.semaphore_signal(left_free, inc=1, device_id=right, device_id_type=MESH)

        for here in range(4):
            @pl.when(z == here)
            def _(here=here):
                when(inside(j, 0, total))(lambda: device(here))

    def reduce_step(i):
        stage_near(i)
        stage_mid(i - 1)
        stage_sum(i - 4)
        stage_line(i, True)
        stage_line(i, False)
        stage_final(i - final_lag)

    def reduce_steps(final, first, end):
        @pl.when(final & (section == 0))
        def _():
            for i in range(first, end):
                reduce_step(i)

    def norm_back(grad, source, gain, row):
        scale = column_scale(source)
        unit = source * scale
        folded = jnp.sum(grad * unit, axis=1, keepdims=True)
        s_gains[:, row : row + 1] = s_gains[:, row : row + 1] + folded
        inner = grad * gain
        return scale * (inner - unit * jnp.mean(inner * unit, axis=0, keepdims=True))

    def rotated_back(front, back):
        cos, sin = cosine[...], sine[...]
        return jnp.concatenate([front * cos + back * sin, back * cos - front * sin], axis=0)

    def finish_micro(m):
        own = at(m * toks, toks)

        @pl.when(place == 0)
        def _():
            kv_copy(m, 0, 0, 0, 0).wait_recv()
            kv_copy(m, 0, 1, 0, 0).wait_recv()
            s_dkv[...] = s_dkv[...] + kv_in[m, 0].astype(F32) + kv_in[m, 1].astype(F32)

        @pl.when((place == 1) | (place == 2))
        def _():
            kv_copy(m, 0, 0, 0, 0).wait_recv()
            s_dkv[...] = s_dkv[...] + kv_in[m, 0].astype(F32)

        for head in range(KV_HEADS):
            front = s_dkv[head * HEAD : head * HEAD + HALF, :]
            back = s_dkv[head * HEAD + HALF : (head + 1) * HEAD, :]
            s_mixed[D + head * HEAD : D + (head + 1) * HEAD, own] = rotated_back(front, back).astype(LOW)
        s_mixed[D + KVW : qkv, own] = s_dkv[KVW : 2 * KVW, :].astype(LOW)

        def rest_tile(i, carry):
            rows = at(i * TILE, TILE)
            s_sum[rows, :] = s_sum[rows, :] + dot(v_joint[rows, D:qkv], s_mixed[D:qkv, own], 1, 0)
            return carry

        lax.fori_loop(0, D // TILE, rest_tile, 0)
        loads(m)[5].wait()
        g_now[...] = g_now[...] + norm_back(s_sum[...], s_x[...].astype(F32), columns[:, 0:1], 0)

        @pl.when(section == 1)
        def _():
            g_in[m] = g_now[...].astype(LOW)
            g_copy(m).start()

        @pl.when(m + 1 < micros)
        def _():
            for load in loads(m + 1):
                load.start()

        @pl.when(section == 0)
        def _():
            copies = result_saves(m)
            for i, save in enumerate(copies):
                if i > 1:
                    copies[i - 2].wait()
                s_dq[0:toks, i % 2 * TILE : (i % 2 + 1) * TILE] = g_now[i * TILE : (i + 1) * TILE, :].T
                save.start()

    def micro(m, carry):
        @pl.when(m > 0)
        def _():
            @pl.when(section == 0)
            def _():
                for save in result_saves(m - 1)[-2:]:
                    save.wait()

        @pl.when(m > 0)
        def _():
            for who, copy in kv_sends(m - 1):
                @pl.when(place == who)
                def _(copy=copy):
                    copy.wait_send()

        fill_bias(bias, segments, m, place, toks)
        own = at(m * toks, toks)
        final = m == micros - 1

        @pl.when(section == 1)
        def _():
            s_grad[:, own] = ends[m].astype(F32).T.astype(LOW)

        @pl.when(section == 0)
        def _():
            g_copy(m).wait_recv()
            s_grad[:, own] = g_in[m]

        @pl.when(m == 0)
        def _():
            w_loads[2].wait()

        now = loads(m)

        def inner_tile(i, carry):
            rows, up_rows = at(i * TILE, TILE), at(FF + i * TILE, TILE)
            for load in gu_loads(m, i):
                load.wait()

            grad_inner = dot(v_down[rows, :], s_grad[:, own], 1, 0)
            gate, up = s_gu[i % AHEAD, 0].astype(F32), s_gu[i % AHEAD, 1].astype(F32)
            sig = jax.nn.sigmoid(gate)
            s_both[rows, own] = (grad_inner * up * sig * (1.0 + gate * (1.0 - sig))).astype(LOW)
            s_both[up_rows, own] = (grad_inner * (gate * sig)).astype(LOW)

            @pl.when(i + AHEAD < tiles)
            def _():
                for load in gu_loads(m, i + AHEAD):
                    load.start()

            return carry

        lax.fori_loop(0, tiles, inner_tile, 0)

        @pl.when(final)
        def _():
            left_loads[0].start()
            left_loads[1].start()

        @pl.when(m == 0)
        def _():
            w_loads[1].wait()

        @pl.when(m + 1 < micros)
        def _():
            for i in range(AHEAD):
                for load in gu_loads(m + 1, i):
                    load.start()

        def second_tile(i, carry):
            rows = at(i * TILE, TILE)
            s_sum[rows, :] = dot(v_gate_up[rows, :], s_both[:, own], 1, 0)
            return carry

        lax.fori_loop(0, D // TILE, second_tile, 0)

        @pl.when(final)
        def _():
            left_loads[2].start()
            left_loads[3].start()
            open_buffers()

        now[0].wait()
        g_now[...] = s_grad[:, own].astype(F32) + norm_back(s_sum[...], s_hid[...], columns[:, 1:2], 1)
        s_hidden[:, own] = g_now[...].astype(LOW)

        @pl.when(m == 0)
        def _():
            w_loads[0].wait()

        for i in (1, 2, 3, 4):
            now[i].wait()
        reduce_steps(final, 0, 1)

        def context_tile(i, carry):
            block = dot(v_joint[at(i * TILE, TILE), qkv:], s_hidden[:, own], 1, 0).astype(LOW)
            for head in range(TILE // HEAD):
                kv_at = i * (TILE // HEAD // GROUP) + head // GROUP
                g = head % GROUP
                part = block[head * HEAD : (head + 1) * HEAD]
                s_context[at(kv_at * HEAD, HEAD, 64), g * toks : (g + 1) * toks] = part
                seen = s_att[at(i * TILE + head * HEAD, HEAD, 64), :]
                s_delta[pl.ds(kv_at, 1), g * toks : (g + 1) * toks] = jnp.sum(
                    part.astype(F32) * seen, axis=0, keepdims=True
                )
            return carry

        lax.fori_loop(0, D // TILE, context_tile, 0)
        sends = kv_sends(m)

        reduce_steps(final, 1, 2)

        @pl.when(place == 2)
        def _():
            block_grads(1, m, True)
            kv_out[0] = s_dkv[...].astype(LOW)
            sends[1][1].start()

        @pl.when(place == 3)
        def _():
            block_grads(2, m, True)
            kv_copy(m, 0, 0, 0, 3).wait_recv()
            kv_out[1] = (s_dkv[...] + kv_in[m, 0].astype(F32)).astype(LOW)
            sends[4][1].start()

        reduce_steps(final, 2, 3)

        @pl.when(place == 1)
        def _():
            block_grads(1, m, True)
            kv_out[0] = s_dkv[...].astype(LOW)
            sends[0][1].start()

        @pl.when(place == 2)
        def _():
            block_grads(2, m, False)
            kv_out[1] = s_dkv[...].astype(LOW)
            sends[2][1].start()

        @pl.when(place == 3)
        def _():
            block_grads(1, m, False)
            kv_out[0] = s_dkv[...].astype(LOW)
            sends[3][1].start()

        reduce_steps(final, 3, 4)

        @pl.when(place == 0)
        def _():
            block_grads(0, m, True)

        @pl.when(place > 0)
        def _():
            block_grads(0, m, False)

        reduce_steps(final, 4, 5)
        def query_back(kv_at, carry):
            for g in range(GROUP):
                lanes = slice(g * toks, (g + 1) * toks)
                front = s_dq[at(kv_at * HEAD, HALF, 32), lanes] * SCALE
                back = s_dq[at(kv_at * HEAD + HALF, HALF, 32), lanes] * SCALE
                rows = at((kv_at * GROUP + g) * HEAD, HEAD, 64)
                s_mixed[rows, own] = rotated_back(front, back).astype(LOW)
            return carry

        lax.fori_loop(0, KV_HEADS, query_back, 0)

        def normed_tile(i, carry):
            rows = at(i * TILE, TILE)
            s_sum[rows, :] = dot(v_joint[rows, :D], s_mixed[:D, own], 1, 0)
            return carry

        lax.fori_loop(0, D // TILE, normed_tile, 0)
        reduce_steps(final, 5, EMBEDDED)

        @pl.when((section == 1) | (m + 1 < micros))
        def _():
            finish_micro(m)

        return carry

    lax.fori_loop(0, micros, micro, 0)
    def reduce_loop(i, carry):
        reduce_step(i)
        return carry

    @pl.when(section == 0)
    def _():
        lax.fori_loop(EMBEDDED, DEFERRED, reduce_loop, 0)
        finish_micro(micros - 1)

    rows = jnp.concatenate([s_gains[...], jnp.zeros((D, 126), F32)], axis=1).T[0:8]
    for owner in range(OWNERS):
        shift = (D - owner * (D // OWNERS)) % D
        gain_out[owner] = (pltpu.roll(rows, shift, 1) if shift else rows)[:, :128]
    for i in range(1, OWNERS):
        gain_copy(i).start()

    lax.fori_loop(jnp.where(section == 0, DEFERRED, 0), total + final_lag, reduce_loop, 0)
    gain = gain_out[place * 4 + z]
    for i in range(1, OWNERS):
        gain_copy(i).wait()
        gain = gain + gain_in[i]
    o_gain[...] = gain

    @pl.when(section == 0)
    def _():
        for save in result_saves(micros - 1)[-2:]:
            save.wait()

    for m in range(2):
        @pl.when(section == 1)
        def _(m=m):
            g_copy(m).wait_send()

    for who, copy in kv_sends(micros - 1):
        @pl.when(place == who)
        def _(copy=copy):
            copy.wait_send()

    for j in range(total - NEAR, total):
        near_copy(j).wait_send()
        for at_z in range(3):
            @pl.when(z == at_z)
            def _(at_z=at_z, j=j):
                line_copy(1, j, at_z, True).wait_send()

            @pl.when(z == at_z + 1)
            def _(at_z=at_z, j=j):
                line_copy(1, j, at_z + 1, False).wait_send()
    for j in range(total - MID, total):
        mid_copy(1, j).wait_send()
    for j in range(total - NEAR, total):
        out_wait(1, j % NEAR)


def run_forward(ends, gains, cosine, sine, seg_own, w_qkv, w_out, w_gate_up, w_down):
    micros, toks = ends.shape[0], ends.shape[1]
    width = GROUP * toks
    vm, hbm = pl.BlockSpec(memory_space=pltpu.VMEM), pl.BlockSpec(memory_space=pl.ANY)
    sem = pltpu.SemaphoreType.DMA
    joint = w_qkv.shape[1] + w_out.shape[1]
    outs = [
        ((D, joint), LOW), ((D, 2 * FF), LOW), ((FF, D), LOW), ((4, micros, toks), jnp.int32),
        ((D, micros * toks), LOW), ((D, micros * toks), LOW), ((D, micros * toks), LOW),
        ((FF, micros * toks), LOW), ((micros, D, toks), LOW), ((micros, KVW, width), LOW),
        ((micros, 3, 2 * KVW, toks), LOW), ((micros, D, toks), F32), ((micros, 8, width), F32),
        ((micros, D, toks), F32), ((micros, 2 * FF, toks), LOW), ((micros, toks, D), F32),
    ]
    scratch = [
        ((joint, D), LOW), ((2 * FF, D), LOW), ((D, FF), LOW), ((2, D, SLAB), LOW), (w_down.shape, LOW),
        ((micros, D, toks), LOW), ((D, toks), F32),
        ((D, toks), LOW), ((D, toks), LOW), ((D, toks), LOW), ((FF, toks), LOW), ((D, toks), LOW),
        ((KVW, width), LOW), ((micros, 3, 2 * KVW, toks), LOW), ((D, toks), F32), ((8, width), F32),
        ((8, width), F32), ((D, toks), F32), ((2 * FF, toks), LOW), ((toks, D), F32), ((3, toks, toks), F32),
        ((4, micros, toks), jnp.int32), ((D, 2), F32),
    ]
    return pl.pallas_call(
        forward_kernel,
        out_shape=tuple(jax.ShapeDtypeStruct(s, t) for s, t in outs),
        in_specs=[vm] * 5 + [hbm] * 4,
        out_specs=(hbm,) * len(outs),
        scratch_shapes=[pltpu.VMEM(s, t) for s, t in scratch]
        + [sem((3,)), sem((2, 4)), sem((12,)), sem((micros, 2)), sem((micros, 3)), sem((micros, 3)), sem((micros, 3))]
        + [sem((2, 4)), sem((CHUNKS,))] + [sem((4, CHUNKS))] * 8,
        compiler_params=pltpu.CompilerParams(
            collective_id=3, has_side_effects=True, vmem_limit_bytes=62 * 2**20
        ),
        name="layer_forward",
    )(ends, gains, cosine, sine, seg_own, w_qkv, w_out, w_gate_up, w_down)


def run_backward(ends, gains, cosine, sine, segments, joint, gate_up, down, saved):
    micros, toks = ends.shape[0], ends.shape[1]
    width = GROUP * toks
    vm, hbm = pl.BlockSpec(memory_space=pltpu.VMEM), pl.BlockSpec(memory_space=pl.ANY)
    sem, plain = pltpu.SemaphoreType.DMA, pltpu.SemaphoreType.REGULAR
    qkv = D + 2 * KVW
    outs = [
        (micros, toks, D), (FF // OWNERS, D), (D // OWNERS, 2 * FF), (D // OWNERS, qkv), (D // OWNERS, D),
        (8, 128),
    ]
    scratch = [
        (joint.shape, LOW), (gate_up.shape, LOW), (down.shape, LOW),
        ((micros, D, toks), LOW), ((D, toks), F32),
        ((D, toks), LOW), ((KVW, width), LOW), ((3, 2 * KVW, toks), LOW), ((D, toks), F32), ((8, width), F32),
        ((D, toks), F32), ((AHEAD, 2, TILE, toks), LOW),
        ((2 * FF, micros * toks), LOW), ((qkv, micros * toks), LOW), ((D, micros * toks), LOW),
        ((D, micros * toks), LOW), ((D, toks), F32),
        ((KVW, width), LOW), ((8, width), F32), ((KVW, width), F32), ((2 * KVW, toks), F32),
        ((2, 2 * KVW, toks), LOW), ((micros, 2, 2 * KVW, toks), LOW),
        ((D, 2), F32), ((3, toks, toks), F32), ((D, 2), F32),
        ((NEAR, D // OWNERS, WIDE_COLS), F32), ((NEAR, FF // OWNERS, DOWN_COLS), F32),
        ((OWNERS, 8, 128), F32), ((OWNERS, 8, 128), F32),
    ]
    return pl.pallas_call(
        backward_kernel,
        out_shape=tuple(jax.ShapeDtypeStruct(s, F32) for s in outs),
        in_specs=[vm] * 5 + [hbm] * 15,
        out_specs=(hbm,) * 5 + (vm,),
        scratch_shapes=[pltpu.VMEM(s, t) for s, t in scratch]
        + [sem((3,)), sem((6,)), sem((AHEAD, 2)), sem((3,)), sem((micros, 2)), sem((micros, 2)), sem((micros,)), sem((micros,))]
        + [sem((4,)), sem((NEAR,)), sem((NEAR,)), sem((MID,)), sem((MID,)), sem((NEAR,)), sem((FAR,)), sem((NEAR,)), sem((FAR,))]
        + [sem((NEAR,)), sem((OWNERS,)), sem((OWNERS,)), plain, plain, plain, plain],
        compiler_params=pltpu.CompilerParams(
            collective_id=4, has_side_effects=True, vmem_limit_bytes=63 * 2**20
        ),
        input_output_aliases={15: 0},
        name="layer_backward",
    )(ends, gains, cosine, sine, segments, joint, gate_up, down, *saved)


def small_mesh():
    return lax.axis_size("ctx") == 4 and lax.axis_size("fsdp") == 4


def whole_weights(w_qkv, w_out, w_gate_up, w_down):
    return tuple(
        lax.all_gather(w, "fsdp", axis=0, tiled=True) for w in (w_qkv, w_out, w_gate_up, w_down)
    )


def owned_grads(lefts, rights):
    return tuple(
        lax.psum_scatter(
            outer_product(left, right).astype(jnp.bfloat16),
            ("ctx", "fsdp"),
            scatter_dimension=0,
            tiled=True,
        ).astype(jnp.float32)
        for left, right in zip(lefts, rights)
    )


def local_small(ends, segment_ids, w_qkv, w_out, w_gate_up, w_down, gains):
    tok_rows = ends.shape[3]
    local_ends = ends[0, :, 0]
    seg_local = segment_ids[:, 0]
    query_pos = lax.axis_index("ctx") * tok_rows + jnp.arange(tok_rows, dtype=jnp.int32)
    frequency = 10000.0 ** (-(jnp.arange(HEAD // 2).astype(jnp.float32) * 2.0 / HEAD))
    angle_table = frequency[:, None] * query_pos.astype(jnp.float32)[None, :]
    shared = (local_ends, gains[0], jnp.cos(angle_table), jnp.sin(angle_table))
    joint, gate_up, down, segments, normed, context, second, inner, *saved, result = run_forward(
        *shared, seg_local, w_qkv[0], w_out[0], w_gate_up[0], w_down[0]
    )
    ends_rows, g_down, g_gate_up, g_qkv, g_out, gain = run_backward(
        *shared, segments, joint, gate_up, down, (*saved, result, normed, context, second, inner)
    )
    return (
        ends_rows[None, :, None], g_qkv[None], g_out[None], g_gate_up[None], g_down[None],
        gain[None, :2, : D // 16],
    )


def local(ends, segment_ids, w_qkv, w_out, w_gate_up, w_down, gains):
    if small_mesh():
        return local_small(ends, segment_ids, w_qkv, w_out, w_gate_up, w_down, gains)
    section_index = lax.axis_index("section")
    micro_count = ends.shape[1]
    tok_rows = ends.shape[3]
    local_ends = ends[0, :, 0]
    seg_local = segment_ids[:, 0]
    seg_whole = lax.all_gather(seg_local, "ctx", axis=1, tiled=True)
    query_pos = lax.axis_index("ctx") * tok_rows + jnp.arange(tok_rows, dtype=jnp.int32)
    frequency = 10000.0 ** (-(jnp.arange(HEAD // 2).astype(jnp.float32) * 2.0 / HEAD))
    angle_table = query_pos.astype(jnp.float32)[:, None] * frequency[None, :]
    cosine = jnp.cos(angle_table)[:, None, :]
    sine_table = jnp.sin(angle_table)[:, None, :]
    gain_pair = gains[0]
    weights = whole_weights(w_qkv[0], w_out[0], w_gate_up[0], w_down[0])
    arrived = jnp.zeros((tok_rows, D), jnp.bfloat16)
    store_bufs = None
    outputs = jnp.zeros((micro_count + 1, tok_rows, D), jnp.float32)
    for tick_num in range(micro_count + 1):
        batch_index = tick_num - section_index
        is_valid = (batch_index >= 0) & (batch_index < micro_count)
        clipped = jnp.clip(batch_index, 0, micro_count - 1)
        slot_index = jnp.where(is_valid, batch_index, micro_count)
        own_rows = lax.dynamic_index_in_dim(local_ends, clipped, 0, keepdims=False)
        layer_in = jnp.where(section_index == 0, own_rows, arrived)
        seg_rows = lax.dynamic_index_in_dim(seg_local, clipped, 0, keepdims=False)
        seg_full = lax.dynamic_index_in_dim(seg_whole, clipped, 0, keepdims=False)
        result, saved_acts = layer_forward(
            layer_in.astype(jnp.float32),
            weights,
            gain_pair,
            seg_rows,
            seg_full,
            query_pos,
            cosine,
            sine_table,
        )
        if tick_num == 0:
            store_bufs = jax.tree.map(
                lambda update: jnp.zeros((micro_count + 1,) + update.shape, update.dtype),
                saved_acts,
            )
        store_bufs = jax.tree.map(
            lambda buffer, update: lax.dynamic_update_index_in_dim(buffer, update, slot_index, 0),
            store_bufs,
            saved_acts,
        )
        outputs = lax.dynamic_update_index_in_dim(outputs, result, slot_index, 0)
        arrived = shifted(result.astype(jnp.bfloat16), "section", 1)
    operand_bufs = None
    gain_sums = jnp.zeros((2, D), jnp.float32)
    arrived_grad = jnp.zeros((tok_rows, D), jnp.bfloat16)
    input_grads = jnp.zeros((micro_count + 1, tok_rows, D), jnp.float32)
    for tick_num in range(micro_count + 1):
        batch_index = tick_num - (1 - section_index)
        is_valid = (batch_index >= 0) & (batch_index < micro_count)
        clipped = jnp.clip(batch_index, 0, micro_count - 1)
        slot_index = jnp.where(is_valid, batch_index, micro_count)
        own_rows = lax.dynamic_index_in_dim(local_ends, clipped, 0, keepdims=False)
        incoming = jnp.where(section_index == 1, own_rows, arrived_grad)
        incoming = jnp.where(is_valid, incoming, jnp.zeros_like(incoming))
        seg_rows = lax.dynamic_index_in_dim(seg_local, clipped, 0, keepdims=False)
        seg_full = lax.dynamic_index_in_dim(seg_whole, clipped, 0, keepdims=False)
        saved_acts = jax.tree.map(
            lambda buffer: lax.dynamic_index_in_dim(buffer, clipped, 0, keepdims=False), store_bufs
        )
        grad_input, operand_pairs, gain_terms = layer_backward(
            incoming,
            saved_acts,
            weights,
            gain_pair,
            seg_rows,
            seg_full,
            query_pos,
            cosine,
            sine_table,
        )
        if tick_num == 0:
            operand_bufs = jax.tree.map(
                lambda update: jnp.zeros((micro_count + 1,) + update.shape, update.dtype),
                operand_pairs,
            )
        operand_bufs = jax.tree.map(
            lambda buffer, update: lax.dynamic_update_index_in_dim(buffer, update, slot_index, 0),
            operand_bufs,
            operand_pairs,
        )
        gain_sums = gain_sums + gain_terms
        input_grads = lax.dynamic_update_index_in_dim(input_grads, grad_input, slot_index, 0)
        arrived_grad = shifted(grad_input.astype(jnp.bfloat16), "section", -1)
    operands = [buffer[:micro_count].reshape(-1, buffer.shape[-1]) for buffer in operand_bufs]
    g_qkv, g_out, g_gate_up, g_down = owned_grads(operands[:4], operands[4:])
    g_gains = lax.psum_scatter(gain_sums, ("ctx", "fsdp"), scatter_dimension=1, tiled=True)
    final_rows = jnp.where(section_index == 0, input_grads[:micro_count], outputs[:micro_count])
    ends_out = final_rows[None, :, None]
    return (ends_out, g_qkv[None], g_out[None], g_gate_up[None], g_down[None], g_gains[None])


def solution(mesh):
    in_specs = (
        P("section", None, "fsdp", "ctx", None),
        P(None, "fsdp", "ctx"),
        P("section", "fsdp", None),
        P("section", "fsdp", None),
        P("section", "fsdp", None),
        P("section", "fsdp", None),
        P("section", None, None),
    )
    out_specs = (
        P("section", None, "fsdp", "ctx", None),
        P("section", ("ctx", "fsdp"), None),
        P("section", ("ctx", "fsdp"), None),
        P("section", ("ctx", "fsdp"), None),
        P("section", ("ctx", "fsdp"), None),
        P("section", None, ("ctx", "fsdp")),
    )
    return jax.shard_map(local, mesh=mesh, in_specs=in_specs, out_specs=out_specs, check_vma=False)
```

```python
import math

import jax
import jax.numpy as jnp
from jax import lax
from jax.experimental import pallas as pl
from jax.experimental.pallas import tpu as pltpu
from jax.sharding import PartitionSpec as P

MESH = pl.DeviceIdType.MESH

D = 1152
HEADS = 18
KV_HEADS = 6
HEAD = 64
FF = 3072
KVW = 384


EPS = 1e-05


def shifted(x, axis, by):
    size = lax.axis_size(axis)
    pairs = [(i, i + by) for i in range(size) if 0 <= i + by < size]
    return lax.ppermute(x, axis, pairs)


def rotate(values_in, cosine, sine_table):
    half_size = values_in.shape[-1] // 2
    front = values_in[..., :half_size]
    back_half = values_in[..., half_size:]
    return jnp.concatenate(
        [front * cosine - back_half * sine_table, back_half * cosine + front * sine_table], axis=-1
    )


def rotate_back(gradient, cosine, sine_table):
    half_size = gradient.shape[-1] // 2
    front = gradient[..., :half_size]
    back_half = gradient[..., half_size:]
    return jnp.concatenate(
        [front * cosine + back_half * sine_table, back_half * cosine - front * sine_table], axis=-1
    )


def norm_forward(inputs, gain_row):
    scale_row = lax.rsqrt(jnp.mean(inputs * inputs, axis=-1, keepdims=True) + EPS)
    unit_rows = inputs * scale_row
    return (unit_rows * gain_row, unit_rows, scale_row)


def norm_backward(gradient, unit_rows, scale_row, gain_row):
    unit_grad = gradient * gain_row
    gain_grad = jnp.sum(gradient * unit_rows, axis=0)
    input_grad = scale_row * (
        unit_grad - unit_rows * jnp.mean(unit_grad * unit_rows, axis=-1, keepdims=True)
    )
    return (input_grad, gain_grad)


def outer_product(left, right):
    return lax.dot_general(
        left, right, (((0,), (0,)), ((), ())), preferred_element_type=jnp.float32
    )


def times_transposed(left, right):
    return lax.dot_general(
        left, right, (((1,), (1,)), ((), ())), preferred_element_type=jnp.float32
    )


def block_needed(first_row, block_rows, seg_full, seg_rows, query_pos):
    last_seg = lax.dynamic_index_in_dim(seg_full, first_row + block_rows - 1, 0, keepdims=False)
    return (first_row <= query_pos[-1]) & (last_seg >= seg_rows[0])


def attend_forward(queries4, key_all, value_all, seg_rows, seg_full, query_pos):
    tok_rows = queries4.shape[0]
    group_size = HEADS // KV_HEADS
    score_scale = HEAD ** (-0.5)
    total_rows = key_all.shape[0]
    block_rows = math.gcd(total_rows, 512)
    block_count = total_rows // block_rows
    key_heads = key_all.reshape(total_rows, KV_HEADS, HEAD)
    value_heads = value_all.reshape(total_rows, KV_HEADS, HEAD)

    def block_scores(block_index):
        first_row = block_index * block_rows
        key_block = lax.dynamic_slice_in_dim(key_heads, first_row, block_rows, 0)
        value_block = lax.dynamic_slice_in_dim(value_heads, first_row, block_rows, 0)
        seg_block = lax.dynamic_slice_in_dim(seg_full, first_row, block_rows, 0)
        key_pos = first_row + jnp.arange(block_rows, dtype=jnp.int32)
        raw_scores = (
            jnp.einsum("qkgd,tkd->kgqt", queries4, key_block, preferred_element_type=jnp.float32)
            * score_scale
        )
        allowed = (key_pos[None, :] <= query_pos[:, None]) & (
            seg_block[None, :] == seg_rows[:, None]
        )
        return (jnp.where(allowed, raw_scores, -1e30), allowed, value_block)

    def first_pass(state_pair, block_index):

        def first_work(state_in):
            row_top, row_total = state_in
            masked, allowed, value_block = block_scores(block_index)
            new_top = jnp.maximum(row_top, jnp.max(masked, axis=-1))
            new_total = row_total * jnp.exp(row_top - new_top) + jnp.sum(
                jnp.exp(masked - new_top[..., None]), axis=-1
            )
            return (new_top, new_total)

        needed = block_needed(block_index * block_rows, block_rows, seg_full, seg_rows, query_pos)
        return (lax.cond(needed, first_work, lambda state_in: state_in, state_pair), None)

    start_state = (
        jnp.full((KV_HEADS, group_size, tok_rows), -1e30, jnp.float32),
        jnp.zeros((KV_HEADS, group_size, tok_rows), jnp.float32),
    )
    block_ids = jnp.arange(block_count, dtype=jnp.int32)
    (row_top, row_total), ignored = lax.scan(first_pass, start_state, block_ids)
    log_total = row_top + jnp.log(row_total)

    def second_pass(summed, block_index):

        def second_work(summed_in):
            masked, allowed, value_block = block_scores(block_index)
            prob_low = jnp.where(allowed, jnp.exp(masked - log_total[..., None]), 0.0).astype(
                jnp.bfloat16
            )
            added = jnp.einsum(
                "kgqt,tkd->qkgd", prob_low, value_block, preferred_element_type=jnp.float32
            )
            return summed_in + added

        needed = block_needed(block_index * block_rows, block_rows, seg_full, seg_rows, query_pos)
        return (lax.cond(needed, second_work, lambda summed_in: summed_in, summed), None)

    start_sum = jnp.zeros((tok_rows, KV_HEADS, group_size, HEAD), jnp.float32)
    attended, ignored = lax.scan(second_pass, start_sum, block_ids)
    return (attended.reshape(tok_rows, D), log_total)


def layer_forward(inputs, weights, gain_pair, seg_rows, seg_full, query_pos, cosine, sine_table):
    w_qkv, w_out, w_gate_up, w_down = weights
    tok_rows = inputs.shape[0]
    group_size = HEADS // KV_HEADS
    normed, unit_one, scale_one = norm_forward(inputs, gain_pair[0])
    normed_low = normed.astype(jnp.bfloat16)
    mixed_proj = jnp.dot(normed_low, w_qkv, preferred_element_type=jnp.float32)
    queries = rotate(mixed_proj[:, :D].reshape(tok_rows, HEADS, HEAD), cosine, sine_table).astype(
        jnp.bfloat16
    )
    key_rows = rotate(
        mixed_proj[:, D : D + KVW].reshape(tok_rows, KV_HEADS, HEAD), cosine, sine_table
    )
    key_rows = key_rows.astype(jnp.bfloat16).reshape(tok_rows, KVW)
    value_rows = mixed_proj[:, D + KVW :].astype(jnp.bfloat16)
    key_all, value_all = (
        lax.all_gather(key_rows, "ctx", axis=0, tiled=True),
        lax.all_gather(value_rows, "ctx", axis=0, tiled=True),
    )
    queries4 = queries.reshape(tok_rows, KV_HEADS, group_size, HEAD)
    attended, log_total = attend_forward(
        queries4, key_all, value_all, seg_rows, seg_full, query_pos
    )
    context = attended.astype(jnp.bfloat16)
    hidden = inputs + jnp.dot(context, w_out, preferred_element_type=jnp.float32)
    second, unit_two, scale_two = norm_forward(hidden, gain_pair[1])
    second_low = second.astype(jnp.bfloat16)
    gate_up = jnp.dot(second_low, w_gate_up, preferred_element_type=jnp.float32)
    gate_pre = gate_up[:, :FF]
    up_pre = gate_up[:, FF:]
    inner_act = (jax.nn.silu(gate_pre) * up_pre).astype(jnp.bfloat16)
    result = hidden + jnp.dot(inner_act, w_down, preferred_element_type=jnp.float32)
    saved_acts = (
        normed_low,
        queries4,
        key_all,
        value_all,
        attended,
        log_total,
        context,
        unit_one,
        scale_one,
        unit_two,
        scale_two,
        second_low,
        gate_pre,
        up_pre,
        inner_act,
    )
    return (result, saved_acts)


def layer_backward(
    grad_low, saved_acts, weights, gain_pair, seg_rows, seg_full, query_pos, cosine, sine_table
):
    w_qkv, w_out, w_gate_up, w_down = weights
    (
        normed_low,
        queries4,
        key_all,
        value_all,
        attended,
        log_total,
        context,
        unit_one,
        scale_one,
        unit_two,
        scale_two,
        second_low,
        gate_pre,
        up_pre,
        inner_act,
    ) = saved_acts
    tok_rows = grad_low.shape[0]
    group_size = HEADS // KV_HEADS
    score_scale = HEAD ** (-0.5)
    grad_out = grad_low.astype(jnp.float32)
    grad_inner = times_transposed(grad_low, w_down)
    sigmoid_gate = jax.nn.sigmoid(gate_pre)
    silu_gate = gate_pre * sigmoid_gate
    grad_gate = grad_inner * up_pre * sigmoid_gate * (1.0 + gate_pre * (1.0 - sigmoid_gate))
    grad_up = grad_inner * silu_gate
    grad_both = jnp.concatenate([grad_gate, grad_up], axis=1).astype(jnp.bfloat16)
    grad_second = times_transposed(grad_both, w_gate_up)
    grad_norm_two, gain_two = norm_backward(grad_second, unit_two, scale_two, gain_pair[1])
    grad_hidden = grad_out + grad_norm_two
    hidden_low = grad_hidden.astype(jnp.bfloat16)
    grad_context = times_transposed(hidden_low, w_out).astype(jnp.bfloat16)
    grad_context4 = grad_context.reshape(tok_rows, KV_HEADS, group_size, HEAD)
    attended4 = attended.reshape(tok_rows, KV_HEADS, group_size, HEAD)
    row_delta = jnp.einsum("qkgd,qkgd->kgq", grad_context4.astype(jnp.float32), attended4)
    total_rows = seg_full.shape[0]
    start_state = (
        jnp.zeros((tok_rows, KV_HEADS, group_size, HEAD), jnp.float32),
        jnp.zeros((total_rows, 2 * KVW), jnp.float32),
    )
    key_piece, value_piece = key_all, value_all
    piece_rows = key_piece.shape[0]
    block_rows = math.gcd(piece_rows, 512)
    block_count = piece_rows // block_rows

    def one_block(block_index, inner_state):
        offset = block_index * block_rows

        def one_work(state_in):
            grad_query, grad_kv = state_in
            key_block = lax.dynamic_slice_in_dim(key_piece, offset, block_rows, 0).reshape(
                block_rows, KV_HEADS, HEAD
            )
            value_block = lax.dynamic_slice_in_dim(value_piece, offset, block_rows, 0).reshape(
                block_rows, KV_HEADS, HEAD
            )
            seg_block = lax.dynamic_slice_in_dim(seg_full, offset, block_rows, 0)
            key_pos = offset + jnp.arange(block_rows, dtype=jnp.int32)
            raw_scores = (
                jnp.einsum(
                    "qkgd,tkd->kgqt", queries4, key_block, preferred_element_type=jnp.float32
                )
                * score_scale
            )
            allowed = (key_pos[None, :] <= query_pos[:, None]) & (
                seg_block[None, :] == seg_rows[:, None]
            )
            prob_full = jnp.where(allowed, jnp.exp(raw_scores - log_total[..., None]), 0.0)
            prob_low = prob_full.astype(jnp.bfloat16)
            grad_value = jnp.einsum(
                "kgqt,qkgd->tkd", prob_low, grad_context4, preferred_element_type=jnp.float32
            )
            grad_prob = jnp.einsum(
                "qkgd,tkd->kgqt", grad_context4, value_block, preferred_element_type=jnp.float32
            )
            grad_scores = (prob_full * (grad_prob - row_delta[..., None])).astype(jnp.bfloat16)
            grad_query = (
                grad_query
                + jnp.einsum(
                    "kgqt,tkd->qkgd", grad_scores, key_block, preferred_element_type=jnp.float32
                )
                * score_scale
            )
            grad_key = (
                jnp.einsum(
                    "kgqt,qkgd->tkd", grad_scores, queries4, preferred_element_type=jnp.float32
                )
                * score_scale
            )
            new_rows = jnp.concatenate(
                [grad_key.reshape(block_rows, KVW), grad_value.reshape(block_rows, KVW)], axis=1
            )
            old_rows = lax.dynamic_slice_in_dim(grad_kv, offset, block_rows, 0)
            grad_kv = lax.dynamic_update_slice_in_dim(grad_kv, old_rows + new_rows, offset, 0)
            return (grad_query, grad_kv)

        needed = block_needed(offset, block_rows, seg_full, seg_rows, query_pos)
        return lax.cond(needed, one_work, lambda state_in: state_in, inner_state)

    grad_query, grad_kv_all = lax.fori_loop(0, block_count, one_block, start_state)
    grad_kv_own = lax.psum_scatter(
        grad_kv_all.astype(jnp.bfloat16), "ctx", scatter_dimension=0, tiled=True
    ).astype(jnp.float32)
    grad_q_pre = rotate_back(grad_query.reshape(tok_rows, HEADS, HEAD), cosine, sine_table).reshape(
        tok_rows, D
    )
    grad_k_pre = rotate_back(
        grad_kv_own[:, :KVW].reshape(tok_rows, KV_HEADS, HEAD), cosine, sine_table
    ).reshape(tok_rows, KVW)
    grad_mixed = jnp.concatenate([grad_q_pre, grad_k_pre, grad_kv_own[:, KVW:]], axis=1).astype(
        jnp.bfloat16
    )
    grad_normed = times_transposed(grad_mixed, w_qkv)
    grad_norm_one, gain_one = norm_backward(grad_normed, unit_one, scale_one, gain_pair[0])
    grad_input = grad_hidden + grad_norm_one
    operand_pairs = (
        normed_low,
        context,
        second_low,
        inner_act,
        grad_mixed,
        hidden_low,
        grad_both,
        grad_low,
    )
    return (grad_input, operand_pairs, jnp.stack([gain_one, gain_two]))


DOWN_COLS = 128
WIDE_COLS = 384
NEAR, MID, FAR, SUMS = 2, 4, 8, 12
OWNERS = 16
EMBEDDED, DEFERRED = 6, 6
AHEAD = 4


F32, LOW = jnp.float32, jnp.bfloat16
GROUP = HEADS // KV_HEADS
HALF = HEAD // 2
SCALE = HEAD ** (-0.5)
NONE = -1e30
TILE = 384
WIDE = 512


def dot(left, right, left_dim, right_dim):
    return lax.dot_general(
        left, right, (((left_dim,), (right_dim,)), ((), ())), preferred_element_type=F32
    )


def at(start, size, step=128):
    return pl.ds(pl.multiple_of(start, step), size)


def column_scale(v):
    return lax.rsqrt(jnp.mean(v * v, axis=0, keepdims=True) + EPS)


def greet(peers):
    barrier = pltpu.get_barrier_semaphore()
    for peer in peers:
        pl.semaphore_signal(barrier, inc=1, device_id=peer, device_id_type=MESH)
    pl.semaphore_wait(barrier, len(peers))


def remote(src, dst, send, recv, peer):
    return pltpu.make_async_remote_copy(
        src_ref=src, dst_ref=dst, send_sem=send, recv_sem=recv, device_id=peer, device_id_type=MESH
    )


def fill_bias(bias, segments, m, place, toks):
    own = segments[place, pl.ds(m, 1), :]
    rows = lax.broadcasted_iota(jnp.int32, (toks, toks), 0)
    cols = lax.broadcasted_iota(jnp.int32, (toks, toks), 1)
    for d in range(3):
        seen = segments[jnp.maximum(place - d, 0), pl.ds(m, 1), :]
        keys = jnp.broadcast_to(seen, (8, toks)).T[:, 0:1]
        allowed = keys == own
        if d == 0:
            allowed = allowed & (rows <= cols)
        bias[d] = jnp.where(allowed, 0.0, NONE)


def gain_columns(gains, columns):
    for row in range(2):
        columns[:, row : row + 1] = jnp.broadcast_to(gains[row : row + 1, :], (8, D)).T[:, 0:1]


JOINT_CHUNKS, WIDE_CHUNKS, DOWN_CHUNKS = 3, 3, 4
CHUNKS = JOINT_CHUNKS + WIDE_CHUNKS + DOWN_CHUNKS
SLAB = 1024


def forward_kernel(
    ends, gains, cosine, sine, seg_own, w_qkv, w_out, w_gate_up, w_down,
    f_joint, f_gate_up, f_down, o_seg,
    o_normed, o_context, o_second, o_inner, o_x, o_q, o_kv, o_att, o_lse, o_hidden, o_gu, o_result,
    t_joint, t_gate_up, t_down, stage, stage_down, x_in, x_now, s_normed, s_context, s_second,
    s_inner, s_x, s_q, s_kv, s_att, s_top, s_lse, s_hidden, s_gu, s_result, bias, segments, columns,
    stage_sem, seg_sem, save_sem, kv_send, kv_recv, x_send, x_recv,
    own_sem, back_sem, zs, zr, ys, yr, cs, cr, es, er,
):
    section = lax.axis_index("section")
    place = lax.axis_index("ctx")
    z = lax.axis_index("fsdp")
    last = lax.axis_size("fsdp") - 1
    y, k = place // 2, place % 2
    y_mate = {"ctx": (1 - y) * 2 + k}
    k_mate = {"ctx": y * 2 + 1 - k}
    micros, toks = ends.shape[0], ends.shape[1]
    qkv = D + 2 * KVW
    width, deep = w_gate_up.shape[0], w_down.shape[0]
    half, joint_half, wide_half = width // 2, f_joint.shape[1] // 2, f_gate_up.shape[1] // 2

    barrier = pltpu.get_barrier_semaphore()
    for peer in [{"ctx": (place + i) % 4} for i in (1, 2, 3)] + [{"section": 1 - section}]:
        pl.semaphore_signal(barrier, inc=1, device_id=peer, device_id_type=MESH)

    @pl.when(z > 0)
    def _():
        pl.semaphore_signal(barrier, inc=1, device_id={"fsdp": z - 1}, device_id_type=MESH)

    @pl.when(z < last)
    def _():
        pl.semaphore_signal(barrier, inc=1, device_id={"fsdp": z + 1}, device_id_type=MESH)

    pl.semaphore_wait(barrier, 4 + jnp.where(z > 0, 1, 0) + jnp.where(z < last, 1, 0))

    def view(shard, yy, kk, j, own=False):
        if j < JOINT_CHUNKS:
            rows = half // JOINT_CHUNKS
            return f_joint.at[
                at(shard * width + yy * half + j * rows, rows, 16), at(kk * joint_half, joint_half)
            ]
        j = j - JOINT_CHUNKS
        if j < WIDE_CHUNKS:
            cols = wide_half // WIDE_CHUNKS
            ref, first = (w_gate_up, 0) if own else (f_gate_up, shard * width)
            return ref.at[at(first + yy * half, half, 16), at(kk * wide_half + j * cols, cols)]
        j = j - WIDE_CHUNKS
        rows = deep // 4 // DOWN_CHUNKS
        ref, first = (w_down, 0) if own else (f_down, shard * deep)
        return ref.at[at(first + (yy * 2 + kk) * (deep // 4) + j * rows, rows, 16), :]

    def z_copy(shard, j, to, own, back):
        ref = view(shard, y, k, j)
        src = view(shard, y, k, j, True) if own and j >= JOINT_CHUNKS else ref
        return remote(
            src, ref, back_sem.at[j] if back else zs.at[shard, j], zr.at[shard, j], {"fsdp": to}
        )

    def own_start(j, to, back):
        if j >= JOINT_CHUNKS:
            z_copy(z, j, to, True, back).start()
            return
        rows = half // JOINT_CHUNKS
        here = at(y * half + j * rows, rows, 16)
        there = at(z * width + y * half + j * rows, rows, 16)
        send, recv = back_sem.at[j] if back else zs.at[z, j], zr.at[z, j]

        @pl.when(k == 0)
        def _():
            remote(
                w_qkv.at[here, 0:joint_half], f_joint.at[there, 0:joint_half], send, recv, {"fsdp": to}
            ).start()

        @pl.when(k == 1)
        def _():
            remote(
                w_qkv.at[here, joint_half:qkv], f_joint.at[there, joint_half:qkv], send, recv, {"fsdp": to}
            ).start()
            remote(w_out.at[here, :], f_joint.at[there, qkv:], send, recv, {"fsdp": to}).start()

    def own_sends(j):
        @pl.when(z < last)
        def _():
            own_start(j, z + 1, False)

        @pl.when(z > 0)
        def _():
            own_start(j, z - 1, True)

    def mate_copy(shard, j, yy, mate, send, recv):
        ref = view(shard, yy, k, j)
        return remote(ref, ref, send.at[shard, j], recv.at[shard, j], mate)

    def arrive(shard, j, yy, kk, recv):
        ref = view(shard, yy, kk, j)
        remote(ref, ref, recv.at[shard, j], recv.at[shard, j], k_mate).wait_recv()

    rows_z, rows_deep = at(z * width, width, 16), at(z * deep, deep, 16)
    own_pairs = (
        (w_qkv, f_joint.at[rows_z, 0:qkv]), (w_out, f_joint.at[rows_z, qkv:]),
        (w_gate_up, f_gate_up.at[rows_z, :]), (w_down, f_down.at[rows_deep, :]),
    )
    own_copies = [
        remote(a, b, own_sem.at[0, i], own_sem.at[1, i], k_mate) for i, (a, b) in enumerate(own_pairs)
    ]

    def sides(d):
        return ((z - d >= 0, z - d, z + 1, z < last), (z + d <= last, z + d, z - 1, z > 0))

    def relay(d, j):
        for valid, shard, onward, more in sides(d):
            @pl.when(valid)
            def _(shard=shard, onward=onward, more=more):
                arrive(shard, j, y, k, zr)
                if d < 3:
                    @pl.when(more)
                    def _():
                        z_copy(shard, j, onward, False, False).start()
                mate_copy(shard, j, y, y_mate, ys, yr).start()
                mate_copy(shard, j, y, k_mate, cs, cr).start()

    def across(d, j):
        for valid, shard, onward, more in sides(d):
            @pl.when(valid)
            def _(shard=shard):
                arrive(shard, j, 1 - y, k, yr)
                mate_copy(shard, j, 1 - y, k_mate, es, er).start()

    def complete(d, j):
        for valid, shard, onward, more in sides(d):
            @pl.when(valid)
            def _(shard=shard):
                arrive(shard, j, y, 1 - k, cr)
                arrive(shard, j, 1 - y, 1 - k, er)

    first_down = JOINT_CHUNKS + WIDE_CHUNKS
    order = [(d, j) for d in (1, 2, 3) for j in range(JOINT_CHUNKS)]
    order += [(d, j) for d in (1, 2, 3) for j in range(JOINT_CHUNKS, CHUNKS)]
    refill = {3: (3,), 5: (4,), 6: (5,), 7: (6, 7), 8: (8, 9)}
    done = {"relay": 0, "across": 0}

    def pump(upto, lag=3):
        while done["relay"] < min(upto, len(order)):
            relay(*order[done["relay"]])
            for extra in refill.get(done["relay"], ()):
                own_sends(extra)
            done["relay"] += 1
            while done["across"] < done["relay"] - lag:
                across(*order[done["across"]])
                done["across"] += 1

    def flush(upto):
        while done["across"] < upto:
            across(*order[done["across"]])
            done["across"] += 1

    def turn_slabs(ref, out, slabs, first, end):
        rows = slice(first, end)
        copies = [
            pltpu.make_async_copy(
                ref.at[rows, q * SLAB : (q + 1) * SLAB], stage.at[i, rows, :], stage_sem.at[i]
            )
            for i, q in enumerate(slabs)
        ]
        for copy in copies:
            copy.start()
        for i, q in enumerate(slabs):
            copies[i].wait()

            def step(c, carry, i=i, q=q):
                cols = at(c * 256, 256)
                out[at(q * SLAB + c * 256, 256), rows] = stage[i, rows, cols].T
                return carry

            lax.fori_loop(0, SLAB // 256, step, 0)

    third = D // 3

    def turn_near(ref, out, slabs):
        for when, first, end in (
            (z == 0, 0, 2 * third), (z == last, third, D), ((z > 0) & (z < last), 0, D),
        ):
            @pl.when(when)
            def _(first=first, end=end):
                turn_slabs(ref, out, slabs, first, end)

    def turn_rest(ref, out, slabs):
        for when, first, end in ((z == 0, 2 * third, D), (z == last, 0, third)):
            @pl.when(when)
            def _(first=first, end=end):
                turn_slabs(ref, out, slabs, first, end)

    def turn_down(shard):
        copy = pltpu.make_async_copy(f_down.at[at(shard * deep, deep), :], stage_down, stage_sem.at[2])
        copy.start()
        copy.wait()

        def step(i, carry):
            t_down[at(i * TILE, TILE), at(shard * deep, deep)] = stage_down[:, at(i * TILE, TILE)].T
            return carry

        lax.fori_loop(0, D // TILE, step, 0)

    def saves(m):
        lanes = at(m * toks, toks)
        pairs = (
            (s_normed, o_normed.at[:, lanes]), (s_context, o_context.at[:, lanes]),
            (s_second, o_second.at[:, lanes]), (s_inner, o_inner.at[:, lanes]),
            (s_x, o_x.at[m]), (s_q, o_q.at[m]), (s_kv.at[m], o_kv.at[m]), (s_att, o_att.at[m]),
            (s_lse, o_lse.at[m]), (s_hidden, o_hidden.at[m]), (s_gu, o_gu.at[m]),
        )
        return [pltpu.make_async_copy(a, b, save_sem.at[i]) for i, (a, b) in enumerate(pairs)]

    def keep(m, *items):
        copies = saves(m)
        for i in items:
            copies[i].start()

    def result_save(m):
        return pltpu.make_async_copy(s_result, o_result.at[m], save_sem.at[11])

    def x_copy(m, i):
        part = x_in.at[m, at(i * TILE, TILE), :]
        return remote(part, part, x_send.at[m, i], x_recv.at[m, i], {"section": 1})

    def kv_copy(m, source, slot, lane, to):
        return remote(
            s_kv.at[m, source], s_kv.at[m, slot], kv_send.at[m, lane], kv_recv.at[m, slot],
            {"ctx": to},
        )

    def kv_sends(m):
        return (
            (0, kv_copy(m, 0, 2, 1, 2)),
            (0, kv_copy(m, 0, 1, 0, 1)),
            (1, kv_copy(m, 0, 2, 0, 3)),
            (2, kv_copy(m, 0, 1, 0, 3)),
        )

    def attend(kv_at, m, blocks, fresh):
        rows = at(kv_at * HEAD, HEAD, 64)
        query = s_q[rows, :]
        parts = []
        for d in blocks:
            part = dot(s_kv[m, d, rows, :], query, 0, 0)
            mask = bias[d]
            parts.append(part + jnp.concatenate([mask] * GROUP, axis=1))
        scores = parts[0] if len(parts) == 1 else jnp.concatenate(parts, axis=0)
        top = jnp.max(scores, axis=0, keepdims=True)
        one = pl.ds(kv_at, 1)
        if not fresh:
            old_top, old_total = s_top[one, :], s_lse[one, :]
            top = jnp.maximum(top, old_top)
        probs = jnp.exp(scores - top)
        total = jnp.sum(probs, axis=0, keepdims=True)
        probs = probs.astype(LOW)
        value_rows = at(KVW + kv_at * HEAD, HEAD, 64)
        summed = None
        for i, d in enumerate(blocks):
            term = dot(s_kv[m, d, value_rows, :], probs[i * toks : (i + 1) * toks], 1, 0)
            summed = term if summed is None else summed + term
        if not fresh:
            keep = jnp.exp(old_top - top)
            total = total + old_total * keep
        s_top[one, :] = top
        s_lse[one, :] = total
        for g in range(GROUP):
            lanes = slice(g * toks, (g + 1) * toks)
            out_rows = at((kv_at * GROUP + g) * HEAD, HEAD, 64)
            value = summed[:, lanes]
            if not fresh:
                value = value + s_att[out_rows, :] * keep[:, lanes]
            s_att[out_rows, :] = value

    def each(m, blocks, fresh):
        def step(kv_at, carry):
            attend(kv_at, m, blocks, fresh)
            return carry

        lax.fori_loop(0, KV_HEADS, step, 0, unroll=3)

    def take_own(m):
        x_now[...] = ends[m].astype(F32).T

    def take_sent(m):
        for i in range(D // TILE):
            x_copy(m, i).wait_recv()
        x_now[...] = x_in[m].astype(F32)

    def first_norm(m):
        x = x_now[...]
        s_x[...] = x.astype(LOW)
        s_normed[...] = (x * column_scale(x) * columns[:, 0:1]).astype(LOW)
        keep(m, 0, 4)
        fill_bias(bias, segments, m, place, toks)

    def rotated(block, head):
        cos, sin = cosine[...], sine[...]
        front = block[head * HEAD : head * HEAD + HALF]
        back = block[head * HEAD + HALF : (head + 1) * HEAD]
        return jnp.concatenate([front * cos - back * sin, back * cos + front * sin], axis=0)

    def keys_values(m):
        keys = dot(t_joint[D : D + KVW, :], s_normed[...], 1, 0)
        for head in range(KV_HEADS):
            s_kv[m, 0, head * HEAD : (head + 1) * HEAD, :] = rotated(keys, head).astype(LOW)
        s_kv[m, 0, KVW : 2 * KVW, :] = dot(t_joint[D + KVW : qkv, :], s_normed[...], 1, 0).astype(LOW)
        for who, copy in kv_sends(m):
            @pl.when(place == who)
            def _(copy=copy):
                copy.start()

    def queries(m):
        def query_tile(i, carry):
            block = dot(t_joint[at(i * TILE, TILE), :], s_normed[...], 1, 0) * SCALE
            for head in range(TILE // HEAD):
                rows = at((i * (TILE // HEAD // GROUP) + head // GROUP) * HEAD, HEAD, 64)
                g = head % GROUP
                s_q[rows, g * toks : (g + 1) * toks] = rotated(block, head).astype(LOW)
            return carry

        lax.fori_loop(0, D // TILE, query_tile, 0)
        keep(m, 5)

    def near_block(m):
        each(m, (0,), True)

    def far_blocks(m):
        @pl.when(place == 1)
        def _():
            kv_copy(m, 0, 1, 0, 1).wait_recv()
            each(m, (1,), False)

        @pl.when(place == 2)
        def _():
            kv_copy(m, 0, 2, 0, 2).wait_recv()
            each(m, (2,), False)
            kv_copy(m, 0, 1, 0, 2).wait_recv()
            each(m, (1,), False)

        @pl.when(place == 3)
        def _():
            kv_copy(m, 0, 1, 0, 3).wait_recv()
            each(m, (1,), False)
            kv_copy(m, 0, 2, 0, 3).wait_recv()
            kv_copy(m, 2, 1, 0, 2).start()
            each(m, (2,), False)

    def contexts(m):
        def finish(kv_at, carry):
            one = pl.ds(kv_at, 1)
            total = s_lse[one, :]
            inverse = 1.0 / total
            for g in range(GROUP):
                rows = at((kv_at * GROUP + g) * HEAD, HEAD, 64)
                value = s_att[rows, :] * inverse[:, g * toks : (g + 1) * toks]
                s_att[rows, :] = value
                s_context[rows, :] = value.astype(LOW)
            s_lse[one, :] = s_top[one, :] + jnp.log(total)
            return carry

        lax.fori_loop(0, KV_HEADS, finish, 0)
        keep(m, 1, 6, 7, 8)

    def seconds(m):
        def out_tile(i, carry):
            rows = at(i * TILE, TILE)
            s_hidden[rows, :] = x_now[rows, :] + dot(
                t_joint[at(qkv + i * TILE, TILE), :], s_context[...], 1, 0
            )
            return carry

        lax.fori_loop(0, D // TILE, out_tile, 0)
        hidden = s_hidden[...]
        s_second[...] = (hidden * column_scale(hidden) * columns[:, 1:2]).astype(LOW)
        keep(m, 2, 9)

    def gates(first, end):
        def gate_tile(i, carry):
            rows, up_rows = at(i * WIDE, WIDE), at(FF + i * WIDE, WIDE)
            gate = dot(t_gate_up[rows, :], s_second[...], 1, 0)
            up = dot(t_gate_up[up_rows, :], s_second[...], 1, 0)
            s_gu[rows, :] = gate.astype(LOW)
            s_gu[up_rows, :] = up.astype(LOW)
            s_inner[rows, :] = (gate * jax.nn.sigmoid(gate) * up).astype(LOW)
            return carry

        lax.fori_loop(first, end, gate_tile, 0)

    def early(work):
        @pl.when(section == 0)
        def _():
            work()

    for j in range(JOINT_CHUNKS):
        own_sends(j)
    for copy in own_copies:
        copy.start()
    segments[place] = seg_own[...]

    def seg_copy(i):
        return remote(
            seg_own, segments.at[place], seg_sem.at[0, i], seg_sem.at[1, i], {"ctx": (place + i) % 4}
        )

    for i in (1, 2, 3):
        seg_copy(i).start()
    gain_columns(gains, columns)
    early(lambda: take_own(0))
    for i in (1, 2, 3):
        seg_copy(i).wait()
    early(lambda: first_norm(0))

    joint_items = 3 * JOINT_CHUNKS
    lap = CHUNKS - JOINT_CHUNKS
    pump(joint_items + 3)
    for j in range(JOINT_CHUNKS):
        for d in (1, 2, 3):
            complete(d, j)
    own_copies[0].wait_recv()
    own_copies[1].wait_recv()

    def turn_all(ref, out, slabs):
        turn_slabs(ref, out, slabs, 0, D)

    turn_all(f_joint, t_joint, (0, 1))
    pump(joint_items + 4)
    turn_all(f_joint, t_joint, (2,))
    pump(joint_items + 5)
    early(lambda: keys_values(0))
    pump(joint_items + 6)
    early(lambda: queries(0))
    pump(joint_items + lap)
    early(lambda: near_block(0))
    pump(joint_items + lap + 3)
    early(lambda: far_blocks(0))
    pump(joint_items + lap + 5)
    early(lambda: contexts(0))
    early(lambda: seconds(0))
    pump(joint_items + 2 * lap)
    own_copies[2].wait_recv()
    for d in (1, 2):
        for j in range(JOINT_CHUNKS, first_down):
            complete(d, j)
    for p in range(WIDE_CHUNKS):
        turn_near(f_gate_up, t_gate_up, (p, WIDE_CHUNKS + p))
        pump(joint_items + 2 * lap + p + 1)

    def turn_downs(d):
        for j in range(first_down, CHUNKS):
            complete(d, j)
        for valid, shard, onward, more in sides(d):
            @pl.when(valid)
            def _(shard=shard):
                turn_down(shard)

    own_copies[3].wait_recv()
    turn_down(z)
    pump(joint_items + 3 * lap - 3)
    turn_downs(1)
    pump(joint_items + 3 * lap - 2)
    turn_downs(2)
    pump(joint_items + 3 * lap - 1)
    per_slab = SLAB // WIDE
    for p in range(WIDE_CHUNKS):
        complete(3, JOINT_CHUNKS + p)
        turn_rest(f_gate_up, t_gate_up, (p, WIDE_CHUNKS + p))
        early(lambda p=p: gates(p * per_slab, (p + 1) * per_slab))
        if p == 0:
            pump(joint_items + 3 * lap)
        flush(joint_items + 3 * lap - 2 + p)
    turn_downs(3)

    def micro(m, carry):
        @pl.when(m > 0)
        def _():
            for save in saves(m - 1):
                save.wait()

            @pl.when(section == 1)
            def _():
                result_save(m - 1).wait()

        @pl.when((section == 1) | (m > 0))
        def _():
            @pl.when(section == 0)
            def _():
                take_own(m)

            @pl.when(section == 1)
            def _():
                take_sent(m)

            first_norm(m)
            keys_values(m)
            queries(m)
            near_block(m)
            far_blocks(m)
            contexts(m)
            seconds(m)
            gates(0, FF // WIDE)

        keep(m, 3, 10)
        for i in range(D // TILE):
            rows = slice(i * TILE, (i + 1) * TILE)
            value = s_hidden[rows, :] + dot(t_down[rows, :], s_inner[...], 1, 0)
            x_now[rows, :] = value

            @pl.when(section == 0)
            def _(i=i, rows=rows, value=value):
                x_in[m, rows, :] = value.astype(LOW)
                x_copy(m, i).start()

        @pl.when(section == 1)
        def _():
            s_result[...] = x_now[...].T
            result_save(m).start()

        return carry

    lax.fori_loop(0, micros, micro, 0)
    seg_save = pltpu.make_async_copy(segments, o_seg, seg_sem.at[0, 0])
    seg_save.start()
    for save in saves(micros - 1):
        save.wait()
    seg_save.wait()

    @pl.when(section == 1)
    def _():
        result_save(micros - 1).wait()

    for m in range(2):
        @pl.when(section == 0)
        def _(m=m):
            for i in range(D // TILE):
                x_copy(m, i).wait_send()

        for who, copy in kv_sends(m):
            @pl.when(place == who)
            def _(copy=copy):
                copy.wait_send()

        @pl.when(place == 3)
        def _(m=m):
            kv_copy(m, 2, 1, 0, 2).wait_send()

    for d, j in order:
        for valid, shard, onward, more in sides(d):
            @pl.when(valid)
            def _(shard=shard, onward=onward, more=more):
                mate_copy(shard, j, y, y_mate, ys, yr).wait_send()
                mate_copy(shard, j, y, k_mate, cs, cr).wait_send()
                mate_copy(shard, j, 1 - y, k_mate, es, er).wait_send()
                if d < 3:
                    @pl.when(more)
                    def _():
                        z_copy(shard, j, onward, False, False).wait_send()
    for j in range(CHUNKS):
        @pl.when(z < last)
        def _(j=j):
            z_copy(z, j, z + 1, True, False).wait_send()

        @pl.when(z > 0)
        def _(j=j):
            z_copy(z, j, z - 1, True, True).wait_send()
    for copy in own_copies:
        copy.wait_send()


def backward_kernel(
    ends, gains, cosine, sine, segments, w_joint, w_gate_up, w_down,
    i_x, i_q, i_kv, i_att, i_lse, i_hidden, i_gu, i_result, i_normed, i_context, i_second, i_inner,
    o_result, o_down, o_gate_up, o_qkv, o_out, o_gain,
    v_joint, v_gate_up, v_down, g_in, g_now, s_x, s_q, s_kv, s_att, s_lse, s_hid, s_gu,
    s_both, s_mixed, s_hidden, s_grad, s_sum, s_context, s_delta, s_dq, s_dkv, kv_out, kv_in,
    s_gains, bias, columns, wide_out, down_out, gain_out, gain_in,
    w_sem, load_sem, gu_sem, save_sem, kv_send, kv_recv, x_send, x_recv,
    left_sem, near_send, near_recv, mid_send, mid_recv, right_send, right_recv, left_send, left_recv,
    out_sem, gain_send, gain_recv, near_free, mid_free, right_free, left_free,
):
    section = lax.axis_index("section")
    place = lax.axis_index("ctx")
    micros, toks = ends.shape[0], ends.shape[1]
    qkv = D + 2 * KVW
    w_loads = [
        pltpu.make_async_copy(src, dst, w_sem.at[i])
        for i, (src, dst) in enumerate(
            ((w_joint, v_joint), (w_gate_up, v_gate_up), (w_down, v_down))
        )
    ]

    def loads(m):
        pairs = (
            (i_hidden, s_hid), (i_att, s_att), (i_q, s_q), (i_kv, s_kv),
            (i_lse, s_lse), (i_x, s_x),
        )
        return [pltpu.make_async_copy(a.at[m], b, load_sem.at[i]) for i, (a, b) in enumerate(pairs)]

    tiles = FF // TILE

    def gu_loads(m, i):
        slot = i % AHEAD
        return [
            pltpu.make_async_copy(
                i_gu.at[m, at(part * FF + i * TILE, TILE), :], s_gu.at[slot, part], gu_sem.at[slot, part]
            )
            for part in range(2)
        ]

    w_loads[2].start()
    for i in range(AHEAD):
        for load in gu_loads(0, i):
            load.start()
    for load in loads(0):
        load.start()
    w_loads[1].start()
    w_loads[0].start()
    z = lax.axis_index("fsdp")
    last = lax.axis_size("fsdp") - 1
    others = [((place + i // 4) % 4, (z + i % 4) % 4) for i in range(1, OWNERS)]
    greet([{"ctx": a, "fsdp": b} for a, b in others] + [{"section": 1 - section}])
    s_gains[...] = jnp.zeros_like(s_gains)
    gain_columns(gains, columns)

    def result_saves(m):
        return [
            pltpu.make_async_copy(
                s_dq.at[0:toks, at(i % 2 * TILE, TILE)], o_result.at[m, :, i * TILE : (i + 1) * TILE], save_sem.at[i]
            )
            for i in range(D // TILE)
        ]

    def g_copy(m):
        return remote(g_in.at[m], g_in.at[m], x_send.at[m], x_recv.at[m], {"section": 0})

    def kv_copy(m, source, slot, lane, to):
        return remote(
            kv_out.at[source], kv_in.at[m, slot], kv_send.at[m, lane], kv_recv.at[m, slot],
            {"ctx": to},
        )

    def kv_sends(m):
        return (
            (1, kv_copy(m, 0, 0, 0, 0)),
            (2, kv_copy(m, 0, 0, 0, 3)),
            (2, kv_copy(m, 1, 1, 1, 0)),
            (3, kv_copy(m, 0, 0, 0, 2)),
            (3, kv_copy(m, 1, 0, 1, 1)),
        )

    def block_grads(d, m, fresh):
        def step(kv_at, carry):
            rows = at(kv_at * HEAD, HEAD, 64)
            value_rows = at(KVW + kv_at * HEAD, HEAD, 64)
            one = pl.ds(kv_at, 1)
            query, grad = s_q[rows, :], s_context[rows, :]
            key, value = s_kv[d, rows, :], s_kv[d, value_rows, :]
            mask = bias[d]
            scores = dot(key, query, 0, 0) + jnp.concatenate([mask] * GROUP, axis=1)
            probs = jnp.exp(scores - s_lse[one, :])
            grad_probs = dot(value, grad, 0, 0)
            grad_scores = (probs * (grad_probs - s_delta[one, :])).astype(LOW)
            s_dkv[rows, :] = dot(query, grad_scores, 1, 1)
            s_dkv[value_rows, :] = dot(grad, probs.astype(LOW), 1, 1)
            grad_query = dot(key, grad_scores, 1, 0)
            if fresh:
                s_dq[rows, :] = grad_query
            else:
                s_dq[rows, :] = s_dq[rows, :] + grad_query
            return carry

        lax.fori_loop(0, KV_HEADS, step, 0, unroll=3)

    y, k = place // 2, place % 2
    y_mate = {"ctx": (1 - y) * 2 + k}
    k_mate = {"ctx": y * 2 + 1 - k}
    right, left = {"fsdp": z + 1}, {"fsdp": z - 1}
    n_down, n_both = D // DOWN_COLS, 2 * FF // WIDE_COLS
    n_mixed, n_out = qkv // WIDE_COLS, D // WIDE_COLS
    end_both = n_down + n_both
    end_mixed = end_both + n_mixed
    total = end_mixed + n_out
    hop, first_z = 2, 4
    final_lag = first_z + hop * 3
    block = D // 4
    parts = (FF // OWNERS // 3, D // OWNERS)
    used = (4 * parts[0], block)
    spare = 13 * WIDE_COLS
    both_toks = micros * toks
    inner_t = v_down.at[:, 0:both_toks]
    normed_t = v_down.at[0:D, both_toks : 2 * both_toks]
    context_t = v_gate_up.at[:, spare : spare + both_toks]
    second_t = v_gate_up.at[:, spare + both_toks : spare + 2 * both_toks]
    left_loads = [
        pltpu.make_async_copy(a, b, left_sem.at[i])
        for i, (a, b) in enumerate(
            ((i_inner, inner_t), (i_normed, normed_t), (i_context, context_t), (i_second, second_t))
        )
    ]

    def cell(column, slot, first=0, count=block):
        rows = at(slot % 4 * block + first, count, 16)
        return v_gate_up.at[rows, at((column + slot // 4) * WIDE_COLS, WIDE_COLS)]

    def out_near(slot, yy):
        return cell(0, slot * 2 + yy)

    def own_near(slot, yy):
        return cell(1, slot * 2 + yy)

    def in_near(slot, yy):
        return cell(2, slot * 2 + yy)

    def gain_copy(i):
        to_place, to_z = others[i - 1]
        return remote(
            gain_out.at[to_place * 4 + to_z], gain_in.at[i], gain_send.at[i], gain_recv.at[i],
            {"ctx": to_place, "fsdp": to_z},
        )

    def near_copy(j):
        slot = j % NEAR
        return remote(
            cell(0, slot * 2, 0, 2 * block), cell(2, slot * 2, 0, 2 * block),
            near_send.at[slot], near_recv.at[slot], k_mate,
        )

    def mid_copy(kind, j):
        slot = j % MID
        return remote(
            cell(3, slot, 0, used[kind]), cell(4, slot, 0, used[kind]),
            mid_send.at[slot], mid_recv.at[slot], y_mate,
        )

    def line_rows(kind, here, rightward):
        part = parts[kind]
        if rightward:
            start = (part * (here + 1)) // 16 * 16
            return start, used[kind] - start
        return 0, (part * here + 15) // 16 * 16

    def line_copy(kind, j, here, rightward):
        start, count = line_rows(kind, here, rightward)
        lane, slot = (0 if rightward else 1), j % NEAR
        return remote(
            cell(8, lane * NEAR + slot, start, count), cell(9 if rightward else 11, j % FAR, start, count),
            (right_send if rightward else left_send).at[slot],
            (right_recv if rightward else left_recv).at[j % FAR],
            right if rightward else left,
        )

    def out_copy(kind, j, first):
        slot = j % NEAR
        if kind == 0:
            return pltpu.make_async_copy(
                down_out.at[slot], o_down.at[:, at(j * DOWN_COLS, DOWN_COLS)], out_sem.at[slot]
            )
        out = {n_down: o_gate_up, end_both: o_qkv, end_mixed: o_out}[first]
        return pltpu.make_async_copy(
            wide_out.at[slot], out.at[:, at((j - first) * WIDE_COLS, WIDE_COLS)], out_sem.at[slot]
        )

    def out_wait(kind, slot):
        src, dst = (wide_out, o_out.at[:, 0:WIDE_COLS]) if kind else (down_out, o_down.at[:, 0:DOWN_COLS])
        pltpu.make_async_copy(src.at[slot], dst, out_sem.at[slot]).wait()

    def open_buffers():
        pl.semaphore_signal(near_free, inc=NEAR, device_id=k_mate, device_id_type=MESH)
        pl.semaphore_signal(mid_free, inc=MID, device_id=y_mate, device_id_type=MESH)

        @pl.when(z > 0)
        def _():
            pl.semaphore_signal(right_free, inc=FAR, device_id=left, device_id_type=MESH)

        @pl.when(z < last)
        def _():
            pl.semaphore_signal(left_free, inc=FAR, device_id=right, device_id_type=MESH)

    def when(condition):
        if isinstance(condition, bool):
            return (lambda work: work()) if condition else (lambda work: None)
        return pl.when(condition)

    def inside(j, first, end):
        if isinstance(j, int):
            return first <= j < end
        return (j >= first) & (j < end)

    def typed(j, work):
        @when(inside(j, 0, n_down))
        def _():
            work(0)

        @when(inside(j, n_down, total))
        def _():
            work(1)

    def multiply_down(j):
        rhs = s_grad[at(j * DOWN_COLS, DOWN_COLS), :]
        rows, piece = FF // 4, parts[0]
        for yy in range(2):
            for mine in (False, True):
                kk = k if mine else 1 - k
                lhs = v_down[at((yy * 2 + kk) * rows, rows), 0:both_toks]
                value = dot(lhs, rhs, 1, 1).astype(LOW)
                out = (own_near if mine else out_near)(j % NEAR, yy)
                for zz in range(4):
                    for t in range(3):
                        start = (zz * 3 + t) * piece
                        out[zz * piece : (zz + 1) * piece, t * 128 : (t + 1) * 128] = value[start : start + piece]

    def multiply_wide(j, lhs, rhs, first):
        right_rows = rhs[at((j - first) * WIDE_COLS, WIDE_COLS), :]
        for yy in range(2):
            for mine in (False, True):
                kk = k if mine else 1 - k
                value = dot(lhs[at((yy * 2 + kk) * block, block, 16), :], right_rows, 1, 1)
                (own_near if mine else out_near)(j % NEAR, yy)[...] = value.astype(LOW)

    def stage_near(j):
        for first, load in ((0, 0), (n_down, 3), (end_both, 1), (end_mixed, 2)):
            @when(inside(j, first, first + 1))
            def _(load=load):
                left_loads[load].wait()

        @when(inside(j, NEAR, total))
        def _():
            near_copy(j - NEAR).wait_send()

        @when(inside(j, 0, n_down))
        def _():
            multiply_down(j)

        @when(inside(j, n_down, end_both))
        def _():
            multiply_wide(j, second_t, s_both, n_down)

        @when(inside(j, end_both, end_mixed))
        def _():
            multiply_wide(j, normed_t, s_mixed, end_both)

        @when(inside(j, end_mixed, total))
        def _():
            multiply_wide(j, context_t, s_hidden, end_mixed)

        @when(inside(j, 0, total))
        def _():
            pl.semaphore_wait(near_free, 1)
            near_copy(j).start()

    def stage_mid(j):
        @when(inside(j, MID, total))
        def _():
            typed(j - MID, lambda kind: mid_copy(kind, j - MID).wait_send())

        @when(inside(j, 0, total))
        def _():
            near_copy(j).wait_recv()
            slot = j % NEAR
            for yy in range(2):
                value = (own_near(slot, yy)[...].astype(F32) + in_near(slot, yy)[...].astype(F32)).astype(LOW)

                @pl.when(y == yy)
                def _(value=value):
                    cell(5, j % SUMS)[...] = value

                @pl.when(y != yy)
                def _(value=value):
                    cell(3, j % MID)[...] = value

            pl.semaphore_wait(mid_free, 1)

        @when(inside(j, 0, total - NEAR))
        def _():
            pl.semaphore_signal(near_free, inc=1, device_id=k_mate, device_id_type=MESH)

        typed(j, lambda kind: mid_copy(kind, j).start())

    def stage_sum(j):
        typed(j, lambda kind: mid_copy(kind, j).wait_recv())

        @when(inside(j, 0, total))
        def _():
            sums = cell(5, j % SUMS)
            sums[...] = (sums[...].astype(F32) + cell(4, j % MID)[...].astype(F32)).astype(LOW)

        @when(inside(j, 0, total - MID))
        def _():
            pl.semaphore_signal(mid_free, inc=1, device_id=y_mate, device_id_type=MESH)

    def stage_line(i, rightward):
        free = right_free if rightward else left_free
        for here in range(4):
            step = here if rightward else 3 - here
            j = i - first_z - hop * step
            if step == 3 or (isinstance(j, int) and not 0 <= j < total):
                continue

            def device(here=here, step=step, j=j):
                @when(inside(j, NEAR, total))
                def _():
                    typed(j - NEAR, lambda kind: line_copy(kind, j - NEAR, here, rightward).wait_send())

                def work(kind):
                    start, count = line_rows(kind, here, rightward)
                    value = cell(5, j % SUMS, start, count)[...].astype(F32)
                    if step > 0:
                        line_copy(kind, j, here - 1 if rightward else here + 1, rightward).wait_recv()
                        came = cell(9 if rightward else 11, j % FAR, start, count)
                        value = value + came[...].astype(F32)
                    cell(8, (0 if rightward else NEAR) + j % NEAR, start, count)[...] = value.astype(LOW)

                typed(j, work)
                pl.semaphore_wait(free, 1)
                typed(j, lambda kind: line_copy(kind, j, here, rightward).start())

            @pl.when(z == here)
            def _(device=device, j=j):
                when(inside(j, 0, total))(device)

    def store(kind, j, value):
        if kind == 0:
            @when(inside(j, NEAR, total))
            def _():
                out_wait(0, j % NEAR)

            piece = parts[0]
            for t in range(3):
                down_out[j % NEAR, t * piece : (t + 1) * piece, :] = value[:, t * 128 : (t + 1) * 128]
            out_copy(0, j, 0).start()
            return
        typed(j - NEAR, lambda old: out_wait(old, j % NEAR))
        wide_out[j % NEAR] = value
        for first, end in ((n_down, end_both), (end_both, end_mixed), (end_mixed, total)):
            @when(inside(j, first, end))
            def _(first=first):
                out_copy(1, j, first).start()

    def stage_final(j):
        if isinstance(j, int) and not 0 <= j < total:
            return

        def device(here):
            def work(kind):
                part = parts[kind]
                if here == 3:
                    line_copy(kind, j, 2, True).wait_recv()
                if here == 0:
                    line_copy(kind, j, 1, False).wait_recv()
                low_at = here * part // 16 * 16
                count = (here * part + part + 15) // 16 * 16 - low_at
                value = cell(5, j % SUMS, low_at, count)[...].astype(F32)
                if here > 0:
                    value = value + cell(9, j % FAR, low_at, count)[...].astype(F32)
                if here < 3:
                    value = value + cell(11, j % FAR, low_at, count)[...].astype(F32)
                shift = here * part - low_at
                store(kind, j, value[shift : shift + part])

            typed(j, work)

            @when(inside(j, 0, total - FAR))
            def _():
                if here > 0:
                    pl.semaphore_signal(right_free, inc=1, device_id=left, device_id_type=MESH)
                if here < 3:
                    pl.semaphore_signal(left_free, inc=1, device_id=right, device_id_type=MESH)

        for here in range(4):
            @pl.when(z == here)
            def _(here=here):
                when(inside(j, 0, total))(lambda: device(here))

    def reduce_step(i):
        stage_near(i)
        stage_mid(i - 1)
        stage_sum(i - 4)
        stage_line(i, True)
        stage_line(i, False)
        stage_final(i - final_lag)

    def reduce_steps(final, first, end):
        @pl.when(final & (section == 0))
        def _():
            for i in range(first, end):
                reduce_step(i)

    def norm_back(grad, source, gain, row):
        scale = column_scale(source)
        unit = source * scale
        folded = jnp.sum(grad * unit, axis=1, keepdims=True)
        s_gains[:, row : row + 1] = s_gains[:, row : row + 1] + folded
        inner = grad * gain
        return scale * (inner - unit * jnp.mean(inner * unit, axis=0, keepdims=True))

    def rotated_back(front, back):
        cos, sin = cosine[...], sine[...]
        return jnp.concatenate([front * cos + back * sin, back * cos - front * sin], axis=0)

    def finish_micro(m):
        own = at(m * toks, toks)

        @pl.when(place == 0)
        def _():
            kv_copy(m, 0, 0, 0, 0).wait_recv()
            kv_copy(m, 0, 1, 0, 0).wait_recv()
            s_dkv[...] = s_dkv[...] + kv_in[m, 0].astype(F32) + kv_in[m, 1].astype(F32)

        @pl.when((place == 1) | (place == 2))
        def _():
            kv_copy(m, 0, 0, 0, 0).wait_recv()
            s_dkv[...] = s_dkv[...] + kv_in[m, 0].astype(F32)

        for head in range(KV_HEADS):
            front = s_dkv[head * HEAD : head * HEAD + HALF, :]
            back = s_dkv[head * HEAD + HALF : (head + 1) * HEAD, :]
            s_mixed[D + head * HEAD : D + (head + 1) * HEAD, own] = rotated_back(front, back).astype(LOW)
        s_mixed[D + KVW : qkv, own] = s_dkv[KVW : 2 * KVW, :].astype(LOW)

        def rest_tile(i, carry):
            rows = at(i * TILE, TILE)
            s_sum[rows, :] = s_sum[rows, :] + dot(v_joint[rows, D:qkv], s_mixed[D:qkv, own], 1, 0)
            return carry

        lax.fori_loop(0, D // TILE, rest_tile, 0)
        loads(m)[5].wait()
        g_now[...] = g_now[...] + norm_back(s_sum[...], s_x[...].astype(F32), columns[:, 0:1], 0)

        @pl.when(section == 1)
        def _():
            g_in[m] = g_now[...].astype(LOW)
            g_copy(m).start()

        @pl.when(m + 1 < micros)
        def _():
            for load in loads(m + 1):
                load.start()

        @pl.when(section == 0)
        def _():
            copies = result_saves(m)
            for i, save in enumerate(copies):
                if i > 1:
                    copies[i - 2].wait()
                s_dq[0:toks, i % 2 * TILE : (i % 2 + 1) * TILE] = g_now[i * TILE : (i + 1) * TILE, :].T
                save.start()

    def micro(m, carry):
        @pl.when(m > 0)
        def _():
            @pl.when(section == 0)
            def _():
                for save in result_saves(m - 1)[-2:]:
                    save.wait()

        @pl.when(m > 0)
        def _():
            for who, copy in kv_sends(m - 1):
                @pl.when(place == who)
                def _(copy=copy):
                    copy.wait_send()

        fill_bias(bias, segments, m, place, toks)
        own = at(m * toks, toks)
        final = m == micros - 1

        @pl.when(section == 1)
        def _():
            s_grad[:, own] = ends[m].astype(F32).T.astype(LOW)

        @pl.when(section == 0)
        def _():
            g_copy(m).wait_recv()
            s_grad[:, own] = g_in[m]

        @pl.when(m == 0)
        def _():
            w_loads[2].wait()

        now = loads(m)

        def inner_tile(i, carry):
            rows, up_rows = at(i * TILE, TILE), at(FF + i * TILE, TILE)
            for load in gu_loads(m, i):
                load.wait()

            grad_inner = dot(v_down[rows, :], s_grad[:, own], 1, 0)
            gate, up = s_gu[i % AHEAD, 0].astype(F32), s_gu[i % AHEAD, 1].astype(F32)
            sig = jax.nn.sigmoid(gate)
            s_both[rows, own] = (grad_inner * up * sig * (1.0 + gate * (1.0 - sig))).astype(LOW)
            s_both[up_rows, own] = (grad_inner * (gate * sig)).astype(LOW)

            @pl.when(i + AHEAD < tiles)
            def _():
                for load in gu_loads(m, i + AHEAD):
                    load.start()

            return carry

        lax.fori_loop(0, tiles, inner_tile, 0)

        @pl.when(final)
        def _():
            left_loads[0].start()
            left_loads[1].start()

        @pl.when(m == 0)
        def _():
            w_loads[1].wait()

        @pl.when(m + 1 < micros)
        def _():
            for i in range(AHEAD):
                for load in gu_loads(m + 1, i):
                    load.start()

        def second_tile(i, carry):
            rows = at(i * TILE, TILE)
            s_sum[rows, :] = dot(v_gate_up[rows, :], s_both[:, own], 1, 0)
            return carry

        lax.fori_loop(0, D // TILE, second_tile, 0)

        @pl.when(final)
        def _():
            left_loads[2].start()
            left_loads[3].start()
            open_buffers()

        now[0].wait()
        g_now[...] = s_grad[:, own].astype(F32) + norm_back(s_sum[...], s_hid[...], columns[:, 1:2], 1)
        s_hidden[:, own] = g_now[...].astype(LOW)

        @pl.when(m == 0)
        def _():
            w_loads[0].wait()

        for i in (1, 2, 3, 4):
            now[i].wait()
        reduce_steps(final, 0, 1)

        def context_tile(i, carry):
            block = dot(v_joint[at(i * TILE, TILE), qkv:], s_hidden[:, own], 1, 0).astype(LOW)
            for head in range(TILE // HEAD):
                kv_at = i * (TILE // HEAD // GROUP) + head // GROUP
                g = head % GROUP
                part = block[head * HEAD : (head + 1) * HEAD]
                s_context[at(kv_at * HEAD, HEAD, 64), g * toks : (g + 1) * toks] = part
                seen = s_att[at(i * TILE + head * HEAD, HEAD, 64), :]
                s_delta[pl.ds(kv_at, 1), g * toks : (g + 1) * toks] = jnp.sum(
                    part.astype(F32) * seen, axis=0, keepdims=True
                )
            return carry

        lax.fori_loop(0, D // TILE, context_tile, 0)
        sends = kv_sends(m)

        reduce_steps(final, 1, 2)

        @pl.when(place == 2)
        def _():
            block_grads(1, m, True)
            kv_out[0] = s_dkv[...].astype(LOW)
            sends[1][1].start()

        @pl.when(place == 3)
        def _():
            block_grads(2, m, True)
            kv_copy(m, 0, 0, 0, 3).wait_recv()
            kv_out[1] = (s_dkv[...] + kv_in[m, 0].astype(F32)).astype(LOW)
            sends[4][1].start()

        reduce_steps(final, 2, 3)

        @pl.when(place == 1)
        def _():
            block_grads(1, m, True)
            kv_out[0] = s_dkv[...].astype(LOW)
            sends[0][1].start()

        @pl.when(place == 2)
        def _():
            block_grads(2, m, False)
            kv_out[1] = s_dkv[...].astype(LOW)
            sends[2][1].start()

        @pl.when(place == 3)
        def _():
            block_grads(1, m, False)
            kv_out[0] = s_dkv[...].astype(LOW)
            sends[3][1].start()

        reduce_steps(final, 3, 4)

        @pl.when(place == 0)
        def _():
            block_grads(0, m, True)

        @pl.when(place > 0)
        def _():
            block_grads(0, m, False)

        reduce_steps(final, 4, 5)
        def query_back(kv_at, carry):
            for g in range(GROUP):
                lanes = slice(g * toks, (g + 1) * toks)
                front = s_dq[at(kv_at * HEAD, HALF, 32), lanes] * SCALE
                back = s_dq[at(kv_at * HEAD + HALF, HALF, 32), lanes] * SCALE
                rows = at((kv_at * GROUP + g) * HEAD, HEAD, 64)
                s_mixed[rows, own] = rotated_back(front, back).astype(LOW)
            return carry

        lax.fori_loop(0, KV_HEADS, query_back, 0)

        def normed_tile(i, carry):
            rows = at(i * TILE, TILE)
            s_sum[rows, :] = dot(v_joint[rows, :D], s_mixed[:D, own], 1, 0)
            return carry

        lax.fori_loop(0, D // TILE, normed_tile, 0)
        reduce_steps(final, 5, EMBEDDED)

        @pl.when((section == 1) | (m + 1 < micros))
        def _():
            finish_micro(m)

        return carry

    lax.fori_loop(0, micros, micro, 0)
    def reduce_loop(i, carry):
        reduce_step(i)
        return carry

    @pl.when(section == 0)
    def _():
        lax.fori_loop(EMBEDDED, DEFERRED, reduce_loop, 0)
        finish_micro(micros - 1)

    rows = jnp.concatenate([s_gains[...], jnp.zeros((D, 126), F32)], axis=1).T[0:8]
    for owner in range(OWNERS):
        shift = (D - owner * (D // OWNERS)) % D
        gain_out[owner] = (pltpu.roll(rows, shift, 1) if shift else rows)[:, :128]
    for i in range(1, OWNERS):
        gain_copy(i).start()

    lax.fori_loop(jnp.where(section == 0, DEFERRED, 0), total + final_lag, reduce_loop, 0)
    gain = gain_out[place * 4 + z]
    for i in range(1, OWNERS):
        gain_copy(i).wait()
        gain = gain + gain_in[i]
    o_gain[...] = gain

    @pl.when(section == 0)
    def _():
        for save in result_saves(micros - 1)[-2:]:
            save.wait()

    for m in range(2):
        @pl.when(section == 1)
        def _(m=m):
            g_copy(m).wait_send()

    for who, copy in kv_sends(micros - 1):
        @pl.when(place == who)
        def _(copy=copy):
            copy.wait_send()

    for j in range(total - NEAR, total):
        near_copy(j).wait_send()
        for at_z in range(3):
            @pl.when(z == at_z)
            def _(at_z=at_z, j=j):
                line_copy(1, j, at_z, True).wait_send()

            @pl.when(z == at_z + 1)
            def _(at_z=at_z, j=j):
                line_copy(1, j, at_z + 1, False).wait_send()
    for j in range(total - MID, total):
        mid_copy(1, j).wait_send()
    for j in range(total - NEAR, total):
        out_wait(1, j % NEAR)


def run_forward(ends, gains, cosine, sine, seg_own, w_qkv, w_out, w_gate_up, w_down):
    micros, toks = ends.shape[0], ends.shape[1]
    width = GROUP * toks
    vm, hbm = pl.BlockSpec(memory_space=pltpu.VMEM), pl.BlockSpec(memory_space=pl.ANY)
    sem = pltpu.SemaphoreType.DMA
    joint = w_qkv.shape[1] + w_out.shape[1]
    outs = [
        ((D, joint), LOW), ((D, 2 * FF), LOW), ((FF, D), LOW), ((4, micros, toks), jnp.int32),
        ((D, micros * toks), LOW), ((D, micros * toks), LOW), ((D, micros * toks), LOW),
        ((FF, micros * toks), LOW), ((micros, D, toks), LOW), ((micros, KVW, width), LOW),
        ((micros, 3, 2 * KVW, toks), LOW), ((micros, D, toks), F32), ((micros, 8, width), F32),
        ((micros, D, toks), F32), ((micros, 2 * FF, toks), LOW), ((micros, toks, D), F32),
    ]
    scratch = [
        ((joint, D), LOW), ((2 * FF, D), LOW), ((D, FF), LOW), ((2, D, SLAB), LOW), (w_down.shape, LOW),
        ((micros, D, toks), LOW), ((D, toks), F32),
        ((D, toks), LOW), ((D, toks), LOW), ((D, toks), LOW), ((FF, toks), LOW), ((D, toks), LOW),
        ((KVW, width), LOW), ((micros, 3, 2 * KVW, toks), LOW), ((D, toks), F32), ((8, width), F32),
        ((8, width), F32), ((D, toks), F32), ((2 * FF, toks), LOW), ((toks, D), F32), ((3, toks, toks), F32),
        ((4, micros, toks), jnp.int32), ((D, 2), F32),
    ]
    return pl.pallas_call(
        forward_kernel,
        out_shape=tuple(jax.ShapeDtypeStruct(s, t) for s, t in outs),
        in_specs=[vm] * 5 + [hbm] * 4,
        out_specs=(hbm,) * len(outs),
        scratch_shapes=[pltpu.VMEM(s, t) for s, t in scratch]
        + [sem((3,)), sem((2, 4)), sem((12,)), sem((micros, 2)), sem((micros, 3)), sem((micros, 3)), sem((micros, 3))]
        + [sem((2, 4)), sem((CHUNKS,))] + [sem((4, CHUNKS))] * 8,
        compiler_params=pltpu.CompilerParams(
            collective_id=3, has_side_effects=True, vmem_limit_bytes=62 * 2**20
        ),
        name="layer_forward",
    )(ends, gains, cosine, sine, seg_own, w_qkv, w_out, w_gate_up, w_down)


def run_backward(ends, gains, cosine, sine, segments, joint, gate_up, down, saved):
    micros, toks = ends.shape[0], ends.shape[1]
    width = GROUP * toks
    vm, hbm = pl.BlockSpec(memory_space=pltpu.VMEM), pl.BlockSpec(memory_space=pl.ANY)
    sem, plain = pltpu.SemaphoreType.DMA, pltpu.SemaphoreType.REGULAR
    qkv = D + 2 * KVW
    outs = [
        (micros, toks, D), (FF // OWNERS, D), (D // OWNERS, 2 * FF), (D // OWNERS, qkv), (D // OWNERS, D),
        (8, 128),
    ]
    scratch = [
        (joint.shape, LOW), (gate_up.shape, LOW), (down.shape, LOW),
        ((micros, D, toks), LOW), ((D, toks), F32),
        ((D, toks), LOW), ((KVW, width), LOW), ((3, 2 * KVW, toks), LOW), ((D, toks), F32), ((8, width), F32),
        ((D, toks), F32), ((AHEAD, 2, TILE, toks), LOW),
        ((2 * FF, micros * toks), LOW), ((qkv, micros * toks), LOW), ((D, micros * toks), LOW),
        ((D, micros * toks), LOW), ((D, toks), F32),
        ((KVW, width), LOW), ((8, width), F32), ((KVW, width), F32), ((2 * KVW, toks), F32),
        ((2, 2 * KVW, toks), LOW), ((micros, 2, 2 * KVW, toks), LOW),
        ((D, 2), F32), ((3, toks, toks), F32), ((D, 2), F32),
        ((NEAR, D // OWNERS, WIDE_COLS), F32), ((NEAR, FF // OWNERS, DOWN_COLS), F32),
        ((OWNERS, 8, 128), F32), ((OWNERS, 8, 128), F32),
    ]
    return pl.pallas_call(
        backward_kernel,
        out_shape=tuple(jax.ShapeDtypeStruct(s, F32) for s in outs),
        in_specs=[vm] * 5 + [hbm] * 15,
        out_specs=(hbm,) * 5 + (vm,),
        scratch_shapes=[pltpu.VMEM(s, t) for s, t in scratch]
        + [sem((3,)), sem((6,)), sem((AHEAD, 2)), sem((3,)), sem((micros, 2)), sem((micros, 2)), sem((micros,)), sem((micros,))]
        + [sem((4,)), sem((NEAR,)), sem((NEAR,)), sem((MID,)), sem((MID,)), sem((NEAR,)), sem((FAR,)), sem((NEAR,)), sem((FAR,))]
        + [sem((NEAR,)), sem((OWNERS,)), sem((OWNERS,)), plain, plain, plain, plain],
        compiler_params=pltpu.CompilerParams(
            collective_id=4, has_side_effects=True, vmem_limit_bytes=63 * 2**20
        ),
        input_output_aliases={15: 0},
        name="layer_backward",
    )(ends, gains, cosine, sine, segments, joint, gate_up, down, *saved)


def small_mesh():
    return lax.axis_size("ctx") == 4 and lax.axis_size("fsdp") == 4


def whole_weights(w_qkv, w_out, w_gate_up, w_down):
    return tuple(
        lax.all_gather(w, "fsdp", axis=0, tiled=True) for w in (w_qkv, w_out, w_gate_up, w_down)
    )


def owned_grads(lefts, rights):
    return tuple(
        lax.psum_scatter(
            outer_product(left, right).astype(jnp.bfloat16),
            ("ctx", "fsdp"),
            scatter_dimension=0,
            tiled=True,
        ).astype(jnp.float32)
        for left, right in zip(lefts, rights)
    )


def local_small(ends, segment_ids, w_qkv, w_out, w_gate_up, w_down, gains):
    tok_rows = ends.shape[3]
    local_ends = ends[0, :, 0]
    seg_local = segment_ids[:, 0]
    query_pos = lax.axis_index("ctx") * tok_rows + jnp.arange(tok_rows, dtype=jnp.int32)
    frequency = 10000.0 ** (-(jnp.arange(HEAD // 2).astype(jnp.float32) * 2.0 / HEAD))
    angle_table = frequency[:, None] * query_pos.astype(jnp.float32)[None, :]
    shared = (local_ends, gains[0], jnp.cos(angle_table), jnp.sin(angle_table))
    joint, gate_up, down, segments, normed, context, second, inner, *saved, result = run_forward(
        *shared, seg_local, w_qkv[0], w_out[0], w_gate_up[0], w_down[0]
    )
    ends_rows, g_down, g_gate_up, g_qkv, g_out, gain = run_backward(
        *shared, segments, joint, gate_up, down, (*saved, result, normed, context, second, inner)
    )
    return (
        ends_rows[None, :, None], g_qkv[None], g_out[None], g_gate_up[None], g_down[None],
        gain[None, :2, : D // 16],
    )


def local(ends, segment_ids, w_qkv, w_out, w_gate_up, w_down, gains):
    if small_mesh():
        return local_small(ends, segment_ids, w_qkv, w_out, w_gate_up, w_down, gains)
    section_index = lax.axis_index("section")
    micro_count = ends.shape[1]
    tok_rows = ends.shape[3]
    local_ends = ends[0, :, 0]
    seg_local = segment_ids[:, 0]
    seg_whole = lax.all_gather(seg_local, "ctx", axis=1, tiled=True)
    query_pos = lax.axis_index("ctx") * tok_rows + jnp.arange(tok_rows, dtype=jnp.int32)
    frequency = 10000.0 ** (-(jnp.arange(HEAD // 2).astype(jnp.float32) * 2.0 / HEAD))
    angle_table = query_pos.astype(jnp.float32)[:, None] * frequency[None, :]
    cosine = jnp.cos(angle_table)[:, None, :]
    sine_table = jnp.sin(angle_table)[:, None, :]
    gain_pair = gains[0]
    weights = whole_weights(w_qkv[0], w_out[0], w_gate_up[0], w_down[0])
    arrived = jnp.zeros((tok_rows, D), jnp.bfloat16)
    store_bufs = None
    outputs = jnp.zeros((micro_count + 1, tok_rows, D), jnp.float32)
    for tick_num in range(micro_count + 1):
        batch_index = tick_num - section_index
        is_valid = (batch_index >= 0) & (batch_index < micro_count)
        clipped = jnp.clip(batch_index, 0, micro_count - 1)
        slot_index = jnp.where(is_valid, batch_index, micro_count)
        own_rows = lax.dynamic_index_in_dim(local_ends, clipped, 0, keepdims=False)
        layer_in = jnp.where(section_index == 0, own_rows, arrived)
        seg_rows = lax.dynamic_index_in_dim(seg_local, clipped, 0, keepdims=False)
        seg_full = lax.dynamic_index_in_dim(seg_whole, clipped, 0, keepdims=False)
        result, saved_acts = layer_forward(
            layer_in.astype(jnp.float32),
            weights,
            gain_pair,
            seg_rows,
            seg_full,
            query_pos,
            cosine,
            sine_table,
        )
        if tick_num == 0:
            store_bufs = jax.tree.map(
                lambda update: jnp.zeros((micro_count + 1,) + update.shape, update.dtype),
                saved_acts,
            )
        store_bufs = jax.tree.map(
            lambda buffer, update: lax.dynamic_update_index_in_dim(buffer, update, slot_index, 0),
            store_bufs,
            saved_acts,
        )
        outputs = lax.dynamic_update_index_in_dim(outputs, result, slot_index, 0)
        arrived = shifted(result.astype(jnp.bfloat16), "section", 1)
    operand_bufs = None
    gain_sums = jnp.zeros((2, D), jnp.float32)
    arrived_grad = jnp.zeros((tok_rows, D), jnp.bfloat16)
    input_grads = jnp.zeros((micro_count + 1, tok_rows, D), jnp.float32)
    for tick_num in range(micro_count + 1):
        batch_index = tick_num - (1 - section_index)
        is_valid = (batch_index >= 0) & (batch_index < micro_count)
        clipped = jnp.clip(batch_index, 0, micro_count - 1)
        slot_index = jnp.where(is_valid, batch_index, micro_count)
        own_rows = lax.dynamic_index_in_dim(local_ends, clipped, 0, keepdims=False)
        incoming = jnp.where(section_index == 1, own_rows, arrived_grad)
        incoming = jnp.where(is_valid, incoming, jnp.zeros_like(incoming))
        seg_rows = lax.dynamic_index_in_dim(seg_local, clipped, 0, keepdims=False)
        seg_full = lax.dynamic_index_in_dim(seg_whole, clipped, 0, keepdims=False)
        saved_acts = jax.tree.map(
            lambda buffer: lax.dynamic_index_in_dim(buffer, clipped, 0, keepdims=False), store_bufs
        )
        grad_input, operand_pairs, gain_terms = layer_backward(
            incoming,
            saved_acts,
            weights,
            gain_pair,
            seg_rows,
            seg_full,
            query_pos,
            cosine,
            sine_table,
        )
        if tick_num == 0:
            operand_bufs = jax.tree.map(
                lambda update: jnp.zeros((micro_count + 1,) + update.shape, update.dtype),
                operand_pairs,
            )
        operand_bufs = jax.tree.map(
            lambda buffer, update: lax.dynamic_update_index_in_dim(buffer, update, slot_index, 0),
            operand_bufs,
            operand_pairs,
        )
        gain_sums = gain_sums + gain_terms
        input_grads = lax.dynamic_update_index_in_dim(input_grads, grad_input, slot_index, 0)
        arrived_grad = shifted(grad_input.astype(jnp.bfloat16), "section", -1)
    operands = [buffer[:micro_count].reshape(-1, buffer.shape[-1]) for buffer in operand_bufs]
    g_qkv, g_out, g_gate_up, g_down = owned_grads(operands[:4], operands[4:])
    g_gains = lax.psum_scatter(gain_sums, ("ctx", "fsdp"), scatter_dimension=1, tiled=True)
    final_rows = jnp.where(section_index == 0, input_grads[:micro_count], outputs[:micro_count])
    ends_out = final_rows[None, :, None]
    return (ends_out, g_qkv[None], g_out[None], g_gate_up[None], g_down[None], g_gains[None])


def solution(mesh):
    in_specs = (
        P("section", None, "fsdp", "ctx", None),
        P(None, "fsdp", "ctx"),
        P("section", "fsdp", None),
        P("section", "fsdp", None),
        P("section", "fsdp", None),
        P("section", "fsdp", None),
        P("section", None, None),
    )
    out_specs = (
        P("section", None, "fsdp", "ctx", None),
        P("section", ("ctx", "fsdp"), None),
        P("section", ("ctx", "fsdp"), None),
        P("section", ("ctx", "fsdp"), None),
        P("section", ("ctx", "fsdp"), None),
        P("section", None, ("ctx", "fsdp")),
    )
    return jax.shard_map(local, mesh=mesh, in_specs=in_specs, out_specs=out_specs, check_vma=False)
```
